32 devices in a mesh: gx: 8 (over z, x), gy: 4 (over y, core).
Axes of the slice: x: 2, y: 2, z: 4, core: 2. Of those that a mesh axis runs over, the one named last changes fastest.
Arguments:
- source_term: float32 [128, 64, 128], P('gx', 'gy'), may hold values from -24 to 24
- initial_guess: float32 [128, 64, 128], P('gx', 'gy'), may hold values from -6 to 6
- face_x: float32 [128, 64, 128], P('gx', 'gy'), may hold values from 0.2 to 5
- face_y: float32 [128, 64, 128], P('gx', 'gy'), may hold values from 0.2 to 5
- face_z: float32 [128, 64, 128], P('gx', 'gy'), may hold values from 0.2 to 5
Outputs:
- pressure: float32 [128, 64, 128], P('gx', 'gy')
The draws below stay inside these ranges and needn't reach their ends.
All inputs are finite; a program needn't handle non-finite values.
Results may differ from the reference program's by a relative error of at most 0.00002.
Values sent between devices are 32-bit elements; how exact they have to be, the bound alone decides.
No kernel may reach another device: no remote copies, remote signals or barrier semaphores. Data moves between devices by JAX's collectives and lax.ppermute only.
A program may use at most 192 MiB of HBM per device.

```python
import math
import jax
import jax.numpy as jnp
from jax import lax

NZ = 128
LEVELS = 6
NX = 128
NY = 64


def block_scale(rng, extent, pieces, least, high):
    loudness = 1.0
    for axis_at, shards_of in pieces:
        steps = jax.random.uniform(jax.random.fold_in(jax.random.fold_in(rng, 6), axis_at), (shards_of,), jnp.float32, least / len(pieces), high / len(pieces))
        loudness = loudness * jnp.repeat(jnp.exp(steps), extent[axis_at] // shards_of).reshape((-1,) + (1,) * (len(extent) - 1 - axis_at))
    return loudness


def noise(rng, shape, scale, most, pieces=(), kind=jnp.bfloat16):
    gain = block_scale(rng, shape, pieces, -0.22, 0.18) if pieces else 1.0
    array = jax.random.normal(rng, shape, jnp.float32) * scale * gain
    return jnp.minimum(jnp.maximum(array, -most), most).astype(kind)


def setup_inputs(seed: int = 0) -> dict:
    streams_of = jax.random.split(jax.random.key(seed), 6)
    source_term = noise(streams_of[0], (NX, NY, NZ), 4.0, 24.0, ((0, 8), (1, 4)), jnp.float32)
    initial_guess = noise(streams_of[1], (NX, NY, NZ), 1.0, 6.0, ((0, 8), (1, 4)), jnp.float32)
    face_x = jnp.clip(jnp.exp(math.log(5.0) - 3.218876 * jax.random.uniform(streams_of[2], (NX, NY, NZ), jnp.float32) ** block_scale(streams_of[2], (NX, NY, NZ), ((0, 8), (1, 4)), -0.2, 0.2)), 0.2, 5.0)
    face_y = jnp.clip(jnp.exp(math.log(5.0) - 3.218876 * jax.random.uniform(streams_of[3], (NX, NY, NZ), jnp.float32) ** block_scale(streams_of[3], (NX, NY, NZ), ((0, 8), (1, 4)), -0.2, 0.2)), 0.2, 5.0)
    face_z = jnp.clip(jnp.exp(math.log(5.0) - 3.218876 * jax.random.uniform(streams_of[4], (NX, NY, NZ), jnp.float32) ** block_scale(streams_of[4], (NX, NY, NZ), ((0, 8), (1, 4)), -0.2, 0.2)), 0.2, 5.0)
    return {"source_term": source_term, "initial_guess": initial_guess, "face_x": face_x, "face_y": face_y, "face_z": face_z}


OMEGA = 0.8


def stencil(padded, padded_x, padded_y, face_z):
    center = padded[1:-1, 1:-1]
    zero_plane = jnp.zeros(center.shape[:2] + (1,), center.dtype)
    above_face = jnp.concatenate((face_z[:, :, 1:], zero_plane), axis=2)
    below_z = jnp.concatenate((zero_plane, center[:, :, :-1]), axis=2)
    above_z = jnp.concatenate((center[:, :, 1:], zero_plane), axis=2)
    lower_x = padded_x[1:-1, 1:-1]
    upper_x = padded_x[2:, 1:-1]
    lower_y = padded_y[1:-1, 1:-1]
    upper_y = padded_y[1:-1, 2:]
    applied = lower_x * (center - padded[:-2, 1:-1]) + upper_x * (center - padded[2:, 1:-1])
    applied = applied + lower_y * (center - padded[1:-1, :-2]) + upper_y * (center - padded[1:-1, 2:])
    applied = applied + face_z * (center - below_z) + above_face * (center - above_z)
    diagonal = lower_x + upper_x + lower_y + upper_y + face_z + above_face
    return applied, diagonal


def jacobi_sweep(padded, source, padded_x, padded_y, face_z):
    applied, diagonal = stencil(padded, padded_x, padded_y, face_z)
    return padded[1:-1, 1:-1] + OMEGA * (source - applied) / diagonal


def pad_plane(values, width):
    return jnp.pad(values, ((width, width), (width, width), (0, 0)))


def restrict(residual):
    shape = residual.shape
    blocks = residual.reshape(shape[0] // 2, 2, shape[1] // 2, 2, shape[2] // 2, 2)
    return 4.0 * jnp.mean(blocks, axis=(1, 3, 5))


def coarsen_faces(face_x, face_y, face_z):
    shape = face_x.shape
    blocks = (shape[0] // 2, 2, shape[1] // 2, 2, shape[2] // 2, 2)
    coarse_x = jnp.mean(face_x.reshape(blocks)[:, 0], axis=(2, 4))
    coarse_y = jnp.mean(face_y.reshape(blocks)[:, :, :, 0], axis=(1, 4))
    coarse_z = jnp.mean(face_z.reshape(blocks)[..., 0], axis=(1, 3))
    return coarse_x, coarse_y, coarse_z


def prolong(coarse):
    return jnp.repeat(jnp.repeat(jnp.repeat(coarse, 2, axis=0), 2, axis=1), 2, axis=2)


def cycle(grid_level, iterate, source, face_x, face_y, face_z):
    padded_x = pad_plane(face_x, 1)
    padded_y = pad_plane(face_y, 1)
    if grid_level == LEVELS - 1:
        count = 4 * max(iterate.shape[0], iterate.shape[1])

        def one_sweep(index, values):
            return jacobi_sweep(pad_plane(values, 1), source, padded_x, padded_y, face_z)

        return lax.fori_loop(0, count, one_sweep, iterate)
    for sweep_index in range(2):
        iterate = jacobi_sweep(pad_plane(iterate, 1), source, padded_x, padded_y, face_z)
    applied, diagonal = stencil(pad_plane(iterate, 1), padded_x, padded_y, face_z)
    coarse_src = restrict(source - applied)
    coarse_x, coarse_y, coarse_z = coarsen_faces(face_x, face_y, face_z)
    correction = cycle(grid_level + 1, jnp.zeros_like(coarse_src), coarse_src, coarse_x, coarse_y, coarse_z)
    iterate = iterate + prolong(correction)
    for sweep_index in range(2):
        iterate = jacobi_sweep(pad_plane(iterate, 1), source, padded_x, padded_y, face_z)
    return iterate


def reference(source_term, initial_guess, face_x, face_y, face_z):
    return cycle(0, initial_guess, source_term, face_x, face_y, face_z)
```

```python
import functools

import jax
import jax.numpy as jnp
from jax import lax
from jax.experimental import pallas as pl
from jax.experimental.pallas import tpu as pltpu
from jax.sharding import PartitionSpec as P

LEVELS = 6
OMEGA = 0.8
LANES = 128
RIM = 4
PAD = 8
F32 = jnp.float32

V, F, FX, FY, ZL, ZH, W, D, U = range(9)


def lanes_of(shape):
    return lax.broadcasted_iota(jnp.int32, shape, len(shape) - 1)


def rows_of(shape):
    return lax.broadcasted_iota(jnp.int32, shape, len(shape) - 2)


def roll_lanes(values, step):
    return pltpu.roll(values, step % LANES, values.ndim - 1)


def roll_rows(values, step):
    return pltpu.roll(values, step % values.shape[-2], values.ndim - 2)


def exact_dot(left, right):
    return jnp.dot(left, right, precision=lax.Precision.HIGHEST, preferred_element_type=F32)


def compact(depth, part, even_only=False):
    source = lax.broadcasted_iota(jnp.int32, (LANES, LANES), 0)
    target = lax.broadcasted_iota(jnp.int32, (LANES, LANES), 1)
    half = depth // 2
    hit = target == (source // depth * 2 + part) * half + source % depth // 2
    if even_only:
        hit = hit & (source % 2 == 0)
    return jnp.where(hit, 1.0, 0.0).astype(F32)


def expand(depth, part):
    target = lax.broadcasted_iota(jnp.int32, (LANES, LANES), 0)
    source = lax.broadcasted_iota(jnp.int32, (LANES, LANES), 1)
    half = depth // 2
    hit = target == (source // depth * 2 + part) * half + source % depth // 2
    return jnp.where(hit, 1.0, 0.0).astype(F32)


def merge_lanes(values, depth, even_only=False):
    count, rows, _ = values.shape
    half = count // 2
    flat = values.reshape(2, half * rows, LANES)
    out = exact_dot(flat[0], compact(depth, 0, even_only))
    out = out + exact_dot(flat[1], compact(depth, 1, even_only))
    return out.reshape(half, rows, LANES)


def even_rows(ref, rows):
    return ref[:, pl.ds(0, rows // 2, stride=2), :]


def odd_rows(ref, rows):
    return ref[:, pl.ds(1, rows // 2, stride=2), :]


def pack_x(*refs):
    fields, (low, high) = refs[:5], refs[5:]
    for index, ref in enumerate(fields):
        low[index] = ref[:RIM]
        high[index] = ref[ref.shape[0] - RIM :]


def pack_y(*refs):
    fields, (x_low, x_high, low, high) = refs[:5], refs[5:]
    for index, ref in enumerate(fields):
        nx, ny = ref.shape[:2]
        for out, start in ((low, 0), (high, ny - RIM)):
            rows = slice(start, start + RIM)
            out[index, :RIM] = x_low[index, :, rows]
            out[index, RIM : RIM + nx] = ref[:, rows]
            out[index, RIM + nx :] = x_high[index, :, rows]


def pair_slabs(ref):
    count = ref.shape[0]
    values = ref[...].reshape((count // 2, 2) + ref.shape[1:])
    return values[:, 0], values[:, 1]


def coarse_faces(fx, fy, fz, out, tmp):
    rows = fx.shape[1]
    tmp[...] = pair_slabs(fx)[0]
    out[0] = 0.25 * merge_lanes(even_rows(tmp, rows) + odd_rows(tmp, rows), LANES)
    first, second = pair_slabs(fy)
    tmp[...] = first + second
    out[1] = 0.25 * merge_lanes(even_rows(tmp, rows), LANES)
    first, second = pair_slabs(fz)
    tmp[...] = first + second
    out[2] = 0.25 * merge_lanes(even_rows(tmp, rows) + odd_rows(tmp, rows), LANES, True)


def weighted(lev, src, slab, start, rows):
    here = pl.ds(start, rows)
    below = pl.ds(start - 1, rows)
    above = pl.ds(start + 1, rows)
    v = src[slab, here]
    total = lev[F, slab, here] + lev[FX, slab, here] * src[slab - 1, here]
    total = total + lev[FX, slab + 1, here] * src[slab + 1, here]
    total = total + lev[FY, slab, here] * src[slab, below]
    total = total + lev[FY, slab, above] * src[slab, above]
    total = total + lev[ZL, slab, here] * roll_lanes(v, 1)
    total = total + lev[ZH, slab, here] * roll_lanes(v, -1)
    return v, total


def swept(lev, src, slab, start, rows):
    v, total = weighted(lev, src, slab, start, rows)
    return (1.0 - OMEGA) * v + lev[W, slab, pl.ds(start, rows)] * total


def set_weights(lev, slab, start, rows, depth, inside=None):
    here = pl.ds(start, rows)
    fz = lev[ZL, slab, here]
    z = lanes_of(fz.shape) % depth
    upper = jnp.where(z == depth - 1, 0.0, roll_lanes(fz, -1))
    diagonal = lev[FX, slab, here] + lev[FX, slab + 1, here]
    diagonal = diagonal + lev[FY, slab, here] + lev[FY, slab, pl.ds(start + 1, rows)] + fz + upper
    valid = diagonal > 0.0
    if inside is not None:
        valid = valid & inside
    lev[ZL, slab, here] = jnp.where(z == 0, 0.0, fz)
    lev[ZH, slab, here] = upper
    lev[D, slab, here] = diagonal
    lev[W, slab, here] = jnp.where(valid, OMEGA / jnp.where(valid, diagonal, 1.0), 0.0)


def run(count, body, unroll=1):
    def step(index, carry):
        body(index)
        return carry

    lax.fori_loop(0, count, step, 0, unroll=unroll)


def level_down(axes, *refs):
    fields, (x_low, x_high, y_low, y_high, lev, chunk, other, tmp) = refs[:5], refs[5:]
    nx, ny = fields[0].shape[:2]
    slabs, rows = nx + 2 * RIM, ny + 2 * RIM
    me_x, me_y = lax.axis_index(axes[0]), lax.axis_index(axes[1])
    for index, slot in enumerate((F, V, FX, FY, ZL)):
        lev[slot, :, :PAD] = jnp.zeros((slabs, PAD, LANES), F32)
        lev[slot, :, PAD + rows :] = jnp.zeros((slabs, PAD, LANES), F32)
        inner = pl.ds(PAD + RIM, ny)
        lev[slot, :RIM, inner] = x_low[index]
        lev[slot, RIM : RIM + nx, inner] = fields[index][...]
        lev[slot, RIM + nx :, inner] = x_high[index]
        lev[slot, :, PAD : PAD + RIM] = y_low[index]
        lev[slot, :, PAD + RIM + ny : PAD + rows] = y_high[index]
    other[:, :PAD] = jnp.zeros((slabs, PAD, LANES), F32)
    other[:, PAD + rows :] = jnp.zeros((slabs, PAD, LANES), F32)
    row_inside = (rows_of((rows, LANES)) >= RIM) | (me_y > 0)
    main = pl.ds(PAD, rows)

    def first(index):
        slab = index + 1
        inside = row_inside & ((slab >= RIM) | (me_x > 0))
        set_weights(lev, slab, PAD, rows, LANES, inside)
        other[slab, main] = swept(lev, lev.at[V], slab, PAD, rows)

    run(slabs - 2, first, 2)

    def second(index):
        slab = index + 2
        lev[V, slab, main] = swept(lev, other, slab, PAD, rows)

    run(slabs - 4, second, 2)

    def rest(slab):
        v, total = weighted(lev, lev.at[V], slab, PAD + RIM, ny)
        return total - lev[D, slab, pl.ds(PAD + RIM, ny)] * v

    def residual(index):
        slab = RIM + 2 * index
        tmp[index] = rest(slab) + rest(slab + 1)

    run(nx // 2, residual, 2)
    chunk[...] = 0.5 * merge_lanes(even_rows(tmp, ny) + odd_rows(tmp, ny), LANES)


def pair_rows(values, stride):
    return values + roll_rows(values, -stride)


def pair_lanes(values, stride):
    return values + roll_lanes(values, -stride)


class Listed:
    def __init__(self, fx, fy, fz, stride, depth):
        self.fx, self.fy, self.fz, self.stride, self.depth = fx, fy, fz, stride, depth
        shape = fx[0].shape
        rows = shape[0]
        row, lane = rows_of(shape), lanes_of(shape)
        z = lane % depth
        count = self.count = len(fx)
        self.x_high = [
            fx[s + 1] if s + 1 < count else jnp.where(lane < LANES - depth, roll_lanes(fx[0], -depth), 0.0)
            for s in range(count)
        ]
        self.x_low = [fx[s] if s > 0 else jnp.where(lane >= depth, fx[0], 0.0) for s in range(count)]
        self.y_high = [jnp.where(row < rows - stride, roll_rows(f, -stride), 0.0) for f in fy]
        self.y_low = [jnp.where(row >= stride, f, 0.0) for f in fy]
        self.z_high = [jnp.where(z < depth - stride, roll_lanes(f, -stride), 0.0) for f in fz]
        self.z_low = [jnp.where(z >= stride, f, 0.0) for f in fz]
        self.d = [
            fx[s] + self.x_high[s] + fy[s] + self.y_high[s] + fz[s] + self.z_high[s] for s in range(count)
        ]
        self.w = [jnp.where(d > 0.0, OMEGA / jnp.where(d > 0.0, d, 1.0), 0.0) for d in self.d]

    def weighted(self, v, f):
        count = self.count
        out = []
        for s in range(count):
            low = v[s - 1] if s > 0 else roll_lanes(v[count - 1], self.depth)
            high = v[s + 1] if s + 1 < count else roll_lanes(v[0], -self.depth)
            total = f[s] + self.x_low[s] * low + self.x_high[s] * high
            total = total + self.y_low[s] * roll_rows(v[s], self.stride)
            total = total + self.y_high[s] * roll_rows(v[s], -self.stride)
            total = total + self.z_low[s] * roll_lanes(v[s], self.stride)
            total = total + self.z_high[s] * roll_lanes(v[s], -self.stride)
            out.append(total)
        return out

    def sweep(self, v, f):
        totals = self.weighted(v, f)
        return [(1.0 - OMEGA) * v[s] + self.w[s] * totals[s] for s in range(self.count)]

    def start(self, f):
        return [self.w[s] * f[s] for s in range(self.count)]

    def residual(self, v, f):
        totals = self.weighted(v, f)
        return [totals[s] - self.d[s] * v[s] for s in range(self.count)]

    def kept(self):
        shape = self.fx[0].shape
        step = 2 * self.stride
        return (rows_of(shape) % step == 0) & (lanes_of(shape) % step == 0)

    def coarser(self):
        keep, stride = self.kept(), self.stride
        half = range(self.count // 2)

        def kept(values):
            return jnp.where(keep, 0.25 * values, 0.0)

        fx = [kept(pair_lanes(pair_rows(self.fx[2 * s], stride), stride)) for s in half]
        fy = [kept(pair_lanes(self.fy[2 * s] + self.fy[2 * s + 1], stride)) for s in half]
        fz = [kept(pair_rows(self.fz[2 * s] + self.fz[2 * s + 1], stride)) for s in half]
        return Listed(fx, fy, fz, 2 * stride, self.depth)

    def restrict(self, r):
        keep, stride = self.kept(), self.stride
        return [
            jnp.where(keep, 0.5 * pair_lanes(pair_rows(r[2 * s] + r[2 * s + 1], stride), stride), 0.0)
            for s in range(self.count // 2)
        ]

    def prolong(self, e):
        out = []
        for values in e:
            values = values + roll_rows(values, self.stride)
            values = values + roll_lanes(values, self.stride)
            out += [values, values]
        return out


def listed_cycle(levels, sweeps, f):
    level = levels[0]
    v = level.start(f)
    if len(levels) == 1:
        return lax.fori_loop(0, sweeps - 1, lambda index, values: level.sweep(values, f), v)
    v = level.sweep(v, f)
    e = listed_cycle(levels[1:], sweeps, level.restrict(level.residual(v, f)))
    v = [a + b for a, b in zip(v, level.prolong(e))]
    return level.sweep(level.sweep(v, f), f)


def wrap_slabs(ref, count, depth, main):
    first, last = ref[1, main], ref[count, main]
    lane = lanes_of(first.shape)
    ref[0, main] = jnp.where(lane < depth, 0.0, roll_lanes(last, depth))
    ref[count + 1, main] = jnp.where(lane >= LANES - depth, 0.0, roll_lanes(first, -depth))


def level_up(axes, grid, sweeps, top, sources, faces, out, lev, post, tmp, up):
    devices_x, devices_y = grid
    me_x, me_y = lax.axis_index(axes[0]), lax.axis_index(axes[1])
    depth = LANES // 2
    count = lev.shape[1] - 2
    rows = lev.shape[2] - 2 * PAD
    main = pl.ds(PAD, rows)
    parts = sources.shape[1]
    low_lanes = lanes_of((PAD, LANES)) < depth
    for slot in (V, U, FY):
        for start in (0, PAD + rows):
            lev[slot, :, start : start + PAD] = jnp.zeros((count + 2, PAD, LANES), F32)

    def unpack(index):
        for y in range(devices_y):
            here = pl.ds(PAD + y * PAD, PAD)
            near = index * devices_y + y
            far = (index + devices_x // 2) * devices_y + y
            for slot, ref, place in ((F, sources, ()), (FX, faces, (0,)), (FY, faces, (1,)), (ZL, faces, (2,))):
                for part in range(parts):
                    a, b = ref[(near,) + place + (part,)], ref[(far,) + place + (part,)]
                    slab = 1 + index * 2 * parts + part
                    lev[slot, slab, here] = jnp.where(low_lanes, a, roll_lanes(b, depth))
                    lev[slot, slab + parts, here] = jnp.where(low_lanes, roll_lanes(a, depth), b)

    run(devices_x // 2, unpack)
    wrap_slabs(lev.at[FX], count, depth, main)

    half = count // 2

    def pairs(slot, combine):
        def pair(index):
            tmp[index] = combine(lev[slot, 1 + 2 * index, main], lev[slot, 2 + 2 * index, main])

        run(half, pair, 2)

    def slabs_of(values):
        return [values[s] for s in range(half // 2)]

    pairs(FX, lambda a, b: a)
    fx = 0.25 * merge_lanes(even_rows(tmp, rows) + odd_rows(tmp, rows), depth)
    pairs(FY, lambda a, b: a + b)
    fy = 0.25 * merge_lanes(even_rows(tmp, rows), depth)
    pairs(ZL, lambda a, b: a + b)
    fz = 0.25 * merge_lanes(even_rows(tmp, rows) + odd_rows(tmp, rows), depth, True)
    levels = [Listed(slabs_of(fx), slabs_of(fy), slabs_of(fz), 1, depth // 2)]
    while len(levels) < LEVELS - 2:
        levels.append(levels[-1].coarser())

    def first(index):
        slab = index + 1
        set_weights(lev, slab, PAD, rows, depth)
        lev[V, slab, main] = lev[W, slab, main] * lev[F, slab, main]

    run(count, first, 2)
    wrap_slabs(lev.at[V], count, depth, main)

    def second(index):
        slab = index + 1
        lev[U, slab, main] = swept(lev, lev.at[V], slab, PAD, rows)

    run(count, second, 2)
    wrap_slabs(lev.at[U], count, depth, main)

    def rest(slab):
        v, total = weighted(lev, lev.at[U], slab, PAD, rows)
        return total - lev[D, slab, main] * v

    def residual(index):
        tmp[index] = rest(1 + 2 * index) + rest(2 + 2 * index)

    run(half, residual)
    coarse = 0.5 * merge_lanes(even_rows(tmp, rows) + odd_rows(tmp, rows), depth)
    e = listed_cycle(levels, sweeps, slabs_of(coarse))

    flat = jnp.stack(e).reshape(half // 2 * rows // 2, LANES)
    for part in range(2):
        fine = exact_dot(flat, expand(depth, part)).reshape(half // 2, rows // 2, LANES)
        for odd in range(2):
            tmp[part * half // 2 : (part + 1) * half // 2, pl.ds(odd, rows // 2, stride=2), :] = fine

    def correct(index):
        for slab in (1 + 2 * index, 2 + 2 * index):
            lev[U, slab, main] = lev[U, slab, main] + tmp[index]

    run(half, correct, 2)
    wrap_slabs(lev.at[U], count, depth, main)

    near = 2 * parts
    base = me_x % (devices_x // 2) * near

    def third(index):
        slab = (base + index - 2 + count) % count + 1
        lev[V, slab, main] = swept(lev, lev.at[U], slab, PAD, rows)

    run(near + 4, third, 2)
    wrap_slabs(lev.at[V], count, depth, main)

    def fourth(index):
        slab = (base + index - 1 + count) % count + 1
        lev[U, slab, main] = swept(lev, lev.at[V], slab, PAD, rows)

    run(near + 2, fourth, 2)
    wrap_slabs(lev.at[U], count, depth, main)

    slabs = near + 2
    nx, ny = out.shape[:2]
    fine_rows = ny + 2 * RIM
    window = ny // 2 + 2 * PAD
    top_row = pl.multiple_of(me_y * (ny // 2), PAD)
    e = lev[U, pl.ds(base, slabs), pl.ds(top_row, window), :]
    side = me_x // (devices_x // 2)
    fine = exact_dot(e.reshape(slabs * window, LANES), expand(LANES, side)).reshape(slabs, window, LANES)
    skip = PAD - RIM // 2
    fine = fine[:, skip : skip + fine_rows // 2]
    for odd in range(2):
        up[:, pl.ds(odd, fine_rows // 2, stride=2), :] = fine
    body = pl.ds(PAD, fine_rows)
    for slot in (0, 1):
        for start in (0, PAD + fine_rows):
            post[slot, :, start : start + PAD] = jnp.zeros((post.shape[1], PAD, LANES), F32)

    def raise_level(index):
        for slab in (RIM - 2 + 2 * index, RIM - 1 + 2 * index):
            post[0, slab, body] = top[V, slab, body] + up[index]

    run(slabs, raise_level, 2)

    def fifth(index):
        slab = RIM - 1 + index
        post[1, slab, body] = swept(top, post.at[0], slab, PAD, fine_rows)

    run(nx + 2, fifth, 2)

    def sixth(index):
        out[index] = swept(top, post.at[1], RIM + index, PAD + RIM, ny)

    run(nx, sixth, 2)


def call(kernel, shapes, scratch=(), **kwargs):
    vmem = pl.BlockSpec(memory_space=pltpu.VMEM)

    def launch(*args):
        return pl.pallas_call(
            kernel,
            out_shape=[jax.ShapeDtypeStruct(shape, F32) for shape in shapes],
            in_specs=[vmem] * len(args),
            out_specs=[vmem] * len(shapes),
            scratch_shapes=[pltpu.VMEM(shape, F32) for shape in scratch],
            compiler_params=pltpu.CompilerParams(vmem_limit_bytes=48 * 2**20),
            **kwargs,
        )(*args)

    return launch


def from_sides(low, high, axis):
    count = lax.axis_size(axis)
    up = [(i, i + 1) for i in range(count - 1)]
    down = [(target, source) for source, target in up]
    return lax.ppermute(high, axis, up), lax.ppermute(low, axis, down)


def gathered(block):
    return lax.all_gather(block, ("gx", "gy"), axis=0, tiled=False)


def fused_cycle(source, guess, face_x, face_y, face_z):
    axes = ("gx", "gy")
    devices_x, devices_y = lax.axis_size("gx"), lax.axis_size("gy")
    nx, ny, nz = source.shape
    fields = (source, guess, face_x, face_y, face_z)
    x_low, x_high = call(pack_x, [(5, RIM, ny, nz)] * 2)(*fields)
    x_low, x_high = from_sides(x_low, x_high, "gx")
    parts = nx // 4
    (faces,) = call(coarse_faces, [(3, parts, ny // 2, LANES)], [(nx // 2, ny, LANES)])(face_x, face_y, face_z)
    faces = gathered(faces)
    slabs, rows = nx + 2 * RIM, ny + 2 * RIM
    y_low, y_high = call(pack_y, [(5, slabs, RIM, nz)] * 2)(*fields, x_low, x_high)
    y_low, y_high = from_sides(y_low, y_high, "gy")
    top, chunk = call(
        functools.partial(level_down, axes),
        [(8, slabs, rows + 2 * PAD, LANES), (parts, ny // 2, LANES)],
        [(slabs, rows + 2 * PAD, LANES), (nx // 2, ny, LANES)],
    )(*fields, x_low, x_high, y_low, y_high)
    sources = gathered(chunk)
    count = devices_x * nx // 4
    rows_1 = devices_y * ny // 2
    coarsest = (devices_x * nx >> LEVELS - 1, devices_y * ny >> LEVELS - 1)
    (out,) = call(
        functools.partial(level_up, axes, (devices_x, devices_y), 4 * max(coarsest)),
        [(nx, ny, nz)],
        [
            (9, count + 2, rows_1 + 2 * PAD, LANES),
            (2, slabs, rows + 2 * PAD, LANES),
            (count // 2, rows_1, LANES),
            (nx // 2 + 2, rows, LANES),
        ],
    )(top, sources, faces)
    return out


def with_halo(block, sides, width):
    for axis, dim in sides:
        count = lax.axis_size(axis)
        forward = [(i, i + 1) for i in range(count - 1)]
        backward = [(target, source) for source, target in forward]
        low = lax.ppermute(
            lax.slice_in_dim(block, block.shape[dim] - width, None, axis=dim), axis, forward
        )
        high = lax.ppermute(lax.slice_in_dim(block, 0, width, axis=dim), axis, backward)
        block = jnp.concatenate([low, block, high], axis=dim)
    return block


def passed_along(block, axis, distance):
    devices = range(lax.axis_size(axis))
    route = [(i - distance, i) for i in devices if i - distance in devices]
    return lax.ppermute(block, axis, route)


def stencil(padded, padded_x, padded_y, face_z):
    center = padded[1:-1, 1:-1]
    zero_plane = jnp.zeros(center.shape[:2] + (1,), center.dtype)
    above_face = jnp.concatenate((face_z[:, :, 1:], zero_plane), axis=2)
    below_z = jnp.concatenate((zero_plane, center[:, :, :-1]), axis=2)
    above_z = jnp.concatenate((center[:, :, 1:], zero_plane), axis=2)
    lower_x = padded_x[1:-1, 1:-1]
    upper_x = padded_x[2:, 1:-1]
    lower_y = padded_y[1:-1, 1:-1]
    upper_y = padded_y[1:-1, 2:]
    applied = lower_x * (center - padded[:-2, 1:-1]) + upper_x * (center - padded[2:, 1:-1])
    applied = (
        applied + lower_y * (center - padded[1:-1, :-2]) + upper_y * (center - padded[1:-1, 2:])
    )
    applied = applied + face_z * (center - below_z) + above_face * (center - above_z)
    diagonal = lower_x + upper_x + lower_y + upper_y + face_z + above_face
    return (applied, diagonal)


def jacobi_sweep(padded, source, padded_x, padded_y, face_z):
    applied, diagonal = stencil(padded, padded_x, padded_y, face_z)
    return padded[1:-1, 1:-1] + OMEGA * (source - applied) / diagonal


def pad_plane(values, width):
    return jnp.pad(values, ((width, width), (width, width), (0, 0)))


def restrict(residual):
    shape = residual.shape
    blocks = residual.reshape(shape[0] // 2, 2, shape[1] // 2, 2, shape[2] // 2, 2)
    return 4.0 * jnp.mean(blocks, axis=(1, 3, 5))


def coarsen_faces(face_x, face_y, face_z):
    shape = face_x.shape
    blocks = (shape[0] // 2, 2, shape[1] // 2, 2, shape[2] // 2, 2)
    coarse_x = jnp.mean(face_x.reshape(blocks)[:, 0], axis=(2, 4))
    coarse_y = jnp.mean(face_y.reshape(blocks)[:, :, :, 0], axis=(1, 4))
    coarse_z = jnp.mean(face_z.reshape(blocks)[..., 0], axis=(1, 3))
    return (coarse_x, coarse_y, coarse_z)


def prolong(coarse):
    return jnp.repeat(jnp.repeat(jnp.repeat(coarse, 2, axis=0), 2, axis=1), 2, axis=2)


def local_cycle(grid_level, iterate, source, face_x, face_y, face_z):
    padded_x = pad_plane(face_x, 1)
    padded_y = pad_plane(face_y, 1)
    if grid_level == LEVELS - 1:
        count = 4 * max(iterate.shape[0], iterate.shape[1])

        def one_sweep(index, values):
            return jacobi_sweep(pad_plane(values, 1), source, padded_x, padded_y, face_z)

        return lax.fori_loop(0, count, one_sweep, iterate)
    for sweep_index in range(2):
        iterate = jacobi_sweep(pad_plane(iterate, 1), source, padded_x, padded_y, face_z)
    applied, diagonal = stencil(pad_plane(iterate, 1), padded_x, padded_y, face_z)
    coarse_src = restrict(source - applied)
    coarse_x, coarse_y, coarse_z = coarsen_faces(face_x, face_y, face_z)
    correction = local_cycle(
        grid_level + 1, jnp.zeros_like(coarse_src), coarse_src, coarse_x, coarse_y, coarse_z
    )
    iterate = iterate + prolong(correction)
    for sweep_index in range(2):
        iterate = jacobi_sweep(pad_plane(iterate, 1), source, padded_x, padded_y, face_z)
    return iterate


def field_rim(iterate):
    return with_halo(iterate, (("gx", 0), ("gy", 1)), 1)


def sweep_pair_narrow(iterate, source, padded_x, padded_y, face_z, zero_start):
    for sweep_index in range(2):
        if sweep_index == 0 and zero_start:
            padded = pad_plane(iterate, 1)
        else:
            padded = field_rim(iterate)
        iterate = jacobi_sweep(padded, source, padded_x, padded_y, face_z)
    return iterate


def descend(grid_level, iterate, source, face_x, face_y, face_z, zero_start, gather_level):
    if grid_level == gather_level:
        pieces = (
            lax.all_gather(source, "gy", axis=1, tiled=True),
            lax.all_gather(face_x, "gy", axis=1, tiled=True),
            lax.all_gather(face_y, "gy", axis=1, tiled=True),
            lax.all_gather(face_z, "gy", axis=1, tiled=True),
        )
        gathered = (
            lax.all_gather(pieces[0], "gx", axis=0, tiled=True),
            lax.all_gather(pieces[1], "gx", axis=0, tiled=True),
            lax.all_gather(pieces[2], "gx", axis=0, tiled=True),
            lax.all_gather(pieces[3], "gx", axis=0, tiled=True),
        )
        correction = local_cycle(
            grid_level,
            jnp.zeros_like(gathered[0]),
            gathered[0],
            gathered[1],
            gathered[2],
            gathered[3],
        )
        start_x = lax.axis_index("gx") * source.shape[0]
        start_y = lax.axis_index("gy") * source.shape[1]
        return lax.dynamic_slice(
            correction, (start_x, start_y, jnp.zeros((), jnp.int32)), source.shape
        )
    next_x = passed_along(face_x[:1], "gx", -1)
    next_y = passed_along(face_y[:, :1], "gy", -1)
    lower_row = jnp.zeros_like(next_x)
    lower_col = jnp.zeros_like(next_y)
    padded_x = jnp.pad(
        jnp.concatenate((lower_row, face_x, next_x), axis=0), ((0, 0), (1, 1), (0, 0))
    )
    padded_y = jnp.pad(
        jnp.concatenate((lower_col, face_y, next_y), axis=1), ((1, 1), (0, 0), (0, 0))
    )

    def smoother(values, starting):
        return sweep_pair_narrow(values, source, padded_x, padded_y, face_z, starting)

    iterate = smoother(iterate, zero_start)
    applied, diagonal = stencil(field_rim(iterate), padded_x, padded_y, face_z)
    coarse_src = restrict(source - applied)
    coarse_x, coarse_y, coarse_z = coarsen_faces(face_x, face_y, face_z)
    correction = descend(
        grid_level + 1,
        jnp.zeros_like(coarse_src),
        coarse_src,
        coarse_x,
        coarse_y,
        coarse_z,
        True,
        gather_level,
    )
    iterate = iterate + prolong(correction)
    return smoother(iterate, False)


def fits(nx, ny, nz, devices_x, devices_y):
    cells = devices_x * nx * devices_y * ny * nz // 8
    return cells <= 2**18 and devices_x % 2 == 0 and (nx, ny, nz) == (16, 16, LANES)


def local(source_term, initial_guess, face_x, face_y, face_z):
    if fits(*source_term.shape, lax.axis_size("gx"), lax.axis_size("gy")):
        return fused_cycle(source_term, initial_guess, face_x, face_y, face_z)
    gather_level = 4
    return descend(0, initial_guess, source_term, face_x, face_y, face_z, False, gather_level)


def solution(mesh):
    placed = (P("gx", "gy", None),) * 5
    return jax.shard_map(
        local, mesh=mesh, in_specs=placed, out_specs=P("gx", "gy", None), check_vma=False
    )
```

```python
import functools

import jax
import jax.numpy as jnp
from jax import lax
from jax.experimental import pallas as pl
from jax.experimental.pallas import tpu as pltpu
from jax.sharding import PartitionSpec as P

LEVELS = 6
OMEGA = 0.8
LANES = 128
RIM = 4
PAD = 8
F32 = jnp.float32

V, F, FX, FY, ZL, ZH, W, D, U = range(9)


def lanes_of(shape):
    return lax.broadcasted_iota(jnp.int32, shape, len(shape) - 1)


def rows_of(shape):
    return lax.broadcasted_iota(jnp.int32, shape, len(shape) - 2)


def roll_lanes(values, step):
    return pltpu.roll(values, step % LANES, values.ndim - 1)


def roll_rows(values, step):
    return pltpu.roll(values, step % values.shape[-2], values.ndim - 2)


def exact_dot(left, right):
    return jnp.dot(left, right, precision=lax.Precision.HIGHEST, preferred_element_type=F32)


def compact(depth, part, even_only=False):
    source = lax.broadcasted_iota(jnp.int32, (LANES, LANES), 0)
    target = lax.broadcasted_iota(jnp.int32, (LANES, LANES), 1)
    half = depth // 2
    hit = target == (source // depth * 2 + part) * half + source % depth // 2
    if even_only:
        hit = hit & (source % 2 == 0)
    return jnp.where(hit, 1.0, 0.0).astype(F32)


def expand(depth, part):
    target = lax.broadcasted_iota(jnp.int32, (LANES, LANES), 0)
    source = lax.broadcasted_iota(jnp.int32, (LANES, LANES), 1)
    half = depth // 2
    hit = target == (source // depth * 2 + part) * half + source % depth // 2
    return jnp.where(hit, 1.0, 0.0).astype(F32)


def merge_lanes(values, depth, even_only=False):
    count, rows, _ = values.shape
    half = count // 2
    flat = values.reshape(2, half * rows, LANES)
    out = exact_dot(flat[0], compact(depth, 0, even_only))
    out = out + exact_dot(flat[1], compact(depth, 1, even_only))
    return out.reshape(half, rows, LANES)


def even_rows(ref, rows):
    return ref[:, pl.ds(0, rows // 2, stride=2), :]


def odd_rows(ref, rows):
    return ref[:, pl.ds(1, rows // 2, stride=2), :]


def pack_x(*refs):
    fields, (own, low, high, done) = refs[:5], refs[5:]
    copies = [pltpu.make_async_copy(ref, own.at[index], done.at[index]) for index, ref in enumerate(fields)]
    for copy in copies:
        copy.start()
    nx = own.shape[1]
    for index, copy in enumerate(copies):
        copy.wait()
        low[index] = own[index, :RIM]
        high[index] = own[index, nx - RIM :]


def pack_y(own, x_low, x_high, low, high):
    count, nx, ny = own.shape[:3]
    for index in range(count):
        for out, start in ((low, 0), (high, ny - RIM)):
            rows = slice(start, start + RIM)
            out[index, :RIM] = x_low[index, :, rows]
            out[index, RIM : RIM + nx] = own[index, :, rows]
            out[index, RIM + nx :] = x_high[index, :, rows]


def pair_slabs(ref):
    count = ref.shape[0]
    values = ref[...].reshape((count // 2, 2) + ref.shape[1:])
    return values[:, 0], values[:, 1]


def coarse_faces(own, out, tmp):
    fx, fy, fz = own.at[2], own.at[3], own.at[4]
    rows = fx.shape[1]
    tmp[...] = pair_slabs(fx)[0]
    out[0] = 0.25 * merge_lanes(even_rows(tmp, rows) + odd_rows(tmp, rows), LANES)
    first, second = pair_slabs(fy)
    tmp[...] = first + second
    out[1] = 0.25 * merge_lanes(even_rows(tmp, rows), LANES)
    first, second = pair_slabs(fz)
    tmp[...] = first + second
    out[2] = 0.25 * merge_lanes(even_rows(tmp, rows) + odd_rows(tmp, rows), LANES, True)


def weighted(lev, src, slab, start, rows):
    here = pl.ds(start, rows)
    below = pl.ds(start - 1, rows)
    above = pl.ds(start + 1, rows)
    v = src[slab, here]
    total = lev[F, slab, here] + lev[FX, slab, here] * src[slab - 1, here]
    total = total + lev[FX, slab + 1, here] * src[slab + 1, here]
    total = total + lev[FY, slab, here] * src[slab, below]
    total = total + lev[FY, slab, above] * src[slab, above]
    total = total + lev[ZL, slab, here] * roll_lanes(v, 1)
    total = total + lev[ZH, slab, here] * roll_lanes(v, -1)
    return v, total


def swept(lev, src, slab, start, rows):
    v, total = weighted(lev, src, slab, start, rows)
    return (1.0 - OMEGA) * v + lev[W, slab, pl.ds(start, rows)] * total


def set_weights(lev, slab, start, rows, depth, inside=None):
    here = pl.ds(start, rows)
    fz = lev[ZL, slab, here]
    z = lanes_of(fz.shape) % depth
    upper = jnp.where(z == depth - 1, 0.0, roll_lanes(fz, -1))
    diagonal = lev[FX, slab, here] + lev[FX, slab + 1, here]
    diagonal = diagonal + lev[FY, slab, here] + lev[FY, slab, pl.ds(start + 1, rows)] + fz + upper
    valid = diagonal > 0.0
    if inside is not None:
        valid = valid & inside
    lev[ZL, slab, here] = jnp.where(z == 0, 0.0, fz)
    lev[ZH, slab, here] = upper
    lev[D, slab, here] = diagonal
    lev[W, slab, here] = jnp.where(valid, OMEGA / jnp.where(valid, diagonal, 1.0), 0.0)


def run(count, body, unroll=1):
    def step(index, carry):
        body(index)
        return carry

    lax.fori_loop(0, count, step, 0, unroll=unroll)


def level_down(axes, *refs):
    own, x_low, x_high, y_low, y_high, lev, chunk, other, tmp = refs
    nx, ny = own.shape[1:3]
    slabs, rows = nx + 2 * RIM, ny + 2 * RIM
    me_x, me_y = lax.axis_index(axes[0]), lax.axis_index(axes[1])
    for index, slot in enumerate((F, V, FX, FY, ZL)):
        lev[slot, :, :PAD] = jnp.zeros((slabs, PAD, LANES), F32)
        lev[slot, :, PAD + rows :] = jnp.zeros((slabs, PAD, LANES), F32)
        inner = pl.ds(PAD + RIM, ny)
        lev[slot, :RIM, inner] = x_low[index]
        lev[slot, RIM : RIM + nx, inner] = own[index]
        lev[slot, RIM + nx :, inner] = x_high[index]
        lev[slot, :, PAD : PAD + RIM] = y_low[index]
        lev[slot, :, PAD + RIM + ny : PAD + rows] = y_high[index]
    other[:, :PAD] = jnp.zeros((slabs, PAD, LANES), F32)
    other[:, PAD + rows :] = jnp.zeros((slabs, PAD, LANES), F32)
    row_inside = (rows_of((rows, LANES)) >= RIM) | (me_y > 0)
    main = pl.ds(PAD, rows)

    def first(index):
        slab = index + 1
        inside = row_inside & ((slab >= RIM) | (me_x > 0))
        set_weights(lev, slab, PAD, rows, LANES, inside)
        other[slab, main] = swept(lev, lev.at[V], slab, PAD, rows)

    run(slabs - 2, first, 2)

    def second(index):
        slab = index + 2
        lev[V, slab, main] = swept(lev, other, slab, PAD, rows)

    run(slabs - 4, second, 2)

    def rest(slab):
        v, total = weighted(lev, lev.at[V], slab, PAD + RIM, ny)
        return total - lev[D, slab, pl.ds(PAD + RIM, ny)] * v

    def residual(index):
        slab = RIM + 2 * index
        tmp[index] = rest(slab) + rest(slab + 1)

    run(nx // 2, residual, 2)
    chunk[...] = 0.5 * merge_lanes(even_rows(tmp, ny) + odd_rows(tmp, ny), LANES)


def pair_rows(values, stride):
    return values + roll_rows(values, -stride)


def pair_lanes(values, stride):
    return values + roll_lanes(values, -stride)


class Listed:
    def __init__(self, fx, fy, fz, stride, depth):
        self.fx, self.fy, self.fz, self.stride, self.depth = fx, fy, fz, stride, depth
        shape = fx[0].shape
        rows = shape[0]
        row, lane = rows_of(shape), lanes_of(shape)
        z = lane % depth
        count = self.count = len(fx)
        self.x_high = [
            fx[s + 1] if s + 1 < count else jnp.where(lane < LANES - depth, roll_lanes(fx[0], -depth), 0.0)
            for s in range(count)
        ]
        self.x_low = [fx[s] if s > 0 else jnp.where(lane >= depth, fx[0], 0.0) for s in range(count)]
        self.y_high = [jnp.where(row < rows - stride, roll_rows(f, -stride), 0.0) for f in fy]
        self.y_low = [jnp.where(row >= stride, f, 0.0) for f in fy]
        self.z_high = [jnp.where(z < depth - stride, roll_lanes(f, -stride), 0.0) for f in fz]
        self.z_low = [jnp.where(z >= stride, f, 0.0) for f in fz]
        self.d = [
            fx[s] + self.x_high[s] + fy[s] + self.y_high[s] + fz[s] + self.z_high[s] for s in range(count)
        ]
        self.w = [jnp.where(d > 0.0, OMEGA / jnp.where(d > 0.0, d, 1.0), 0.0) for d in self.d]

    def weighted(self, v, f):
        count = self.count
        out = []
        for s in range(count):
            low = v[s - 1] if s > 0 else roll_lanes(v[count - 1], self.depth)
            high = v[s + 1] if s + 1 < count else roll_lanes(v[0], -self.depth)
            total = f[s] + self.x_low[s] * low + self.x_high[s] * high
            total = total + self.y_low[s] * roll_rows(v[s], self.stride)
            total = total + self.y_high[s] * roll_rows(v[s], -self.stride)
            total = total + self.z_low[s] * roll_lanes(v[s], self.stride)
            total = total + self.z_high[s] * roll_lanes(v[s], -self.stride)
            out.append(total)
        return out

    def sweep(self, v, f):
        totals = self.weighted(v, f)
        return [(1.0 - OMEGA) * v[s] + self.w[s] * totals[s] for s in range(self.count)]

    def start(self, f):
        return [self.w[s] * f[s] for s in range(self.count)]

    def residual(self, v, f):
        totals = self.weighted(v, f)
        return [totals[s] - self.d[s] * v[s] for s in range(self.count)]

    def kept(self):
        shape = self.fx[0].shape
        step = 2 * self.stride
        return (rows_of(shape) % step == 0) & (lanes_of(shape) % step == 0)

    def coarser(self):
        keep, stride = self.kept(), self.stride
        half = range(self.count // 2)

        def kept(values):
            return jnp.where(keep, 0.25 * values, 0.0)

        fx = [kept(pair_lanes(pair_rows(self.fx[2 * s], stride), stride)) for s in half]
        fy = [kept(pair_lanes(self.fy[2 * s] + self.fy[2 * s + 1], stride)) for s in half]
        fz = [kept(pair_rows(self.fz[2 * s] + self.fz[2 * s + 1], stride)) for s in half]
        return Listed(fx, fy, fz, 2 * stride, self.depth)

    def restrict(self, r):
        keep, stride = self.kept(), self.stride
        return [
            jnp.where(keep, 0.5 * pair_lanes(pair_rows(r[2 * s] + r[2 * s + 1], stride), stride), 0.0)
            for s in range(self.count // 2)
        ]

    def prolong(self, e):
        out = []
        for values in e:
            values = values + roll_rows(values, self.stride)
            values = values + roll_lanes(values, self.stride)
            out += [values, values]
        return out


def listed_cycle(levels, sweeps, f):
    level = levels[0]
    v = level.start(f)
    if len(levels) == 1:
        return lax.fori_loop(0, sweeps - 1, lambda index, values: level.sweep(values, f), v)
    v = level.sweep(v, f)
    e = listed_cycle(levels[1:], sweeps, level.restrict(level.residual(v, f)))
    v = [a + b for a, b in zip(v, level.prolong(e))]
    return level.sweep(level.sweep(v, f), f)


def wrap_slabs(ref, count, depth, main):
    first, last = ref[1, main], ref[count, main]
    lane = lanes_of(first.shape)
    ref[0, main] = jnp.where(lane < depth, 0.0, roll_lanes(last, depth))
    ref[count + 1, main] = jnp.where(lane >= LANES - depth, 0.0, roll_lanes(first, -depth))


def level_up(axes, grid, sweeps, top, sources, faces, out, lev, post, tmp, up):
    devices_x, devices_y = grid
    me_x, me_y = lax.axis_index(axes[0]), lax.axis_index(axes[1])
    depth = LANES // 2
    count = lev.shape[1] - 2
    rows = lev.shape[2] - 2 * PAD
    main = pl.ds(PAD, rows)
    parts = sources.shape[1]
    low_lanes = lanes_of((PAD, LANES)) < depth
    for slot in (V, U, FY):
        for start in (0, PAD + rows):
            lev[slot, :, start : start + PAD] = jnp.zeros((count + 2, PAD, LANES), F32)

    def unpack(index):
        for y in range(devices_y):
            here = pl.ds(PAD + y * PAD, PAD)
            near = index * devices_y + y
            far = (index + devices_x // 2) * devices_y + y
            for slot, ref, place in ((F, sources, ()), (FX, faces, (0,)), (FY, faces, (1,)), (ZL, faces, (2,))):
                for part in range(parts):
                    a, b = ref[(near,) + place + (part,)], ref[(far,) + place + (part,)]
                    slab = 1 + index * 2 * parts + part
                    lev[slot, slab, here] = jnp.where(low_lanes, a, roll_lanes(b, depth))
                    lev[slot, slab + parts, here] = jnp.where(low_lanes, roll_lanes(a, depth), b)

    run(devices_x // 2, unpack)
    wrap_slabs(lev.at[FX], count, depth, main)

    half = count // 2

    def pairs(slot, combine):
        def pair(index):
            tmp[index] = combine(lev[slot, 1 + 2 * index, main], lev[slot, 2 + 2 * index, main])

        run(half, pair, 2)

    def slabs_of(values):
        return [values[s] for s in range(half // 2)]

    pairs(FX, lambda a, b: a)
    fx = 0.25 * merge_lanes(even_rows(tmp, rows) + odd_rows(tmp, rows), depth)
    pairs(FY, lambda a, b: a + b)
    fy = 0.25 * merge_lanes(even_rows(tmp, rows), depth)
    pairs(ZL, lambda a, b: a + b)
    fz = 0.25 * merge_lanes(even_rows(tmp, rows) + odd_rows(tmp, rows), depth, True)
    levels = [Listed(slabs_of(fx), slabs_of(fy), slabs_of(fz), 1, depth // 2)]
    while len(levels) < LEVELS - 2:
        levels.append(levels[-1].coarser())

    def first(index):
        slab = index + 1
        set_weights(lev, slab, PAD, rows, depth)
        lev[V, slab, main] = lev[W, slab, main] * lev[F, slab, main]

    run(count, first, 2)
    wrap_slabs(lev.at[V], count, depth, main)

    def second(index):
        slab = index + 1
        lev[U, slab, main] = swept(lev, lev.at[V], slab, PAD, rows)

    run(count, second, 2)
    wrap_slabs(lev.at[U], count, depth, main)

    def rest(slab):
        v, total = weighted(lev, lev.at[U], slab, PAD, rows)
        return total - lev[D, slab, main] * v

    def residual(index):
        tmp[index] = rest(1 + 2 * index) + rest(2 + 2 * index)

    run(half, residual)
    coarse = 0.5 * merge_lanes(even_rows(tmp, rows) + odd_rows(tmp, rows), depth)
    e = listed_cycle(levels, sweeps, slabs_of(coarse))

    flat = jnp.stack(e).reshape(half // 2 * rows // 2, LANES)
    for part in range(2):
        fine = exact_dot(flat, expand(depth, part)).reshape(half // 2, rows // 2, LANES)
        for odd in range(2):
            tmp[part * half // 2 : (part + 1) * half // 2, pl.ds(odd, rows // 2, stride=2), :] = fine

    def correct(index):
        for slab in (1 + 2 * index, 2 + 2 * index):
            lev[U, slab, main] = lev[U, slab, main] + tmp[index]

    run(half, correct, 2)
    wrap_slabs(lev.at[U], count, depth, main)

    near = 2 * parts
    base = me_x % (devices_x // 2) * near

    def third(index):
        slab = (base + index - 2 + count) % count + 1
        lev[V, slab, main] = swept(lev, lev.at[U], slab, PAD, rows)

    run(near + 4, third, 2)
    wrap_slabs(lev.at[V], count, depth, main)

    def fourth(index):
        slab = (base + index - 1 + count) % count + 1
        lev[U, slab, main] = swept(lev, lev.at[V], slab, PAD, rows)

    run(near + 2, fourth, 2)
    wrap_slabs(lev.at[U], count, depth, main)

    slabs = near + 2
    nx, ny = out.shape[:2]
    fine_rows = ny + 2 * RIM
    window = ny // 2 + 2 * PAD
    top_row = pl.multiple_of(me_y * (ny // 2), PAD)
    e = lev[U, pl.ds(base, slabs), pl.ds(top_row, window), :]
    side = me_x // (devices_x // 2)
    fine = exact_dot(e.reshape(slabs * window, LANES), expand(LANES, side)).reshape(slabs, window, LANES)
    skip = PAD - RIM // 2
    fine = fine[:, skip : skip + fine_rows // 2]
    for odd in range(2):
        up[:, pl.ds(odd, fine_rows // 2, stride=2), :] = fine
    body = pl.ds(PAD, fine_rows)
    for slot in (0, 1):
        for start in (0, PAD + fine_rows):
            post[slot, :, start : start + PAD] = jnp.zeros((post.shape[1], PAD, LANES), F32)

    def raise_level(index):
        for slab in (RIM - 2 + 2 * index, RIM - 1 + 2 * index):
            post[0, slab, body] = top[V, slab, body] + up[index]

    run(slabs, raise_level, 2)

    def fifth(index):
        slab = RIM - 1 + index
        post[1, slab, body] = swept(top, post.at[0], slab, PAD, fine_rows)

    run(nx + 2, fifth, 2)

    def sixth(index):
        out[index] = swept(top, post.at[1], RIM + index, PAD + RIM, ny)

    run(nx, sixth, 2)


def call(kernel, shapes, scratch=(), space=pltpu.VMEM):
    vmem = pl.BlockSpec(memory_space=pltpu.VMEM)

    def launch(*args):
        return pl.pallas_call(
            kernel,
            out_shape=[jax.ShapeDtypeStruct(shape, F32) for shape in shapes],
            in_specs=[pl.BlockSpec(memory_space=space)] * len(args),
            out_specs=[vmem] * len(shapes),
            scratch_shapes=[pltpu.VMEM(s, F32) if isinstance(s, tuple) else s for s in scratch],
            compiler_params=pltpu.CompilerParams(vmem_limit_bytes=24 * 2**20),
        )(*args)

    return launch


def from_sides(low, high, axis):
    count = lax.axis_size(axis)
    up = [(i, i + 1) for i in range(count - 1)]
    down = [(target, source) for source, target in up]
    return lax.ppermute(high, axis, up), lax.ppermute(low, axis, down)


def summed(block):
    count = lax.axis_size("gx") * lax.axis_size("gy")
    index = lax.axis_index("gx") * lax.axis_size("gy") + lax.axis_index("gy")
    zeros = jnp.zeros((count,) + block.shape, block.dtype)
    start = (index,) + (0,) * block.ndim
    return lax.psum(lax.dynamic_update_slice(zeros, block[None], start), ("gx", "gy"))


def handed_out(block):
    for axis in ("gx", "gy"):
        copies = jnp.broadcast_to(block, (lax.axis_size(axis),) + block.shape)
        block = lax.all_to_all(copies, axis, 0, 0)
    block = jnp.swapaxes(block, 0, 1)
    return block.reshape((-1,) + block.shape[2:])


def fused_cycle(*fields):
    axes = ("gx", "gy")
    devices_x, devices_y = lax.axis_size("gx"), lax.axis_size("gy")
    nx, ny, nz = fields[0].shape
    parts = nx // 4
    slabs, rows = nx + 2 * RIM, ny + 2 * RIM
    own, x_low, x_high = call(
        pack_x,
        [(5, nx, ny, nz)] + [(5, RIM, ny, nz)] * 2,
        [pltpu.SemaphoreType.DMA((5,))],
        pl.ANY,
    )(*fields)
    x_low, x_high = from_sides(x_low, x_high, "gx")
    (faces,) = call(coarse_faces, [(3, parts, ny // 2, LANES)], [(nx // 2, ny, LANES)])(own)
    faces = handed_out(faces)
    y_low, y_high = call(pack_y, [(5, slabs, RIM, nz)] * 2)(own, x_low, x_high)
    y_low, y_high = from_sides(y_low, y_high, "gy")
    top, chunk = call(
        functools.partial(level_down, axes),
        [(8, slabs, rows + 2 * PAD, LANES), (parts, ny // 2, LANES)],
        [(slabs, rows + 2 * PAD, LANES), (nx // 2, ny, LANES)],
    )(own, x_low, x_high, y_low, y_high)
    sources = summed(chunk)
    count = devices_x * nx // 4
    rows_1 = devices_y * ny // 2
    coarsest = (devices_x * nx >> LEVELS - 1, devices_y * ny >> LEVELS - 1)
    (out,) = call(
        functools.partial(level_up, axes, (devices_x, devices_y), 4 * max(coarsest)),
        [(nx, ny, nz)],
        [
            (9, count + 2, rows_1 + 2 * PAD, LANES),
            (2, slabs, rows + 2 * PAD, LANES),
            (count // 2, rows_1, LANES),
            (nx // 2 + 2, rows, LANES),
        ],
    )(top, sources, faces)
    return out


def with_halo(block, sides, width):
    for axis, dim in sides:
        count = lax.axis_size(axis)
        forward = [(i, i + 1) for i in range(count - 1)]
        backward = [(target, source) for source, target in forward]
        low = lax.ppermute(
            lax.slice_in_dim(block, block.shape[dim] - width, None, axis=dim), axis, forward
        )
        high = lax.ppermute(lax.slice_in_dim(block, 0, width, axis=dim), axis, backward)
        block = jnp.concatenate([low, block, high], axis=dim)
    return block


def passed_along(block, axis, distance):
    devices = range(lax.axis_size(axis))
    route = [(i - distance, i) for i in devices if i - distance in devices]
    return lax.ppermute(block, axis, route)


def stencil(padded, padded_x, padded_y, face_z):
    center = padded[1:-1, 1:-1]
    zero_plane = jnp.zeros(center.shape[:2] + (1,), center.dtype)
    above_face = jnp.concatenate((face_z[:, :, 1:], zero_plane), axis=2)
    below_z = jnp.concatenate((zero_plane, center[:, :, :-1]), axis=2)
    above_z = jnp.concatenate((center[:, :, 1:], zero_plane), axis=2)
    lower_x = padded_x[1:-1, 1:-1]
    upper_x = padded_x[2:, 1:-1]
    lower_y = padded_y[1:-1, 1:-1]
    upper_y = padded_y[1:-1, 2:]
    applied = lower_x * (center - padded[:-2, 1:-1]) + upper_x * (center - padded[2:, 1:-1])
    applied = (
        applied + lower_y * (center - padded[1:-1, :-2]) + upper_y * (center - padded[1:-1, 2:])
    )
    applied = applied + face_z * (center - below_z) + above_face * (center - above_z)
    diagonal = lower_x + upper_x + lower_y + upper_y + face_z + above_face
    return (applied, diagonal)


def jacobi_sweep(padded, source, padded_x, padded_y, face_z):
    applied, diagonal = stencil(padded, padded_x, padded_y, face_z)
    return padded[1:-1, 1:-1] + OMEGA * (source - applied) / diagonal


def pad_plane(values, width):
    return jnp.pad(values, ((width, width), (width, width), (0, 0)))


def restrict(residual):
    shape = residual.shape
    blocks = residual.reshape(shape[0] // 2, 2, shape[1] // 2, 2, shape[2] // 2, 2)
    return 4.0 * jnp.mean(blocks, axis=(1, 3, 5))


def coarsen_faces(face_x, face_y, face_z):
    shape = face_x.shape
    blocks = (shape[0] // 2, 2, shape[1] // 2, 2, shape[2] // 2, 2)
    coarse_x = jnp.mean(face_x.reshape(blocks)[:, 0], axis=(2, 4))
    coarse_y = jnp.mean(face_y.reshape(blocks)[:, :, :, 0], axis=(1, 4))
    coarse_z = jnp.mean(face_z.reshape(blocks)[..., 0], axis=(1, 3))
    return (coarse_x, coarse_y, coarse_z)


def prolong(coarse):
    return jnp.repeat(jnp.repeat(jnp.repeat(coarse, 2, axis=0), 2, axis=1), 2, axis=2)


def local_cycle(grid_level, iterate, source, face_x, face_y, face_z):
    padded_x = pad_plane(face_x, 1)
    padded_y = pad_plane(face_y, 1)
    if grid_level == LEVELS - 1:
        count = 4 * max(iterate.shape[0], iterate.shape[1])

        def one_sweep(index, values):
            return jacobi_sweep(pad_plane(values, 1), source, padded_x, padded_y, face_z)

        return lax.fori_loop(0, count, one_sweep, iterate)
    for sweep_index in range(2):
        iterate = jacobi_sweep(pad_plane(iterate, 1), source, padded_x, padded_y, face_z)
    applied, diagonal = stencil(pad_plane(iterate, 1), padded_x, padded_y, face_z)
    coarse_src = restrict(source - applied)
    coarse_x, coarse_y, coarse_z = coarsen_faces(face_x, face_y, face_z)
    correction = local_cycle(
        grid_level + 1, jnp.zeros_like(coarse_src), coarse_src, coarse_x, coarse_y, coarse_z
    )
    iterate = iterate + prolong(correction)
    for sweep_index in range(2):
        iterate = jacobi_sweep(pad_plane(iterate, 1), source, padded_x, padded_y, face_z)
    return iterate


def field_rim(iterate):
    return with_halo(iterate, (("gx", 0), ("gy", 1)), 1)


def sweep_pair_narrow(iterate, source, padded_x, padded_y, face_z, zero_start):
    for sweep_index in range(2):
        if sweep_index == 0 and zero_start:
            padded = pad_plane(iterate, 1)
        else:
            padded = field_rim(iterate)
        iterate = jacobi_sweep(padded, source, padded_x, padded_y, face_z)
    return iterate


def descend(grid_level, iterate, source, face_x, face_y, face_z, zero_start, gather_level):
    if grid_level == gather_level:
        pieces = (
            lax.all_gather(source, "gy", axis=1, tiled=True),
            lax.all_gather(face_x, "gy", axis=1, tiled=True),
            lax.all_gather(face_y, "gy", axis=1, tiled=True),
            lax.all_gather(face_z, "gy", axis=1, tiled=True),
        )
        gathered = (
            lax.all_gather(pieces[0], "gx", axis=0, tiled=True),
            lax.all_gather(pieces[1], "gx", axis=0, tiled=True),
            lax.all_gather(pieces[2], "gx", axis=0, tiled=True),
            lax.all_gather(pieces[3], "gx", axis=0, tiled=True),
        )
        correction = local_cycle(
            grid_level,
            jnp.zeros_like(gathered[0]),
            gathered[0],
            gathered[1],
            gathered[2],
            gathered[3],
        )
        start_x = lax.axis_index("gx") * source.shape[0]
        start_y = lax.axis_index("gy") * source.shape[1]
        return lax.dynamic_slice(
            correction, (start_x, start_y, jnp.zeros((), jnp.int32)), source.shape
        )
    next_x = passed_along(face_x[:1], "gx", -1)
    next_y = passed_along(face_y[:, :1], "gy", -1)
    lower_row = jnp.zeros_like(next_x)
    lower_col = jnp.zeros_like(next_y)
    padded_x = jnp.pad(
        jnp.concatenate((lower_row, face_x, next_x), axis=0), ((0, 0), (1, 1), (0, 0))
    )
    padded_y = jnp.pad(
        jnp.concatenate((lower_col, face_y, next_y), axis=1), ((1, 1), (0, 0), (0, 0))
    )

    def smoother(values, starting):
        return sweep_pair_narrow(values, source, padded_x, padded_y, face_z, starting)

    iterate = smoother(iterate, zero_start)
    applied, diagonal = stencil(field_rim(iterate), padded_x, padded_y, face_z)
    coarse_src = restrict(source - applied)
    coarse_x, coarse_y, coarse_z = coarsen_faces(face_x, face_y, face_z)
    correction = descend(
        grid_level + 1,
        jnp.zeros_like(coarse_src),
        coarse_src,
        coarse_x,
        coarse_y,
        coarse_z,
        True,
        gather_level,
    )
    iterate = iterate + prolong(correction)
    return smoother(iterate, False)


def fits(nx, ny, nz, devices_x, devices_y):
    cells = devices_x * nx * devices_y * ny * nz // 8
    return cells <= 2**18 and devices_x % 2 == 0 and (nx, ny, nz) == (16, 16, LANES)


def local(source_term, initial_guess, face_x, face_y, face_z):
    if fits(*source_term.shape, lax.axis_size("gx"), lax.axis_size("gy")):
        return fused_cycle(source_term, initial_guess, face_x, face_y, face_z)
    gather_level = 4
    return descend(0, initial_guess, source_term, face_x, face_y, face_z, False, gather_level)


def solution(mesh):
    placed = (P("gx", "gy", None),) * 5
    return jax.shard_map(
        local, mesh=mesh, in_specs=placed, out_specs=P("gx", "gy", None), check_vma=False
    )
```

```python
import functools

import jax
import jax.numpy as jnp
from jax import lax
from jax.experimental import pallas as pl
from jax.experimental.pallas import tpu as pltpu
from jax.sharding import PartitionSpec as P

LEVELS = 6
OMEGA = 0.8
LANES = 128
RIM = 4
PAD = 8
F32 = jnp.float32

V, F, FX, FY, ZL, ZH, W, D, U = range(9)


def lanes_of(shape):
    return lax.broadcasted_iota(jnp.int32, shape, len(shape) - 1)


def rows_of(shape):
    return lax.broadcasted_iota(jnp.int32, shape, len(shape) - 2)


def roll_lanes(values, step):
    return pltpu.roll(values, step % LANES, values.ndim - 1)


def roll_rows(values, step):
    return pltpu.roll(values, step % values.shape[-2], values.ndim - 2)


def exact_dot(left, right):
    return jnp.dot(left, right, precision=lax.Precision.HIGHEST, preferred_element_type=F32)


def compact(depth, part, even_only=False):
    source = lax.broadcasted_iota(jnp.int32, (LANES, LANES), 0)
    target = lax.broadcasted_iota(jnp.int32, (LANES, LANES), 1)
    half = depth // 2
    hit = target == (source // depth * 2 + part) * half + source % depth // 2
    if even_only:
        hit = hit & (source % 2 == 0)
    return jnp.where(hit, 1.0, 0.0).astype(F32)


def expand(depth, part):
    target = lax.broadcasted_iota(jnp.int32, (LANES, LANES), 0)
    source = lax.broadcasted_iota(jnp.int32, (LANES, LANES), 1)
    half = depth // 2
    hit = target == (source // depth * 2 + part) * half + source % depth // 2
    return jnp.where(hit, 1.0, 0.0).astype(F32)


def merge_lanes(values, depth, even_only=False):
    count, rows, _ = values.shape
    half = count // 2
    flat = values.reshape(2, half * rows, LANES)
    out = exact_dot(flat[0], compact(depth, 0, even_only))
    out = out + exact_dot(flat[1], compact(depth, 1, even_only))
    return out.reshape(half, rows, LANES)


def even_rows(ref, rows):
    return ref[:, pl.ds(0, rows // 2, stride=2), :]


def odd_rows(ref, rows):
    return ref[:, pl.ds(1, rows // 2, stride=2), :]


def pack_x(*refs):
    fields, (own, low, high, done) = refs[:5], refs[5:]
    copies = [pltpu.make_async_copy(ref, own.at[index], done.at[index]) for index, ref in enumerate(fields)]
    for copy in copies:
        copy.start()
    nx = own.shape[1]
    for index, copy in enumerate(copies):
        copy.wait()
        low[index] = own[index, :RIM]
        high[index] = own[index, nx - RIM :]


def pack_y(own, x_low, x_high, low, high):
    count, nx, ny = own.shape[:3]
    for index in range(count):
        for out, start in ((low, 0), (high, ny - RIM)):
            rows = slice(start, start + RIM)
            out[index, :RIM] = x_low[index, :, rows]
            out[index, RIM : RIM + nx] = own[index, :, rows]
            out[index, RIM + nx :] = x_high[index, :, rows]


def pair_slabs(ref):
    count = ref.shape[0]
    values = ref[...].reshape((count // 2, 2) + ref.shape[1:])
    return values[:, 0], values[:, 1]


def coarse_faces(own, out, tmp):
    fx, fy, fz = own.at[2], own.at[3], own.at[4]
    rows = fx.shape[1]
    tmp[...] = pair_slabs(fx)[0]
    out[0] = 0.25 * merge_lanes(even_rows(tmp, rows) + odd_rows(tmp, rows), LANES)
    first, second = pair_slabs(fy)
    tmp[...] = first + second
    out[1] = 0.25 * merge_lanes(even_rows(tmp, rows), LANES)
    first, second = pair_slabs(fz)
    tmp[...] = first + second
    out[2] = 0.25 * merge_lanes(even_rows(tmp, rows) + odd_rows(tmp, rows), LANES, True)


def weighted(lev, src, slab, start, rows):
    here = pl.ds(start, rows)
    below = pl.ds(start - 1, rows)
    above = pl.ds(start + 1, rows)
    v = src[slab, here]
    total = lev[F, slab, here] + lev[FX, slab, here] * src[slab - 1, here]
    total = total + lev[FX, slab + 1, here] * src[slab + 1, here]
    total = total + lev[FY, slab, here] * src[slab, below]
    total = total + lev[FY, slab, above] * src[slab, above]
    total = total + lev[ZL, slab, here] * roll_lanes(v, 1)
    total = total + lev[ZH, slab, here] * roll_lanes(v, -1)
    return v, total


def swept(lev, src, slab, start, rows):
    v, total = weighted(lev, src, slab, start, rows)
    return (1.0 - OMEGA) * v + lev[W, slab, pl.ds(start, rows)] * total


def set_weights(lev, slab, start, rows, depth, inside=None):
    here = pl.ds(start, rows)
    fz = lev[ZL, slab, here]
    z = lanes_of(fz.shape) % depth
    upper = jnp.where(z == depth - 1, 0.0, roll_lanes(fz, -1))
    diagonal = lev[FX, slab, here] + lev[FX, slab + 1, here]
    diagonal = diagonal + lev[FY, slab, here] + lev[FY, slab, pl.ds(start + 1, rows)] + fz + upper
    valid = diagonal > 0.0
    if inside is not None:
        valid = valid & inside
    lev[ZL, slab, here] = jnp.where(z == 0, 0.0, fz)
    lev[ZH, slab, here] = upper
    lev[D, slab, here] = diagonal
    lev[W, slab, here] = jnp.where(valid, OMEGA / jnp.where(valid, diagonal, 1.0), 0.0)


def run(count, body, unroll=1):
    def step(index, carry):
        body(index)
        return carry

    lax.fori_loop(0, count, step, 0, unroll=unroll)


def level_down(axes, *refs):
    own, x_low, x_high, y_low, y_high, top, chunk, lev, other, tmp, done = refs
    nx, ny = own.shape[1:3]
    slabs, rows = nx + 2 * RIM, ny + 2 * RIM
    me_x, me_y = lax.axis_index(axes[0]), lax.axis_index(axes[1])
    for index, slot in enumerate((F, V, FX, FY, ZL)):
        lev[slot, :, :PAD] = jnp.zeros((slabs, PAD, LANES), F32)
        lev[slot, :, PAD + rows :] = jnp.zeros((slabs, PAD, LANES), F32)
        inner = pl.ds(PAD + RIM, ny)
        lev[slot, :RIM, inner] = x_low[index]
        lev[slot, RIM : RIM + nx, inner] = own[index]
        lev[slot, RIM + nx :, inner] = x_high[index]
        lev[slot, :, PAD : PAD + RIM] = y_low[index]
        lev[slot, :, PAD + RIM + ny : PAD + rows] = y_high[index]
    other[:, :PAD] = jnp.zeros((slabs, PAD, LANES), F32)
    other[:, PAD + rows :] = jnp.zeros((slabs, PAD, LANES), F32)
    row_inside = (rows_of((rows, LANES)) >= RIM) | (me_y > 0)
    main = pl.ds(PAD, rows)

    def first(index):
        slab = index + 1
        inside = row_inside & ((slab >= RIM) | (me_x > 0))
        set_weights(lev, slab, PAD, rows, LANES, inside)
        other[slab, main] = swept(lev, lev.at[V], slab, PAD, rows)

    run(slabs - 2, first, 2)
    copies = [pltpu.make_async_copy(lev.at[slot], top.at[slot], done.at[slot]) for slot in range(D)]
    for copy in copies[1:]:
        copy.start()

    def second(index):
        slab = index + 2
        lev[V, slab, main] = swept(lev, other, slab, PAD, rows)

    run(slabs - 4, second, 2)
    copies[0].start()

    def rest(slab):
        v, total = weighted(lev, lev.at[V], slab, PAD + RIM, ny)
        return total - lev[D, slab, pl.ds(PAD + RIM, ny)] * v

    def residual(index):
        slab = RIM + 2 * index
        tmp[index] = rest(slab) + rest(slab + 1)

    run(nx // 2, residual, 2)
    chunk[...] = 0.5 * merge_lanes(even_rows(tmp, ny) + odd_rows(tmp, ny), LANES)
    for copy in copies:
        copy.wait()


def pair_rows(values, stride):
    return values + roll_rows(values, -stride)


def pair_lanes(values, stride):
    return values + roll_lanes(values, -stride)


class Listed:
    def __init__(self, fx, fy, fz, stride, depth):
        self.fx, self.fy, self.fz, self.stride, self.depth = fx, fy, fz, stride, depth
        shape = fx[0].shape
        rows = shape[0]
        row, lane = rows_of(shape), lanes_of(shape)
        z = lane % depth
        count = self.count = len(fx)
        self.x_high = [
            fx[s + 1] if s + 1 < count else jnp.where(lane < LANES - depth, roll_lanes(fx[0], -depth), 0.0)
            for s in range(count)
        ]
        self.x_low = [fx[s] if s > 0 else jnp.where(lane >= depth, fx[0], 0.0) for s in range(count)]
        self.y_high = [jnp.where(row < rows - stride, roll_rows(f, -stride), 0.0) for f in fy]
        self.y_low = [jnp.where(row >= stride, f, 0.0) for f in fy]
        self.z_high = [jnp.where(z < depth - stride, roll_lanes(f, -stride), 0.0) for f in fz]
        self.z_low = [jnp.where(z >= stride, f, 0.0) for f in fz]
        self.d = [
            fx[s] + self.x_high[s] + fy[s] + self.y_high[s] + fz[s] + self.z_high[s] for s in range(count)
        ]
        self.w = [jnp.where(d > 0.0, OMEGA / jnp.where(d > 0.0, d, 1.0), 0.0) for d in self.d]

    def weighted(self, v, f):
        count = self.count
        out = []
        for s in range(count):
            low = v[s - 1] if s > 0 else roll_lanes(v[count - 1], self.depth)
            high = v[s + 1] if s + 1 < count else roll_lanes(v[0], -self.depth)
            total = f[s] + self.x_low[s] * low + self.x_high[s] * high
            total = total + self.y_low[s] * roll_rows(v[s], self.stride)
            total = total + self.y_high[s] * roll_rows(v[s], -self.stride)
            total = total + self.z_low[s] * roll_lanes(v[s], self.stride)
            total = total + self.z_high[s] * roll_lanes(v[s], -self.stride)
            out.append(total)
        return out

    def sweep(self, v, f):
        totals = self.weighted(v, f)
        return [(1.0 - OMEGA) * v[s] + self.w[s] * totals[s] for s in range(self.count)]

    def start(self, f):
        return [self.w[s] * f[s] for s in range(self.count)]

    def residual(self, v, f):
        totals = self.weighted(v, f)
        return [totals[s] - self.d[s] * v[s] for s in range(self.count)]

    def kept(self):
        shape = self.fx[0].shape
        step = 2 * self.stride
        return (rows_of(shape) % step == 0) & (lanes_of(shape) % step == 0)

    def coarser(self):
        keep, stride = self.kept(), self.stride
        half = range(self.count // 2)

        def kept(values):
            return jnp.where(keep, 0.25 * values, 0.0)

        fx = [kept(pair_lanes(pair_rows(self.fx[2 * s], stride), stride)) for s in half]
        fy = [kept(pair_lanes(self.fy[2 * s] + self.fy[2 * s + 1], stride)) for s in half]
        fz = [kept(pair_rows(self.fz[2 * s] + self.fz[2 * s + 1], stride)) for s in half]
        return Listed(fx, fy, fz, 2 * stride, self.depth)

    def restrict(self, r):
        keep, stride = self.kept(), self.stride
        return [
            jnp.where(keep, 0.5 * pair_lanes(pair_rows(r[2 * s] + r[2 * s + 1], stride), stride), 0.0)
            for s in range(self.count // 2)
        ]

    def prolong(self, e):
        out = []
        for values in e:
            values = values + roll_rows(values, self.stride)
            values = values + roll_lanes(values, self.stride)
            out += [values, values]
        return out


def listed_cycle(levels, sweeps, f):
    level = levels[0]
    v = level.start(f)
    if len(levels) == 1:
        return lax.fori_loop(0, sweeps - 1, lambda index, values: level.sweep(values, f), v)
    v = level.sweep(v, f)
    e = listed_cycle(levels[1:], sweeps, level.restrict(level.residual(v, f)))
    v = [a + b for a, b in zip(v, level.prolong(e))]
    return level.sweep(level.sweep(v, f), f)


def wrap_slabs(ref, count, depth, main):
    first, last = ref[1, main], ref[count, main]
    lane = lanes_of(first.shape)
    ref[0, main] = jnp.where(lane < depth, 0.0, roll_lanes(last, depth))
    ref[count + 1, main] = jnp.where(lane >= LANES - depth, 0.0, roll_lanes(first, -depth))


def level_up(axes, grid, sweeps, sources, faces, stored, out, lev, top, post, tmp, up, done):
    devices_x, devices_y = grid
    fetch = pltpu.make_async_copy(stored, top, done.at[0])
    fetch.start()
    me_x, me_y = lax.axis_index(axes[0]), lax.axis_index(axes[1])
    depth = LANES // 2
    count = lev.shape[1] - 2
    rows = lev.shape[2] - 2 * PAD
    main = pl.ds(PAD, rows)
    parts = sources.shape[2]
    low_lanes = lanes_of((PAD, LANES)) < depth
    for slot in (V, U, FY):
        for start in (0, PAD + rows):
            lev[slot, :, start : start + PAD] = jnp.zeros((count + 2, PAD, LANES), F32)

    def unpack(index):
        for y in range(devices_y):
            here = pl.ds(PAD + y * PAD, PAD)
            near, far = index, index + devices_x // 2

            def place(slot, part, a, b):
                slab = 1 + index * 2 * parts + part
                lev[slot, slab, here] = jnp.where(low_lanes, a, roll_lanes(b, depth))
                lev[slot, slab + parts, here] = jnp.where(low_lanes, roll_lanes(a, depth), b)

            for part in range(parts):
                place(F, part, sources[y, near, part], sources[y, far, part])
                a = (me_x - near + devices_x) % devices_x
                b = (me_x - far + devices_x) % devices_x
                for face, slot in enumerate((FX, FY, ZL)):
                    place(slot, part, faces[y, a, face, part], faces[y, b, face, part])

    run(devices_x // 2, unpack)
    wrap_slabs(lev.at[FX], count, depth, main)

    half = count // 2

    def pairs(slot, combine):
        def pair(index):
            tmp[index] = combine(lev[slot, 1 + 2 * index, main], lev[slot, 2 + 2 * index, main])

        run(half, pair, 2)

    def slabs_of(values):
        return [values[s] for s in range(half // 2)]

    pairs(FX, lambda a, b: a)
    fx = 0.25 * merge_lanes(even_rows(tmp, rows) + odd_rows(tmp, rows), depth)
    pairs(FY, lambda a, b: a + b)
    fy = 0.25 * merge_lanes(even_rows(tmp, rows), depth)
    pairs(ZL, lambda a, b: a + b)
    fz = 0.25 * merge_lanes(even_rows(tmp, rows) + odd_rows(tmp, rows), depth, True)
    levels = [Listed(slabs_of(fx), slabs_of(fy), slabs_of(fz), 1, depth // 2)]
    while len(levels) < LEVELS - 2:
        levels.append(levels[-1].coarser())

    def first(index):
        slab = index + 1
        set_weights(lev, slab, PAD, rows, depth)
        lev[V, slab, main] = lev[W, slab, main] * lev[F, slab, main]

    run(count, first, 2)
    wrap_slabs(lev.at[V], count, depth, main)

    def second(index):
        slab = index + 1
        lev[U, slab, main] = swept(lev, lev.at[V], slab, PAD, rows)

    run(count, second, 2)
    wrap_slabs(lev.at[U], count, depth, main)

    def rest(slab):
        v, total = weighted(lev, lev.at[U], slab, PAD, rows)
        return total - lev[D, slab, main] * v

    def residual(index):
        tmp[index] = rest(1 + 2 * index) + rest(2 + 2 * index)

    run(half, residual)
    coarse = 0.5 * merge_lanes(even_rows(tmp, rows) + odd_rows(tmp, rows), depth)
    e = listed_cycle(levels, sweeps, slabs_of(coarse))

    flat = jnp.stack(e).reshape(half // 2 * rows // 2, LANES)
    for part in range(2):
        fine = exact_dot(flat, expand(depth, part)).reshape(half // 2, rows // 2, LANES)
        for odd in range(2):
            tmp[part * half // 2 : (part + 1) * half // 2, pl.ds(odd, rows // 2, stride=2), :] = fine

    def correct(index):
        for slab in (1 + 2 * index, 2 + 2 * index):
            lev[U, slab, main] = lev[U, slab, main] + tmp[index]

    run(half, correct, 2)
    wrap_slabs(lev.at[U], count, depth, main)

    near = 2 * parts
    base = me_x % (devices_x // 2) * near

    def third(index):
        slab = (base + index - 2 + count) % count + 1
        lev[V, slab, main] = swept(lev, lev.at[U], slab, PAD, rows)

    run(near + 4, third, 2)
    wrap_slabs(lev.at[V], count, depth, main)

    def fourth(index):
        slab = (base + index - 1 + count) % count + 1
        lev[U, slab, main] = swept(lev, lev.at[V], slab, PAD, rows)

    run(near + 2, fourth, 2)
    wrap_slabs(lev.at[U], count, depth, main)

    slabs = near + 2
    nx, ny = out.shape[:2]
    fine_rows = ny + 2 * RIM
    window = ny // 2 + 2 * PAD
    top_row = pl.multiple_of(me_y * (ny // 2), PAD)
    e = lev[U, pl.ds(base, slabs), pl.ds(top_row, window), :]
    side = me_x // (devices_x // 2)
    fine = exact_dot(e.reshape(slabs * window, LANES), expand(LANES, side)).reshape(slabs, window, LANES)
    skip = PAD - RIM // 2
    fine = fine[:, skip : skip + fine_rows // 2]
    for odd in range(2):
        up[:, pl.ds(odd, fine_rows // 2, stride=2), :] = fine
    body = pl.ds(PAD, fine_rows)
    fetch.wait()
    for slot in (0, 1):
        for start in (0, PAD + fine_rows):
            post[slot, :, start : start + PAD] = jnp.zeros((post.shape[1], PAD, LANES), F32)

    def raise_level(index):
        for slab in (RIM - 2 + 2 * index, RIM - 1 + 2 * index):
            post[0, slab, body] = top[V, slab, body] + up[index]

    run(slabs, raise_level, 2)

    def fifth(index):
        slab = RIM - 1 + index
        post[1, slab, body] = swept(top, post.at[0], slab, PAD, fine_rows)

    run(nx + 2, fifth, 2)

    def sixth(index):
        out[index] = swept(top, post.at[1], RIM + index, PAD + RIM, ny)

    run(nx, sixth, 2)


IN_VMEM = pl.BlockSpec(memory_space=pltpu.VMEM)
ANYWHERE = pl.BlockSpec(memory_space=pl.ANY)


def call(kernel, ins, outs, scratch=(), limit=24 * 2**20):
    def launch(*args):
        return pl.pallas_call(
            kernel,
            out_shape=[jax.ShapeDtypeStruct(shape, F32) for shape, _ in outs],
            in_specs=ins,
            out_specs=[spec for _, spec in outs],
            scratch_shapes=[pltpu.VMEM(s, F32) if isinstance(s, tuple) else s for s in scratch],
            compiler_params=pltpu.CompilerParams(vmem_limit_bytes=limit),
        )(*args)

    return launch


def from_sides(low, high, axis):
    count = lax.axis_size(axis)
    up = [(i, i + 1) for i in range(count - 1)]
    down = [(target, source) for source, target in up]
    return lax.ppermute(high, axis, up), lax.ppermute(low, axis, down)


def handed_out(block, axis):
    copies = jnp.broadcast_to(block, (lax.axis_size(axis),) + block.shape)
    return lax.all_to_all(copies, axis, 0, 0)


def passed_round(block, axis):
    count = lax.axis_size(axis)
    blocks = [block]
    for distance in range(1, count):
        blocks.append(lax.ppermute(block, axis, [(i, (i + distance) % count) for i in range(count)]))
    return jnp.stack(blocks)


def fused_cycle(*fields):
    axes = ("gx", "gy")
    devices_x, devices_y = lax.axis_size("gx"), lax.axis_size("gy")
    nx, ny, nz = fields[0].shape
    parts = nx // 4
    slabs, rows = nx + 2 * RIM, ny + 2 * RIM
    own, x_low, x_high = call(
        pack_x,
        [ANYWHERE] * 5,
        [((5, nx, ny, nz), IN_VMEM), ((5, RIM, ny, nz), IN_VMEM), ((5, RIM, ny, nz), IN_VMEM)],
        [pltpu.SemaphoreType.DMA((5,))],
        None,
    )(*fields)
    x_low, x_high = from_sides(x_low, x_high, "gx")
    (faces,) = call(
        coarse_faces, [IN_VMEM], [((3, parts, ny // 2, LANES), IN_VMEM)], [(nx // 2, ny, LANES)]
    )(own)
    faces = handed_out(passed_round(faces, "gx"), "gy")
    y_low, y_high = call(pack_y, [IN_VMEM] * 3, [((5, slabs, RIM, nz), IN_VMEM)] * 2)(own, x_low, x_high)
    y_low, y_high = from_sides(y_low, y_high, "gy")
    stack = (slabs, rows + 2 * PAD, LANES)
    top, chunk = call(
        functools.partial(level_down, axes),
        [IN_VMEM] * 5,
        [((D,) + stack, ANYWHERE), ((parts, ny // 2, LANES), IN_VMEM)],
        [(D + 1,) + stack, stack, (nx // 2, ny, LANES), pltpu.SemaphoreType.DMA((D,))],
    )(own, x_low, x_high, y_low, y_high)
    sources = handed_out(handed_out(chunk, "gx"), "gy")
    count = devices_x * nx // 4
    rows_1 = devices_y * ny // 2
    coarsest = (devices_x * nx >> LEVELS - 1, devices_y * ny >> LEVELS - 1)
    (out,) = call(
        functools.partial(level_up, axes, (devices_x, devices_y), 4 * max(coarsest)),
        [IN_VMEM, IN_VMEM, ANYWHERE],
        [((nx, ny, nz), IN_VMEM)],
        [
            (9, count + 2, rows_1 + 2 * PAD, LANES),
            (D,) + stack,
            (2,) + stack,
            (count // 2, rows_1, LANES),
            (nx // 2 + 2, rows, LANES),
            pltpu.SemaphoreType.DMA((1,)),
        ],
    )(sources, faces, top)
    return out


def with_halo(block, sides, width):
    for axis, dim in sides:
        count = lax.axis_size(axis)
        forward = [(i, i + 1) for i in range(count - 1)]
        backward = [(target, source) for source, target in forward]
        low = lax.ppermute(
            lax.slice_in_dim(block, block.shape[dim] - width, None, axis=dim), axis, forward
        )
        high = lax.ppermute(lax.slice_in_dim(block, 0, width, axis=dim), axis, backward)
        block = jnp.concatenate([low, block, high], axis=dim)
    return block


def passed_along(block, axis, distance):
    devices = range(lax.axis_size(axis))
    route = [(i - distance, i) for i in devices if i - distance in devices]
    return lax.ppermute(block, axis, route)


def stencil(padded, padded_x, padded_y, face_z):
    center = padded[1:-1, 1:-1]
    zero_plane = jnp.zeros(center.shape[:2] + (1,), center.dtype)
    above_face = jnp.concatenate((face_z[:, :, 1:], zero_plane), axis=2)
    below_z = jnp.concatenate((zero_plane, center[:, :, :-1]), axis=2)
    above_z = jnp.concatenate((center[:, :, 1:], zero_plane), axis=2)
    lower_x = padded_x[1:-1, 1:-1]
    upper_x = padded_x[2:, 1:-1]
    lower_y = padded_y[1:-1, 1:-1]
    upper_y = padded_y[1:-1, 2:]
    applied = lower_x * (center - padded[:-2, 1:-1]) + upper_x * (center - padded[2:, 1:-1])
    applied = (
        applied + lower_y * (center - padded[1:-1, :-2]) + upper_y * (center - padded[1:-1, 2:])
    )
    applied = applied + face_z * (center - below_z) + above_face * (center - above_z)
    diagonal = lower_x + upper_x + lower_y + upper_y + face_z + above_face
    return (applied, diagonal)


def jacobi_sweep(padded, source, padded_x, padded_y, face_z):
    applied, diagonal = stencil(padded, padded_x, padded_y, face_z)
    return padded[1:-1, 1:-1] + OMEGA * (source - applied) / diagonal


def pad_plane(values, width):
    return jnp.pad(values, ((width, width), (width, width), (0, 0)))


def restrict(residual):
    shape = residual.shape
    blocks = residual.reshape(shape[0] // 2, 2, shape[1] // 2, 2, shape[2] // 2, 2)
    return 4.0 * jnp.mean(blocks, axis=(1, 3, 5))


def coarsen_faces(face_x, face_y, face_z):
    shape = face_x.shape
    blocks = (shape[0] // 2, 2, shape[1] // 2, 2, shape[2] // 2, 2)
    coarse_x = jnp.mean(face_x.reshape(blocks)[:, 0], axis=(2, 4))
    coarse_y = jnp.mean(face_y.reshape(blocks)[:, :, :, 0], axis=(1, 4))
    coarse_z = jnp.mean(face_z.reshape(blocks)[..., 0], axis=(1, 3))
    return (coarse_x, coarse_y, coarse_z)


def prolong(coarse):
    return jnp.repeat(jnp.repeat(jnp.repeat(coarse, 2, axis=0), 2, axis=1), 2, axis=2)


def local_cycle(grid_level, iterate, source, face_x, face_y, face_z):
    padded_x = pad_plane(face_x, 1)
    padded_y = pad_plane(face_y, 1)
    if grid_level == LEVELS - 1:
        count = 4 * max(iterate.shape[0], iterate.shape[1])

        def one_sweep(index, values):
            return jacobi_sweep(pad_plane(values, 1), source, padded_x, padded_y, face_z)

        return lax.fori_loop(0, count, one_sweep, iterate)
    for sweep_index in range(2):
        iterate = jacobi_sweep(pad_plane(iterate, 1), source, padded_x, padded_y, face_z)
    applied, diagonal = stencil(pad_plane(iterate, 1), padded_x, padded_y, face_z)
    coarse_src = restrict(source - applied)
    coarse_x, coarse_y, coarse_z = coarsen_faces(face_x, face_y, face_z)
    correction = local_cycle(
        grid_level + 1, jnp.zeros_like(coarse_src), coarse_src, coarse_x, coarse_y, coarse_z
    )
    iterate = iterate + prolong(correction)
    for sweep_index in range(2):
        iterate = jacobi_sweep(pad_plane(iterate, 1), source, padded_x, padded_y, face_z)
    return iterate


def field_rim(iterate):
    return with_halo(iterate, (("gx", 0), ("gy", 1)), 1)


def sweep_pair_narrow(iterate, source, padded_x, padded_y, face_z, zero_start):
    for sweep_index in range(2):
        if sweep_index == 0 and zero_start:
            padded = pad_plane(iterate, 1)
        else:
            padded = field_rim(iterate)
        iterate = jacobi_sweep(padded, source, padded_x, padded_y, face_z)
    return iterate


def descend(grid_level, iterate, source, face_x, face_y, face_z, zero_start, gather_level):
    if grid_level == gather_level:
        pieces = (
            lax.all_gather(source, "gy", axis=1, tiled=True),
            lax.all_gather(face_x, "gy", axis=1, tiled=True),
            lax.all_gather(face_y, "gy", axis=1, tiled=True),
            lax.all_gather(face_z, "gy", axis=1, tiled=True),
        )
        gathered = (
            lax.all_gather(pieces[0], "gx", axis=0, tiled=True),
            lax.all_gather(pieces[1], "gx", axis=0, tiled=True),
            lax.all_gather(pieces[2], "gx", axis=0, tiled=True),
            lax.all_gather(pieces[3], "gx", axis=0, tiled=True),
        )
        correction = local_cycle(
            grid_level,
            jnp.zeros_like(gathered[0]),
            gathered[0],
            gathered[1],
            gathered[2],
            gathered[3],
        )
        start_x = lax.axis_index("gx") * source.shape[0]
        start_y = lax.axis_index("gy") * source.shape[1]
        return lax.dynamic_slice(
            correction, (start_x, start_y, jnp.zeros((), jnp.int32)), source.shape
        )
    next_x = passed_along(face_x[:1], "gx", -1)
    next_y = passed_along(face_y[:, :1], "gy", -1)
    lower_row = jnp.zeros_like(next_x)
    lower_col = jnp.zeros_like(next_y)
    padded_x = jnp.pad(
        jnp.concatenate((lower_row, face_x, next_x), axis=0), ((0, 0), (1, 1), (0, 0))
    )
    padded_y = jnp.pad(
        jnp.concatenate((lower_col, face_y, next_y), axis=1), ((1, 1), (0, 0), (0, 0))
    )

    def smoother(values, starting):
        return sweep_pair_narrow(values, source, padded_x, padded_y, face_z, starting)

    iterate = smoother(iterate, zero_start)
    applied, diagonal = stencil(field_rim(iterate), padded_x, padded_y, face_z)
    coarse_src = restrict(source - applied)
    coarse_x, coarse_y, coarse_z = coarsen_faces(face_x, face_y, face_z)
    correction = descend(
        grid_level + 1,
        jnp.zeros_like(coarse_src),
        coarse_src,
        coarse_x,
        coarse_y,
        coarse_z,
        True,
        gather_level,
    )
    iterate = iterate + prolong(correction)
    return smoother(iterate, False)


def fits(nx, ny, nz, devices_x, devices_y):
    cells = devices_x * nx * devices_y * ny * nz // 8
    return cells <= 2**18 and devices_x % 2 == 0 and (nx, ny, nz) == (16, 16, LANES)


def local(source_term, initial_guess, face_x, face_y, face_z):
    if fits(*source_term.shape, lax.axis_size("gx"), lax.axis_size("gy")):
        return fused_cycle(source_term, initial_guess, face_x, face_y, face_z)
    gather_level = 4
    return descend(0, initial_guess, source_term, face_x, face_y, face_z, False, gather_level)


def solution(mesh):
    placed = (P("gx", "gy", None),) * 5
    return jax.shard_map(
        local, mesh=mesh, in_specs=placed, out_specs=P("gx", "gy", None), check_vma=False
    )
```

```python
import functools

import jax
import jax.numpy as jnp
from jax import lax
from jax.experimental import pallas as pl
from jax.experimental.pallas import tpu as pltpu
from jax.sharding import PartitionSpec as P

LEVELS = 6
OMEGA = 0.8
LANES = 128
RIM = 4
PAD = 8
F32 = jnp.float32

V, F, FX, FY, ZL, ZH, W, D, U = range(9)


def lanes_of(shape):
    return lax.broadcasted_iota(jnp.int32, shape, len(shape) - 1)


def rows_of(shape):
    return lax.broadcasted_iota(jnp.int32, shape, len(shape) - 2)


def roll_lanes(values, step):
    return pltpu.roll(values, step % LANES, values.ndim - 1)


def roll_rows(values, step):
    return pltpu.roll(values, step % values.shape[-2], values.ndim - 2)


def exact_dot(left, right):
    return jnp.dot(left, right, precision=lax.Precision.HIGHEST, preferred_element_type=F32)


def compact(depth, part, even_only=False):
    source = lax.broadcasted_iota(jnp.int32, (LANES, LANES), 0)
    target = lax.broadcasted_iota(jnp.int32, (LANES, LANES), 1)
    half = depth // 2
    hit = target == (source // depth * 2 + part) * half + source % depth // 2
    if even_only:
        hit = hit & (source % 2 == 0)
    return jnp.where(hit, 1.0, 0.0).astype(F32)


def expand(depth, part):
    target = lax.broadcasted_iota(jnp.int32, (LANES, LANES), 0)
    source = lax.broadcasted_iota(jnp.int32, (LANES, LANES), 1)
    half = depth // 2
    hit = target == (source // depth * 2 + part) * half + source % depth // 2
    return jnp.where(hit, 1.0, 0.0).astype(F32)


def merge_lanes(values, depth, even_only=False):
    count, rows, _ = values.shape
    half = count // 2
    flat = values.reshape(2, half * rows, LANES)
    out = exact_dot(flat[0], compact(depth, 0, even_only))
    out = out + exact_dot(flat[1], compact(depth, 1, even_only))
    return out.reshape(half, rows, LANES)


def even_rows(ref, rows):
    return ref[:, pl.ds(0, rows // 2, stride=2), :]


def odd_rows(ref, rows):
    return ref[:, pl.ds(1, rows // 2, stride=2), :]


HALF = LANES // 2


def low_half(values):
    return jnp.where(lanes_of(values.shape) < HALF, values, 0.0)


def two_in_one(first, second):
    return first + roll_lanes(second, HALF)


def one_of_two(values):
    return low_half(values), low_half(roll_lanes(values, HALF))


def x_rows(nx, ny):
    return 5 * RIM * ny, 3 * RIM // 2 * (ny // 2)


def y_rows(nx, ny):
    return 5 * (nx + 2 * RIM) * RIM, 3 * (nx // 2 + 2 * RIM) // 2 * RIM


def start_pack(*refs):
    fields, (x_low, x_high, y_low, y_high, faces, own, tmp, done) = refs[:5], refs[5:]
    copies = [pltpu.make_async_copy(ref, own.at[index], done.at[index]) for index, ref in enumerate(fields)]
    for copy in copies:
        copy.start()
    nx, ny = own.shape[1:3]
    for index, copy in enumerate(copies):
        copy.wait()
        for layer in range(RIM):
            rows = pl.ds((index * RIM + layer) * ny, ny)
            x_low[rows] = own[index, layer]
            x_high[rows] = own[index, nx - RIM + layer]
        for slab in range(nx):
            rows = pl.ds((index * nx + slab) * RIM, RIM)
            y_low[rows] = own[index, slab, :RIM]
            y_high[rows] = own[index, slab, ny - RIM :]
    fx, fy, fz = own.at[2], own.at[3], own.at[4]
    halve = compact(LANES, 0)

    def stored(index, values, matrix):
        count, rows, _ = values.shape
        flat = exact_dot(values.reshape(count * rows, LANES), matrix)
        faces[index] = 0.25 * flat.reshape(count, rows, LANES)

    tmp[...] = pair_slabs(fx)[0]
    stored(0, even_rows(tmp, ny) + odd_rows(tmp, ny), halve)
    first, second = pair_slabs(fy)
    tmp[...] = first + second
    stored(1, even_rows(tmp, ny), halve)
    first, second = pair_slabs(fz)
    tmp[...] = first + second
    stored(2, even_rows(tmp, ny) + odd_rows(tmp, ny), compact(LANES, 0, True))
    base = x_rows(nx, ny)[0]
    coarse_rows = ny // 2
    for face in range(3):
        for layer in range(RIM // 2):
            rows = pl.ds(base + (face * (RIM // 2) + layer) * coarse_rows, coarse_rows)
            top = nx // 2 - RIM + layer
            x_low[rows] = two_in_one(faces[face, layer], faces[face, layer + RIM // 2])
            x_high[rows] = two_in_one(faces[face, top], faces[face, top + RIM // 2])


def pair_slabs(ref):
    count = ref.shape[0]
    values = ref[...].reshape((count // 2, 2) + ref.shape[1:])
    return values[:, 0], values[:, 1]


def wide_slab(slab, from_low, own, from_high):
    count = own.shape[0]
    if slab < RIM:
        return from_low(slab)
    if slab < RIM + count:
        return own[slab - RIM]
    return from_high(slab - RIM - count)


def rim_slab(ref, base, rows, layer):
    place = pl.ds(base + layer % (RIM // 2) * rows, rows)
    return one_of_two(ref[place])[layer // (RIM // 2)]


def pack_y(faces, y_own_low, y_own_high, x_low, x_high, low, high):
    coarse_x, coarse_y = faces.shape[1:3]
    nx, ny = 2 * coarse_x, 2 * coarse_y
    for out, own, start in ((low, y_own_low, 0), (high, y_own_high, ny - RIM)):
        for index in range(5):
            base = index * (nx + 2 * RIM) * RIM
            out[pl.ds(base + RIM * RIM, nx * RIM)] = own[pl.ds(index * nx * RIM, nx * RIM)]
            for layer in range(RIM):
                rows = pl.ds((index * RIM + layer) * ny + start, RIM)
                out[pl.ds(base + layer * RIM, RIM)] = x_low[rows]
                out[pl.ds(base + (RIM + nx + layer) * RIM, RIM)] = x_high[rows]
    base_x, base_y = x_rows(nx, ny)[0], y_rows(nx, ny)[0]
    half = (coarse_x + 2 * RIM) // 2
    for face in range(3):
        place = base_x + face * (RIM // 2) * coarse_y
        slabs = [
            wide_slab(
                slab,
                lambda layer: rim_slab(x_low, place, coarse_y, layer),
                faces.at[face],
                lambda layer: rim_slab(x_high, place, coarse_y, layer),
            )
            for slab in range(2 * half)
        ]
        for slab in range(half):
            both = two_in_one(slabs[slab], slabs[slab + half])
            rows = pl.ds(base_y + (face * half + slab) * RIM, RIM)
            low[rows] = both[:RIM]
            high[rows] = both[coarse_y - RIM :]


def fold_four(slabs, even_only=False):
    out = None
    for part in range(2):
        term = exact_dot(two_in_one(slabs[part], slabs[2 + part]), compact(HALF, part, even_only))
        out = term if out is None else out + term
    return out


def coarse_faces(faces, out, tmp):
    rows = faces.shape[2]
    coarse = rows // 2
    fx, fy, fz = faces.at[0], faces.at[1], faces.at[2]
    tmp[...] = pair_slabs(fx)[0]
    x = even_rows(tmp, rows) + odd_rows(tmp, rows)
    first, second = pair_slabs(fy)
    tmp[...] = first + second
    y = even_rows(tmp, rows)
    first, second = pair_slabs(fz)
    tmp[...] = first + second
    z = even_rows(tmp, rows) + odd_rows(tmp, rows)
    out[...] = jnp.zeros(out.shape, F32)
    out[:coarse] = 0.25 * fold_four([x[i] for i in range(4)])
    out[coarse : 2 * coarse] = 0.25 * fold_four([y[i] for i in range(4)])
    out[2 * coarse : 3 * coarse] = 0.25 * fold_four([z[i] for i in range(4)], True)


def weighted(lev, src, slab, start, rows):
    here = pl.ds(start, rows)
    below = pl.ds(start - 1, rows)
    above = pl.ds(start + 1, rows)
    v = src[slab, here]
    total = lev[F, slab, here] + lev[FX, slab, here] * src[slab - 1, here]
    total = total + lev[FX, slab + 1, here] * src[slab + 1, here]
    total = total + lev[FY, slab, here] * src[slab, below]
    total = total + lev[FY, slab, above] * src[slab, above]
    total = total + lev[ZL, slab, here] * roll_lanes(v, 1)
    total = total + lev[ZH, slab, here] * roll_lanes(v, -1)
    return v, total


def swept(lev, src, slab, start, rows):
    v, total = weighted(lev, src, slab, start, rows)
    return (1.0 - OMEGA) * v + lev[W, slab, pl.ds(start, rows)] * total


def set_weights(lev, slab, start, rows, depth, inside=None):
    here = pl.ds(start, rows)
    fz = lev[ZL, slab, here]
    z = lanes_of(fz.shape) % depth
    upper = jnp.where(z == depth - 1, 0.0, roll_lanes(fz, -1))
    diagonal = lev[FX, slab, here] + lev[FX, slab + 1, here]
    diagonal = diagonal + lev[FY, slab, here] + lev[FY, slab, pl.ds(start + 1, rows)] + fz + upper
    valid = diagonal > 0.0
    if inside is not None:
        valid = valid & inside
    lev[ZL, slab, here] = jnp.where(z == 0, 0.0, fz)
    lev[ZH, slab, here] = upper
    lev[D, slab, here] = diagonal
    lev[W, slab, here] = jnp.where(valid, OMEGA / jnp.where(valid, diagonal, 1.0), 0.0)


def run(count, body, unroll=1):
    def step(index, carry):
        body(index)
        return carry

    lax.fori_loop(0, count, step, 0, unroll=unroll)


def clear_pads(ref, rows):
    for start in (0, RIM + rows):
        ref[:, start : start + RIM] = jnp.zeros((ref.shape[0], RIM, LANES), F32)


def level_down(axes, *refs):
    fields = refs[:5]
    faces, coefficients, x_low, x_high, y_low, y_high, top, mid, chunk, v_low, v_high, other, tmp, one, two = refs[5:]
    nx, ny = fields[0].shape[:2]
    slabs, rows = nx + 2 * RIM, ny + 2 * RIM
    me_x, me_y = lax.axis_index(axes[0]), lax.axis_index(axes[1])
    inner = pl.ds(2 * RIM, ny)
    for index, slot in enumerate((F, V, FX, FY, ZL)):
        clear_pads(top.at[slot], rows)
        top[slot, RIM : RIM + nx, inner] = fields[index][...]
        for layer in range(RIM):
            place = pl.ds((index * RIM + layer) * ny, ny)
            top[slot, layer, inner] = x_low[place]
            top[slot, RIM + nx + layer, inner] = x_high[place]
        for slab in range(slabs):
            place = pl.ds((index * slabs + slab) * RIM, RIM)
            top[slot, slab, RIM : 2 * RIM] = y_low[place]
            top[slot, slab, 2 * RIM + ny : RIM + rows] = y_high[place]
    clear_pads(other, rows)
    row_inside = (rows_of((rows, LANES)) >= RIM) | (me_y > 0)
    main = pl.ds(RIM, rows)

    def first(index):
        slab = index + 1
        inside = row_inside & ((slab >= RIM) | (me_x > 0))
        set_weights(top, slab, RIM, rows, LANES, inside)
        other[slab, main] = swept(top, other_v, slab, RIM, rows)

    other_v = top.at[V]
    run(slabs - 2, first, 2)

    def second(index):
        slab = index + 2
        top[V, slab, main] = swept(top, other, slab, RIM, rows)

    run(slabs - 4, second, 2)

    def rest(slab):
        v, total = weighted(top, top.at[V], slab, 2 * RIM, ny)
        return total - top[D, slab, inner] * v

    def residual(index):
        slab = RIM + 2 * index
        tmp[index] = rest(slab) + rest(slab + 1)

    run(nx // 2, residual, 2)

    coarse_x, coarse_y = nx // 2, ny // 2
    slabs, rows = coarse_x + 2 * RIM, coarse_y + 2 * RIM
    half = slabs // 2
    inner = pl.ds(2 * RIM, coarse_y)
    main = pl.ds(RIM, rows)
    base_x, base_y = x_rows(nx, ny)[0], y_rows(nx, ny)[0]
    for face, slot in enumerate((FX, FY, ZL)):
        clear_pads(mid.at[slot], rows)
        mid[slot, RIM : RIM + coarse_x, inner] = faces[face]
        place = base_x + face * (RIM // 2) * coarse_y
        for layer in range(RIM):
            mid[slot, layer, inner] = rim_slab(x_low, place, coarse_y, layer)
            mid[slot, RIM + coarse_x + layer, inner] = rim_slab(x_high, place, coarse_y, layer)
        for slab in range(half):
            place = pl.ds(base_y + (face * half + slab) * RIM, RIM)
            for message, row in ((y_low, RIM), (y_high, 2 * RIM + coarse_y)):
                pair = one_of_two(message[place])
                mid[slot, slab, row : row + RIM] = pair[0]
                mid[slot, slab + half, row : row + RIM] = pair[1]
    row_inside = (rows_of((rows, LANES)) >= RIM) | (me_y > 0)
    for slab in range(slabs - 1):
        inside = row_inside & (me_x > 0) if slab < RIM else row_inside
        set_weights(mid, slab, RIM, rows, HALF, inside)

    source = even_rows(tmp, ny) + odd_rows(tmp, ny)
    source = 0.5 * exact_dot(source.reshape(coarse_x * coarse_y, LANES), compact(LANES, 0))
    for ref in (mid.at[F], mid.at[V], one):
        ref[...] = jnp.zeros(ref.shape, F32)
    mid[F, RIM : RIM + coarse_x, inner] = source.reshape(coarse_x, coarse_y, LANES)
    for slab in range(RIM, RIM + coarse_x):
        mid[V, slab, inner] = mid[W, slab, inner] * mid[F, slab, inner]
    for layer in range(RIM // 2):
        near, far = RIM + layer, coarse_x + layer
        v_low[layer * coarse_y : (layer + 1) * coarse_y] = two_in_one(
            mid[V, near, inner], mid[V, near + RIM // 2, inner]
        )
        v_high[layer * coarse_y : (layer + 1) * coarse_y] = two_in_one(
            mid[V, far, inner], mid[V, far + RIM // 2, inner]
        )
    for slab in range(RIM - 1, RIM + coarse_x + 1):
        one[slab, main] = swept(mid, mid.at[V], slab, RIM, rows)

    def rest_1(slab):
        v, total = weighted(mid, one, slab, RIM, rows)
        return total - mid[D, slab, main] * v

    two[...] = jnp.zeros(two.shape, F32)
    for pair in range(1, half - 1):
        two[pair] = rest_1(2 * pair) + rest_1(2 * pair + 1)
    pieces = even_rows(two, rows) + odd_rows(two, rows)
    for part in range(half // 4):
        folded = fold_four([pieces[4 * part + i] for i in range(4)])
        chunk[part * rows // 2 : (part + 1) * rows // 2] = 0.5 * folded
    chunk[half // 4 * rows // 2 :] = coefficients[...]


def pack_v(mid_v, x_low, x_high, low, high):
    slabs = mid_v.shape[1]
    coarse_x = slabs - 2 * RIM
    coarse_y = mid_v.shape[2] - 4 * RIM
    half = slabs // 2
    own = mid_v[V, RIM : RIM + coarse_x, 2 * RIM : 2 * RIM + coarse_y]
    values = [
        wide_slab(
            slab,
            lambda layer: rim_slab(x_low, 0, coarse_y, layer),
            own,
            lambda layer: rim_slab(x_high, 0, coarse_y, layer),
        )
        for slab in range(slabs)
    ]
    for slab in range(half):
        both = two_in_one(values[slab], values[slab + half])
        low[slab * RIM : (slab + 1) * RIM] = both[:RIM]
        high[slab * RIM : (slab + 1) * RIM] = both[coarse_y - RIM :]


def pair_rows(values, stride):
    return values + roll_rows(values, -stride)


def pair_lanes(values, stride):
    return values + roll_lanes(values, -stride)


class Listed:
    def __init__(self, fx, fy, fz, stride, depth):
        self.fx, self.fy, self.fz, self.stride, self.depth = fx, fy, fz, stride, depth
        shape = fx[0].shape
        rows = shape[0]
        row, lane = rows_of(shape), lanes_of(shape)
        z = lane % depth
        count = self.count = len(fx)
        self.x_high = [
            fx[s + 1] if s + 1 < count else jnp.where(lane < LANES - depth, roll_lanes(fx[0], -depth), 0.0)
            for s in range(count)
        ]
        self.x_low = [fx[s] if s > 0 else jnp.where(lane >= depth, fx[0], 0.0) for s in range(count)]
        self.y_high = [jnp.where(row < rows - stride, roll_rows(f, -stride), 0.0) for f in fy]
        self.y_low = [jnp.where(row >= stride, f, 0.0) for f in fy]
        self.z_high = [jnp.where(z < depth - stride, roll_lanes(f, -stride), 0.0) for f in fz]
        self.z_low = [jnp.where(z >= stride, f, 0.0) for f in fz]
        self.d = [
            fx[s] + self.x_high[s] + fy[s] + self.y_high[s] + fz[s] + self.z_high[s] for s in range(count)
        ]
        self.w = [jnp.where(d > 0.0, OMEGA / jnp.where(d > 0.0, d, 1.0), 0.0) for d in self.d]

    def weighted(self, v, f):
        count = self.count
        out = []
        for s in range(count):
            low = v[s - 1] if s > 0 else roll_lanes(v[count - 1], self.depth)
            high = v[s + 1] if s + 1 < count else roll_lanes(v[0], -self.depth)
            total = f[s] + self.x_low[s] * low + self.x_high[s] * high
            total = total + self.y_low[s] * roll_rows(v[s], self.stride)
            total = total + self.y_high[s] * roll_rows(v[s], -self.stride)
            total = total + self.z_low[s] * roll_lanes(v[s], self.stride)
            total = total + self.z_high[s] * roll_lanes(v[s], -self.stride)
            out.append(total)
        return out

    def sweep(self, v, f):
        totals = self.weighted(v, f)
        return [(1.0 - OMEGA) * v[s] + self.w[s] * totals[s] for s in range(self.count)]

    def start(self, f):
        return [self.w[s] * f[s] for s in range(self.count)]

    def residual(self, v, f):
        totals = self.weighted(v, f)
        return [totals[s] - self.d[s] * v[s] for s in range(self.count)]

    def kept(self):
        shape = self.fx[0].shape
        step = 2 * self.stride
        return (rows_of(shape) % step == 0) & (lanes_of(shape) % step == 0)

    def coarser(self):
        keep, stride = self.kept(), self.stride
        half = range(self.count // 2)

        def kept(values):
            return jnp.where(keep, 0.25 * values, 0.0)

        fx = [kept(pair_lanes(pair_rows(self.fx[2 * s], stride), stride)) for s in half]
        fy = [kept(pair_lanes(self.fy[2 * s] + self.fy[2 * s + 1], stride)) for s in half]
        fz = [kept(pair_rows(self.fz[2 * s] + self.fz[2 * s + 1], stride)) for s in half]
        return Listed(fx, fy, fz, 2 * stride, self.depth)

    def restrict(self, r):
        keep, stride = self.kept(), self.stride
        return [
            jnp.where(keep, 0.5 * pair_lanes(pair_rows(r[2 * s] + r[2 * s + 1], stride), stride), 0.0)
            for s in range(self.count // 2)
        ]

    def prolong(self, e):
        out = []
        for values in e:
            values = values + roll_rows(values, self.stride)
            values = values + roll_lanes(values, self.stride)
            out += [values, values]
        return out


def listed_cycle(levels, sweeps, f):
    level = levels[0]
    v = level.start(f)
    if len(levels) == 1:
        return lax.fori_loop(0, sweeps - 1, lambda index, values: level.sweep(values, f), v)
    v = level.sweep(v, f)
    e = listed_cycle(levels[1:], sweeps, level.restrict(level.residual(v, f)))
    v = [a + b for a, b in zip(v, level.prolong(e))]
    return level.sweep(level.sweep(v, f), f)


def level_up(axes, grid, sweeps, pieces, top, mid, x_low, x_high, y_low, y_high, out, wide, one, two, tall, post, up):
    devices_x, devices_y = grid
    me_x, me_y = lax.axis_index(axes[0]), lax.axis_index(axes[1])
    coarse_x, coarse_y = mid.shape[1] - 2 * RIM, mid.shape[2] - 4 * RIM
    own_x, own_y = coarse_x // 2, coarse_y // 2
    quarter = LANES // 4
    reach = RIM // 2
    blocks = 4
    count = devices_x * own_x // blocks
    rows = devices_y * own_y
    main = pl.ds(PAD, rows)
    window = own_y + RIM

    def piece(gx, gy):
        slow = (me_x // 2 - gx // 2 + devices_x // 2) % (devices_x // 2)
        far = (me_y // 2 - gy // 2 + devices_y // 2) % (devices_y // 2)
        return ((me_y + gy) % 2, far, (me_x + gx) % 2, slow)

    for ref in (wide, tall):
        ref[...] = jnp.zeros(ref.shape, F32)
    lane = lanes_of((window, LANES))
    for gy in range(devices_y):
        sums = [None] * count
        for gx in range(devices_x):
            where = piece(gx, gy)
            layers = [pieces[where + (pl.ds(part * window, window),)] for part in range(2)]
            for local in range(1, 2 * blocks - 1):
                x = own_x * gx - reach + local
                if not 0 <= x < devices_x * own_x:
                    continue
                block, slab = x // count, x % count
                moved = roll_lanes(layers[local // blocks], (block - local % blocks) * quarter)
                moved = jnp.where(lane // quarter == block, moved, 0.0)
                sums[slab] = moved if sums[slab] is None else sums[slab] + moved
        place = pl.ds(PAD + own_y * gy - reach, window)
        for slab in range(count):
            tall[slab, place] = tall[slab, place] + sums[slab]
    f = [tall[slab, main] for slab in range(count)]

    lane = lanes_of((rows, LANES))
    for gx in range(devices_x):
        for gy in range(devices_y):
            where = piece(gx, gy)
            for face in range(3):
                values = pieces[where + (pl.ds(2 * window + face * own_y, own_y),)]
                wide[face, gx, gy * own_y : (gy + 1) * own_y] = values
    faces = []
    for face in range(3):
        slabs = [None] * count
        for gx in range(devices_x):
            values = wide[face, gx]
            for local in range(own_x):
                x = own_x * gx + local
                block, slab = x // count, x % count
                moved = roll_lanes(values, (block - local) * quarter)
                moved = jnp.where(lane // quarter == block, moved, 0.0)
                slabs[slab] = moved if slabs[slab] is None else slabs[slab] + moved
        faces.append(slabs)
    levels = [Listed(*faces, 1, quarter)]
    while len(levels) < LEVELS - 2:
        levels.append(levels[-1].coarser())
    e = listed_cycle(levels, sweeps, f)

    slabs, high = coarse_x + 2 * RIM, coarse_y + 2 * RIM
    half = slabs // 2
    inner = pl.ds(2 * RIM, coarse_y)
    body = pl.ds(RIM, high)
    one[...] = mid[V]
    clear_pads(two, high)
    for layer in range(RIM):
        one[layer, inner] = rim_slab(x_low, 0, coarse_y, layer)
        one[RIM + coarse_x + layer, inner] = rim_slab(x_high, 0, coarse_y, layer)
    for slab in range(half):
        place = pl.ds(slab * RIM, RIM)
        for message, row in ((y_low, RIM), (y_high, 2 * RIM + coarse_y)):
            pair = one_of_two(message[place])
            one[slab, row : row + RIM] = pair[0]
            one[slab + half, row : row + RIM] = pair[1]
    row = rows_of((high, LANES))
    own_row = (row >= RIM) & (row < RIM + coarse_y)
    for slab in range(1, slabs - 1):
        f_rim = one[slab, body] * mid[D, slab, body] * (1.0 / OMEGA)
        if RIM <= slab < RIM + coarse_x:
            f_rim = jnp.where(own_row, mid[F, slab, body], f_rim)
        mid[F, slab, body] = f_rim
        two[slab, body] = swept(mid, one, slab, RIM, high)

    extra = reach
    tall[:, :PAD] = jnp.zeros((count + 2 * extra, PAD, LANES), F32)
    tall[:, PAD + rows :] = jnp.zeros((count + 2 * extra, PAD, LANES), F32)
    for slab in range(count):
        tall[extra + slab, main] = e[slab]
    for slab in range(extra):
        tall[slab, main] = jnp.where(lane < quarter, 0.0, roll_lanes(e[count - extra + slab], quarter))
        tall[extra + count + slab, main] = jnp.where(
            lane >= LANES - quarter, 0.0, roll_lanes(e[slab], -quarter)
        )
    per_block = count // own_x
    base = me_x % per_block * own_x
    mine = None
    for gy in range(devices_y):
        place = pl.ds(PAD + gy * own_y - reach, window)
        values = tall[pl.ds(base, half), place, :]
        values = jnp.where(me_y == gy, values, 0.0)
        mine = values if mine is None else mine + values
    source = lax.broadcasted_iota(jnp.int32, (LANES, LANES), 0)
    target = lax.broadcasted_iota(jnp.int32, (LANES, LANES), 1)
    hit = (source == me_x // per_block * quarter + target // 2) & (target < HALF)
    fine = exact_dot(mine.reshape(half * window, LANES), jnp.where(hit, 1.0, 0.0).astype(F32))
    fine = fine.reshape(half, window, LANES)
    for odd in range(2):
        up[:half, pl.ds(odd, window, stride=2), :] = fine
    for pair in range(half):
        for slab in (2 * pair, 2 * pair + 1):
            if 1 <= slab < slabs - 1:
                two[slab, body] = two[slab, body] + up[pair, :high]
    for slab in range(2, slabs - 2):
        one[slab, body] = swept(mid, two, slab, RIM, high)
    for slab in range(3, slabs - 3):
        two[slab, body] = swept(mid, one, slab, RIM, high)

    nx, ny = out.shape[:2]
    steps = coarse_x + 2
    fine_rows = ny + 2 * RIM
    e = two[RIM - 1 : RIM - 1 + steps, body]
    fine = exact_dot(e.reshape(steps * high, LANES), expand(LANES, 0)).reshape(steps, high, LANES)
    fine = fine[:, reach : reach + fine_rows // 2]
    for odd in range(2):
        up[:, pl.ds(odd, fine_rows // 2, stride=2), :] = fine
    body = pl.ds(RIM, fine_rows)
    for slot in (0, 1):
        clear_pads(post.at[slot], fine_rows)

    def raise_level(index):
        for slab in (RIM - 2 + 2 * index, RIM - 1 + 2 * index):
            post[0, slab, body] = top[V, slab, body] + up[index]

    run(steps, raise_level, 2)

    def fifth(index):
        slab = RIM - 1 + index
        post[1, slab, body] = swept(top, post.at[0], slab, RIM, fine_rows)

    run(nx + 2, fifth, 2)

    def sixth(index):
        out[index] = swept(top, post.at[1], RIM + index, 2 * RIM, ny)

    run(nx, sixth, 2)


IN_VMEM = pl.BlockSpec(memory_space=pltpu.VMEM)
ANYWHERE = pl.BlockSpec(memory_space=pl.ANY)


def call(kernel, ins, outs, scratch=(), limit=24 * 2**20):
    def launch(*args):
        return pl.pallas_call(
            kernel,
            out_shape=[jax.ShapeDtypeStruct(shape, F32) for shape, _ in outs],
            in_specs=ins,
            out_specs=[spec for _, spec in outs],
            scratch_shapes=[pltpu.VMEM(s, F32) if isinstance(s, tuple) else s for s in scratch],
            compiler_params=pltpu.CompilerParams(vmem_limit_bytes=limit),
        )(*args)

    return launch


def from_sides(low, high, axis):
    count = lax.axis_size(axis)
    up = [(i, i + 1) for i in range(count - 1)]
    down = [(target, source) for source, target in up]
    return lax.ppermute(high, axis, up), lax.ppermute(low, axis, down)


def paired(block, axis, stride):
    count = lax.axis_size(axis)
    return jnp.stack((block, lax.ppermute(block, axis, [(i, i ^ stride) for i in range(count)])))


def passed_round(block, axis, stride):
    count = lax.axis_size(axis)
    blocks = [block]
    for distance in range(stride, count, stride):
        blocks.append(lax.ppermute(block, axis, [(i, (i + distance) % count) for i in range(count)]))
    return jnp.stack(blocks)


def gathered(block):
    block = passed_round(block, "gx", 2)
    block = paired(block, "gx", 1)
    block = passed_round(block, "gy", 2)
    return paired(block, "gy", 1)


def fused_cycle(*fields):
    axes = ("gx", "gy")
    devices_x, devices_y = lax.axis_size("gx"), lax.axis_size("gy")
    nx, ny, nz = fields[0].shape
    coarse_x, coarse_y = nx // 2, ny // 2
    x_shape = (sum(x_rows(nx, ny)), LANES)
    y_shape = (sum(y_rows(nx, ny)), LANES)
    x_low, x_high, y_own_low, y_own_high, faces = call(
        start_pack,
        [ANYWHERE] * 5,
        [(shape, IN_VMEM) for shape in (x_shape, x_shape) + ((5 * nx * RIM, LANES),) * 2 + ((3, coarse_x, coarse_y, LANES),)],
        [(5, nx, ny, LANES), (coarse_x, ny, LANES), pltpu.SemaphoreType.DMA((5,))],
        None,
    )(*fields)
    x_low, x_high = from_sides(x_low, x_high, "gx")
    (coefficients,) = call(
        coarse_faces, [IN_VMEM], [((16, LANES), IN_VMEM)], [(coarse_x // 2, coarse_y, LANES)]
    )(faces)
    y_low, y_high = call(pack_y, [IN_VMEM] * 5, [(y_shape, IN_VMEM)] * 2)(
        faces, y_own_low, y_own_high, x_low, x_high
    )
    y_low, y_high = from_sides(y_low, y_high, "gy")
    stack = (nx + 2 * RIM, ny + 4 * RIM, LANES)
    stack_1 = (coarse_x + 2 * RIM, coarse_y + 4 * RIM, LANES)
    half = stack_1[0] // 2
    v_shape = (RIM // 2 * coarse_y, LANES)
    top, mid, chunk, v_low, v_high = call(
        functools.partial(level_down, axes),
        [IN_VMEM] * 11,
        [
            (shape, IN_VMEM)
            for shape in ((D + 1,) + stack, (D + 1,) + stack_1, (32, LANES), v_shape, v_shape)
        ],
        [stack, (nx // 2, ny, LANES), stack_1, (half, coarse_y + 2 * RIM, LANES)],
    )(*fields, faces, coefficients, x_low, x_high, y_low, y_high)
    pieces = gathered(chunk)
    v_low, v_high = from_sides(v_low, v_high, "gx")
    w_low, w_high = call(pack_v, [IN_VMEM] * 3, [((half * RIM, LANES), IN_VMEM)] * 2)(mid, v_low, v_high)
    w_low, w_high = from_sides(w_low, w_high, "gy")
    count = devices_x * nx // 16
    rows = devices_y * ny // 4
    coarsest = (devices_x * nx >> LEVELS - 1, devices_y * ny >> LEVELS - 1)
    (out,) = call(
        functools.partial(level_up, axes, (devices_x, devices_y), 4 * max(coarsest)),
        [IN_VMEM] * 7,
        [((nx, ny, nz), IN_VMEM)],
        [
            (3, devices_x, rows, LANES),
            stack_1,
            stack_1,
            (count + RIM, rows + 2 * PAD, LANES),
            (2,) + stack,
            (coarse_x + 2, ny + 2 * RIM, LANES),
        ],
    )(pieces, top, mid, v_low, v_high, w_low, w_high)
    return out


def with_halo(block, sides, width):
    for axis, dim in sides:
        count = lax.axis_size(axis)
        forward = [(i, i + 1) for i in range(count - 1)]
        backward = [(target, source) for source, target in forward]
        low = lax.ppermute(
            lax.slice_in_dim(block, block.shape[dim] - width, None, axis=dim), axis, forward
        )
        high = lax.ppermute(lax.slice_in_dim(block, 0, width, axis=dim), axis, backward)
        block = jnp.concatenate([low, block, high], axis=dim)
    return block


def passed_along(block, axis, distance):
    devices = range(lax.axis_size(axis))
    route = [(i - distance, i) for i in devices if i - distance in devices]
    return lax.ppermute(block, axis, route)


def stencil(padded, padded_x, padded_y, face_z):
    center = padded[1:-1, 1:-1]
    zero_plane = jnp.zeros(center.shape[:2] + (1,), center.dtype)
    above_face = jnp.concatenate((face_z[:, :, 1:], zero_plane), axis=2)
    below_z = jnp.concatenate((zero_plane, center[:, :, :-1]), axis=2)
    above_z = jnp.concatenate((center[:, :, 1:], zero_plane), axis=2)
    lower_x = padded_x[1:-1, 1:-1]
    upper_x = padded_x[2:, 1:-1]
    lower_y = padded_y[1:-1, 1:-1]
    upper_y = padded_y[1:-1, 2:]
    applied = lower_x * (center - padded[:-2, 1:-1]) + upper_x * (center - padded[2:, 1:-1])
    applied = (
        applied + lower_y * (center - padded[1:-1, :-2]) + upper_y * (center - padded[1:-1, 2:])
    )
    applied = applied + face_z * (center - below_z) + above_face * (center - above_z)
    diagonal = lower_x + upper_x + lower_y + upper_y + face_z + above_face
    return (applied, diagonal)


def jacobi_sweep(padded, source, padded_x, padded_y, face_z):
    applied, diagonal = stencil(padded, padded_x, padded_y, face_z)
    return padded[1:-1, 1:-1] + OMEGA * (source - applied) / diagonal


def pad_plane(values, width):
    return jnp.pad(values, ((width, width), (width, width), (0, 0)))


def restrict(residual):
    shape = residual.shape
    blocks = residual.reshape(shape[0] // 2, 2, shape[1] // 2, 2, shape[2] // 2, 2)
    return 4.0 * jnp.mean(blocks, axis=(1, 3, 5))


def coarsen_faces(face_x, face_y, face_z):
    shape = face_x.shape
    blocks = (shape[0] // 2, 2, shape[1] // 2, 2, shape[2] // 2, 2)
    coarse_x = jnp.mean(face_x.reshape(blocks)[:, 0], axis=(2, 4))
    coarse_y = jnp.mean(face_y.reshape(blocks)[:, :, :, 0], axis=(1, 4))
    coarse_z = jnp.mean(face_z.reshape(blocks)[..., 0], axis=(1, 3))
    return (coarse_x, coarse_y, coarse_z)


def prolong(coarse):
    return jnp.repeat(jnp.repeat(jnp.repeat(coarse, 2, axis=0), 2, axis=1), 2, axis=2)


def local_cycle(grid_level, iterate, source, face_x, face_y, face_z):
    padded_x = pad_plane(face_x, 1)
    padded_y = pad_plane(face_y, 1)
    if grid_level == LEVELS - 1:
        count = 4 * max(iterate.shape[0], iterate.shape[1])

        def one_sweep(index, values):
            return jacobi_sweep(pad_plane(values, 1), source, padded_x, padded_y, face_z)

        return lax.fori_loop(0, count, one_sweep, iterate)
    for sweep_index in range(2):
        iterate = jacobi_sweep(pad_plane(iterate, 1), source, padded_x, padded_y, face_z)
    applied, diagonal = stencil(pad_plane(iterate, 1), padded_x, padded_y, face_z)
    coarse_src = restrict(source - applied)
    coarse_x, coarse_y, coarse_z = coarsen_faces(face_x, face_y, face_z)
    correction = local_cycle(
        grid_level + 1, jnp.zeros_like(coarse_src), coarse_src, coarse_x, coarse_y, coarse_z
    )
    iterate = iterate + prolong(correction)
    for sweep_index in range(2):
        iterate = jacobi_sweep(pad_plane(iterate, 1), source, padded_x, padded_y, face_z)
    return iterate


def field_rim(iterate):
    return with_halo(iterate, (("gx", 0), ("gy", 1)), 1)


def sweep_pair_narrow(iterate, source, padded_x, padded_y, face_z, zero_start):
    for sweep_index in range(2):
        if sweep_index == 0 and zero_start:
            padded = pad_plane(iterate, 1)
        else:
            padded = field_rim(iterate)
        iterate = jacobi_sweep(padded, source, padded_x, padded_y, face_z)
    return iterate


def descend(grid_level, iterate, source, face_x, face_y, face_z, zero_start, gather_level):
    if grid_level == gather_level:
        pieces = (
            lax.all_gather(source, "gy", axis=1, tiled=True),
            lax.all_gather(face_x, "gy", axis=1, tiled=True),
            lax.all_gather(face_y, "gy", axis=1, tiled=True),
            lax.all_gather(face_z, "gy", axis=1, tiled=True),
        )
        gathered = (
            lax.all_gather(pieces[0], "gx", axis=0, tiled=True),
            lax.all_gather(pieces[1], "gx", axis=0, tiled=True),
            lax.all_gather(pieces[2], "gx", axis=0, tiled=True),
            lax.all_gather(pieces[3], "gx", axis=0, tiled=True),
        )
        correction = local_cycle(
            grid_level,
            jnp.zeros_like(gathered[0]),
            gathered[0],
            gathered[1],
            gathered[2],
            gathered[3],
        )
        start_x = lax.axis_index("gx") * source.shape[0]
        start_y = lax.axis_index("gy") * source.shape[1]
        return lax.dynamic_slice(
            correction, (start_x, start_y, jnp.zeros((), jnp.int32)), source.shape
        )
    next_x = passed_along(face_x[:1], "gx", -1)
    next_y = passed_along(face_y[:, :1], "gy", -1)
    lower_row = jnp.zeros_like(next_x)
    lower_col = jnp.zeros_like(next_y)
    padded_x = jnp.pad(
        jnp.concatenate((lower_row, face_x, next_x), axis=0), ((0, 0), (1, 1), (0, 0))
    )
    padded_y = jnp.pad(
        jnp.concatenate((lower_col, face_y, next_y), axis=1), ((1, 1), (0, 0), (0, 0))
    )

    def smoother(values, starting):
        return sweep_pair_narrow(values, source, padded_x, padded_y, face_z, starting)

    iterate = smoother(iterate, zero_start)
    applied, diagonal = stencil(field_rim(iterate), padded_x, padded_y, face_z)
    coarse_src = restrict(source - applied)
    coarse_x, coarse_y, coarse_z = coarsen_faces(face_x, face_y, face_z)
    correction = descend(
        grid_level + 1,
        jnp.zeros_like(coarse_src),
        coarse_src,
        coarse_x,
        coarse_y,
        coarse_z,
        True,
        gather_level,
    )
    iterate = iterate + prolong(correction)
    return smoother(iterate, False)


def fits(nx, ny, nz, devices_x, devices_y):
    cells = devices_x * nx * devices_y * ny * nz // 8
    even = devices_x % 8 == 0 and devices_y % 4 == 0
    return cells <= 2**18 and even and (nx, ny, nz) == (16, 16, LANES)


def local(source_term, initial_guess, face_x, face_y, face_z):
    if fits(*source_term.shape, lax.axis_size("gx"), lax.axis_size("gy")):
        return fused_cycle(source_term, initial_guess, face_x, face_y, face_z)
    gather_level = 4
    return descend(0, initial_guess, source_term, face_x, face_y, face_z, False, gather_level)


def solution(mesh):
    placed = (P("gx", "gy", None),) * 5
    return jax.shard_map(
        local, mesh=mesh, in_specs=placed, out_specs=P("gx", "gy", None), check_vma=False
    )
```

```python
import functools

import jax
import jax.numpy as jnp
from jax import lax
from jax.experimental import pallas as pl
from jax.experimental.pallas import tpu as pltpu
from jax.sharding import PartitionSpec as P

LEVELS = 6
OMEGA = 0.8
LANES = 128
RIM = 4
EDGE = 3
PAD = 8
F32 = jnp.float32

V, F, FX, FY, ZL, ZH, W, D = range(8)
SLOTS = (F, V, FX, FY, ZL)
X_LAYERS = (2, 3, 3, 2, 2)
Y_LAYERS = (2, 3, 2, 3, 2)


def lanes_of(shape):
    return lax.broadcasted_iota(jnp.int32, shape, len(shape) - 1)


def rows_of(shape):
    return lax.broadcasted_iota(jnp.int32, shape, len(shape) - 2)


def roll_lanes(values, step):
    return pltpu.roll(values, step % LANES, values.ndim - 1)


def roll_rows(values, step):
    return pltpu.roll(values, step % values.shape[-2], values.ndim - 2)


def exact_dot(left, right):
    return jnp.dot(left, right, precision=lax.Precision.HIGHEST, preferred_element_type=F32)


def compact(depth, part, even_only=False):
    source = lax.broadcasted_iota(jnp.int32, (LANES, LANES), 0)
    target = lax.broadcasted_iota(jnp.int32, (LANES, LANES), 1)
    half = depth // 2
    hit = target == (source // depth * 2 + part) * half + source % depth // 2
    if even_only:
        hit = hit & (source % 2 == 0)
    return jnp.where(hit, 1.0, 0.0).astype(F32)


def expand(depth, part):
    target = lax.broadcasted_iota(jnp.int32, (LANES, LANES), 0)
    source = lax.broadcasted_iota(jnp.int32, (LANES, LANES), 1)
    half = depth // 2
    hit = target == (source // depth * 2 + part) * half + source % depth // 2
    return jnp.where(hit, 1.0, 0.0).astype(F32)


def merge_lanes(values, depth, even_only=False):
    count, rows, _ = values.shape
    half = count // 2
    flat = values.reshape(2, half * rows, LANES)
    out = exact_dot(flat[0], compact(depth, 0, even_only))
    out = out + exact_dot(flat[1], compact(depth, 1, even_only))
    return out.reshape(half, rows, LANES)


def even_rows(ref, rows):
    return ref[:, pl.ds(0, rows // 2, stride=2), :]


def odd_rows(ref, rows):
    return ref[:, pl.ds(1, rows // 2, stride=2), :]


HALF = LANES // 2


def low_half(values):
    return jnp.where(lanes_of(values.shape) < HALF, values, 0.0)


def two_in_one(first, second):
    return first + roll_lanes(second, HALF)


def one_of_two(values):
    return low_half(values), low_half(roll_lanes(values, HALF))


def x_rows(nx, ny):
    return sum(X_LAYERS) * ny, 3 * RIM // 2 * (ny // 2)


def y_rows(nx, ny):
    return sum(Y_LAYERS) * (nx + 2 * EDGE), 3 * (nx // 2 + 2 * RIM) // 2 * RIM


def x_place(index, layer, ny):
    return pl.ds((sum(X_LAYERS[:index]) + layer) * ny, ny)


def y_place(index, slab, slabs):
    return pl.ds(sum(Y_LAYERS[:index]) * slabs + slab * Y_LAYERS[index], Y_LAYERS[index])


def start_pack(*refs):
    fields, (own, x_low, x_high, faces, tmp, done) = refs[:5], refs[5:]
    copies = [pltpu.make_async_copy(ref, own.at[index], done.at[index]) for index, ref in enumerate(fields)]
    for copy in copies:
        copy.start()
    nx, ny = own.shape[1:3]
    for index, copy in enumerate(copies):
        copy.wait()
        for layer in range(X_LAYERS[index]):
            x_low[x_place(index, layer, ny)] = own[index, layer]
            x_high[x_place(index, layer, ny)] = own[index, nx - X_LAYERS[index] + layer]
    fx, fy, fz = own.at[2], own.at[3], own.at[4]
    halve = compact(LANES, 0)

    def stored(index, values, matrix):
        count, rows, _ = values.shape
        flat = exact_dot(values.reshape(count * rows, LANES), matrix)
        faces[index] = 0.25 * flat.reshape(count, rows, LANES)

    tmp[...] = pair_slabs(fx)[0]
    stored(0, even_rows(tmp, ny) + odd_rows(tmp, ny), halve)
    first, second = pair_slabs(fy)
    tmp[...] = first + second
    stored(1, even_rows(tmp, ny), halve)
    first, second = pair_slabs(fz)
    tmp[...] = first + second
    stored(2, even_rows(tmp, ny) + odd_rows(tmp, ny), compact(LANES, 0, True))
    base = x_rows(nx, ny)[0]
    coarse_rows = ny // 2
    for face in range(3):
        for layer in range(RIM // 2):
            rows = pl.ds(base + (face * (RIM // 2) + layer) * coarse_rows, coarse_rows)
            top = nx // 2 - RIM + layer
            x_low[rows] = two_in_one(faces[face, layer], faces[face, layer + RIM // 2])
            x_high[rows] = two_in_one(faces[face, top], faces[face, top + RIM // 2])


def pair_slabs(ref):
    count = ref.shape[0]
    values = ref[...].reshape((count // 2, 2) + ref.shape[1:])
    return values[:, 0], values[:, 1]


def wide_slab(slab, from_low, own, from_high):
    count = own.shape[0]
    if slab < RIM:
        return from_low(slab)
    if slab < RIM + count:
        return own[slab - RIM]
    return from_high(slab - RIM - count)


def rim_slab(ref, base, rows, layer):
    place = pl.ds(base + layer % (RIM // 2) * rows, rows)
    return one_of_two(ref[place])[layer // (RIM // 2)]


def pack_y(own, faces, x_low, x_high, low, high):
    coarse_x, coarse_y = faces.shape[1:3]
    nx, ny = 2 * coarse_x, 2 * coarse_y
    slabs = nx + 2 * EDGE
    for index in range(5):
        width, layers = Y_LAYERS[index], X_LAYERS[index]
        for out, start in ((low, 0), (high, ny - width)):
            for slab in range(nx):
                out[y_place(index, EDGE + slab, slabs)] = own[index, slab, start : start + width]
            for layer in range(EDGE):
                near, far = layer + layers - EDGE, layer
                rows = pl.ds(x_place(index, max(near, 0), ny).start + start, width)
                out[y_place(index, layer, slabs)] = x_low[rows]
                rows = pl.ds(x_place(index, min(far, layers - 1), ny).start + start, width)
                out[y_place(index, EDGE + nx + layer, slabs)] = x_high[rows]
    base_x, base_y = x_rows(nx, ny)[0], y_rows(nx, ny)[0]
    half = (coarse_x + 2 * RIM) // 2
    for face in range(3):
        place = base_x + face * (RIM // 2) * coarse_y
        slabs = [
            wide_slab(
                slab,
                lambda layer: rim_slab(x_low, place, coarse_y, layer),
                faces.at[face],
                lambda layer: rim_slab(x_high, place, coarse_y, layer),
            )
            for slab in range(2 * half)
        ]
        for slab in range(half):
            both = two_in_one(slabs[slab], slabs[slab + half])
            rows = pl.ds(base_y + (face * half + slab) * RIM, RIM)
            low[rows] = both[:RIM]
            high[rows] = both[coarse_y - RIM :]


def fold_four(slabs, even_only=False):
    out = None
    for part in range(2):
        term = exact_dot(two_in_one(slabs[part], slabs[2 + part]), compact(HALF, part, even_only))
        out = term if out is None else out + term
    return out


def coarse_faces(faces, out, tmp):
    rows = faces.shape[2]
    coarse = rows // 2
    fx, fy, fz = faces.at[0], faces.at[1], faces.at[2]
    tmp[...] = pair_slabs(fx)[0]
    x = even_rows(tmp, rows) + odd_rows(tmp, rows)
    first, second = pair_slabs(fy)
    tmp[...] = first + second
    y = even_rows(tmp, rows)
    first, second = pair_slabs(fz)
    tmp[...] = first + second
    z = even_rows(tmp, rows) + odd_rows(tmp, rows)
    out[...] = jnp.zeros(out.shape, F32)
    out[:coarse] = 0.25 * fold_four([x[i] for i in range(4)])
    out[coarse : 2 * coarse] = 0.25 * fold_four([y[i] for i in range(4)])
    out[2 * coarse : 3 * coarse] = 0.25 * fold_four([z[i] for i in range(4)], True)


def weighted(lev, src, slab, start, rows):
    here = pl.ds(start, rows)
    below = pl.ds(start - 1, rows)
    above = pl.ds(start + 1, rows)
    v = src[slab, here]
    total = lev[F, slab, here] + lev[FX, slab, here] * src[slab - 1, here]
    total = total + lev[FX, slab + 1, here] * src[slab + 1, here]
    total = total + lev[FY, slab, here] * src[slab, below]
    total = total + lev[FY, slab, above] * src[slab, above]
    total = total + lev[ZL, slab, here] * roll_lanes(v, 1)
    total = total + lev[ZH, slab, here] * roll_lanes(v, -1)
    return v, total


def swept(lev, src, slab, start, rows):
    v, total = weighted(lev, src, slab, start, rows)
    return (1.0 - OMEGA) * v + lev[W, slab, pl.ds(start, rows)] * total


def set_weights(lev, slab, start, rows, depth, inside=None):
    here = pl.ds(start, rows)
    fz = lev[ZL, slab, here]
    z = lanes_of(fz.shape) % depth
    upper = jnp.where(z == depth - 1, 0.0, roll_lanes(fz, -1))
    diagonal = lev[FX, slab, here] + lev[FX, slab + 1, here]
    diagonal = diagonal + lev[FY, slab, here] + lev[FY, slab, pl.ds(start + 1, rows)] + fz + upper
    valid = diagonal > 0.0
    if inside is not None:
        valid = valid & inside
    lev[ZL, slab, here] = jnp.where(z == 0, 0.0, fz)
    lev[ZH, slab, here] = upper
    lev[D, slab, here] = diagonal
    lev[W, slab, here] = jnp.where(valid, OMEGA / jnp.where(valid, diagonal, 1.0), 0.0)


def run(count, body, unroll=1):
    def step(index, carry):
        body(index)
        return carry

    lax.fori_loop(0, count, step, 0, unroll=unroll)


def clear_pads(ref, rows):
    for start in (0, RIM + rows):
        ref[:, start : start + RIM] = jnp.zeros((ref.shape[0], RIM, LANES), F32)


def level_down(axes, own, faces, coefficients, x_low, x_high, y_low, y_high, *refs):
    top, mid, chunk, v_low, v_high, other, tmp, one, two = refs
    nx, ny = own.shape[1:3]
    slabs, rows = nx + 2 * EDGE, ny + 2 * RIM
    me_x, me_y = lax.axis_index(axes[0]), lax.axis_index(axes[1])
    inner = pl.ds(PAD, ny)
    for index, slot in enumerate(SLOTS):
        layers, width = X_LAYERS[index], Y_LAYERS[index]
        top[slot, :, :PAD] = jnp.zeros((slabs, PAD, LANES), F32)
        top[slot, :, PAD + ny :] = jnp.zeros((slabs, PAD, LANES), F32)
        top[slot, EDGE : EDGE + nx, inner] = own[index]
        for layer in range(EDGE):
            if layer < layers:
                top[slot, EDGE - layers + layer, inner] = x_low[x_place(index, layer, ny)]
                top[slot, EDGE + nx + layer, inner] = x_high[x_place(index, layer, ny)]
            else:
                top[slot, EDGE - 1 - layer, inner] = jnp.zeros((ny, LANES), F32)
                top[slot, EDGE + nx + layer, inner] = jnp.zeros((ny, LANES), F32)
        for slab in range(slabs):
            top[slot, slab, PAD - width : PAD] = y_low[y_place(index, slab, slabs)]
            top[slot, slab, PAD + ny : PAD + ny + width] = y_high[y_place(index, slab, slabs)]
    clear_pads(other, rows)
    row_inside = (rows_of((rows, LANES)) >= RIM) | (me_y > 0)
    main = pl.ds(RIM, rows)
    start_v = top.at[V]

    def first(index):
        slab = index + 1
        inside = row_inside & ((slab >= EDGE) | (me_x > 0))
        set_weights(top, slab, RIM, rows, LANES, inside)
        other[slab, main] = swept(top, start_v, slab, RIM, rows)

    run(slabs - 2, first, 2)

    def second(index):
        slab = index + 2
        top[V, slab, main] = swept(top, other, slab, RIM, rows)

    run(slabs - 4, second, 2)

    def rest(slab):
        v, total = weighted(top, top.at[V], slab, PAD, ny)
        return total - top[D, slab, inner] * v

    def residual(index):
        slab = EDGE + 2 * index
        tmp[index] = rest(slab) + rest(slab + 1)

    run(nx // 2, residual, 2)

    coarse_x, coarse_y = nx // 2, ny // 2
    slabs, rows = coarse_x + 2 * RIM, coarse_y + 2 * RIM
    half = slabs // 2
    inner = pl.ds(2 * RIM, coarse_y)
    main = pl.ds(RIM, rows)
    base_x, base_y = x_rows(nx, ny)[0], y_rows(nx, ny)[0]
    for face, slot in enumerate((FX, FY, ZL)):
        clear_pads(mid.at[slot], rows)
        mid[slot, RIM : RIM + coarse_x, inner] = faces[face]
        place = base_x + face * (RIM // 2) * coarse_y
        for layer in range(RIM):
            mid[slot, layer, inner] = rim_slab(x_low, place, coarse_y, layer)
            mid[slot, RIM + coarse_x + layer, inner] = rim_slab(x_high, place, coarse_y, layer)
        for slab in range(half):
            place = pl.ds(base_y + (face * half + slab) * RIM, RIM)
            for message, row in ((y_low, RIM), (y_high, 2 * RIM + coarse_y)):
                pair = one_of_two(message[place])
                mid[slot, slab, row : row + RIM] = pair[0]
                mid[slot, slab + half, row : row + RIM] = pair[1]
    row_inside = (rows_of((rows, LANES)) >= RIM) | (me_y > 0)
    for slab in range(slabs - 1):
        inside = row_inside & (me_x > 0) if slab < RIM else row_inside
        set_weights(mid, slab, RIM, rows, HALF, inside)

    source = even_rows(tmp, ny) + odd_rows(tmp, ny)
    source = 0.5 * exact_dot(source.reshape(coarse_x * coarse_y, LANES), compact(LANES, 0))
    for ref in (mid.at[F], mid.at[V], one):
        ref[...] = jnp.zeros(ref.shape, F32)
    mid[F, RIM : RIM + coarse_x, inner] = source.reshape(coarse_x, coarse_y, LANES)
    for slab in range(RIM, RIM + coarse_x):
        mid[V, slab, inner] = mid[W, slab, inner] * mid[F, slab, inner]
    for layer in range(RIM // 2):
        near, far = RIM + layer, coarse_x + layer
        v_low[layer * coarse_y : (layer + 1) * coarse_y] = two_in_one(
            mid[V, near, inner], mid[V, near + RIM // 2, inner]
        )
        v_high[layer * coarse_y : (layer + 1) * coarse_y] = two_in_one(
            mid[V, far, inner], mid[V, far + RIM // 2, inner]
        )
    base = RIM // 2 * coarse_y
    for layer in range(2):
        place = pl.ds(base + layer * ny, ny)
        v_low[place] = top[V, EDGE + layer, pl.ds(PAD, ny)]
        v_high[place] = top[V, EDGE + nx - 2 + layer, pl.ds(PAD, ny)]
    for slab in range(RIM - 1, RIM + coarse_x + 1):
        one[slab, main] = swept(mid, mid.at[V], slab, RIM, rows)

    def rest_1(slab):
        v, total = weighted(mid, one, slab, RIM, rows)
        return total - mid[D, slab, main] * v

    two[...] = jnp.zeros(two.shape, F32)
    for pair in range(1, half - 1):
        two[pair] = rest_1(2 * pair) + rest_1(2 * pair + 1)
    pieces = even_rows(two, rows) + odd_rows(two, rows)
    for part in range(half // 4):
        folded = fold_four([pieces[4 * part + i] for i in range(4)])
        chunk[part * rows // 2 : (part + 1) * rows // 2] = 0.5 * folded
    chunk[half // 4 * rows // 2 :] = coefficients[...]


def pack_v(top, mid, x_low, x_high, low, high):
    slabs = mid.shape[1]
    coarse_x = slabs - 2 * RIM
    coarse_y = mid.shape[2] - 4 * RIM
    half = slabs // 2
    own = mid[V, RIM : RIM + coarse_x, 2 * RIM : 2 * RIM + coarse_y]
    values = [
        wide_slab(
            slab,
            lambda layer: rim_slab(x_low, 0, coarse_y, layer),
            own,
            lambda layer: rim_slab(x_high, 0, coarse_y, layer),
        )
        for slab in range(slabs)
    ]
    for slab in range(half):
        both = two_in_one(values[slab], values[slab + half])
        low[slab * RIM : (slab + 1) * RIM] = both[:RIM]
        high[slab * RIM : (slab + 1) * RIM] = both[coarse_y - RIM :]
    nx, ny = 2 * coarse_x, 2 * coarse_y
    base_x, base_y = RIM // 2 * coarse_y, half * RIM
    for out, start in ((low, 0), (high, ny - 2)):
        for layer in range(2):
            rows = pl.ds(base_x + layer * ny + start, 2)
            out[pl.ds(base_y + 2 * layer, 2)] = x_low[rows]
            out[pl.ds(base_y + 2 * (2 + nx + layer), 2)] = x_high[rows]
        for slab in range(nx):
            out[pl.ds(base_y + 2 * (2 + slab), 2)] = top[V, EDGE + slab, pl.ds(PAD + start, 2)]


def stack_blocks(count, *refs):
    out = refs[-1]
    for index in range(count):
        out[index] = refs[index][...]


def pair_rows(values, stride):
    return values + roll_rows(values, -stride)


def pair_lanes(values, stride):
    return values + roll_lanes(values, -stride)


class Listed:
    def __init__(self, fx, fy, fz, stride, depth):
        self.fx, self.fy, self.fz, self.stride, self.depth = fx, fy, fz, stride, depth
        shape = fx[0].shape
        rows = shape[0]
        row, lane = rows_of(shape), lanes_of(shape)
        z = lane % depth
        count = self.count = len(fx)
        self.x_high = [
            fx[s + 1] if s + 1 < count else jnp.where(lane < LANES - depth, roll_lanes(fx[0], -depth), 0.0)
            for s in range(count)
        ]
        self.x_low = [fx[s] if s > 0 else jnp.where(lane >= depth, fx[0], 0.0) for s in range(count)]
        self.y_high = [jnp.where(row < rows - stride, roll_rows(f, -stride), 0.0) for f in fy]
        self.y_low = [jnp.where(row >= stride, f, 0.0) for f in fy]
        self.z_high = [jnp.where(z < depth - stride, roll_lanes(f, -stride), 0.0) for f in fz]
        self.z_low = [jnp.where(z >= stride, f, 0.0) for f in fz]
        self.d = [
            fx[s] + self.x_high[s] + fy[s] + self.y_high[s] + fz[s] + self.z_high[s] for s in range(count)
        ]
        self.w = [jnp.where(d > 0.0, OMEGA / jnp.where(d > 0.0, d, 1.0), 0.0) for d in self.d]

    def weighted(self, v, f):
        count = self.count
        out = []
        for s in range(count):
            low = v[s - 1] if s > 0 else roll_lanes(v[count - 1], self.depth)
            high = v[s + 1] if s + 1 < count else roll_lanes(v[0], -self.depth)
            total = f[s] + self.x_low[s] * low + self.x_high[s] * high
            total = total + self.y_low[s] * roll_rows(v[s], self.stride)
            total = total + self.y_high[s] * roll_rows(v[s], -self.stride)
            total = total + self.z_low[s] * roll_lanes(v[s], self.stride)
            total = total + self.z_high[s] * roll_lanes(v[s], -self.stride)
            out.append(total)
        return out

    def sweep(self, v, f):
        totals = self.weighted(v, f)
        return [(1.0 - OMEGA) * v[s] + self.w[s] * totals[s] for s in range(self.count)]

    def start(self, f):
        return [self.w[s] * f[s] for s in range(self.count)]

    def residual(self, v, f):
        totals = self.weighted(v, f)
        return [totals[s] - self.d[s] * v[s] for s in range(self.count)]

    def kept(self):
        shape = self.fx[0].shape
        step = 2 * self.stride
        return (rows_of(shape) % step == 0) & (lanes_of(shape) % step == 0)

    def coarser(self):
        keep, stride = self.kept(), self.stride
        half = range(self.count // 2)

        def kept(values):
            return jnp.where(keep, 0.25 * values, 0.0)

        fx = [kept(pair_lanes(pair_rows(self.fx[2 * s], stride), stride)) for s in half]
        fy = [kept(pair_lanes(self.fy[2 * s] + self.fy[2 * s + 1], stride)) for s in half]
        fz = [kept(pair_rows(self.fz[2 * s] + self.fz[2 * s + 1], stride)) for s in half]
        return Listed(fx, fy, fz, 2 * stride, self.depth)

    def restrict(self, r):
        keep, stride = self.kept(), self.stride
        return [
            jnp.where(keep, 0.5 * pair_lanes(pair_rows(r[2 * s] + r[2 * s + 1], stride), stride), 0.0)
            for s in range(self.count // 2)
        ]

    def prolong(self, e):
        out = []
        for values in e:
            values = values + roll_rows(values, self.stride)
            values = values + roll_lanes(values, self.stride)
            out += [values, values]
        return out


def listed_cycle(levels, sweeps, f):
    level = levels[0]
    v = level.start(f)
    if len(levels) == 1:
        return lax.fori_loop(0, sweeps - 1, lambda index, values: level.sweep(values, f), v)
    v = level.sweep(v, f)
    e = listed_cycle(levels[1:], sweeps, level.restrict(level.residual(v, f)))
    v = [a + b for a, b in zip(v, level.prolong(e))]
    return level.sweep(level.sweep(v, f), f)


def level_up(axes, grid, sweeps, pieces, top, mid, x_low, x_high, y_low, y_high, out, wide, one, two, tall, post, up):
    devices_x, devices_y = grid
    me_x, me_y = lax.axis_index(axes[0]), lax.axis_index(axes[1])
    coarse_x, coarse_y = mid.shape[1] - 2 * RIM, mid.shape[2] - 4 * RIM
    own_x, own_y = coarse_x // 2, coarse_y // 2
    quarter = LANES // 4
    reach = RIM // 2
    blocks = 4
    count = devices_x * own_x // blocks
    rows = devices_y * own_y
    main = pl.ds(PAD, rows)
    window = own_y + RIM

    def piece(gx, gy):
        slow = (me_x // 2 - gx // 2 + devices_x // 2) % (devices_x // 2)
        far = (me_y // 2 - gy // 2 + devices_y // 2) % (devices_y // 2)
        return ((me_y + gy) % 2, far, (me_x + gx) % 2, slow)

    for ref in (wide, tall):
        ref[...] = jnp.zeros(ref.shape, F32)
    lane = lanes_of((window, LANES))
    for gy in range(devices_y):
        sums = [None] * count
        for gx in range(devices_x):
            where = piece(gx, gy)
            layers = [pieces[where + (pl.ds(part * window, window),)] for part in range(2)]
            for local in range(1, 2 * blocks - 1):
                x = own_x * gx - reach + local
                if not 0 <= x < devices_x * own_x:
                    continue
                block, slab = x // count, x % count
                moved = roll_lanes(layers[local // blocks], (block - local % blocks) * quarter)
                moved = jnp.where(lane // quarter == block, moved, 0.0)
                sums[slab] = moved if sums[slab] is None else sums[slab] + moved
        place = pl.ds(PAD + own_y * gy - reach, window)
        for slab in range(count):
            tall[slab, place] = tall[slab, place] + sums[slab]
    f = [tall[slab, main] for slab in range(count)]

    lane = lanes_of((rows, LANES))
    for gx in range(devices_x):
        for gy in range(devices_y):
            where = piece(gx, gy)
            for face in range(3):
                values = pieces[where + (pl.ds(2 * window + face * own_y, own_y),)]
                wide[face, gx, gy * own_y : (gy + 1) * own_y] = values
    faces = []
    for face in range(3):
        slabs = [None] * count
        for gx in range(devices_x):
            values = wide[face, gx]
            for local in range(own_x):
                x = own_x * gx + local
                block, slab = x // count, x % count
                moved = roll_lanes(values, (block - local) * quarter)
                moved = jnp.where(lane // quarter == block, moved, 0.0)
                slabs[slab] = moved if slabs[slab] is None else slabs[slab] + moved
        faces.append(slabs)
    levels = [Listed(*faces, 1, quarter)]
    while len(levels) < LEVELS - 2:
        levels.append(levels[-1].coarser())
    e = listed_cycle(levels, sweeps, f)

    slabs, high = coarse_x + 2 * RIM, coarse_y + 2 * RIM
    half = slabs // 2
    inner = pl.ds(2 * RIM, coarse_y)
    body = pl.ds(RIM, high)
    one[...] = mid[V]
    clear_pads(two, high)
    for layer in range(RIM):
        one[layer, inner] = rim_slab(x_low, 0, coarse_y, layer)
        one[RIM + coarse_x + layer, inner] = rim_slab(x_high, 0, coarse_y, layer)
    for slab in range(half):
        place = pl.ds(slab * RIM, RIM)
        for message, row in ((y_low, RIM), (y_high, 2 * RIM + coarse_y)):
            pair = one_of_two(message[place])
            one[slab, row : row + RIM] = pair[0]
            one[slab + half, row : row + RIM] = pair[1]
    row = rows_of((high, LANES))
    own_row = (row >= RIM) & (row < RIM + coarse_y)
    for slab in range(1, slabs - 1):
        f_rim = one[slab, body] * mid[D, slab, body] * (1.0 / OMEGA)
        if RIM <= slab < RIM + coarse_x:
            f_rim = jnp.where(own_row, mid[F, slab, body], f_rim)
        mid[F, slab, body] = f_rim
        two[slab, body] = swept(mid, one, slab, RIM, high)

    extra = reach
    tall[:, :PAD] = jnp.zeros((count + 2 * extra, PAD, LANES), F32)
    tall[:, PAD + rows :] = jnp.zeros((count + 2 * extra, PAD, LANES), F32)
    for slab in range(count):
        tall[extra + slab, main] = e[slab]
    for slab in range(extra):
        tall[slab, main] = jnp.where(lane < quarter, 0.0, roll_lanes(e[count - extra + slab], quarter))
        tall[extra + count + slab, main] = jnp.where(
            lane >= LANES - quarter, 0.0, roll_lanes(e[slab], -quarter)
        )
    per_block = count // own_x
    base = me_x % per_block * own_x
    mine = None
    for gy in range(devices_y):
        place = pl.ds(PAD + gy * own_y - reach, window)
        values = tall[pl.ds(base, half), place, :]
        values = jnp.where(me_y == gy, values, 0.0)
        mine = values if mine is None else mine + values
    source = lax.broadcasted_iota(jnp.int32, (LANES, LANES), 0)
    target = lax.broadcasted_iota(jnp.int32, (LANES, LANES), 1)
    hit = (source == me_x // per_block * quarter + target // 2) & (target < HALF)
    fine = exact_dot(mine.reshape(half * window, LANES), jnp.where(hit, 1.0, 0.0).astype(F32))
    fine = fine.reshape(half, window, LANES)
    for odd in range(2):
        up[:half, pl.ds(odd, window, stride=2), :] = fine
    for pair in range(half):
        for slab in (2 * pair, 2 * pair + 1):
            if 1 <= slab < slabs - 1:
                two[slab, body] = two[slab, body] + up[pair, :high]
    for slab in range(2, slabs - 2):
        one[slab, body] = swept(mid, two, slab, RIM, high)
    for slab in range(3, slabs - 3):
        two[slab, body] = swept(mid, one, slab, RIM, high)

    nx, ny = out.shape[:2]
    steps = coarse_x + 2
    fine_rows = ny + 2 * RIM
    e = two[RIM - 1 : RIM - 1 + steps, body]
    fine = exact_dot(e.reshape(steps * high, LANES), expand(LANES, 0)).reshape(steps, high, LANES)
    fine = fine[:, reach : reach + fine_rows // 2]
    for odd in range(2):
        up[:, pl.ds(odd, fine_rows // 2, stride=2), :] = fine
    body = pl.ds(RIM, fine_rows)
    for slot in (0, 1):
        clear_pads(post.at[slot], fine_rows)
    inner = pl.ds(PAD, ny)
    post[0, EDGE : EDGE + nx, inner] = top[V, EDGE : EDGE + nx, inner]
    base_x, base_y = RIM // 2 * coarse_y, half * RIM
    for layer in range(2):
        place = pl.ds(base_x + layer * ny, ny)
        post[0, EDGE - 2 + layer, inner] = x_low[place]
        post[0, EDGE + nx + layer, inner] = x_high[place]
    for slab in range(nx + 4):
        place = pl.ds(base_y + 2 * slab, 2)
        post[0, slab + EDGE - 2, RIM:PAD] = jnp.zeros((RIM, LANES), F32)
        post[0, slab + EDGE - 2, PAD + ny : PAD + ny + RIM] = jnp.zeros((RIM, LANES), F32)
        post[0, slab + EDGE - 2, PAD - 2 : PAD] = y_low[place]
        post[0, slab + EDGE - 2, PAD + ny : PAD + ny + 2] = y_high[place]

    def raise_level(index):
        for slab in (EDGE - 2 + 2 * index, EDGE - 1 + 2 * index):
            post[0, slab, body] = post[0, slab, body] + up[index]

    run(steps, raise_level, 2)

    def fifth(index):
        slab = EDGE - 1 + index
        post[1, slab, body] = swept(top, post.at[0], slab, RIM, fine_rows)

    run(nx + 2, fifth, 2)

    def sixth(index):
        out[index] = swept(top, post.at[1], EDGE + index, PAD, ny)

    run(nx, sixth, 2)


IN_VMEM = pl.BlockSpec(memory_space=pltpu.VMEM)


def call(kernel, outs, scratch=(), from_hbm=False):
    ins = pl.BlockSpec(memory_space=pl.ANY) if from_hbm else IN_VMEM

    def launch(*args):
        if from_hbm:
            args = [pltpu.with_memory_space_constraint(arg, pltpu.HBM) for arg in args]
        return pl.pallas_call(
            kernel,
            out_shape=[pltpu.VMEM(shape, F32) for shape in outs],
            in_specs=[ins] * len(args),
            out_specs=[IN_VMEM] * len(outs),
            scratch_shapes=[pltpu.VMEM(s, F32) if isinstance(s, tuple) else s for s in scratch],
            compiler_params=pltpu.CompilerParams(vmem_limit_bytes=24 * 2**20),
        )(*args)

    return launch


def from_sides(low, high, axis):
    count = lax.axis_size(axis)
    up = [(i, i + 1) for i in range(count - 1)]
    down = [(target, source) for source, target in up]
    return lax.ppermute(high, axis, up), lax.ppermute(low, axis, down)


def paired(block, axis, stride):
    count = lax.axis_size(axis)
    return jnp.stack((block, lax.ppermute(block, axis, [(i, i ^ stride) for i in range(count)])))


def passed_round(block, axis, stride):
    count = lax.axis_size(axis)
    blocks = [block]
    for distance in range(stride, count, stride):
        blocks.append(lax.ppermute(block, axis, [(i, (i + distance) % count) for i in range(count)]))
    return blocks


def fused_cycle(*fields):
    axes = ("gx", "gy")
    devices_x, devices_y = lax.axis_size("gx"), lax.axis_size("gy")
    nx, ny, nz = fields[0].shape
    coarse_x, coarse_y = nx // 2, ny // 2
    x_shape = (sum(x_rows(nx, ny)), LANES)
    y_shape = (sum(y_rows(nx, ny)), LANES)
    own, x_low, x_high, faces = call(
        start_pack,
        [(5, nx, ny, nz), x_shape, x_shape, (3, coarse_x, coarse_y, LANES)],
        [(coarse_x, ny, LANES), pltpu.SemaphoreType.DMA((5,))],
        True,
    )(*fields)
    x_low, x_high = from_sides(x_low, x_high, "gx")
    (coefficients,) = call(coarse_faces, [(16, LANES)], [(coarse_x // 2, coarse_y, LANES)])(faces)
    y_low, y_high = call(pack_y, [y_shape] * 2)(own, faces, x_low, x_high)
    y_low, y_high = from_sides(y_low, y_high, "gy")
    stack = (nx + 2 * EDGE, ny + 4 * RIM, LANES)
    stack_1 = (coarse_x + 2 * RIM, coarse_y + 4 * RIM, LANES)
    half = stack_1[0] // 2
    v_shape = (RIM // 2 * coarse_y + 2 * ny, LANES)
    w_shape = (half * RIM + 2 * (nx + 4), LANES)
    top, mid, chunk, v_low, v_high = call(
        functools.partial(level_down, axes),
        [(D + 1,) + stack, (D + 1,) + stack_1, (32, LANES), v_shape, v_shape],
        [stack, (nx // 2, ny, LANES), stack_1, (half, coarse_y + 2 * RIM, LANES)],
    )(own, faces, coefficients, x_low, x_high, y_low, y_high)

    blocks = passed_round(chunk, "gx", 2)
    v_low, v_high = from_sides(v_low, v_high, "gx")
    slow = (len(blocks),) + chunk.shape
    (pieces,) = call(functools.partial(stack_blocks, len(blocks)), [slow])(*blocks, v_low, v_high)
    w_low, w_high = call(pack_v, [w_shape] * 2)(top, mid, v_low, v_high)
    pieces = paired(pieces, "gx", 1)
    w_low, w_high = from_sides(w_low, w_high, "gy")
    blocks = passed_round(pieces, "gy", 2)
    slow = (len(blocks),) + pieces.shape
    (pieces,) = call(functools.partial(stack_blocks, len(blocks)), [slow])(*blocks, w_low, w_high)
    pieces = paired(pieces, "gy", 1)
    count = devices_x * nx // 16
    rows = devices_y * ny // 4
    coarsest = (devices_x * nx >> LEVELS - 1, devices_y * ny >> LEVELS - 1)
    out = pl.pallas_call(
        functools.partial(level_up, axes, (devices_x, devices_y), 4 * max(coarsest)),
        out_shape=jax.ShapeDtypeStruct((nx, ny, nz), F32),
        in_specs=[IN_VMEM] * 7,
        out_specs=IN_VMEM,
        scratch_shapes=[
            pltpu.VMEM(shape, F32)
            for shape in (
                (3, devices_x, rows, LANES),
                stack_1,
                stack_1,
                (count + RIM, rows + 2 * PAD, LANES),
                (2,) + stack,
                (coarse_x + 2, ny + 2 * RIM, LANES),
            )
        ],
        compiler_params=pltpu.CompilerParams(vmem_limit_bytes=24 * 2**20),
    )(pieces, top, mid, v_low, v_high, w_low, w_high)
    return out


def with_halo(block, sides, width):
    for axis, dim in sides:
        count = lax.axis_size(axis)
        forward = [(i, i + 1) for i in range(count - 1)]
        backward = [(target, source) for source, target in forward]
        low = lax.ppermute(
            lax.slice_in_dim(block, block.shape[dim] - width, None, axis=dim), axis, forward
        )
        high = lax.ppermute(lax.slice_in_dim(block, 0, width, axis=dim), axis, backward)
        block = jnp.concatenate([low, block, high], axis=dim)
    return block


def passed_along(block, axis, distance):
    devices = range(lax.axis_size(axis))
    route = [(i - distance, i) for i in devices if i - distance in devices]
    return lax.ppermute(block, axis, route)


def stencil(padded, padded_x, padded_y, face_z):
    center = padded[1:-1, 1:-1]
    zero_plane = jnp.zeros(center.shape[:2] + (1,), center.dtype)
    above_face = jnp.concatenate((face_z[:, :, 1:], zero_plane), axis=2)
    below_z = jnp.concatenate((zero_plane, center[:, :, :-1]), axis=2)
    above_z = jnp.concatenate((center[:, :, 1:], zero_plane), axis=2)
    lower_x = padded_x[1:-1, 1:-1]
    upper_x = padded_x[2:, 1:-1]
    lower_y = padded_y[1:-1, 1:-1]
    upper_y = padded_y[1:-1, 2:]
    applied = lower_x * (center - padded[:-2, 1:-1]) + upper_x * (center - padded[2:, 1:-1])
    applied = (
        applied + lower_y * (center - padded[1:-1, :-2]) + upper_y * (center - padded[1:-1, 2:])
    )
    applied = applied + face_z * (center - below_z) + above_face * (center - above_z)
    diagonal = lower_x + upper_x + lower_y + upper_y + face_z + above_face
    return (applied, diagonal)


def jacobi_sweep(padded, source, padded_x, padded_y, face_z):
    applied, diagonal = stencil(padded, padded_x, padded_y, face_z)
    return padded[1:-1, 1:-1] + OMEGA * (source - applied) / diagonal


def pad_plane(values, width):
    return jnp.pad(values, ((width, width), (width, width), (0, 0)))


def restrict(residual):
    shape = residual.shape
    blocks = residual.reshape(shape[0] // 2, 2, shape[1] // 2, 2, shape[2] // 2, 2)
    return 4.0 * jnp.mean(blocks, axis=(1, 3, 5))


def coarsen_faces(face_x, face_y, face_z):
    shape = face_x.shape
    blocks = (shape[0] // 2, 2, shape[1] // 2, 2, shape[2] // 2, 2)
    coarse_x = jnp.mean(face_x.reshape(blocks)[:, 0], axis=(2, 4))
    coarse_y = jnp.mean(face_y.reshape(blocks)[:, :, :, 0], axis=(1, 4))
    coarse_z = jnp.mean(face_z.reshape(blocks)[..., 0], axis=(1, 3))
    return (coarse_x, coarse_y, coarse_z)


def prolong(coarse):
    return jnp.repeat(jnp.repeat(jnp.repeat(coarse, 2, axis=0), 2, axis=1), 2, axis=2)


def local_cycle(grid_level, iterate, source, face_x, face_y, face_z):
    padded_x = pad_plane(face_x, 1)
    padded_y = pad_plane(face_y, 1)
    if grid_level == LEVELS - 1:
        count = 4 * max(iterate.shape[0], iterate.shape[1])

        def one_sweep(index, values):
            return jacobi_sweep(pad_plane(values, 1), source, padded_x, padded_y, face_z)

        return lax.fori_loop(0, count, one_sweep, iterate)
    for sweep_index in range(2):
        iterate = jacobi_sweep(pad_plane(iterate, 1), source, padded_x, padded_y, face_z)
    applied, diagonal = stencil(pad_plane(iterate, 1), padded_x, padded_y, face_z)
    coarse_src = restrict(source - applied)
    coarse_x, coarse_y, coarse_z = coarsen_faces(face_x, face_y, face_z)
    correction = local_cycle(
        grid_level + 1, jnp.zeros_like(coarse_src), coarse_src, coarse_x, coarse_y, coarse_z
    )
    iterate = iterate + prolong(correction)
    for sweep_index in range(2):
        iterate = jacobi_sweep(pad_plane(iterate, 1), source, padded_x, padded_y, face_z)
    return iterate


def field_rim(iterate):
    return with_halo(iterate, (("gx", 0), ("gy", 1)), 1)


def sweep_pair_narrow(iterate, source, padded_x, padded_y, face_z, zero_start):
    for sweep_index in range(2):
        if sweep_index == 0 and zero_start:
            padded = pad_plane(iterate, 1)
        else:
            padded = field_rim(iterate)
        iterate = jacobi_sweep(padded, source, padded_x, padded_y, face_z)
    return iterate


def descend(grid_level, iterate, source, face_x, face_y, face_z, zero_start, gather_level):
    if grid_level == gather_level:
        pieces = (
            lax.all_gather(source, "gy", axis=1, tiled=True),
            lax.all_gather(face_x, "gy", axis=1, tiled=True),
            lax.all_gather(face_y, "gy", axis=1, tiled=True),
            lax.all_gather(face_z, "gy", axis=1, tiled=True),
        )
        gathered = (
            lax.all_gather(pieces[0], "gx", axis=0, tiled=True),
            lax.all_gather(pieces[1], "gx", axis=0, tiled=True),
            lax.all_gather(pieces[2], "gx", axis=0, tiled=True),
            lax.all_gather(pieces[3], "gx", axis=0, tiled=True),
        )
        correction = local_cycle(
            grid_level,
            jnp.zeros_like(gathered[0]),
            gathered[0],
            gathered[1],
            gathered[2],
            gathered[3],
        )
        start_x = lax.axis_index("gx") * source.shape[0]
        start_y = lax.axis_index("gy") * source.shape[1]
        return lax.dynamic_slice(
            correction, (start_x, start_y, jnp.zeros((), jnp.int32)), source.shape
        )
    next_x = passed_along(face_x[:1], "gx", -1)
    next_y = passed_along(face_y[:, :1], "gy", -1)
    lower_row = jnp.zeros_like(next_x)
    lower_col = jnp.zeros_like(next_y)
    padded_x = jnp.pad(
        jnp.concatenate((lower_row, face_x, next_x), axis=0), ((0, 0), (1, 1), (0, 0))
    )
    padded_y = jnp.pad(
        jnp.concatenate((lower_col, face_y, next_y), axis=1), ((1, 1), (0, 0), (0, 0))
    )

    def smoother(values, starting):
        return sweep_pair_narrow(values, source, padded_x, padded_y, face_z, starting)

    iterate = smoother(iterate, zero_start)
    applied, diagonal = stencil(field_rim(iterate), padded_x, padded_y, face_z)
    coarse_src = restrict(source - applied)
    coarse_x, coarse_y, coarse_z = coarsen_faces(face_x, face_y, face_z)
    correction = descend(
        grid_level + 1,
        jnp.zeros_like(coarse_src),
        coarse_src,
        coarse_x,
        coarse_y,
        coarse_z,
        True,
        gather_level,
    )
    iterate = iterate + prolong(correction)
    return smoother(iterate, False)


def fits(nx, ny, nz, devices_x, devices_y):
    cells = devices_x * nx * devices_y * ny * nz // 8
    even = devices_x % 8 == 0 and devices_y % 4 == 0
    return cells <= 2**18 and even and (nx, ny, nz) == (16, 16, LANES)


def local(source_term, initial_guess, face_x, face_y, face_z):
    if fits(*source_term.shape, lax.axis_size("gx"), lax.axis_size("gy")):
        return fused_cycle(source_term, initial_guess, face_x, face_y, face_z)
    gather_level = 4
    return descend(0, initial_guess, source_term, face_x, face_y, face_z, False, gather_level)


def solution(mesh):
    placed = (P("gx", "gy", None),) * 5
    return jax.shard_map(
        local, mesh=mesh, in_specs=placed, out_specs=P("gx", "gy", None), check_vma=False
    )
```

```python
import functools

import jax
import jax.numpy as jnp
from jax import lax
from jax.experimental import pallas as pl
from jax.experimental.pallas import tpu as pltpu
from jax.sharding import PartitionSpec as P

LEVELS = 6
OMEGA = 0.8
LANES = 128
RIM = 4
EDGE = 3
PAD = 8
F32 = jnp.float32

V, F, FX, FY, ZL, ZH, W, D = range(8)
SLOTS = (F, V, FX, FY, ZL)
X_LAYERS = (2, 3, 3, 2, 2)
Y_LAYERS = (2, 3, 2, 3, 2)


def lanes_of(shape):
    return lax.broadcasted_iota(jnp.int32, shape, len(shape) - 1)


def rows_of(shape):
    return lax.broadcasted_iota(jnp.int32, shape, len(shape) - 2)


def roll_lanes(values, step):
    return pltpu.roll(values, step % LANES, values.ndim - 1)


def roll_rows(values, step):
    return pltpu.roll(values, step % values.shape[-2], values.ndim - 2)


def exact_dot(left, right):
    return jnp.dot(left, right, precision=lax.Precision.HIGHEST, preferred_element_type=F32)


def compact(depth, part, even_only=False):
    source = lax.broadcasted_iota(jnp.int32, (LANES, LANES), 0)
    target = lax.broadcasted_iota(jnp.int32, (LANES, LANES), 1)
    half = depth // 2
    hit = target == (source // depth * 2 + part) * half + source % depth // 2
    if even_only:
        hit = hit & (source % 2 == 0)
    return jnp.where(hit, 1.0, 0.0).astype(F32)


def expand(depth, part):
    target = lax.broadcasted_iota(jnp.int32, (LANES, LANES), 0)
    source = lax.broadcasted_iota(jnp.int32, (LANES, LANES), 1)
    half = depth // 2
    hit = target == (source // depth * 2 + part) * half + source % depth // 2
    return jnp.where(hit, 1.0, 0.0).astype(F32)


def merge_lanes(values, depth, even_only=False):
    count, rows, _ = values.shape
    half = count // 2
    flat = values.reshape(2, half * rows, LANES)
    out = exact_dot(flat[0], compact(depth, 0, even_only))
    out = out + exact_dot(flat[1], compact(depth, 1, even_only))
    return out.reshape(half, rows, LANES)


def even_rows(ref, rows):
    return ref[:, pl.ds(0, rows // 2, stride=2), :]


def odd_rows(ref, rows):
    return ref[:, pl.ds(1, rows // 2, stride=2), :]


HALF = LANES // 2


def low_half(values):
    return jnp.where(lanes_of(values.shape) < HALF, values, 0.0)


def two_in_one(first, second):
    return first + roll_lanes(second, HALF)


def one_of_two(values):
    return low_half(values), low_half(roll_lanes(values, HALF))


def x_rows(nx, ny):
    return sum(X_LAYERS) * ny, 3 * RIM // 2 * (ny // 2)


def y_rows(nx, ny):
    return sum(Y_LAYERS) * (nx + 2 * EDGE), 3 * (nx // 2 + 2 * RIM) // 2 * RIM


def x_place(index, layer, ny):
    return pl.ds((sum(X_LAYERS[:index]) + layer) * ny, ny)


def y_place(index, slab, slabs):
    return pl.ds(sum(Y_LAYERS[:index]) * slabs + slab * Y_LAYERS[index], Y_LAYERS[index])


def start_pack(*refs):
    fields, (own, x_low, x_high, faces, tmp, done) = refs[:5], refs[5:]
    copies = [pltpu.make_async_copy(ref, own.at[index], done.at[index]) for index, ref in enumerate(fields)]
    for copy in copies:
        copy.start()
    nx, ny = own.shape[1:3]
    for index, copy in enumerate(copies):
        copy.wait()
        for layer in range(X_LAYERS[index]):
            x_low[x_place(index, layer, ny)] = own[index, layer]
            x_high[x_place(index, layer, ny)] = own[index, nx - X_LAYERS[index] + layer]
    fx, fy, fz = own.at[2], own.at[3], own.at[4]
    halve = compact(LANES, 0)

    def stored(index, values, matrix):
        count, rows, _ = values.shape
        flat = exact_dot(values.reshape(count * rows, LANES), matrix)
        faces[index] = 0.25 * flat.reshape(count, rows, LANES)

    tmp[...] = pair_slabs(fx)[0]
    stored(0, even_rows(tmp, ny) + odd_rows(tmp, ny), halve)
    first, second = pair_slabs(fy)
    tmp[...] = first + second
    stored(1, even_rows(tmp, ny), halve)
    first, second = pair_slabs(fz)
    tmp[...] = first + second
    stored(2, even_rows(tmp, ny) + odd_rows(tmp, ny), compact(LANES, 0, True))
    base = x_rows(nx, ny)[0]
    coarse_rows = ny // 2
    for face in range(3):
        for layer in range(RIM // 2):
            rows = pl.ds(base + (face * (RIM // 2) + layer) * coarse_rows, coarse_rows)
            top = nx // 2 - RIM + layer
            x_low[rows] = two_in_one(faces[face, layer], faces[face, layer + RIM // 2])
            x_high[rows] = two_in_one(faces[face, top], faces[face, top + RIM // 2])


def pair_slabs(ref):
    count = ref.shape[0]
    values = ref[...].reshape((count // 2, 2) + ref.shape[1:])
    return values[:, 0], values[:, 1]


def wide_slab(slab, from_low, own, from_high):
    count = own.shape[0]
    if slab < RIM:
        return from_low(slab)
    if slab < RIM + count:
        return own[slab - RIM]
    return from_high(slab - RIM - count)


def rim_slab(ref, base, rows, layer):
    place = pl.ds(base + layer % (RIM // 2) * rows, rows)
    return one_of_two(ref[place])[layer // (RIM // 2)]


def pack_y(own, faces, x_low, x_high, low, high):
    coarse_x, coarse_y = faces.shape[1:3]
    nx, ny = 2 * coarse_x, 2 * coarse_y
    slabs = nx + 2 * EDGE
    for index in range(5):
        width, layers = Y_LAYERS[index], X_LAYERS[index]
        for out, start in ((low, 0), (high, ny - width)):
            for slab in range(nx):
                out[y_place(index, EDGE + slab, slabs)] = own[index, slab, start : start + width]
            for layer in range(EDGE):
                near, far = layer + layers - EDGE, layer
                rows = pl.ds(x_place(index, max(near, 0), ny).start + start, width)
                out[y_place(index, layer, slabs)] = x_low[rows]
                rows = pl.ds(x_place(index, min(far, layers - 1), ny).start + start, width)
                out[y_place(index, EDGE + nx + layer, slabs)] = x_high[rows]
    base_x, base_y = x_rows(nx, ny)[0], y_rows(nx, ny)[0]
    half = (coarse_x + 2 * RIM) // 2
    for face in range(3):
        place = base_x + face * (RIM // 2) * coarse_y
        slabs = [
            wide_slab(
                slab,
                lambda layer: rim_slab(x_low, place, coarse_y, layer),
                faces.at[face],
                lambda layer: rim_slab(x_high, place, coarse_y, layer),
            )
            for slab in range(2 * half)
        ]
        for slab in range(half):
            both = two_in_one(slabs[slab], slabs[slab + half])
            rows = pl.ds(base_y + (face * half + slab) * RIM, RIM)
            low[rows] = both[:RIM]
            high[rows] = both[coarse_y - RIM :]


def fold_four(slabs, even_only=False):
    out = None
    for part in range(2):
        term = exact_dot(two_in_one(slabs[part], slabs[2 + part]), compact(HALF, part, even_only))
        out = term if out is None else out + term
    return out


def coarse_faces(faces, out, tmp):
    rows = faces.shape[2]
    coarse = rows // 2
    fx, fy, fz = faces.at[0], faces.at[1], faces.at[2]
    tmp[...] = pair_slabs(fx)[0]
    x = even_rows(tmp, rows) + odd_rows(tmp, rows)
    first, second = pair_slabs(fy)
    tmp[...] = first + second
    y = even_rows(tmp, rows)
    first, second = pair_slabs(fz)
    tmp[...] = first + second
    z = even_rows(tmp, rows) + odd_rows(tmp, rows)
    out[...] = jnp.zeros(out.shape, F32)
    out[:coarse] = 0.25 * fold_four([x[i] for i in range(4)])
    out[coarse : 2 * coarse] = 0.25 * fold_four([y[i] for i in range(4)])
    out[2 * coarse : 3 * coarse] = 0.25 * fold_four([z[i] for i in range(4)], True)


def weighted(lev, src, slab, start, rows, f=None):
    here = pl.ds(start, rows)
    below = pl.ds(start - 1, rows)
    above = pl.ds(start + 1, rows)
    v = src[slab, here]
    f = lev.at[F] if f is None else f
    total = f[slab, here] + lev[FX, slab, here] * src[slab - 1, here]
    total = total + lev[FX, slab + 1, here] * src[slab + 1, here]
    total = total + lev[FY, slab, here] * src[slab, below]
    total = total + lev[FY, slab, above] * src[slab, above]
    total = total + lev[ZL, slab, here] * roll_lanes(v, 1)
    total = total + lev[ZH, slab, here] * roll_lanes(v, -1)
    return v, total


def swept(lev, src, slab, start, rows, f=None):
    v, total = weighted(lev, src, slab, start, rows, f)
    return (1.0 - OMEGA) * v + lev[W, slab, pl.ds(start, rows)] * total


def set_weights(lev, slab, start, rows, depth, inside=None):
    here = pl.ds(start, rows)
    fz = lev[ZL, slab, here]
    z = lanes_of(fz.shape) % depth
    upper = jnp.where(z == depth - 1, 0.0, roll_lanes(fz, -1))
    diagonal = lev[FX, slab, here] + lev[FX, slab + 1, here]
    diagonal = diagonal + lev[FY, slab, here] + lev[FY, slab, pl.ds(start + 1, rows)] + fz + upper
    valid = diagonal > 0.0
    if inside is not None:
        valid = valid & inside
    lev[ZL, slab, here] = jnp.where(z == 0, 0.0, fz)
    lev[ZH, slab, here] = upper
    lev[D, slab, here] = diagonal
    lev[W, slab, here] = jnp.where(valid, OMEGA / jnp.where(valid, diagonal, 1.0), 0.0)


def run(count, body, unroll=1):
    def step(index, carry):
        body(index)
        return carry

    lax.fori_loop(0, count, step, 0, unroll=unroll)


def clear_pads(ref, rows):
    for start in (0, RIM + rows):
        ref[:, start : start + RIM] = jnp.zeros((ref.shape[0], RIM, LANES), F32)


def level_down(axes, own, faces, coefficients, x_low, x_high, y_low, y_high, *refs):
    top, mid, chunk, v_low, v_high, other, tmp, one, two = refs
    nx, ny = own.shape[1:3]
    slabs, rows = nx + 2 * EDGE, ny + 2 * RIM
    me_x, me_y = lax.axis_index(axes[0]), lax.axis_index(axes[1])
    inner = pl.ds(PAD, ny)
    for index, slot in enumerate(SLOTS):
        layers, width = X_LAYERS[index], Y_LAYERS[index]
        top[slot, :, :PAD] = jnp.zeros((slabs, PAD, LANES), F32)
        top[slot, :, PAD + ny :] = jnp.zeros((slabs, PAD, LANES), F32)
        top[slot, EDGE : EDGE + nx, inner] = own[index]
        for layer in range(EDGE):
            if layer < layers:
                top[slot, EDGE - layers + layer, inner] = x_low[x_place(index, layer, ny)]
                top[slot, EDGE + nx + layer, inner] = x_high[x_place(index, layer, ny)]
            else:
                top[slot, EDGE - 1 - layer, inner] = jnp.zeros((ny, LANES), F32)
                top[slot, EDGE + nx + layer, inner] = jnp.zeros((ny, LANES), F32)
        for slab in range(slabs):
            top[slot, slab, PAD - width : PAD] = y_low[y_place(index, slab, slabs)]
            top[slot, slab, PAD + ny : PAD + ny + width] = y_high[y_place(index, slab, slabs)]
    clear_pads(other, rows)
    row_inside = (rows_of((rows, LANES)) >= RIM) | (me_y > 0)
    main = pl.ds(RIM, rows)
    start_v = top.at[V]

    def first(index):
        slab = index + 1
        inside = row_inside & ((slab >= EDGE) | (me_x > 0))
        set_weights(top, slab, RIM, rows, LANES, inside)
        other[slab, main] = swept(top, start_v, slab, RIM, rows)

    run(slabs - 2, first, 2)

    def second(index):
        slab = index + 2
        top[V, slab, main] = swept(top, other, slab, RIM, rows)

    run(slabs - 4, second, 2)

    def rest(slab):
        v, total = weighted(top, top.at[V], slab, PAD, ny)
        return total - top[D, slab, inner] * v

    def residual(index):
        slab = EDGE + 2 * index
        tmp[index] = rest(slab) + rest(slab + 1)

    run(nx // 2, residual, 2)

    coarse_x, coarse_y = nx // 2, ny // 2
    slabs, rows = coarse_x + 2 * RIM, coarse_y + 2 * RIM
    half = slabs // 2
    inner = pl.ds(2 * RIM, coarse_y)
    main = pl.ds(RIM, rows)
    base_x, base_y = x_rows(nx, ny)[0], y_rows(nx, ny)[0]
    for face, slot in enumerate((FX, FY, ZL)):
        clear_pads(mid.at[slot], rows)
        mid[slot, RIM : RIM + coarse_x, inner] = faces[face]
        place = base_x + face * (RIM // 2) * coarse_y
        for layer in range(RIM):
            mid[slot, layer, inner] = rim_slab(x_low, place, coarse_y, layer)
            mid[slot, RIM + coarse_x + layer, inner] = rim_slab(x_high, place, coarse_y, layer)
        for slab in range(half):
            place = pl.ds(base_y + (face * half + slab) * RIM, RIM)
            for message, row in ((y_low, RIM), (y_high, 2 * RIM + coarse_y)):
                pair = one_of_two(message[place])
                mid[slot, slab, row : row + RIM] = pair[0]
                mid[slot, slab + half, row : row + RIM] = pair[1]
    row_inside = (rows_of((rows, LANES)) >= RIM) | (me_y > 0)
    for slab in range(slabs - 1):
        inside = row_inside & (me_x > 0) if slab < RIM else row_inside
        set_weights(mid, slab, RIM, rows, HALF, inside)

    source = even_rows(tmp, ny) + odd_rows(tmp, ny)
    source = 0.5 * exact_dot(source.reshape(coarse_x * coarse_y, LANES), compact(LANES, 0))
    for ref in (mid.at[F], mid.at[V], one):
        ref[...] = jnp.zeros(ref.shape, F32)
    mid[F, RIM : RIM + coarse_x, inner] = source.reshape(coarse_x, coarse_y, LANES)
    for slab in range(RIM, RIM + coarse_x):
        mid[V, slab, inner] = mid[W, slab, inner] * mid[F, slab, inner]
    for layer in range(RIM // 2):
        near, far = RIM + layer, coarse_x + layer
        v_low[layer * coarse_y : (layer + 1) * coarse_y] = two_in_one(
            mid[V, near, inner], mid[V, near + RIM // 2, inner]
        )
        v_high[layer * coarse_y : (layer + 1) * coarse_y] = two_in_one(
            mid[V, far, inner], mid[V, far + RIM // 2, inner]
        )
    base = RIM // 2 * coarse_y
    for layer in range(2):
        place = pl.ds(base + layer * ny, ny)
        v_low[place] = top[V, EDGE + layer, pl.ds(PAD, ny)]
        v_high[place] = top[V, EDGE + nx - 2 + layer, pl.ds(PAD, ny)]
    for slab in range(RIM - 1, RIM + coarse_x + 1):
        one[slab, main] = swept(mid, mid.at[V], slab, RIM, rows)

    def rest_1(slab):
        v, total = weighted(mid, one, slab, RIM, rows)
        return total - mid[D, slab, main] * v

    two[...] = jnp.zeros(two.shape, F32)
    for pair in range(1, half - 1):
        two[pair] = rest_1(2 * pair) + rest_1(2 * pair + 1)
    pieces = even_rows(two, rows) + odd_rows(two, rows)
    for part in range(half // 4):
        folded = fold_four([pieces[4 * part + i] for i in range(4)])
        chunk[part * rows // 2 : (part + 1) * rows // 2] = 0.5 * folded
    chunk[half // 4 * rows // 2 :] = coefficients[...]


def pack_v(top, mid, x_low, x_high, low, high):
    slabs = mid.shape[1]
    coarse_x = slabs - 2 * RIM
    coarse_y = mid.shape[2] - 4 * RIM
    half = slabs // 2
    own = mid[V, RIM : RIM + coarse_x, 2 * RIM : 2 * RIM + coarse_y]
    values = [
        wide_slab(
            slab,
            lambda layer: rim_slab(x_low, 0, coarse_y, layer),
            own,
            lambda layer: rim_slab(x_high, 0, coarse_y, layer),
        )
        for slab in range(slabs)
    ]
    for slab in range(half):
        both = two_in_one(values[slab], values[slab + half])
        low[slab * RIM : (slab + 1) * RIM] = both[:RIM]
        high[slab * RIM : (slab + 1) * RIM] = both[coarse_y - RIM :]
    nx, ny = 2 * coarse_x, 2 * coarse_y
    base_x, base_y = RIM // 2 * coarse_y, half * RIM
    for out, start in ((low, 0), (high, ny - 2)):
        for layer in range(2):
            rows = pl.ds(base_x + layer * ny + start, 2)
            out[pl.ds(base_y + 2 * layer, 2)] = x_low[rows]
            out[pl.ds(base_y + 2 * (2 + nx + layer), 2)] = x_high[rows]
        for slab in range(nx):
            out[pl.ds(base_y + 2 * (2 + slab), 2)] = top[V, EDGE + slab, pl.ds(PAD + start, 2)]


def stack_blocks(count, blocks, *refs):
    for index in range(blocks):
        refs[count][index] = refs[index][...]
    for index in range(blocks, count):
        if index + 1 - blocks < len(refs) - count:
            refs[count + 1 + index - blocks][...] = refs[index][...]


def pair_rows(values, stride):
    return values + roll_rows(values, -stride)


def pair_lanes(values, stride):
    return values + roll_lanes(values, -stride)


class Listed:
    def __init__(self, fx, fy, fz, stride, depth):
        self.fx, self.fy, self.fz, self.stride, self.depth = fx, fy, fz, stride, depth
        shape = fx[0].shape
        rows = shape[0]
        row, lane = rows_of(shape), lanes_of(shape)
        z = lane % depth
        count = self.count = len(fx)
        self.x_high = [
            fx[s + 1] if s + 1 < count else jnp.where(lane < LANES - depth, roll_lanes(fx[0], -depth), 0.0)
            for s in range(count)
        ]
        self.x_low = [fx[s] if s > 0 else jnp.where(lane >= depth, fx[0], 0.0) for s in range(count)]
        self.y_high = [jnp.where(row < rows - stride, roll_rows(f, -stride), 0.0) for f in fy]
        self.y_low = [jnp.where(row >= stride, f, 0.0) for f in fy]
        self.z_high = [jnp.where(z < depth - stride, roll_lanes(f, -stride), 0.0) for f in fz]
        self.z_low = [jnp.where(z >= stride, f, 0.0) for f in fz]
        self.d = [
            fx[s] + self.x_high[s] + fy[s] + self.y_high[s] + fz[s] + self.z_high[s] for s in range(count)
        ]
        self.w = [jnp.where(d > 0.0, OMEGA / jnp.where(d > 0.0, d, 1.0), 0.0) for d in self.d]

    def weighted(self, v, f):
        count = self.count
        out = []
        for s in range(count):
            low = v[s - 1] if s > 0 else roll_lanes(v[count - 1], self.depth)
            high = v[s + 1] if s + 1 < count else roll_lanes(v[0], -self.depth)
            total = f[s] + self.x_low[s] * low + self.x_high[s] * high
            total = total + self.y_low[s] * roll_rows(v[s], self.stride)
            total = total + self.y_high[s] * roll_rows(v[s], -self.stride)
            total = total + self.z_low[s] * roll_lanes(v[s], self.stride)
            total = total + self.z_high[s] * roll_lanes(v[s], -self.stride)
            out.append(total)
        return out

    def sweep(self, v, f):
        totals = self.weighted(v, f)
        return [(1.0 - OMEGA) * v[s] + self.w[s] * totals[s] for s in range(self.count)]

    def start(self, f):
        return [self.w[s] * f[s] for s in range(self.count)]

    def residual(self, v, f):
        totals = self.weighted(v, f)
        return [totals[s] - self.d[s] * v[s] for s in range(self.count)]

    def kept(self):
        shape = self.fx[0].shape
        step = 2 * self.stride
        return (rows_of(shape) % step == 0) & (lanes_of(shape) % step == 0)

    def coarser(self):
        keep, stride = self.kept(), self.stride
        half = range(self.count // 2)

        def kept(values):
            return jnp.where(keep, 0.25 * values, 0.0)

        fx = [kept(pair_lanes(pair_rows(self.fx[2 * s], stride), stride)) for s in half]
        fy = [kept(pair_lanes(self.fy[2 * s] + self.fy[2 * s + 1], stride)) for s in half]
        fz = [kept(pair_rows(self.fz[2 * s] + self.fz[2 * s + 1], stride)) for s in half]
        return Listed(fx, fy, fz, 2 * stride, self.depth)

    def restrict(self, r):
        keep, stride = self.kept(), self.stride
        return [
            jnp.where(keep, 0.5 * pair_lanes(pair_rows(r[2 * s] + r[2 * s + 1], stride), stride), 0.0)
            for s in range(self.count // 2)
        ]

    def prolong(self, e):
        out = []
        for values in e:
            values = values + roll_rows(values, self.stride)
            values = values + roll_lanes(values, self.stride)
            out += [values, values]
        return out


def listed_cycle(levels, sweeps, f):
    level = levels[0]
    v = level.start(f)
    if len(levels) == 1:
        return lax.fori_loop(0, sweeps - 1, lambda index, values: level.sweep(values, f), v)
    v = level.sweep(v, f)
    e = listed_cycle(levels[1:], sweeps, level.restrict(level.residual(v, f)))
    v = [a + b for a, b in zip(v, level.prolong(e))]
    return level.sweep(level.sweep(v, f), f)


def level_two(axes, grid, sweeps, shape, pieces, out, wide, tall):
    devices_x, devices_y = grid
    me_x, me_y = lax.axis_index(axes[0]), lax.axis_index(axes[1])
    own_x, own_y = shape
    quarter = LANES // 4
    reach = RIM // 2
    blocks = 4
    count = devices_x * own_x // blocks
    rows = devices_y * own_y
    main = pl.ds(PAD, rows)
    window = own_y + RIM

    def piece(gx, gy):
        slow = (me_x // 2 - gx // 2 + devices_x // 2) % (devices_x // 2)
        far = (me_y // 2 - gy // 2 + devices_y // 2) % (devices_y // 2)
        return ((me_y + gy) % 2, (me_x + gx) % 2 * (devices_y // 2) + far, slow)

    for ref in (wide, tall):
        ref[...] = jnp.zeros(ref.shape, F32)
    lane = lanes_of((window, LANES))
    for gy in range(devices_y):
        sums = [None] * count
        for gx in range(devices_x):
            where = piece(gx, gy)
            layers = [pieces[where + (pl.ds(part * window, window),)] for part in range(2)]
            for local in range(1, 2 * blocks - 1):
                x = own_x * gx - reach + local
                if not 0 <= x < devices_x * own_x:
                    continue
                block, slab = x // count, x % count
                moved = roll_lanes(layers[local // blocks], (block - local % blocks) * quarter)
                moved = jnp.where(lane // quarter == block, moved, 0.0)
                sums[slab] = moved if sums[slab] is None else sums[slab] + moved
        place = pl.ds(PAD + own_y * gy - reach, window)
        for slab in range(count):
            tall[slab, place] = tall[slab, place] + sums[slab]
    f = [tall[slab, main] for slab in range(count)]

    lane = lanes_of((rows, LANES))
    for gx in range(devices_x):
        for gy in range(devices_y):
            where = piece(gx, gy)
            for face in range(3):
                values = pieces[where + (pl.ds(2 * window + face * own_y, own_y),)]
                wide[face, gx, gy * own_y : (gy + 1) * own_y] = values
    faces = []
    for face in range(3):
        slabs = [None] * count
        for gx in range(devices_x):
            values = wide[face, gx]
            for local in range(own_x):
                x = own_x * gx + local
                block, slab = x // count, x % count
                moved = roll_lanes(values, (block - local) * quarter)
                moved = jnp.where(lane // quarter == block, moved, 0.0)
                slabs[slab] = moved if slabs[slab] is None else slabs[slab] + moved
        faces.append(slabs)
    levels = [Listed(*faces, 1, quarter)]
    while len(levels) < LEVELS - 2:
        levels.append(levels[-1].coarser())
    e = listed_cycle(levels, sweeps, f)

    for slab in range(count):
        out[reach + slab, main] = e[slab]
    for slab in range(reach):
        out[slab, main] = jnp.where(lane < quarter, 0.0, roll_lanes(e[count - reach + slab], quarter))
        out[reach + count + slab, main] = jnp.where(
            lane >= LANES - quarter, 0.0, roll_lanes(e[slab], -quarter)
        )
    out[:, :PAD] = jnp.zeros((count + 2 * reach, PAD, LANES), F32)
    out[:, PAD + rows :] = jnp.zeros((count + 2 * reach, PAD, LANES), F32)


def level_up(axes, grid, coarse, top, mid, x_low, x_high, y_low, y_high, out, one, two, right, post, up):
    devices_x, devices_y = grid
    me_x, me_y = lax.axis_index(axes[0]), lax.axis_index(axes[1])
    coarse_x, coarse_y = mid.shape[1] - 2 * RIM, mid.shape[2] - 4 * RIM
    own_x, own_y = coarse_x // 2, coarse_y // 2
    quarter = LANES // 4
    reach = RIM // 2
    window = own_y + RIM

    slabs, high = coarse_x + 2 * RIM, coarse_y + 2 * RIM
    half = slabs // 2
    inner = pl.ds(2 * RIM, coarse_y)
    body = pl.ds(RIM, high)
    one[...] = mid[V]
    clear_pads(two, high)
    for layer in range(RIM):
        one[layer, inner] = rim_slab(x_low, 0, coarse_y, layer)
        one[RIM + coarse_x + layer, inner] = rim_slab(x_high, 0, coarse_y, layer)
    for slab in range(half):
        place = pl.ds(slab * RIM, RIM)
        for message, row in ((y_low, RIM), (y_high, 2 * RIM + coarse_y)):
            pair = one_of_two(message[place])
            one[slab, row : row + RIM] = pair[0]
            one[slab + half, row : row + RIM] = pair[1]
    row = rows_of((high, LANES))
    own_row = (row >= RIM) & (row < RIM + coarse_y)
    for slab in range(1, slabs - 1):
        f_rim = one[slab, body] * mid[D, slab, body] * (1.0 / OMEGA)
        if RIM <= slab < RIM + coarse_x:
            f_rim = jnp.where(own_row, mid[F, slab, body], f_rim)
        right[slab, body] = f_rim
        two[slab, body] = swept(mid, one, slab, RIM, high, right)

    per_block = (coarse.shape[0] - 2 * reach) // own_x
    base = me_x % per_block * own_x
    mine = None
    for gy in range(devices_y):
        place = pl.ds(PAD + gy * own_y - reach, window)
        values = jnp.where(me_y == gy, coarse[pl.ds(base, half), place, :], 0.0)
        mine = values if mine is None else mine + values
    source = lax.broadcasted_iota(jnp.int32, (LANES, LANES), 0)
    target = lax.broadcasted_iota(jnp.int32, (LANES, LANES), 1)
    hit = (source == me_x // per_block * quarter + target // 2) & (target < HALF)
    fine = exact_dot(mine.reshape(half * window, LANES), jnp.where(hit, 1.0, 0.0).astype(F32))
    fine = fine.reshape(half, window, LANES)
    for odd in range(2):
        up[:half, pl.ds(odd, window, stride=2), :] = fine
    for pair in range(half):
        for slab in (2 * pair, 2 * pair + 1):
            if 1 <= slab < slabs - 1:
                two[slab, body] = two[slab, body] + up[pair, :high]
    for slab in range(2, slabs - 2):
        one[slab, body] = swept(mid, two, slab, RIM, high, right)
    for slab in range(3, slabs - 3):
        two[slab, body] = swept(mid, one, slab, RIM, high, right)

    nx, ny = out.shape[:2]
    steps = coarse_x + 2
    fine_rows = ny + 2 * RIM
    e = two[RIM - 1 : RIM - 1 + steps, body]
    fine = exact_dot(e.reshape(steps * high, LANES), expand(LANES, 0)).reshape(steps, high, LANES)
    fine = fine[:, reach : reach + fine_rows // 2]
    for odd in range(2):
        up[:, pl.ds(odd, fine_rows // 2, stride=2), :] = fine
    body = pl.ds(RIM, fine_rows)
    for slot in (0, 1):
        clear_pads(post.at[slot], fine_rows)
    inner = pl.ds(PAD, ny)
    post[0, EDGE : EDGE + nx, inner] = top[V, EDGE : EDGE + nx, inner]
    base_x, base_y = RIM // 2 * coarse_y, half * RIM
    for layer in range(2):
        place = pl.ds(base_x + layer * ny, ny)
        post[0, EDGE - 2 + layer, inner] = x_low[place]
        post[0, EDGE + nx + layer, inner] = x_high[place]
    for slab in range(nx + 4):
        place = pl.ds(base_y + 2 * slab, 2)
        post[0, slab + EDGE - 2, RIM:PAD] = jnp.zeros((RIM, LANES), F32)
        post[0, slab + EDGE - 2, PAD + ny : PAD + ny + RIM] = jnp.zeros((RIM, LANES), F32)
        post[0, slab + EDGE - 2, PAD - 2 : PAD] = y_low[place]
        post[0, slab + EDGE - 2, PAD + ny : PAD + ny + 2] = y_high[place]

    def raise_level(index):
        for slab in (EDGE - 2 + 2 * index, EDGE - 1 + 2 * index):
            post[0, slab, body] = post[0, slab, body] + up[index]

    run(steps, raise_level, 2)

    def fifth(index):
        slab = EDGE - 1 + index
        post[1, slab, body] = swept(top, post.at[0], slab, RIM, fine_rows)

    run(nx + 2, fifth, 2)

    def sixth(index):
        out[index] = swept(top, post.at[1], EDGE + index, PAD, ny)

    run(nx, sixth, 2)


IN_VMEM = pl.BlockSpec(memory_space=pltpu.VMEM)


def call(kernel, outs, scratch=(), from_hbm=False):
    ins = pl.BlockSpec(memory_space=pl.ANY) if from_hbm else IN_VMEM

    def launch(*args):
        if from_hbm:
            args = [pltpu.with_memory_space_constraint(arg, pltpu.HBM) for arg in args]
        return pl.pallas_call(
            kernel,
            out_shape=[pltpu.VMEM(shape, F32) for shape in outs],
            in_specs=[ins] * len(args),
            out_specs=[IN_VMEM] * len(outs),
            scratch_shapes=[pltpu.VMEM(s, F32) if isinstance(s, tuple) else s for s in scratch],
            compiler_params=pltpu.CompilerParams(vmem_limit_bytes=24 * 2**20),
        )(*args)

    return launch


def from_sides(low, high, axis):
    count = lax.axis_size(axis)
    up = [(i, i + 1) for i in range(count - 1)]
    down = [(target, source) for source, target in up]
    return lax.ppermute(high, axis, up), lax.ppermute(low, axis, down)


def paired(block, axis, stride):
    count = lax.axis_size(axis)
    return jnp.stack((block, lax.ppermute(block, axis, [(i, i ^ stride) for i in range(count)])))


def passed_round(block, axis, stride):
    count = lax.axis_size(axis)
    blocks = [block]
    for distance in range(stride, count, stride):
        blocks.append(lax.ppermute(block, axis, [(i, (i + distance) % count) for i in range(count)]))
    return blocks


def passed_across(block):
    count, size = lax.axis_size("gx"), lax.axis_size("gy")
    blocks = []
    for side in range(2):
        for distance in range(0, size, 2):
            route = [
                (x * size + y, (x ^ side) * size + (y + distance) % size)
                for x in range(count)
                for y in range(size)
            ]
            moved = side + distance > 0
            blocks.append(lax.ppermute(block, ("gx", "gy"), route) if moved else block)
    return blocks


def fused_cycle(*fields):
    axes = ("gx", "gy")
    devices_x, devices_y = lax.axis_size("gx"), lax.axis_size("gy")
    nx, ny, nz = fields[0].shape
    coarse_x, coarse_y = nx // 2, ny // 2
    x_shape = (sum(x_rows(nx, ny)), LANES)
    y_shape = (sum(y_rows(nx, ny)), LANES)
    own, x_low, x_high, faces = call(
        start_pack,
        [(5, nx, ny, nz), x_shape, x_shape, (3, coarse_x, coarse_y, LANES)],
        [(coarse_x, ny, LANES), pltpu.SemaphoreType.DMA((5,))],
        True,
    )(*fields)
    x_low, x_high = from_sides(x_low, x_high, "gx")
    (coefficients,) = call(coarse_faces, [(16, LANES)], [(coarse_x // 2, coarse_y, LANES)])(faces)
    y_low, y_high = call(pack_y, [y_shape] * 2)(own, faces, x_low, x_high)
    y_low, y_high = from_sides(y_low, y_high, "gy")
    stack = (nx + 2 * EDGE, ny + 4 * RIM, LANES)
    stack_1 = (coarse_x + 2 * RIM, coarse_y + 4 * RIM, LANES)
    half = stack_1[0] // 2
    v_shape = (RIM // 2 * coarse_y + 2 * ny, LANES)
    w_shape = (half * RIM + 2 * (nx + 4), LANES)
    top, mid, chunk, v_low, v_high = call(
        functools.partial(level_down, axes),
        [(D + 1,) + stack, (D + 1,) + stack_1, (32, LANES), v_shape, v_shape],
        [stack, (nx // 2, ny, LANES), stack_1, (half, coarse_y + 2 * RIM, LANES)],
    )(own, faces, coefficients, x_low, x_high, y_low, y_high)

    blocks = passed_round(chunk, "gx", 2)
    slow = (len(blocks),) + chunk.shape
    pieces, v_low, v_high = call(
        functools.partial(stack_blocks, len(blocks) + 2, len(blocks)), [slow, v_shape, v_shape]
    )(*blocks, v_low, v_high)
    blocks = passed_across(pieces)
    v_low, v_high = from_sides(v_low, v_high, "gx")
    slow = (len(blocks),) + pieces.shape
    (pieces,) = call(functools.partial(stack_blocks, len(blocks) + 2, len(blocks)), [slow])(
        *blocks, v_low, v_high
    )
    pieces = paired(pieces, "gy", 1)
    w_low, w_high = call(pack_v, [w_shape] * 2)(top, mid, v_low, v_high)
    w_low, w_high = from_sides(w_low, w_high, "gy")
    count = devices_x * nx // 16
    rows = devices_y * ny // 4
    grid = (devices_x, devices_y)
    coarsest = (devices_x * nx >> LEVELS - 1, devices_y * ny >> LEVELS - 1)
    wide = (count + RIM, rows + 2 * PAD, LANES)
    (coarse,) = call(
        functools.partial(level_two, axes, grid, 4 * max(coarsest), (nx // 4, ny // 4)),
        [wide],
        [(3, devices_x, rows, LANES), wide],
    )(pieces)
    return pl.pallas_call(
        functools.partial(level_up, axes, grid),
        out_shape=jax.ShapeDtypeStruct((nx, ny, nz), F32),
        in_specs=[IN_VMEM] * 7,
        out_specs=IN_VMEM,
        scratch_shapes=[
            pltpu.VMEM(shape, F32)
            for shape in (stack_1, stack_1, stack_1, (2,) + stack, (coarse_x + 2, ny + 2 * RIM, LANES))
        ],
        compiler_params=pltpu.CompilerParams(vmem_limit_bytes=24 * 2**20),
    )(coarse, top, mid, v_low, v_high, w_low, w_high)


def with_halo(block, sides, width):
    for axis, dim in sides:
        count = lax.axis_size(axis)
        forward = [(i, i + 1) for i in range(count - 1)]
        backward = [(target, source) for source, target in forward]
        low = lax.ppermute(
            lax.slice_in_dim(block, block.shape[dim] - width, None, axis=dim), axis, forward
        )
        high = lax.ppermute(lax.slice_in_dim(block, 0, width, axis=dim), axis, backward)
        block = jnp.concatenate([low, block, high], axis=dim)
    return block


def passed_along(block, axis, distance):
    devices = range(lax.axis_size(axis))
    route = [(i - distance, i) for i in devices if i - distance in devices]
    return lax.ppermute(block, axis, route)


def stencil(padded, padded_x, padded_y, face_z):
    center = padded[1:-1, 1:-1]
    zero_plane = jnp.zeros(center.shape[:2] + (1,), center.dtype)
    above_face = jnp.concatenate((face_z[:, :, 1:], zero_plane), axis=2)
    below_z = jnp.concatenate((zero_plane, center[:, :, :-1]), axis=2)
    above_z = jnp.concatenate((center[:, :, 1:], zero_plane), axis=2)
    lower_x = padded_x[1:-1, 1:-1]
    upper_x = padded_x[2:, 1:-1]
    lower_y = padded_y[1:-1, 1:-1]
    upper_y = padded_y[1:-1, 2:]
    applied = lower_x * (center - padded[:-2, 1:-1]) + upper_x * (center - padded[2:, 1:-1])
    applied = (
        applied + lower_y * (center - padded[1:-1, :-2]) + upper_y * (center - padded[1:-1, 2:])
    )
    applied = applied + face_z * (center - below_z) + above_face * (center - above_z)
    diagonal = lower_x + upper_x + lower_y + upper_y + face_z + above_face
    return (applied, diagonal)


def jacobi_sweep(padded, source, padded_x, padded_y, face_z):
    applied, diagonal = stencil(padded, padded_x, padded_y, face_z)
    return padded[1:-1, 1:-1] + OMEGA * (source - applied) / diagonal


def pad_plane(values, width):
    return jnp.pad(values, ((width, width), (width, width), (0, 0)))


def restrict(residual):
    shape = residual.shape
    blocks = residual.reshape(shape[0] // 2, 2, shape[1] // 2, 2, shape[2] // 2, 2)
    return 4.0 * jnp.mean(blocks, axis=(1, 3, 5))


def coarsen_faces(face_x, face_y, face_z):
    shape = face_x.shape
    blocks = (shape[0] // 2, 2, shape[1] // 2, 2, shape[2] // 2, 2)
    coarse_x = jnp.mean(face_x.reshape(blocks)[:, 0], axis=(2, 4))
    coarse_y = jnp.mean(face_y.reshape(blocks)[:, :, :, 0], axis=(1, 4))
    coarse_z = jnp.mean(face_z.reshape(blocks)[..., 0], axis=(1, 3))
    return (coarse_x, coarse_y, coarse_z)


def prolong(coarse):
    return jnp.repeat(jnp.repeat(jnp.repeat(coarse, 2, axis=0), 2, axis=1), 2, axis=2)


def local_cycle(grid_level, iterate, source, face_x, face_y, face_z):
    padded_x = pad_plane(face_x, 1)
    padded_y = pad_plane(face_y, 1)
    if grid_level == LEVELS - 1:
        count = 4 * max(iterate.shape[0], iterate.shape[1])

        def one_sweep(index, values):
            return jacobi_sweep(pad_plane(values, 1), source, padded_x, padded_y, face_z)

        return lax.fori_loop(0, count, one_sweep, iterate)
    for sweep_index in range(2):
        iterate = jacobi_sweep(pad_plane(iterate, 1), source, padded_x, padded_y, face_z)
    applied, diagonal = stencil(pad_plane(iterate, 1), padded_x, padded_y, face_z)
    coarse_src = restrict(source - applied)
    coarse_x, coarse_y, coarse_z = coarsen_faces(face_x, face_y, face_z)
    correction = local_cycle(
        grid_level + 1, jnp.zeros_like(coarse_src), coarse_src, coarse_x, coarse_y, coarse_z
    )
    iterate = iterate + prolong(correction)
    for sweep_index in range(2):
        iterate = jacobi_sweep(pad_plane(iterate, 1), source, padded_x, padded_y, face_z)
    return iterate


def field_rim(iterate):
    return with_halo(iterate, (("gx", 0), ("gy", 1)), 1)


def sweep_pair_narrow(iterate, source, padded_x, padded_y, face_z, zero_start):
    for sweep_index in range(2):
        if sweep_index == 0 and zero_start:
            padded = pad_plane(iterate, 1)
        else:
            padded = field_rim(iterate)
        iterate = jacobi_sweep(padded, source, padded_x, padded_y, face_z)
    return iterate


def descend(grid_level, iterate, source, face_x, face_y, face_z, zero_start, gather_level):
    if grid_level == gather_level:
        pieces = (
            lax.all_gather(source, "gy", axis=1, tiled=True),
            lax.all_gather(face_x, "gy", axis=1, tiled=True),
            lax.all_gather(face_y, "gy", axis=1, tiled=True),
            lax.all_gather(face_z, "gy", axis=1, tiled=True),
        )
        gathered = (
            lax.all_gather(pieces[0], "gx", axis=0, tiled=True),
            lax.all_gather(pieces[1], "gx", axis=0, tiled=True),
            lax.all_gather(pieces[2], "gx", axis=0, tiled=True),
            lax.all_gather(pieces[3], "gx", axis=0, tiled=True),
        )
        correction = local_cycle(
            grid_level,
            jnp.zeros_like(gathered[0]),
            gathered[0],
            gathered[1],
            gathered[2],
            gathered[3],
        )
        start_x = lax.axis_index("gx") * source.shape[0]
        start_y = lax.axis_index("gy") * source.shape[1]
        return lax.dynamic_slice(
            correction, (start_x, start_y, jnp.zeros((), jnp.int32)), source.shape
        )
    next_x = passed_along(face_x[:1], "gx", -1)
    next_y = passed_along(face_y[:, :1], "gy", -1)
    lower_row = jnp.zeros_like(next_x)
    lower_col = jnp.zeros_like(next_y)
    padded_x = jnp.pad(
        jnp.concatenate((lower_row, face_x, next_x), axis=0), ((0, 0), (1, 1), (0, 0))
    )
    padded_y = jnp.pad(
        jnp.concatenate((lower_col, face_y, next_y), axis=1), ((1, 1), (0, 0), (0, 0))
    )

    def smoother(values, starting):
        return sweep_pair_narrow(values, source, padded_x, padded_y, face_z, starting)

    iterate = smoother(iterate, zero_start)
    applied, diagonal = stencil(field_rim(iterate), padded_x, padded_y, face_z)
    coarse_src = restrict(source - applied)
    coarse_x, coarse_y, coarse_z = coarsen_faces(face_x, face_y, face_z)
    correction = descend(
        grid_level + 1,
        jnp.zeros_like(coarse_src),
        coarse_src,
        coarse_x,
        coarse_y,
        coarse_z,
        True,
        gather_level,
    )
    iterate = iterate + prolong(correction)
    return smoother(iterate, False)


def fits(nx, ny, nz, devices_x, devices_y):
    cells = devices_x * nx * devices_y * ny * nz // 8
    even = devices_x % 8 == 0 and devices_y % 4 == 0
    return cells <= 2**18 and even and (nx, ny, nz) == (16, 16, LANES)


def local(source_term, initial_guess, face_x, face_y, face_z):
    if fits(*source_term.shape, lax.axis_size("gx"), lax.axis_size("gy")):
        return fused_cycle(source_term, initial_guess, face_x, face_y, face_z)
    gather_level = 4
    return descend(0, initial_guess, source_term, face_x, face_y, face_z, False, gather_level)


def solution(mesh):
    placed = (P("gx", "gy", None),) * 5
    return jax.shard_map(
        local, mesh=mesh, in_specs=placed, out_specs=P("gx", "gy", None), check_vma=False
    )
```

```python
import functools

import jax
import jax.numpy as jnp
from jax import lax
from jax.experimental import pallas as pl
from jax.experimental.pallas import tpu as pltpu
from jax.sharding import PartitionSpec as P

LEVELS = 6
OMEGA = 0.8
LANES = 128
RIM = 4
EDGE = 3
PAD = 8
F32 = jnp.float32

V, F, FX, FY, ZL, ZH, W, D = range(8)
SLOTS = (F, V, FX, FY, ZL)
X_LAYERS = (2, 3, 3, 2, 2)
Y_LAYERS = (2, 3, 2, 3, 2)


def lanes_of(shape):
    return lax.broadcasted_iota(jnp.int32, shape, len(shape) - 1)


def rows_of(shape):
    return lax.broadcasted_iota(jnp.int32, shape, len(shape) - 2)


def roll_lanes(values, step):
    return pltpu.roll(values, step % LANES, values.ndim - 1)


def roll_rows(values, step):
    return pltpu.roll(values, step % values.shape[-2], values.ndim - 2)


def exact_dot(left, right):
    return jnp.dot(left, right, precision=lax.Precision.HIGHEST, preferred_element_type=F32)


def compact(depth, part, even_only=False):
    source = lax.broadcasted_iota(jnp.int32, (LANES, LANES), 0)
    target = lax.broadcasted_iota(jnp.int32, (LANES, LANES), 1)
    half = depth // 2
    hit = target == (source // depth * 2 + part) * half + source % depth // 2
    if even_only:
        hit = hit & (source % 2 == 0)
    return jnp.where(hit, 1.0, 0.0).astype(F32)


def expand(depth, part):
    target = lax.broadcasted_iota(jnp.int32, (LANES, LANES), 0)
    source = lax.broadcasted_iota(jnp.int32, (LANES, LANES), 1)
    half = depth // 2
    hit = target == (source // depth * 2 + part) * half + source % depth // 2
    return jnp.where(hit, 1.0, 0.0).astype(F32)


def merge_lanes(values, depth, even_only=False):
    count, rows, _ = values.shape
    half = count // 2
    flat = values.reshape(2, half * rows, LANES)
    out = exact_dot(flat[0], compact(depth, 0, even_only))
    out = out + exact_dot(flat[1], compact(depth, 1, even_only))
    return out.reshape(half, rows, LANES)


def even_rows(ref, rows):
    return ref[:, pl.ds(0, rows // 2, stride=2), :]


def odd_rows(ref, rows):
    return ref[:, pl.ds(1, rows // 2, stride=2), :]


HALF = LANES // 2


def low_half(values):
    return jnp.where(lanes_of(values.shape) < HALF, values, 0.0)


def two_in_one(first, second):
    return first + roll_lanes(second, HALF)


def one_of_two(values):
    return low_half(values), low_half(roll_lanes(values, HALF))


def x_rows(nx, ny):
    return sum(X_LAYERS) * ny, 3 * RIM // 2 * (ny // 2)


def y_rows(nx, ny):
    return sum(Y_LAYERS) * (nx + 2 * EDGE), 3 * (nx // 2 + 2 * RIM) // 2 * RIM


def x_place(index, layer, ny):
    return pl.ds((sum(X_LAYERS[:index]) + layer) * ny, ny)


def y_place(index, slab, slabs):
    return pl.ds(sum(Y_LAYERS[:index]) * slabs + slab * Y_LAYERS[index], Y_LAYERS[index])


def start_pack(*refs):
    fields, (own, x_low, x_high, faces, tmp, done) = refs[:5], refs[5:]
    copies = [pltpu.make_async_copy(ref, own.at[index], done.at[index]) for index, ref in enumerate(fields)]
    for copy in copies:
        copy.start()
    nx, ny = own.shape[1:3]
    for index, copy in enumerate(copies):
        copy.wait()
        for layer in range(X_LAYERS[index]):
            x_low[x_place(index, layer, ny)] = own[index, layer]
            x_high[x_place(index, layer, ny)] = own[index, nx - X_LAYERS[index] + layer]
    fx, fy, fz = own.at[2], own.at[3], own.at[4]
    halve = compact(LANES, 0)

    def stored(index, values, matrix):
        count, rows, _ = values.shape
        flat = exact_dot(values.reshape(count * rows, LANES), matrix)
        faces[index] = 0.25 * flat.reshape(count, rows, LANES)

    tmp[...] = pair_slabs(fx)[0]
    stored(0, even_rows(tmp, ny) + odd_rows(tmp, ny), halve)
    first, second = pair_slabs(fy)
    tmp[...] = first + second
    stored(1, even_rows(tmp, ny), halve)
    first, second = pair_slabs(fz)
    tmp[...] = first + second
    stored(2, even_rows(tmp, ny) + odd_rows(tmp, ny), compact(LANES, 0, True))
    base = x_rows(nx, ny)[0]
    coarse_rows = ny // 2
    for face in range(3):
        for layer in range(RIM // 2):
            rows = pl.ds(base + (face * (RIM // 2) + layer) * coarse_rows, coarse_rows)
            top = nx // 2 - RIM + layer
            x_low[rows] = two_in_one(faces[face, layer], faces[face, layer + RIM // 2])
            x_high[rows] = two_in_one(faces[face, top], faces[face, top + RIM // 2])


def pair_slabs(ref):
    count = ref.shape[0]
    values = ref[...].reshape((count // 2, 2) + ref.shape[1:])
    return values[:, 0], values[:, 1]


def wide_slab(slab, from_low, own, from_high):
    count = own.shape[0]
    if slab < RIM:
        return from_low(slab)
    if slab < RIM + count:
        return own[slab - RIM]
    return from_high(slab - RIM - count)


def rim_slab(ref, base, rows, layer):
    place = pl.ds(base + layer % (RIM // 2) * rows, rows)
    return one_of_two(ref[place])[layer // (RIM // 2)]


def pack_y(own, faces, x_low, x_high, low, high):
    coarse_x, coarse_y = faces.shape[1:3]
    nx, ny = 2 * coarse_x, 2 * coarse_y
    slabs = nx + 2 * EDGE
    for index in range(5):
        width, layers = Y_LAYERS[index], X_LAYERS[index]
        for out, start in ((low, 0), (high, ny - width)):
            for slab in range(nx):
                out[y_place(index, EDGE + slab, slabs)] = own[index, slab, start : start + width]
            for layer in range(EDGE):
                near, far = layer + layers - EDGE, layer
                rows = pl.ds(x_place(index, max(near, 0), ny).start + start, width)
                out[y_place(index, layer, slabs)] = x_low[rows]
                rows = pl.ds(x_place(index, min(far, layers - 1), ny).start + start, width)
                out[y_place(index, EDGE + nx + layer, slabs)] = x_high[rows]
    base_x, base_y = x_rows(nx, ny)[0], y_rows(nx, ny)[0]
    half = (coarse_x + 2 * RIM) // 2
    for face in range(3):
        place = base_x + face * (RIM // 2) * coarse_y
        slabs = [
            wide_slab(
                slab,
                lambda layer: rim_slab(x_low, place, coarse_y, layer),
                faces.at[face],
                lambda layer: rim_slab(x_high, place, coarse_y, layer),
            )
            for slab in range(2 * half)
        ]
        for slab in range(half):
            both = two_in_one(slabs[slab], slabs[slab + half])
            rows = pl.ds(base_y + (face * half + slab) * RIM, RIM)
            low[rows] = both[:RIM]
            high[rows] = both[coarse_y - RIM :]


def fold_four(slabs, even_only=False):
    out = None
    for part in range(2):
        term = exact_dot(two_in_one(slabs[part], slabs[2 + part]), compact(HALF, part, even_only))
        out = term if out is None else out + term
    return out


def coarse_faces(faces, out, tmp):
    rows = faces.shape[2]
    coarse = rows // 2
    fx, fy, fz = faces.at[0], faces.at[1], faces.at[2]
    tmp[...] = pair_slabs(fx)[0]
    x = even_rows(tmp, rows) + odd_rows(tmp, rows)
    first, second = pair_slabs(fy)
    tmp[...] = first + second
    y = even_rows(tmp, rows)
    first, second = pair_slabs(fz)
    tmp[...] = first + second
    z = even_rows(tmp, rows) + odd_rows(tmp, rows)
    out[...] = jnp.zeros(out.shape, F32)
    out[:coarse] = 0.25 * fold_four([x[i] for i in range(4)])
    out[coarse : 2 * coarse] = 0.25 * fold_four([y[i] for i in range(4)])
    out[2 * coarse : 3 * coarse] = 0.25 * fold_four([z[i] for i in range(4)], True)


def weighted(lev, src, slab, start, rows, f=None):
    here = pl.ds(start, rows)
    below = pl.ds(start - 1, rows)
    above = pl.ds(start + 1, rows)
    v = src[slab, here]
    f = lev.at[F] if f is None else f
    total = f[slab, here] + lev[FX, slab, here] * src[slab - 1, here]
    total = total + lev[FX, slab + 1, here] * src[slab + 1, here]
    total = total + lev[FY, slab, here] * src[slab, below]
    total = total + lev[FY, slab, above] * src[slab, above]
    total = total + lev[ZL, slab, here] * roll_lanes(v, 1)
    total = total + lev[ZH, slab, here] * roll_lanes(v, -1)
    return v, total


def swept(lev, src, slab, start, rows, f=None):
    v, total = weighted(lev, src, slab, start, rows, f)
    return (1.0 - OMEGA) * v + lev[W, slab, pl.ds(start, rows)] * total


def set_weights(lev, slab, start, rows, depth, inside=None):
    here = pl.ds(start, rows)
    fz = lev[ZL, slab, here]
    z = lanes_of(fz.shape) % depth
    upper = jnp.where(z == depth - 1, 0.0, roll_lanes(fz, -1))
    diagonal = lev[FX, slab, here] + lev[FX, slab + 1, here]
    diagonal = diagonal + lev[FY, slab, here] + lev[FY, slab, pl.ds(start + 1, rows)] + fz + upper
    valid = diagonal > 0.0
    if inside is not None:
        valid = valid & inside
    lev[ZL, slab, here] = jnp.where(z == 0, 0.0, fz)
    lev[ZH, slab, here] = upper
    lev[D, slab, here] = diagonal
    lev[W, slab, here] = jnp.where(valid, OMEGA / jnp.where(valid, diagonal, 1.0), 0.0)


def run(count, body, unroll=1):
    def step(index, carry):
        body(index)
        return carry

    lax.fori_loop(0, count, step, 0, unroll=unroll)


def clear_pads(ref, rows):
    for start in (0, RIM + rows):
        ref[:, start : start + RIM] = jnp.zeros((ref.shape[0], RIM, LANES), F32)


def level_down(axes, own, faces, coefficients, x_low, x_high, y_low, y_high, *refs):
    top, mid, chunk, v_low, v_high, other, tmp, one, two = refs
    nx, ny = own.shape[1:3]
    slabs, rows = nx + 2 * EDGE, ny + 2 * RIM
    me_x, me_y = lax.axis_index(axes[0]), lax.axis_index(axes[1])
    inner = pl.ds(PAD, ny)
    for index, slot in enumerate(SLOTS):
        layers, width = X_LAYERS[index], Y_LAYERS[index]
        top[slot, :, :PAD] = jnp.zeros((slabs, PAD, LANES), F32)
        top[slot, :, PAD + ny :] = jnp.zeros((slabs, PAD, LANES), F32)
        top[slot, EDGE : EDGE + nx, inner] = own[index]
        for layer in range(EDGE):
            if layer < layers:
                top[slot, EDGE - layers + layer, inner] = x_low[x_place(index, layer, ny)]
                top[slot, EDGE + nx + layer, inner] = x_high[x_place(index, layer, ny)]
            else:
                top[slot, EDGE - 1 - layer, inner] = jnp.zeros((ny, LANES), F32)
                top[slot, EDGE + nx + layer, inner] = jnp.zeros((ny, LANES), F32)
        for slab in range(slabs):
            top[slot, slab, PAD - width : PAD] = y_low[y_place(index, slab, slabs)]
            top[slot, slab, PAD + ny : PAD + ny + width] = y_high[y_place(index, slab, slabs)]
    clear_pads(other, rows)
    row_inside = (rows_of((rows, LANES)) >= RIM) | (me_y > 0)
    main = pl.ds(RIM, rows)
    start_v = top.at[V]

    def first(index):
        slab = index + 1
        inside = row_inside & ((slab >= EDGE) | (me_x > 0))
        set_weights(top, slab, RIM, rows, LANES, inside)
        other[slab, main] = swept(top, start_v, slab, RIM, rows)

    run(slabs - 2, first, 2)

    def second(index):
        slab = index + 2
        top[V, slab, main] = swept(top, other, slab, RIM, rows)

    run(slabs - 4, second, 2)

    def rest(slab):
        v, total = weighted(top, top.at[V], slab, PAD, ny)
        return total - top[D, slab, inner] * v

    def residual(index):
        slab = EDGE + 2 * index
        tmp[index] = rest(slab) + rest(slab + 1)

    run(nx // 2, residual, 2)

    coarse_x, coarse_y = nx // 2, ny // 2
    slabs, rows = coarse_x + 2 * RIM, coarse_y + 2 * RIM
    half = slabs // 2
    inner = pl.ds(2 * RIM, coarse_y)
    main = pl.ds(RIM, rows)
    base_x, base_y = x_rows(nx, ny)[0], y_rows(nx, ny)[0]
    for face, slot in enumerate((FX, FY, ZL)):
        clear_pads(mid.at[slot], rows)
        mid[slot, RIM : RIM + coarse_x, inner] = faces[face]
        place = base_x + face * (RIM // 2) * coarse_y
        for layer in range(RIM):
            mid[slot, layer, inner] = rim_slab(x_low, place, coarse_y, layer)
            mid[slot, RIM + coarse_x + layer, inner] = rim_slab(x_high, place, coarse_y, layer)
        for slab in range(half):
            place = pl.ds(base_y + (face * half + slab) * RIM, RIM)
            for message, row in ((y_low, RIM), (y_high, 2 * RIM + coarse_y)):
                pair = one_of_two(message[place])
                mid[slot, slab, row : row + RIM] = pair[0]
                mid[slot, slab + half, row : row + RIM] = pair[1]
    row_inside = (rows_of((rows, LANES)) >= RIM) | (me_y > 0)
    for slab in range(slabs - 1):
        inside = row_inside & (me_x > 0) if slab < RIM else row_inside
        set_weights(mid, slab, RIM, rows, HALF, inside)

    source = even_rows(tmp, ny) + odd_rows(tmp, ny)
    source = 0.5 * exact_dot(source.reshape(coarse_x * coarse_y, LANES), compact(LANES, 0))
    for ref in (mid.at[F], mid.at[V], one):
        ref[...] = jnp.zeros(ref.shape, F32)
    mid[F, RIM : RIM + coarse_x, inner] = source.reshape(coarse_x, coarse_y, LANES)
    for slab in range(RIM, RIM + coarse_x):
        mid[V, slab, inner] = mid[W, slab, inner] * mid[F, slab, inner]
    for layer in range(RIM // 2):
        near, far = RIM + layer, coarse_x + layer
        v_low[layer * coarse_y : (layer + 1) * coarse_y] = two_in_one(
            mid[V, near, inner], mid[V, near + RIM // 2, inner]
        )
        v_high[layer * coarse_y : (layer + 1) * coarse_y] = two_in_one(
            mid[V, far, inner], mid[V, far + RIM // 2, inner]
        )
    base = RIM // 2 * coarse_y
    for layer in range(2):
        place = pl.ds(base + layer * ny, ny)
        v_low[place] = top[V, EDGE + layer, pl.ds(PAD, ny)]
        v_high[place] = top[V, EDGE + nx - 2 + layer, pl.ds(PAD, ny)]
    for slab in range(RIM - 1, RIM + coarse_x + 1):
        one[slab, main] = swept(mid, mid.at[V], slab, RIM, rows)

    def rest_1(slab):
        v, total = weighted(mid, one, slab, RIM, rows)
        return total - mid[D, slab, main] * v

    two[...] = jnp.zeros(two.shape, F32)
    for pair in range(1, half - 1):
        two[pair] = rest_1(2 * pair) + rest_1(2 * pair + 1)
    pieces = even_rows(two, rows) + odd_rows(two, rows)
    for part in range(half // 4):
        folded = fold_four([pieces[4 * part + i] for i in range(4)])
        chunk[part * rows // 2 : (part + 1) * rows // 2] = 0.5 * folded
    chunk[half // 4 * rows // 2 :] = coefficients[...]


def pack_v(top, mid, x_low, x_high, low, high):
    slabs = mid.shape[1]
    coarse_x = slabs - 2 * RIM
    coarse_y = mid.shape[2] - 4 * RIM
    half = slabs // 2
    own = mid[V, RIM : RIM + coarse_x, 2 * RIM : 2 * RIM + coarse_y]
    values = [
        wide_slab(
            slab,
            lambda layer: rim_slab(x_low, 0, coarse_y, layer),
            own,
            lambda layer: rim_slab(x_high, 0, coarse_y, layer),
        )
        for slab in range(slabs)
    ]
    for slab in range(half):
        both = two_in_one(values[slab], values[slab + half])
        low[slab * RIM : (slab + 1) * RIM] = both[:RIM]
        high[slab * RIM : (slab + 1) * RIM] = both[coarse_y - RIM :]
    nx, ny = 2 * coarse_x, 2 * coarse_y
    base_x, base_y = RIM // 2 * coarse_y, half * RIM
    for out, start in ((low, 0), (high, ny - 2)):
        for layer in range(2):
            rows = pl.ds(base_x + layer * ny + start, 2)
            out[pl.ds(base_y + 2 * layer, 2)] = x_low[rows]
            out[pl.ds(base_y + 2 * (2 + nx + layer), 2)] = x_high[rows]
        for slab in range(nx):
            out[pl.ds(base_y + 2 * (2 + slab), 2)] = top[V, EDGE + slab, pl.ds(PAD + start, 2)]


def stack_blocks(count, blocks, *refs):
    for index in range(blocks):
        refs[count][index] = refs[index][...]
    for index in range(blocks, count):
        if index + 1 - blocks < len(refs) - count:
            refs[count + 1 + index - blocks][...] = refs[index][...]


def pair_rows(values, stride):
    return values + roll_rows(values, -stride)


def pair_lanes(values, stride):
    return values + roll_lanes(values, -stride)


class Listed:
    def __init__(self, fx, fy, fz, stride, depth):
        self.fx, self.fy, self.fz, self.stride, self.depth = fx, fy, fz, stride, depth
        shape = fx[0].shape
        rows = shape[0]
        row, lane = rows_of(shape), lanes_of(shape)
        z = lane % depth
        count = self.count = len(fx)
        self.x_high = [
            fx[s + 1] if s + 1 < count else jnp.where(lane < LANES - depth, roll_lanes(fx[0], -depth), 0.0)
            for s in range(count)
        ]
        self.x_low = [fx[s] if s > 0 else jnp.where(lane >= depth, fx[0], 0.0) for s in range(count)]
        self.y_high = [jnp.where(row < rows - stride, roll_rows(f, -stride), 0.0) for f in fy]
        self.y_low = [jnp.where(row >= stride, f, 0.0) for f in fy]
        self.z_high = [jnp.where(z < depth - stride, roll_lanes(f, -stride), 0.0) for f in fz]
        self.z_low = [jnp.where(z >= stride, f, 0.0) for f in fz]
        self.d = [
            fx[s] + self.x_high[s] + fy[s] + self.y_high[s] + fz[s] + self.z_high[s] for s in range(count)
        ]
        self.w = [jnp.where(d > 0.0, OMEGA / jnp.where(d > 0.0, d, 1.0), 0.0) for d in self.d]

    def weighted(self, v, f):
        count = self.count
        out = []
        for s in range(count):
            low = v[s - 1] if s > 0 else roll_lanes(v[count - 1], self.depth)
            high = v[s + 1] if s + 1 < count else roll_lanes(v[0], -self.depth)
            total = f[s] + self.x_low[s] * low + self.x_high[s] * high
            total = total + self.y_low[s] * roll_rows(v[s], self.stride)
            total = total + self.y_high[s] * roll_rows(v[s], -self.stride)
            total = total + self.z_low[s] * roll_lanes(v[s], self.stride)
            total = total + self.z_high[s] * roll_lanes(v[s], -self.stride)
            out.append(total)
        return out

    def sweep(self, v, f):
        totals = self.weighted(v, f)
        return [(1.0 - OMEGA) * v[s] + self.w[s] * totals[s] for s in range(self.count)]

    def start(self, f):
        return [self.w[s] * f[s] for s in range(self.count)]

    def residual(self, v, f):
        totals = self.weighted(v, f)
        return [totals[s] - self.d[s] * v[s] for s in range(self.count)]

    def kept(self):
        shape = self.fx[0].shape
        step = 2 * self.stride
        return (rows_of(shape) % step == 0) & (lanes_of(shape) % step == 0)

    def coarser(self):
        keep, stride = self.kept(), self.stride
        half = range(self.count // 2)

        def kept(values):
            return jnp.where(keep, 0.25 * values, 0.0)

        fx = [kept(pair_lanes(pair_rows(self.fx[2 * s], stride), stride)) for s in half]
        fy = [kept(pair_lanes(self.fy[2 * s] + self.fy[2 * s + 1], stride)) for s in half]
        fz = [kept(pair_rows(self.fz[2 * s] + self.fz[2 * s + 1], stride)) for s in half]
        return Listed(fx, fy, fz, 2 * stride, self.depth)

    def restrict(self, r):
        keep, stride = self.kept(), self.stride
        return [
            jnp.where(keep, 0.5 * pair_lanes(pair_rows(r[2 * s] + r[2 * s + 1], stride), stride), 0.0)
            for s in range(self.count // 2)
        ]

    def prolong(self, e):
        out = []
        for values in e:
            values = values + roll_rows(values, self.stride)
            values = values + roll_lanes(values, self.stride)
            out += [values, values]
        return out


def listed_cycle(levels, sweeps, f):
    level = levels[0]
    v = level.start(f)
    if len(levels) == 1:
        return lax.fori_loop(0, sweeps - 1, lambda index, values: level.sweep(values, f), v)
    v = level.sweep(v, f)
    e = listed_cycle(levels[1:], sweeps, level.restrict(level.residual(v, f)))
    v = [a + b for a, b in zip(v, level.prolong(e))]
    return level.sweep(level.sweep(v, f), f)


def level_two(axes, grid, sweeps, shape, pieces, out, wide, tall):
    devices_x, devices_y = grid
    me_x, me_y = lax.axis_index(axes[0]), lax.axis_index(axes[1])
    own_x, own_y = shape
    quarter = LANES // 4
    reach = RIM // 2
    blocks = 4
    count = devices_x * own_x // blocks
    rows = devices_y * own_y
    main = pl.ds(PAD, rows)
    window = own_y + RIM

    def piece(gx, gy):
        slow, far = (me_x // 2) ^ (gx // 2), (me_y // 2) ^ (gy // 2)
        return ((me_y + gy) % 2, (me_x + gx) % 2 * (devices_y // 2) + far, slow)

    for ref in (wide, tall):
        ref[...] = jnp.zeros(ref.shape, F32)
    lane = lanes_of((window, LANES))
    for gy in range(devices_y):
        sums = [None] * count
        for gx in range(devices_x):
            where = piece(gx, gy)
            layers = [pieces[where + (pl.ds(part * window, window),)] for part in range(2)]
            for local in range(1, 2 * blocks - 1):
                x = own_x * gx - reach + local
                if not 0 <= x < devices_x * own_x:
                    continue
                block, slab = x // count, x % count
                moved = roll_lanes(layers[local // blocks], (block - local % blocks) * quarter)
                moved = jnp.where(lane // quarter == block, moved, 0.0)
                sums[slab] = moved if sums[slab] is None else sums[slab] + moved
        place = pl.ds(PAD + own_y * gy - reach, window)
        for slab in range(count):
            tall[slab, place] = tall[slab, place] + sums[slab]
    f = [tall[slab, main] for slab in range(count)]

    lane = lanes_of((rows, LANES))
    for gx in range(devices_x):
        for gy in range(devices_y):
            where = piece(gx, gy)
            for face in range(3):
                values = pieces[where + (pl.ds(2 * window + face * own_y, own_y),)]
                wide[face, gx, gy * own_y : (gy + 1) * own_y] = values
    faces = []
    for face in range(3):
        slabs = [None] * count
        for gx in range(devices_x):
            values = wide[face, gx]
            for local in range(own_x):
                x = own_x * gx + local
                block, slab = x // count, x % count
                moved = roll_lanes(values, (block - local) * quarter)
                moved = jnp.where(lane // quarter == block, moved, 0.0)
                slabs[slab] = moved if slabs[slab] is None else slabs[slab] + moved
        faces.append(slabs)
    levels = [Listed(*faces, 1, quarter)]
    while len(levels) < LEVELS - 2:
        levels.append(levels[-1].coarser())
    e = listed_cycle(levels, sweeps, f)

    for slab in range(count):
        out[reach + slab, main] = e[slab]
    for slab in range(reach):
        out[slab, main] = jnp.where(lane < quarter, 0.0, roll_lanes(e[count - reach + slab], quarter))
        out[reach + count + slab, main] = jnp.where(
            lane >= LANES - quarter, 0.0, roll_lanes(e[slab], -quarter)
        )
    out[:, :PAD] = jnp.zeros((count + 2 * reach, PAD, LANES), F32)
    out[:, PAD + rows :] = jnp.zeros((count + 2 * reach, PAD, LANES), F32)


def level_up(axes, grid, coarse, top, mid, x_low, x_high, y_low, y_high, out, one, two, right, post, up):
    devices_x, devices_y = grid
    me_x, me_y = lax.axis_index(axes[0]), lax.axis_index(axes[1])
    coarse_x, coarse_y = mid.shape[1] - 2 * RIM, mid.shape[2] - 4 * RIM
    own_x, own_y = coarse_x // 2, coarse_y // 2
    quarter = LANES // 4
    reach = RIM // 2
    window = own_y + RIM

    slabs, high = coarse_x + 2 * RIM, coarse_y + 2 * RIM
    half = slabs // 2
    inner = pl.ds(2 * RIM, coarse_y)
    body = pl.ds(RIM, high)
    one[...] = mid[V]
    clear_pads(two, high)
    for layer in range(RIM):
        one[layer, inner] = rim_slab(x_low, 0, coarse_y, layer)
        one[RIM + coarse_x + layer, inner] = rim_slab(x_high, 0, coarse_y, layer)
    for slab in range(half):
        place = pl.ds(slab * RIM, RIM)
        for message, row in ((y_low, RIM), (y_high, 2 * RIM + coarse_y)):
            pair = one_of_two(message[place])
            one[slab, row : row + RIM] = pair[0]
            one[slab + half, row : row + RIM] = pair[1]
    row = rows_of((high, LANES))
    own_row = (row >= RIM) & (row < RIM + coarse_y)
    for slab in range(1, slabs - 1):
        f_rim = one[slab, body] * mid[D, slab, body] * (1.0 / OMEGA)
        if RIM <= slab < RIM + coarse_x:
            f_rim = jnp.where(own_row, mid[F, slab, body], f_rim)
        right[slab, body] = f_rim
        two[slab, body] = swept(mid, one, slab, RIM, high, right)

    per_block = (coarse.shape[0] - 2 * reach) // own_x
    base = me_x % per_block * own_x
    mine = None
    for gy in range(devices_y):
        place = pl.ds(PAD + gy * own_y - reach, window)
        values = jnp.where(me_y == gy, coarse[pl.ds(base, half), place, :], 0.0)
        mine = values if mine is None else mine + values
    source = lax.broadcasted_iota(jnp.int32, (LANES, LANES), 0)
    target = lax.broadcasted_iota(jnp.int32, (LANES, LANES), 1)
    hit = (source == me_x // per_block * quarter + target // 2) & (target < HALF)
    fine = exact_dot(mine.reshape(half * window, LANES), jnp.where(hit, 1.0, 0.0).astype(F32))
    fine = fine.reshape(half, window, LANES)
    for odd in range(2):
        up[:half, pl.ds(odd, window, stride=2), :] = fine
    for pair in range(half):
        for slab in (2 * pair, 2 * pair + 1):
            if 1 <= slab < slabs - 1:
                two[slab, body] = two[slab, body] + up[pair, :high]
    for slab in range(2, slabs - 2):
        one[slab, body] = swept(mid, two, slab, RIM, high, right)
    for slab in range(3, slabs - 3):
        two[slab, body] = swept(mid, one, slab, RIM, high, right)

    nx, ny = out.shape[:2]
    steps = coarse_x + 2
    fine_rows = ny + 2 * RIM
    e = two[RIM - 1 : RIM - 1 + steps, body]
    fine = exact_dot(e.reshape(steps * high, LANES), expand(LANES, 0)).reshape(steps, high, LANES)
    fine = fine[:, reach : reach + fine_rows // 2]
    for odd in range(2):
        up[:, pl.ds(odd, fine_rows // 2, stride=2), :] = fine
    body = pl.ds(RIM, fine_rows)
    for slot in (0, 1):
        clear_pads(post.at[slot], fine_rows)
    inner = pl.ds(PAD, ny)
    post[0, EDGE : EDGE + nx, inner] = top[V, EDGE : EDGE + nx, inner]
    base_x, base_y = RIM // 2 * coarse_y, half * RIM
    for layer in range(2):
        place = pl.ds(base_x + layer * ny, ny)
        post[0, EDGE - 2 + layer, inner] = x_low[place]
        post[0, EDGE + nx + layer, inner] = x_high[place]
    for slab in range(nx + 4):
        place = pl.ds(base_y + 2 * slab, 2)
        post[0, slab + EDGE - 2, RIM:PAD] = jnp.zeros((RIM, LANES), F32)
        post[0, slab + EDGE - 2, PAD + ny : PAD + ny + RIM] = jnp.zeros((RIM, LANES), F32)
        post[0, slab + EDGE - 2, PAD - 2 : PAD] = y_low[place]
        post[0, slab + EDGE - 2, PAD + ny : PAD + ny + 2] = y_high[place]

    def raise_level(index):
        for slab in (EDGE - 2 + 2 * index, EDGE - 1 + 2 * index):
            post[0, slab, body] = post[0, slab, body] + up[index]

    run(steps, raise_level, 2)

    def fifth(index):
        slab = EDGE - 1 + index
        post[1, slab, body] = swept(top, post.at[0], slab, RIM, fine_rows)

    run(nx + 2, fifth, 2)

    def sixth(index):
        out[index] = swept(top, post.at[1], EDGE + index, PAD, ny)

    run(nx, sixth, 2)


IN_VMEM = pl.BlockSpec(memory_space=pltpu.VMEM)


def call(kernel, outs, scratch=(), from_hbm=False):
    ins = pl.BlockSpec(memory_space=pl.ANY) if from_hbm else IN_VMEM

    def launch(*args):
        if from_hbm:
            args = [pltpu.with_memory_space_constraint(arg, pltpu.HBM) for arg in args]
        return pl.pallas_call(
            kernel,
            out_shape=[pltpu.VMEM(shape, F32) for shape in outs],
            in_specs=[ins] * len(args),
            out_specs=[IN_VMEM] * len(outs),
            scratch_shapes=[pltpu.VMEM(s, F32) if isinstance(s, tuple) else s for s in scratch],
            compiler_params=pltpu.CompilerParams(vmem_limit_bytes=24 * 2**20),
        )(*args)

    return launch


def pair_route(axis):
    return [(i, i ^ 1) for i in range(lax.axis_size(axis))]


def swap_route(axis):
    count = lax.axis_size(axis)
    return [(i, (i + 1 ^ 1) - 1) for i in range(1, count - 1)]


def by_partner(low, high, axis):
    odd = lax.axis_index(axis) % 2 == 1
    return jnp.where(odd, low, high), jnp.where(odd, high, low)


def from_sides(low, high, axis):
    pair, swap = by_partner(low, high, axis)
    pair = lax.ppermute(pair, axis, pair_route(axis))
    swap = lax.ppermute(swap, axis, swap_route(axis))
    return by_partner(pair, swap, axis)


def passed_round(block, axis, stride):
    count = lax.axis_size(axis)
    return [block] + [
        lax.ppermute(block, axis, [(i, i ^ distance) for i in range(count)])
        for distance in range(stride, count, stride)
    ]


def passed_across(block, rider):
    count, size = lax.axis_size("gx"), lax.axis_size("gy")
    rows = block.shape[0]
    blocks = [block]
    for side in range(2):
        for distance in range(0, size, 2):
            route = [
                (x * size + y, (x ^ side) * size + (y ^ distance)) for x in range(count) for y in range(size)
            ]
            if side == 1 and distance == 0:
                both = lax.ppermute(jnp.concatenate((block, rider)), ("gx", "gy"), route)
                blocks.append(both[:rows])
                rider = both[rows:]
            elif distance > 0:
                blocks.append(lax.ppermute(block, ("gx", "gy"), route))
    return blocks, rider


def fused_cycle(*fields):
    axes = ("gx", "gy")
    devices_x, devices_y = lax.axis_size("gx"), lax.axis_size("gy")
    nx, ny, nz = fields[0].shape
    coarse_x, coarse_y = nx // 2, ny // 2
    x_shape = (sum(x_rows(nx, ny)), LANES)
    y_shape = (sum(y_rows(nx, ny)), LANES)
    own, x_low, x_high, faces = call(
        start_pack,
        [(5, nx, ny, nz), x_shape, x_shape, (3, coarse_x, coarse_y, LANES)],
        [(coarse_x, ny, LANES), pltpu.SemaphoreType.DMA((5,))],
        True,
    )(*fields)
    x_low, x_high = from_sides(x_low, x_high, "gx")
    (coefficients,) = call(coarse_faces, [(16, LANES)], [(coarse_x // 2, coarse_y, LANES)])(faces)
    y_low, y_high = call(pack_y, [y_shape] * 2)(own, faces, x_low, x_high)
    y_low, y_high = from_sides(y_low, y_high, "gy")
    stack = (nx + 2 * EDGE, ny + 4 * RIM, LANES)
    stack_1 = (coarse_x + 2 * RIM, coarse_y + 4 * RIM, LANES)
    half = stack_1[0] // 2
    v_shape = (RIM // 2 * coarse_y + 2 * ny, LANES)
    w_shape = (half * RIM + 2 * (nx + 4), LANES)
    top, mid, chunk, v_low, v_high = call(
        functools.partial(level_down, axes),
        [(D + 1,) + stack, (D + 1,) + stack_1, (32, LANES), v_shape, v_shape],
        [stack, (nx // 2, ny, LANES), stack_1, (half, coarse_y + 2 * RIM, LANES)],
    )(own, faces, coefficients, x_low, x_high, y_low, y_high)

    blocks = passed_round(chunk, "gx", 2)
    slow = (len(blocks),) + chunk.shape
    pieces, v_low, v_high = call(
        functools.partial(stack_blocks, len(blocks) + 2, len(blocks)), [slow, v_shape, v_shape]
    )(*blocks, v_low, v_high)
    pair, swap = by_partner(v_low, v_high, "gx")
    swap = lax.ppermute(swap, "gx", swap_route("gx"))
    blocks, pair = passed_across(pieces.reshape(-1, LANES), pair)
    v_low, v_high = by_partner(pair, swap, "gx")
    w_low, w_high = call(pack_v, [w_shape] * 2)(top, mid, v_low, v_high)
    pair, swap = by_partner(w_low, w_high, "gy")
    message = jnp.concatenate(blocks + [pair])
    swap = lax.ppermute(swap, "gy", swap_route("gy"))
    other = lax.ppermute(message, "gy", pair_route("gy"))
    rows = message.shape[0] - w_shape[0]
    pieces = jnp.stack((message[:rows], other[:rows])).reshape((2, len(blocks)) + slow)
    w_low, w_high = by_partner(other[rows:], swap, "gy")
    count = devices_x * nx // 16
    rows = devices_y * ny // 4
    grid = (devices_x, devices_y)
    coarsest = (devices_x * nx >> LEVELS - 1, devices_y * ny >> LEVELS - 1)
    wide = (count + RIM, rows + 2 * PAD, LANES)
    (coarse,) = call(
        functools.partial(level_two, axes, grid, 4 * max(coarsest), (nx // 4, ny // 4)),
        [wide],
        [(3, devices_x, rows, LANES), wide],
    )(pieces)
    return pl.pallas_call(
        functools.partial(level_up, axes, grid),
        out_shape=jax.ShapeDtypeStruct((nx, ny, nz), F32),
        in_specs=[IN_VMEM] * 7,
        out_specs=IN_VMEM,
        scratch_shapes=[
            pltpu.VMEM(shape, F32)
            for shape in (stack_1, stack_1, stack_1, (2,) + stack, (coarse_x + 2, ny + 2 * RIM, LANES))
        ],
        compiler_params=pltpu.CompilerParams(vmem_limit_bytes=24 * 2**20),
    )(coarse, top, mid, v_low, v_high, w_low, w_high)


def with_halo(block, sides, width):
    for axis, dim in sides:
        count = lax.axis_size(axis)
        forward = [(i, i + 1) for i in range(count - 1)]
        backward = [(target, source) for source, target in forward]
        low = lax.ppermute(
            lax.slice_in_dim(block, block.shape[dim] - width, None, axis=dim), axis, forward
        )
        high = lax.ppermute(lax.slice_in_dim(block, 0, width, axis=dim), axis, backward)
        block = jnp.concatenate([low, block, high], axis=dim)
    return block


def passed_along(block, axis, distance):
    devices = range(lax.axis_size(axis))
    route = [(i - distance, i) for i in devices if i - distance in devices]
    return lax.ppermute(block, axis, route)


def stencil(padded, padded_x, padded_y, face_z):
    center = padded[1:-1, 1:-1]
    zero_plane = jnp.zeros(center.shape[:2] + (1,), center.dtype)
    above_face = jnp.concatenate((face_z[:, :, 1:], zero_plane), axis=2)
    below_z = jnp.concatenate((zero_plane, center[:, :, :-1]), axis=2)
    above_z = jnp.concatenate((center[:, :, 1:], zero_plane), axis=2)
    lower_x = padded_x[1:-1, 1:-1]
    upper_x = padded_x[2:, 1:-1]
    lower_y = padded_y[1:-1, 1:-1]
    upper_y = padded_y[1:-1, 2:]
    applied = lower_x * (center - padded[:-2, 1:-1]) + upper_x * (center - padded[2:, 1:-1])
    applied = (
        applied + lower_y * (center - padded[1:-1, :-2]) + upper_y * (center - padded[1:-1, 2:])
    )
    applied = applied + face_z * (center - below_z) + above_face * (center - above_z)
    diagonal = lower_x + upper_x + lower_y + upper_y + face_z + above_face
    return (applied, diagonal)


def jacobi_sweep(padded, source, padded_x, padded_y, face_z):
    applied, diagonal = stencil(padded, padded_x, padded_y, face_z)
    return padded[1:-1, 1:-1] + OMEGA * (source - applied) / diagonal


def pad_plane(values, width):
    return jnp.pad(values, ((width, width), (width, width), (0, 0)))


def restrict(residual):
    shape = residual.shape
    blocks = residual.reshape(shape[0] // 2, 2, shape[1] // 2, 2, shape[2] // 2, 2)
    return 4.0 * jnp.mean(blocks, axis=(1, 3, 5))


def coarsen_faces(face_x, face_y, face_z):
    shape = face_x.shape
    blocks = (shape[0] // 2, 2, shape[1] // 2, 2, shape[2] // 2, 2)
    coarse_x = jnp.mean(face_x.reshape(blocks)[:, 0], axis=(2, 4))
    coarse_y = jnp.mean(face_y.reshape(blocks)[:, :, :, 0], axis=(1, 4))
    coarse_z = jnp.mean(face_z.reshape(blocks)[..., 0], axis=(1, 3))
    return (coarse_x, coarse_y, coarse_z)


def prolong(coarse):
    return jnp.repeat(jnp.repeat(jnp.repeat(coarse, 2, axis=0), 2, axis=1), 2, axis=2)


def local_cycle(grid_level, iterate, source, face_x, face_y, face_z):
    padded_x = pad_plane(face_x, 1)
    padded_y = pad_plane(face_y, 1)
    if grid_level == LEVELS - 1:
        count = 4 * max(iterate.shape[0], iterate.shape[1])

        def one_sweep(index, values):
            return jacobi_sweep(pad_plane(values, 1), source, padded_x, padded_y, face_z)

        return lax.fori_loop(0, count, one_sweep, iterate)
    for sweep_index in range(2):
        iterate = jacobi_sweep(pad_plane(iterate, 1), source, padded_x, padded_y, face_z)
    applied, diagonal = stencil(pad_plane(iterate, 1), padded_x, padded_y, face_z)
    coarse_src = restrict(source - applied)
    coarse_x, coarse_y, coarse_z = coarsen_faces(face_x, face_y, face_z)
    correction = local_cycle(
        grid_level + 1, jnp.zeros_like(coarse_src), coarse_src, coarse_x, coarse_y, coarse_z
    )
    iterate = iterate + prolong(correction)
    for sweep_index in range(2):
        iterate = jacobi_sweep(pad_plane(iterate, 1), source, padded_x, padded_y, face_z)
    return iterate


def field_rim(iterate):
    return with_halo(iterate, (("gx", 0), ("gy", 1)), 1)


def sweep_pair_narrow(iterate, source, padded_x, padded_y, face_z, zero_start):
    for sweep_index in range(2):
        if sweep_index == 0 and zero_start:
            padded = pad_plane(iterate, 1)
        else:
            padded = field_rim(iterate)
        iterate = jacobi_sweep(padded, source, padded_x, padded_y, face_z)
    return iterate


def descend(grid_level, iterate, source, face_x, face_y, face_z, zero_start, gather_level):
    if grid_level == gather_level:
        pieces = (
            lax.all_gather(source, "gy", axis=1, tiled=True),
            lax.all_gather(face_x, "gy", axis=1, tiled=True),
            lax.all_gather(face_y, "gy", axis=1, tiled=True),
            lax.all_gather(face_z, "gy", axis=1, tiled=True),
        )
        gathered = (
            lax.all_gather(pieces[0], "gx", axis=0, tiled=True),
            lax.all_gather(pieces[1], "gx", axis=0, tiled=True),
            lax.all_gather(pieces[2], "gx", axis=0, tiled=True),
            lax.all_gather(pieces[3], "gx", axis=0, tiled=True),
        )
        correction = local_cycle(
            grid_level,
            jnp.zeros_like(gathered[0]),
            gathered[0],
            gathered[1],
            gathered[2],
            gathered[3],
        )
        start_x = lax.axis_index("gx") * source.shape[0]
        start_y = lax.axis_index("gy") * source.shape[1]
        return lax.dynamic_slice(
            correction, (start_x, start_y, jnp.zeros((), jnp.int32)), source.shape
        )
    next_x = passed_along(face_x[:1], "gx", -1)
    next_y = passed_along(face_y[:, :1], "gy", -1)
    lower_row = jnp.zeros_like(next_x)
    lower_col = jnp.zeros_like(next_y)
    padded_x = jnp.pad(
        jnp.concatenate((lower_row, face_x, next_x), axis=0), ((0, 0), (1, 1), (0, 0))
    )
    padded_y = jnp.pad(
        jnp.concatenate((lower_col, face_y, next_y), axis=1), ((1, 1), (0, 0), (0, 0))
    )

    def smoother(values, starting):
        return sweep_pair_narrow(values, source, padded_x, padded_y, face_z, starting)

    iterate = smoother(iterate, zero_start)
    applied, diagonal = stencil(field_rim(iterate), padded_x, padded_y, face_z)
    coarse_src = restrict(source - applied)
    coarse_x, coarse_y, coarse_z = coarsen_faces(face_x, face_y, face_z)
    correction = descend(
        grid_level + 1,
        jnp.zeros_like(coarse_src),
        coarse_src,
        coarse_x,
        coarse_y,
        coarse_z,
        True,
        gather_level,
    )
    iterate = iterate + prolong(correction)
    return smoother(iterate, False)


def fits(nx, ny, nz, devices_x, devices_y):
    cells = devices_x * nx * devices_y * ny * nz // 8
    even = devices_x % 8 == 0 and devices_y % 4 == 0
    even = even and devices_x & (devices_x - 1) == 0 and devices_y & (devices_y - 1) == 0
    return cells <= 2**18 and even and (nx, ny, nz) == (16, 16, LANES)


def local(source_term, initial_guess, face_x, face_y, face_z):
    if fits(*source_term.shape, lax.axis_size("gx"), lax.axis_size("gy")):
        return fused_cycle(source_term, initial_guess, face_x, face_y, face_z)
    gather_level = 4
    return descend(0, initial_guess, source_term, face_x, face_y, face_z, False, gather_level)


def solution(mesh):
    placed = (P("gx", "gy", None),) * 5
    return jax.shard_map(
        local, mesh=mesh, in_specs=placed, out_specs=P("gx", "gy", None), check_vma=False
    )
```

```python
import functools

import jax
import jax.numpy as jnp
from jax import lax
from jax.experimental import pallas as pl
from jax.experimental.pallas import tpu as pltpu
from jax.sharding import PartitionSpec as P

LEVELS = 6
OMEGA = 0.8
LANES = 128
RIM = 4
EDGE = 3
PAD = 8
F32 = jnp.float32

V, F, FX, FY, ZL, ZH, W, D = range(8)
SLOTS = (F, V, FX, FY, ZL)
X_LAYERS = (2, 3, 3, 2, 2)
Y_LAYERS = (2, 3, 2, 3, 2)


def lanes_of(shape):
    return lax.broadcasted_iota(jnp.int32, shape, len(shape) - 1)


def rows_of(shape):
    return lax.broadcasted_iota(jnp.int32, shape, len(shape) - 2)


def roll_lanes(values, step):
    return pltpu.roll(values, step % LANES, values.ndim - 1)


def roll_rows(values, step):
    return pltpu.roll(values, step % values.shape[-2], values.ndim - 2)


def exact_dot(left, right):
    return jnp.dot(left, right, precision=lax.Precision.HIGHEST, preferred_element_type=F32)


def compact(depth, part, even_only=False):
    source = lax.broadcasted_iota(jnp.int32, (LANES, LANES), 0)
    target = lax.broadcasted_iota(jnp.int32, (LANES, LANES), 1)
    half = depth // 2
    hit = target == (source // depth * 2 + part) * half + source % depth // 2
    if even_only:
        hit = hit & (source % 2 == 0)
    return jnp.where(hit, 1.0, 0.0).astype(F32)


def expand(depth, part):
    target = lax.broadcasted_iota(jnp.int32, (LANES, LANES), 0)
    source = lax.broadcasted_iota(jnp.int32, (LANES, LANES), 1)
    half = depth // 2
    hit = target == (source // depth * 2 + part) * half + source % depth // 2
    return jnp.where(hit, 1.0, 0.0).astype(F32)


def merge_lanes(values, depth, even_only=False):
    count, rows, _ = values.shape
    half = count // 2
    flat = values.reshape(2, half * rows, LANES)
    out = exact_dot(flat[0], compact(depth, 0, even_only))
    out = out + exact_dot(flat[1], compact(depth, 1, even_only))
    return out.reshape(half, rows, LANES)


def even_rows(ref, rows):
    return ref[:, pl.ds(0, rows // 2, stride=2), :]


def odd_rows(ref, rows):
    return ref[:, pl.ds(1, rows // 2, stride=2), :]


HALF = LANES // 2


def low_half(values):
    return jnp.where(lanes_of(values.shape) < HALF, values, 0.0)


def two_in_one(first, second):
    return first + roll_lanes(second, HALF)


def one_of_two(values):
    return low_half(values), low_half(roll_lanes(values, HALF))


def x_rows(nx, ny):
    return sum(X_LAYERS) * ny, 3 * RIM // 2 * (ny // 2)


def y_rows(nx, ny):
    return sum(Y_LAYERS) * nx, 3 * (nx // 4) * RIM


def corner_rows():
    return sum(x * y for x, y in zip(X_LAYERS, Y_LAYERS)) + 3, 3 * RIM // 2 * RIM


def x_place(index, layer, ny):
    return pl.ds((sum(X_LAYERS[:index]) + layer) * ny, ny)


def y_place(index, slab, nx):
    return pl.ds(sum(Y_LAYERS[:index]) * nx + slab * Y_LAYERS[index], Y_LAYERS[index])


def corner_place(index, layer):
    start = sum(x * y for x, y in zip(X_LAYERS[:index], Y_LAYERS[:index]))
    return pl.ds(start + layer * Y_LAYERS[index], Y_LAYERS[index])


def start_pack(*refs):
    fields, (own, x_low, x_high, y_low, y_high, *corners, faces, tmp, done) = refs[:5], refs[5:]
    copies = [pltpu.make_async_copy(ref, own.at[index], done.at[index]) for index, ref in enumerate(fields)]
    for copy in copies:
        copy.start()
    nx, ny = own.shape[1:3]
    for index, copy in enumerate(copies):
        copy.wait()
        layers, width = X_LAYERS[index], Y_LAYERS[index]
        for layer in range(layers):
            x_low[x_place(index, layer, ny)] = own[index, layer]
            x_high[x_place(index, layer, ny)] = own[index, nx - layers + layer]
        for slab in range(nx):
            y_low[y_place(index, slab, nx)] = own[index, slab, :width]
            y_high[y_place(index, slab, nx)] = own[index, slab, ny - width :]
        for side_x, first in enumerate((0, nx - layers)):
            for side_y, start in enumerate((0, ny - width)):
                for layer in range(layers):
                    rows = own[index, first + layer, start : start + width]
                    corners[2 * side_x + side_y][corner_place(index, layer)] = rows
    fx, fy, fz = own.at[2], own.at[3], own.at[4]
    halve = compact(LANES, 0)

    def stored(index, values, matrix):
        count, rows, _ = values.shape
        flat = exact_dot(values.reshape(count * rows, LANES), matrix)
        faces[index] = 0.25 * flat.reshape(count, rows, LANES)

    tmp[...] = pair_slabs(fx)[0]
    stored(0, even_rows(tmp, ny) + odd_rows(tmp, ny), halve)
    first, second = pair_slabs(fy)
    tmp[...] = first + second
    stored(1, even_rows(tmp, ny), halve)
    first, second = pair_slabs(fz)
    tmp[...] = first + second
    stored(2, even_rows(tmp, ny) + odd_rows(tmp, ny), compact(LANES, 0, True))
    base, base_y, base_c = x_rows(nx, ny)[0], y_rows(nx, ny)[0], corner_rows()[0]
    coarse_x, coarse_y = nx // 2, ny // 2
    pairs = RIM // 2
    for face in range(3):
        low = [two_in_one(faces[face, i], faces[face, i + pairs]) for i in range(pairs)]
        top = coarse_x - RIM
        high = [two_in_one(faces[face, top + i], faces[face, top + i + pairs]) for i in range(pairs)]
        for layer in range(pairs):
            rows = pl.ds(base + (face * pairs + layer) * coarse_y, coarse_y)
            x_low[rows] = low[layer]
            x_high[rows] = high[layer]
            rows = pl.ds(base_c + (face * pairs + layer) * RIM, RIM)
            for side_x, both in enumerate((low[layer], high[layer])):
                corners[2 * side_x][rows] = both[:RIM]
                corners[2 * side_x + 1][rows] = both[coarse_y - RIM :]
        for slab in range(coarse_x // 2):
            both = two_in_one(faces[face, slab], faces[face, slab + coarse_x // 2])
            rows = pl.ds(base_y + (face * (coarse_x // 2) + slab) * RIM, RIM)
            y_low[rows] = both[:RIM]
            y_high[rows] = both[coarse_y - RIM :]


def pair_slabs(ref):
    count = ref.shape[0]
    values = ref[...].reshape((count // 2, 2) + ref.shape[1:])
    return values[:, 0], values[:, 1]


def wide_slab(slab, from_low, own, from_high):
    count = own.shape[0]
    if slab < RIM:
        return from_low(slab)
    if slab < RIM + count:
        return own[slab - RIM]
    return from_high(slab - RIM - count)


def rim_slab(ref, base, rows, layer):
    place = pl.ds(base + layer % (RIM // 2) * rows, rows)
    return one_of_two(ref[place])[layer // (RIM // 2)]


def fold_four(slabs, even_only=False):
    out = None
    for part in range(2):
        term = exact_dot(two_in_one(slabs[part], slabs[2 + part]), compact(HALF, part, even_only))
        out = term if out is None else out + term
    return out


def coarse_faces(faces, out, tmp):
    rows = faces.shape[2]
    coarse = rows // 2
    fx, fy, fz = faces.at[0], faces.at[1], faces.at[2]
    tmp[...] = pair_slabs(fx)[0]
    x = even_rows(tmp, rows) + odd_rows(tmp, rows)
    first, second = pair_slabs(fy)
    tmp[...] = first + second
    y = even_rows(tmp, rows)
    first, second = pair_slabs(fz)
    tmp[...] = first + second
    z = even_rows(tmp, rows) + odd_rows(tmp, rows)
    out[...] = jnp.zeros(out.shape, F32)
    out[:coarse] = 0.25 * fold_four([x[i] for i in range(4)])
    out[coarse : 2 * coarse] = 0.25 * fold_four([y[i] for i in range(4)])
    out[2 * coarse : 3 * coarse] = 0.25 * fold_four([z[i] for i in range(4)], True)


def weighted(lev, src, slab, start, rows, f=None):
    here = pl.ds(start, rows)
    below = pl.ds(start - 1, rows)
    above = pl.ds(start + 1, rows)
    v = src[slab, here]
    f = lev.at[F] if f is None else f
    total = f[slab, here] + lev[FX, slab, here] * src[slab - 1, here]
    total = total + lev[FX, slab + 1, here] * src[slab + 1, here]
    total = total + lev[FY, slab, here] * src[slab, below]
    total = total + lev[FY, slab, above] * src[slab, above]
    total = total + lev[ZL, slab, here] * roll_lanes(v, 1)
    total = total + lev[ZH, slab, here] * roll_lanes(v, -1)
    return v, total


def swept(lev, src, slab, start, rows, f=None):
    v, total = weighted(lev, src, slab, start, rows, f)
    return (1.0 - OMEGA) * v + lev[W, slab, pl.ds(start, rows)] * total


def omega_over(values):
    inverse = pl.reciprocal(values, approx=True)
    inverse = inverse * (2.0 - values * inverse)
    return OMEGA * inverse * (2.0 - values * inverse)


def set_weights(lev, slab, start, rows, depth, inside=None):
    here = pl.ds(start, rows)
    fz = lev[ZL, slab, here]
    z = lanes_of(fz.shape) % depth
    upper = jnp.where(z == depth - 1, 0.0, roll_lanes(fz, -1))
    diagonal = lev[FX, slab, here] + lev[FX, slab + 1, here]
    diagonal = diagonal + lev[FY, slab, here] + lev[FY, slab, pl.ds(start + 1, rows)] + fz + upper
    valid = diagonal > 0.0
    if inside is not None:
        valid = valid & inside
    lev[ZL, slab, here] = jnp.where(z == 0, 0.0, fz)
    lev[ZH, slab, here] = upper
    lev[D, slab, here] = diagonal
    lev[W, slab, here] = jnp.where(valid, omega_over(jnp.where(valid, diagonal, 1.0)), 0.0)


def run(count, body, unroll=1):
    def step(index, carry):
        body(index)
        return carry

    lax.fori_loop(0, count, step, 0, unroll=unroll)


def clear_pads(ref, rows):
    for start in (0, RIM + rows):
        ref[:, start : start + RIM] = jnp.zeros((ref.shape[0], RIM, LANES), F32)


def level_down(axes, own, faces, coefficients, x_low, x_high, y_low, y_high, *refs):
    corners, refs = refs[:4], refs[4:]
    top, mid, chunk, v_low, v_high, other, tmp, one, two = refs
    nx, ny = own.shape[1:3]
    slabs, rows = nx + 2 * EDGE, ny + 2 * RIM
    me_x, me_y = lax.axis_index(axes[0]), lax.axis_index(axes[1])
    inner = pl.ds(PAD, ny)
    for index, slot in enumerate(SLOTS):
        layers, width = X_LAYERS[index], Y_LAYERS[index]
        top[slot, :, :PAD] = jnp.zeros((slabs, PAD, LANES), F32)
        top[slot, :, PAD + ny :] = jnp.zeros((slabs, PAD, LANES), F32)
        top[slot, EDGE : EDGE + nx, inner] = own[index]
        for layer in range(EDGE):
            if layer < layers:
                top[slot, EDGE - layers + layer, inner] = x_low[x_place(index, layer, ny)]
                top[slot, EDGE + nx + layer, inner] = x_high[x_place(index, layer, ny)]
            else:
                top[slot, EDGE - 1 - layer, inner] = jnp.zeros((ny, LANES), F32)
                top[slot, EDGE + nx + layer, inner] = jnp.zeros((ny, LANES), F32)
        for slab in range(nx):
            top[slot, EDGE + slab, PAD - width : PAD] = y_low[y_place(index, slab, nx)]
            top[slot, EDGE + slab, PAD + ny : PAD + ny + width] = y_high[y_place(index, slab, nx)]
        for side_x, start in enumerate((EDGE - layers, EDGE + nx)):
            for layer in range(layers):
                place = corner_place(index, layer)
                top[slot, start + layer, PAD - width : PAD] = corners[2 * side_x][place]
                top[slot, start + layer, PAD + ny : PAD + ny + width] = corners[2 * side_x + 1][place]
    clear_pads(other, rows)
    row_inside = (rows_of((rows, LANES)) >= RIM) | (me_y > 0)
    main = pl.ds(RIM, rows)
    start_v = top.at[V]

    def first(index):
        slab = index + 1
        inside = row_inside & ((slab >= EDGE) | (me_x > 0))
        set_weights(top, slab, RIM, rows, LANES, inside)
        other[slab, main] = swept(top, start_v, slab, RIM, rows)

    run(slabs - 2, first, 2)

    def second(index):
        slab = index + 2
        top[V, slab, main] = swept(top, other, slab, RIM, rows)

    run(slabs - 4, second, 2)

    def rest(slab):
        v, total = weighted(top, top.at[V], slab, PAD, ny)
        return total - top[D, slab, inner] * v

    def residual(index):
        slab = EDGE + 2 * index
        tmp[index] = rest(slab) + rest(slab + 1)

    run(nx // 2, residual, 2)

    coarse_x, coarse_y = nx // 2, ny // 2
    slabs, rows = coarse_x + 2 * RIM, coarse_y + 2 * RIM
    half = slabs // 2
    inner = pl.ds(2 * RIM, coarse_y)
    main = pl.ds(RIM, rows)
    base_x, base_y = x_rows(nx, ny)[0], y_rows(nx, ny)[0]
    for face, slot in enumerate((FX, FY, ZL)):
        clear_pads(mid.at[slot], rows)
        mid[slot, RIM : RIM + coarse_x, inner] = faces[face]
        place = base_x + face * (RIM // 2) * coarse_y
        for layer in range(RIM):
            mid[slot, layer, inner] = rim_slab(x_low, place, coarse_y, layer)
            mid[slot, RIM + coarse_x + layer, inner] = rim_slab(x_high, place, coarse_y, layer)
        parts = coarse_x // 2
        for slab in range(parts):
            place = pl.ds(base_y + (face * parts + slab) * RIM, RIM)
            for message, row in ((y_low, RIM), (y_high, 2 * RIM + coarse_y)):
                pair = one_of_two(message[place])
                mid[slot, RIM + slab, row : row + RIM] = pair[0]
                mid[slot, RIM + slab + parts, row : row + RIM] = pair[1]
        for side_x, start in enumerate((0, RIM + coarse_x)):
            for side_y, row in enumerate((RIM, 2 * RIM + coarse_y)):
                place = corner_rows()[0] + face * (RIM // 2) * RIM
                for layer in range(RIM):
                    values = rim_slab(corners[2 * side_x + side_y], place, RIM, layer)
                    mid[slot, start + layer, row : row + RIM] = values
    row_inside = (rows_of((rows, LANES)) >= RIM) | (me_y > 0)
    for slab in range(slabs - 1):
        inside = row_inside & (me_x > 0) if slab < RIM else row_inside
        set_weights(mid, slab, RIM, rows, HALF, inside)

    source = even_rows(tmp, ny) + odd_rows(tmp, ny)
    source = 0.5 * exact_dot(source.reshape(coarse_x * coarse_y, LANES), compact(LANES, 0))
    for ref in (mid.at[F], mid.at[V], one):
        ref[...] = jnp.zeros(ref.shape, F32)
    mid[F, RIM : RIM + coarse_x, inner] = source.reshape(coarse_x, coarse_y, LANES)
    for slab in range(RIM, RIM + coarse_x):
        mid[V, slab, inner] = mid[W, slab, inner] * mid[F, slab, inner]
    for layer in range(RIM // 2):
        near, far = RIM + layer, coarse_x + layer
        v_low[layer * coarse_y : (layer + 1) * coarse_y] = two_in_one(
            mid[V, near, inner], mid[V, near + RIM // 2, inner]
        )
        v_high[layer * coarse_y : (layer + 1) * coarse_y] = two_in_one(
            mid[V, far, inner], mid[V, far + RIM // 2, inner]
        )
    base = RIM // 2 * coarse_y
    for layer in range(2):
        place = pl.ds(base + layer * ny, ny)
        v_low[place] = top[V, EDGE + layer, pl.ds(PAD, ny)]
        v_high[place] = top[V, EDGE + nx - 2 + layer, pl.ds(PAD, ny)]
    for slab in range(RIM - 1, RIM + coarse_x + 1):
        one[slab, main] = swept(mid, mid.at[V], slab, RIM, rows)

    def rest_1(slab):
        v, total = weighted(mid, one, slab, RIM, rows)
        return total - mid[D, slab, main] * v

    two[...] = jnp.zeros(two.shape, F32)
    for pair in range(1, half - 1):
        two[pair] = rest_1(2 * pair) + rest_1(2 * pair + 1)
    pieces = even_rows(two, rows) + odd_rows(two, rows)
    for part in range(half // 4):
        folded = fold_four([pieces[4 * part + i] for i in range(4)])
        chunk[part * rows // 2 : (part + 1) * rows // 2] = 0.5 * folded
    chunk[half // 4 * rows // 2 :] = coefficients[...]


def pack_v(top, mid, x_low, x_high, low, high):
    slabs = mid.shape[1]
    coarse_x = slabs - 2 * RIM
    coarse_y = mid.shape[2] - 4 * RIM
    half = slabs // 2
    own = mid[V, RIM : RIM + coarse_x, 2 * RIM : 2 * RIM + coarse_y]
    values = [
        wide_slab(
            slab,
            lambda layer: rim_slab(x_low, 0, coarse_y, layer),
            own,
            lambda layer: rim_slab(x_high, 0, coarse_y, layer),
        )
        for slab in range(slabs)
    ]
    for slab in range(half):
        both = two_in_one(values[slab], values[slab + half])
        low[slab * RIM : (slab + 1) * RIM] = both[:RIM]
        high[slab * RIM : (slab + 1) * RIM] = both[coarse_y - RIM :]
    nx, ny = 2 * coarse_x, 2 * coarse_y
    base_x, base_y = RIM // 2 * coarse_y, half * RIM
    for out, start in ((low, 0), (high, ny - 2)):
        for layer in range(2):
            rows = pl.ds(base_x + layer * ny + start, 2)
            out[pl.ds(base_y + 2 * layer, 2)] = x_low[rows]
            out[pl.ds(base_y + 2 * (2 + nx + layer), 2)] = x_high[rows]
        for slab in range(nx):
            out[pl.ds(base_y + 2 * (2 + slab), 2)] = top[V, EDGE + slab, pl.ds(PAD + start, 2)]


def stack_blocks(count, blocks, *refs):
    for index in range(blocks):
        refs[count][index] = refs[index][...]
    for index in range(blocks, count):
        if index + 1 - blocks < len(refs) - count:
            refs[count + 1 + index - blocks][...] = refs[index][...]


def pair_rows(values, stride):
    return values + roll_rows(values, -stride)


def pair_lanes(values, stride):
    return values + roll_lanes(values, -stride)


class Listed:
    def __init__(self, fx, fy, fz, stride, depth):
        self.fx, self.fy, self.fz, self.stride, self.depth = fx, fy, fz, stride, depth
        shape = fx[0].shape
        rows = shape[0]
        row, lane = rows_of(shape), lanes_of(shape)
        z = lane % depth
        count = self.count = len(fx)
        self.x_high = [
            fx[s + 1] if s + 1 < count else jnp.where(lane < LANES - depth, roll_lanes(fx[0], -depth), 0.0)
            for s in range(count)
        ]
        self.x_low = [fx[s] if s > 0 else jnp.where(lane >= depth, fx[0], 0.0) for s in range(count)]
        self.y_high = [jnp.where(row < rows - stride, roll_rows(f, -stride), 0.0) for f in fy]
        self.y_low = [jnp.where(row >= stride, f, 0.0) for f in fy]
        self.z_high = [jnp.where(z < depth - stride, roll_lanes(f, -stride), 0.0) for f in fz]
        self.z_low = [jnp.where(z >= stride, f, 0.0) for f in fz]
        self.d = [
            fx[s] + self.x_high[s] + fy[s] + self.y_high[s] + fz[s] + self.z_high[s] for s in range(count)
        ]
        self.w = [jnp.where(d > 0.0, omega_over(jnp.where(d > 0.0, d, 1.0)), 0.0) for d in self.d]

    def weighted(self, v, f):
        count = self.count
        out = []
        for s in range(count):
            low = v[s - 1] if s > 0 else roll_lanes(v[count - 1], self.depth)
            high = v[s + 1] if s + 1 < count else roll_lanes(v[0], -self.depth)
            total = f[s] + self.x_low[s] * low + self.x_high[s] * high
            total = total + self.y_low[s] * roll_rows(v[s], self.stride)
            total = total + self.y_high[s] * roll_rows(v[s], -self.stride)
            total = total + self.z_low[s] * roll_lanes(v[s], self.stride)
            total = total + self.z_high[s] * roll_lanes(v[s], -self.stride)
            out.append(total)
        return out

    def sweep(self, v, f):
        totals = self.weighted(v, f)
        return [(1.0 - OMEGA) * v[s] + self.w[s] * totals[s] for s in range(self.count)]

    def start(self, f):
        return [self.w[s] * f[s] for s in range(self.count)]

    def residual(self, v, f):
        totals = self.weighted(v, f)
        return [totals[s] - self.d[s] * v[s] for s in range(self.count)]

    def kept(self):
        shape = self.fx[0].shape
        step = 2 * self.stride
        return (rows_of(shape) % step == 0) & (lanes_of(shape) % step == 0)

    def coarser(self):
        keep, stride = self.kept(), self.stride
        half = range(self.count // 2)

        def kept(values):
            return jnp.where(keep, 0.25 * values, 0.0)

        fx = [kept(pair_lanes(pair_rows(self.fx[2 * s], stride), stride)) for s in half]
        fy = [kept(pair_lanes(self.fy[2 * s] + self.fy[2 * s + 1], stride)) for s in half]
        fz = [kept(pair_rows(self.fz[2 * s] + self.fz[2 * s + 1], stride)) for s in half]
        return Listed(fx, fy, fz, 2 * stride, self.depth)

    def restrict(self, r):
        keep, stride = self.kept(), self.stride
        return [
            jnp.where(keep, 0.5 * pair_lanes(pair_rows(r[2 * s] + r[2 * s + 1], stride), stride), 0.0)
            for s in range(self.count // 2)
        ]

    def prolong(self, e):
        out = []
        for values in e:
            values = values + roll_rows(values, self.stride)
            values = values + roll_lanes(values, self.stride)
            out += [values, values]
        return out


def listed_cycle(levels, sweeps, f):
    level = levels[0]
    v = level.start(f)
    if len(levels) == 1:
        return lax.fori_loop(0, sweeps - 1, lambda index, values: level.sweep(values, f), v)
    v = level.sweep(v, f)
    e = listed_cycle(levels[1:], sweeps, level.restrict(level.residual(v, f)))
    v = [a + b for a, b in zip(v, level.prolong(e))]
    return level.sweep(level.sweep(v, f), f)


def level_two(axes, grid, sweeps, shape, pieces, out, wide, tall):
    devices_x, devices_y = grid
    me_x, me_y = lax.axis_index(axes[0]), lax.axis_index(axes[1])
    own_x, own_y = shape
    quarter = LANES // 4
    reach = RIM // 2
    blocks = 4
    count = devices_x * own_x // blocks
    rows = devices_y * own_y
    main = pl.ds(PAD, rows)
    window = own_y + RIM

    def piece(gx, gy):
        slow, far = (me_x // 2) ^ (gx // 2), (me_y // 2) ^ (gy // 2)
        return ((me_y + gy) % 2, (me_x + gx) % 2 * (devices_y // 2) + far, slow)

    for ref in (wide, tall):
        ref[...] = jnp.zeros(ref.shape, F32)
    lane = lanes_of((window, LANES))
    for gy in range(devices_y):
        sums = [None] * count
        for gx in range(devices_x):
            where = piece(gx, gy)
            layers = [pieces[where + (pl.ds(part * window, window),)] for part in range(2)]
            for local in range(1, 2 * blocks - 1):
                x = own_x * gx - reach + local
                if not 0 <= x < devices_x * own_x:
                    continue
                block, slab = x // count, x % count
                moved = roll_lanes(layers[local // blocks], (block - local % blocks) * quarter)
                moved = jnp.where(lane // quarter == block, moved, 0.0)
                sums[slab] = moved if sums[slab] is None else sums[slab] + moved
        place = pl.ds(PAD + own_y * gy - reach, window)
        for slab in range(count):
            tall[slab, place] = tall[slab, place] + sums[slab]
    f = [tall[slab, main] for slab in range(count)]

    lane = lanes_of((rows, LANES))
    for gx in range(devices_x):
        for gy in range(devices_y):
            where = piece(gx, gy)
            for face in range(3):
                values = pieces[where + (pl.ds(2 * window + face * own_y, own_y),)]
                wide[face, gx, gy * own_y : (gy + 1) * own_y] = values
    faces = []
    for face in range(3):
        slabs = [None] * count
        for gx in range(devices_x):
            values = wide[face, gx]
            for local in range(own_x):
                x = own_x * gx + local
                block, slab = x // count, x % count
                moved = roll_lanes(values, (block - local) * quarter)
                moved = jnp.where(lane // quarter == block, moved, 0.0)
                slabs[slab] = moved if slabs[slab] is None else slabs[slab] + moved
        faces.append(slabs)
    levels = [Listed(*faces, 1, quarter)]
    while len(levels) < LEVELS - 2:
        levels.append(levels[-1].coarser())
    e = listed_cycle(levels, sweeps, f)

    for slab in range(count):
        out[reach + slab, main] = e[slab]
    for slab in range(reach):
        out[slab, main] = jnp.where(lane < quarter, 0.0, roll_lanes(e[count - reach + slab], quarter))
        out[reach + count + slab, main] = jnp.where(
            lane >= LANES - quarter, 0.0, roll_lanes(e[slab], -quarter)
        )
    out[:, :PAD] = jnp.zeros((count + 2 * reach, PAD, LANES), F32)
    out[:, PAD + rows :] = jnp.zeros((count + 2 * reach, PAD, LANES), F32)


def level_up(axes, grid, coarse, top, mid, x_low, x_high, y_low, y_high, out, one, two, right, post, up):
    devices_x, devices_y = grid
    me_x, me_y = lax.axis_index(axes[0]), lax.axis_index(axes[1])
    coarse_x, coarse_y = mid.shape[1] - 2 * RIM, mid.shape[2] - 4 * RIM
    own_x, own_y = coarse_x // 2, coarse_y // 2
    quarter = LANES // 4
    reach = RIM // 2
    window = own_y + RIM

    slabs, high = coarse_x + 2 * RIM, coarse_y + 2 * RIM
    half = slabs // 2
    inner = pl.ds(2 * RIM, coarse_y)
    body = pl.ds(RIM, high)
    one[...] = mid[V]
    clear_pads(two, high)
    for layer in range(RIM):
        one[layer, inner] = rim_slab(x_low, 0, coarse_y, layer)
        one[RIM + coarse_x + layer, inner] = rim_slab(x_high, 0, coarse_y, layer)
    for slab in range(half):
        place = pl.ds(slab * RIM, RIM)
        for message, row in ((y_low, RIM), (y_high, 2 * RIM + coarse_y)):
            pair = one_of_two(message[place])
            one[slab, row : row + RIM] = pair[0]
            one[slab + half, row : row + RIM] = pair[1]
    row = rows_of((high, LANES))
    own_row = (row >= RIM) & (row < RIM + coarse_y)
    for slab in range(1, slabs - 1):
        f_rim = one[slab, body] * mid[D, slab, body] * (1.0 / OMEGA)
        if RIM <= slab < RIM + coarse_x:
            f_rim = jnp.where(own_row, mid[F, slab, body], f_rim)
        right[slab, body] = f_rim
        two[slab, body] = swept(mid, one, slab, RIM, high, right)

    per_block = (coarse.shape[0] - 2 * reach) // own_x
    base = me_x % per_block * own_x
    mine = None
    for gy in range(devices_y):
        place = pl.ds(PAD + gy * own_y - reach, window)
        values = jnp.where(me_y == gy, coarse[pl.ds(base, half), place, :], 0.0)
        mine = values if mine is None else mine + values
    source = lax.broadcasted_iota(jnp.int32, (LANES, LANES), 0)
    target = lax.broadcasted_iota(jnp.int32, (LANES, LANES), 1)
    hit = (source == me_x // per_block * quarter + target // 2) & (target < HALF)
    fine = exact_dot(mine.reshape(half * window, LANES), jnp.where(hit, 1.0, 0.0).astype(F32))
    fine = fine.reshape(half, window, LANES)
    for odd in range(2):
        up[:half, pl.ds(odd, window, stride=2), :] = fine
    for pair in range(half):
        for slab in (2 * pair, 2 * pair + 1):
            if 1 <= slab < slabs - 1:
                two[slab, body] = two[slab, body] + up[pair, :high]
    for slab in range(2, slabs - 2):
        one[slab, body] = swept(mid, two, slab, RIM, high, right)
    for slab in range(3, slabs - 3):
        two[slab, body] = swept(mid, one, slab, RIM, high, right)

    nx, ny = out.shape[:2]
    steps = coarse_x + 2
    fine_rows = ny + 2 * RIM
    e = two[RIM - 1 : RIM - 1 + steps, body]
    fine = exact_dot(e.reshape(steps * high, LANES), expand(LANES, 0)).reshape(steps, high, LANES)
    fine = fine[:, reach : reach + fine_rows // 2]
    for odd in range(2):
        up[:, pl.ds(odd, fine_rows // 2, stride=2), :] = fine
    body = pl.ds(RIM, fine_rows)
    for slot in (0, 1):
        clear_pads(post.at[slot], fine_rows)
    inner = pl.ds(PAD, ny)
    post[0, EDGE : EDGE + nx, inner] = top[V, EDGE : EDGE + nx, inner]
    base_x, base_y = RIM // 2 * coarse_y, half * RIM
    for layer in range(2):
        place = pl.ds(base_x + layer * ny, ny)
        post[0, EDGE - 2 + layer, inner] = x_low[place]
        post[0, EDGE + nx + layer, inner] = x_high[place]
    for slab in range(nx + 4):
        place = pl.ds(base_y + 2 * slab, 2)
        post[0, slab + EDGE - 2, RIM:PAD] = jnp.zeros((RIM, LANES), F32)
        post[0, slab + EDGE - 2, PAD + ny : PAD + ny + RIM] = jnp.zeros((RIM, LANES), F32)
        post[0, slab + EDGE - 2, PAD - 2 : PAD] = y_low[place]
        post[0, slab + EDGE - 2, PAD + ny : PAD + ny + 2] = y_high[place]

    def raise_level(index):
        for slab in (EDGE - 2 + 2 * index, EDGE - 1 + 2 * index):
            post[0, slab, body] = post[0, slab, body] + up[index]

    run(steps, raise_level, 2)

    def fifth(index):
        slab = EDGE - 1 + index
        post[1, slab, body] = swept(top, post.at[0], slab, RIM, fine_rows)

    run(nx + 2, fifth, 2)

    def sixth(index):
        out[index] = swept(top, post.at[1], EDGE + index, PAD, ny)

    run(nx, sixth, 2)


IN_VMEM = pl.BlockSpec(memory_space=pltpu.VMEM)


def call(kernel, outs, scratch=(), from_hbm=False):
    ins = pl.BlockSpec(memory_space=pl.ANY) if from_hbm else IN_VMEM

    def launch(*args):
        if from_hbm:
            args = [pltpu.with_memory_space_constraint(arg, pltpu.HBM) for arg in args]
        return pl.pallas_call(
            kernel,
            out_shape=[pltpu.VMEM(shape, F32) for shape in outs],
            in_specs=[ins] * len(args),
            out_specs=[IN_VMEM] * len(outs),
            scratch_shapes=[pltpu.VMEM(s, F32) if isinstance(s, tuple) else s for s in scratch],
            compiler_params=pltpu.CompilerParams(vmem_limit_bytes=24 * 2**20),
        )(*args)

    return launch


def pair_route(axis):
    return [(i, i ^ 1) for i in range(lax.axis_size(axis))]


def swap_route(axis):
    count = lax.axis_size(axis)
    return [(i, (i + 1 ^ 1) - 1) for i in range(1, count - 1)]


def by_partner(low, high, axis):
    odd = lax.axis_index(axis) % 2 == 1
    return jnp.where(odd, low, high), jnp.where(odd, high, low)


def partner(kind, index, count):
    other = index if kind is None else index ^ 1 if kind == 0 else (index + 1 ^ 1) - 1
    return other if 0 <= other < count else None


def across(block, kind_x, kind_y):
    count, size = lax.axis_size("gx"), lax.axis_size("gy")
    route = []
    for x in range(count):
        for y in range(size):
            to_x, to_y = partner(kind_x, x, count), partner(kind_y, y, size)
            if to_x is not None and to_y is not None:
                route.append((x * size + y, to_x * size + to_y))
    return lax.ppermute(block, ("gx", "gy"), route)


def by_partners(corners):
    low = by_partner(corners[0], corners[2], "gx")
    high = by_partner(corners[1], corners[3], "gx")
    out = [by_partner(low[kind], high[kind], "gy") for kind in range(2)]
    return [out[0][0], out[0][1], out[1][0], out[1][1]]


def from_around(x_low, x_high, y_low, y_high, corners):
    x = by_partner(x_low, x_high, "gx")
    y = by_partner(y_low, y_high, "gy")
    corners = by_partners(corners)
    x = [across(x[kind], kind, None) for kind in (1, 0)]
    corners = [across(corners[2 * kx + ky], kx, ky) for kx in range(2) for ky in range(2)]
    y = [across(y[kind], None, kind) for kind in (1, 0)]
    return by_partner(x[1], x[0], "gx") + by_partner(y[1], y[0], "gy") + tuple(by_partners(corners))


def passed_round(block, axis, stride):
    count = lax.axis_size(axis)
    return [block] + [
        lax.ppermute(block, axis, [(i, i ^ distance) for i in range(count)])
        for distance in range(stride, count, stride)
    ]


def passed_across(block, rider):
    count, size = lax.axis_size("gx"), lax.axis_size("gy")
    rows = block.shape[0]
    blocks = [block]
    for side in range(2):
        for distance in range(0, size, 2):
            route = [
                (x * size + y, (x ^ side) * size + (y ^ distance)) for x in range(count) for y in range(size)
            ]
            if side == 1 and distance == 0:
                both = lax.ppermute(jnp.concatenate((block, rider)), ("gx", "gy"), route)
                blocks.append(both[:rows])
                rider = both[rows:]
            elif distance > 0:
                blocks.append(lax.ppermute(block, ("gx", "gy"), route))
    return blocks, rider


def fused_cycle(*fields):
    axes = ("gx", "gy")
    devices_x, devices_y = lax.axis_size("gx"), lax.axis_size("gy")
    nx, ny, nz = fields[0].shape
    coarse_x, coarse_y = nx // 2, ny // 2
    x_shape = (sum(x_rows(nx, ny)), LANES)
    y_shape = (sum(y_rows(nx, ny)), LANES)
    corner_shape = (sum(corner_rows()), LANES)
    own, x_low, x_high, y_low, y_high, *corners, faces = call(
        start_pack,
        [(5, nx, ny, nz), x_shape, x_shape, y_shape, y_shape]
        + [corner_shape] * 4
        + [(3, coarse_x, coarse_y, LANES)],
        [(coarse_x, ny, LANES), pltpu.SemaphoreType.DMA((5,))],
        True,
    )(*fields)
    around = from_around(x_low, x_high, y_low, y_high, corners)
    (coefficients,) = call(coarse_faces, [(16, LANES)], [(coarse_x // 2, coarse_y, LANES)])(faces)
    stack = (nx + 2 * EDGE, ny + 4 * RIM, LANES)
    stack_1 = (coarse_x + 2 * RIM, coarse_y + 4 * RIM, LANES)
    half = stack_1[0] // 2
    v_shape = (RIM // 2 * coarse_y + 2 * ny, LANES)
    w_shape = (half * RIM + 2 * (nx + 4), LANES)
    top, mid, chunk, v_low, v_high = call(
        functools.partial(level_down, axes),
        [(D + 1,) + stack, (D + 1,) + stack_1, (32, LANES), v_shape, v_shape],
        [stack, (nx // 2, ny, LANES), stack_1, (half, coarse_y + 2 * RIM, LANES)],
    )(own, faces, coefficients, *around)

    blocks = passed_round(chunk, "gx", 2)
    slow = (len(blocks),) + chunk.shape
    pieces, v_low, v_high = call(
        functools.partial(stack_blocks, len(blocks) + 2, len(blocks)), [slow, v_shape, v_shape]
    )(*blocks, v_low, v_high)
    pair, swap = by_partner(v_low, v_high, "gx")
    swap = lax.ppermute(swap, "gx", swap_route("gx"))
    blocks, pair = passed_across(pieces.reshape(-1, LANES), pair)
    v_low, v_high = by_partner(pair, swap, "gx")
    w_low, w_high = call(pack_v, [w_shape] * 2)(top, mid, v_low, v_high)
    pair, swap = by_partner(w_low, w_high, "gy")
    message = jnp.concatenate(blocks + [pair])
    swap = lax.ppermute(swap, "gy", swap_route("gy"))
    other = lax.ppermute(message, "gy", pair_route("gy"))
    rows = message.shape[0] - w_shape[0]
    pieces = jnp.stack((message[:rows], other[:rows])).reshape((2, len(blocks)) + slow)
    w_low, w_high = by_partner(other[rows:], swap, "gy")
    count = devices_x * nx // 16
    rows = devices_y * ny // 4
    grid = (devices_x, devices_y)
    coarsest = (devices_x * nx >> LEVELS - 1, devices_y * ny >> LEVELS - 1)
    wide = (count + RIM, rows + 2 * PAD, LANES)
    (coarse,) = call(
        functools.partial(level_two, axes, grid, 4 * max(coarsest), (nx // 4, ny // 4)),
        [wide],
        [(3, devices_x, rows, LANES), wide],
    )(pieces)
    return pl.pallas_call(
        functools.partial(level_up, axes, grid),
        out_shape=jax.ShapeDtypeStruct((nx, ny, nz), F32),
        in_specs=[IN_VMEM] * 7,
        out_specs=IN_VMEM,
        scratch_shapes=[
            pltpu.VMEM(shape, F32)
            for shape in (stack_1, stack_1, stack_1, (2,) + stack, (coarse_x + 2, ny + 2 * RIM, LANES))
        ],
        compiler_params=pltpu.CompilerParams(vmem_limit_bytes=24 * 2**20),
    )(coarse, top, mid, v_low, v_high, w_low, w_high)


def with_halo(block, sides, width):
    for axis, dim in sides:
        count = lax.axis_size(axis)
        forward = [(i, i + 1) for i in range(count - 1)]
        backward = [(target, source) for source, target in forward]
        low = lax.ppermute(
            lax.slice_in_dim(block, block.shape[dim] - width, None, axis=dim), axis, forward
        )
        high = lax.ppermute(lax.slice_in_dim(block, 0, width, axis=dim), axis, backward)
        block = jnp.concatenate([low, block, high], axis=dim)
    return block


def passed_along(block, axis, distance):
    devices = range(lax.axis_size(axis))
    route = [(i - distance, i) for i in devices if i - distance in devices]
    return lax.ppermute(block, axis, route)


def stencil(padded, padded_x, padded_y, face_z):
    center = padded[1:-1, 1:-1]
    zero_plane = jnp.zeros(center.shape[:2] + (1,), center.dtype)
    above_face = jnp.concatenate((face_z[:, :, 1:], zero_plane), axis=2)
    below_z = jnp.concatenate((zero_plane, center[:, :, :-1]), axis=2)
    above_z = jnp.concatenate((center[:, :, 1:], zero_plane), axis=2)
    lower_x = padded_x[1:-1, 1:-1]
    upper_x = padded_x[2:, 1:-1]
    lower_y = padded_y[1:-1, 1:-1]
    upper_y = padded_y[1:-1, 2:]
    applied = lower_x * (center - padded[:-2, 1:-1]) + upper_x * (center - padded[2:, 1:-1])
    applied = (
        applied + lower_y * (center - padded[1:-1, :-2]) + upper_y * (center - padded[1:-1, 2:])
    )
    applied = applied + face_z * (center - below_z) + above_face * (center - above_z)
    diagonal = lower_x + upper_x + lower_y + upper_y + face_z + above_face
    return (applied, diagonal)


def jacobi_sweep(padded, source, padded_x, padded_y, face_z):
    applied, diagonal = stencil(padded, padded_x, padded_y, face_z)
    return padded[1:-1, 1:-1] + OMEGA * (source - applied) / diagonal


def pad_plane(values, width):
    return jnp.pad(values, ((width, width), (width, width), (0, 0)))


def restrict(residual):
    shape = residual.shape
    blocks = residual.reshape(shape[0] // 2, 2, shape[1] // 2, 2, shape[2] // 2, 2)
    return 4.0 * jnp.mean(blocks, axis=(1, 3, 5))


def coarsen_faces(face_x, face_y, face_z):
    shape = face_x.shape
    blocks = (shape[0] // 2, 2, shape[1] // 2, 2, shape[2] // 2, 2)
    coarse_x = jnp.mean(face_x.reshape(blocks)[:, 0], axis=(2, 4))
    coarse_y = jnp.mean(face_y.reshape(blocks)[:, :, :, 0], axis=(1, 4))
    coarse_z = jnp.mean(face_z.reshape(blocks)[..., 0], axis=(1, 3))
    return (coarse_x, coarse_y, coarse_z)


def prolong(coarse):
    return jnp.repeat(jnp.repeat(jnp.repeat(coarse, 2, axis=0), 2, axis=1), 2, axis=2)


def local_cycle(grid_level, iterate, source, face_x, face_y, face_z):
    padded_x = pad_plane(face_x, 1)
    padded_y = pad_plane(face_y, 1)
    if grid_level == LEVELS - 1:
        count = 4 * max(iterate.shape[0], iterate.shape[1])

        def one_sweep(index, values):
            return jacobi_sweep(pad_plane(values, 1), source, padded_x, padded_y, face_z)

        return lax.fori_loop(0, count, one_sweep, iterate)
    for sweep_index in range(2):
        iterate = jacobi_sweep(pad_plane(iterate, 1), source, padded_x, padded_y, face_z)
    applied, diagonal = stencil(pad_plane(iterate, 1), padded_x, padded_y, face_z)
    coarse_src = restrict(source - applied)
    coarse_x, coarse_y, coarse_z = coarsen_faces(face_x, face_y, face_z)
    correction = local_cycle(
        grid_level + 1, jnp.zeros_like(coarse_src), coarse_src, coarse_x, coarse_y, coarse_z
    )
    iterate = iterate + prolong(correction)
    for sweep_index in range(2):
        iterate = jacobi_sweep(pad_plane(iterate, 1), source, padded_x, padded_y, face_z)
    return iterate


def field_rim(iterate):
    return with_halo(iterate, (("gx", 0), ("gy", 1)), 1)


def sweep_pair_narrow(iterate, source, padded_x, padded_y, face_z, zero_start):
    for sweep_index in range(2):
        if sweep_index == 0 and zero_start:
            padded = pad_plane(iterate, 1)
        else:
            padded = field_rim(iterate)
        iterate = jacobi_sweep(padded, source, padded_x, padded_y, face_z)
    return iterate


def descend(grid_level, iterate, source, face_x, face_y, face_z, zero_start, gather_level):
    if grid_level == gather_level:
        pieces = (
            lax.all_gather(source, "gy", axis=1, tiled=True),
            lax.all_gather(face_x, "gy", axis=1, tiled=True),
            lax.all_gather(face_y, "gy", axis=1, tiled=True),
            lax.all_gather(face_z, "gy", axis=1, tiled=True),
        )
        gathered = (
            lax.all_gather(pieces[0], "gx", axis=0, tiled=True),
            lax.all_gather(pieces[1], "gx", axis=0, tiled=True),
            lax.all_gather(pieces[2], "gx", axis=0, tiled=True),
            lax.all_gather(pieces[3], "gx", axis=0, tiled=True),
        )
        correction = local_cycle(
            grid_level,
            jnp.zeros_like(gathered[0]),
            gathered[0],
            gathered[1],
            gathered[2],
            gathered[3],
        )
        start_x = lax.axis_index("gx") * source.shape[0]
        start_y = lax.axis_index("gy") * source.shape[1]
        return lax.dynamic_slice(
            correction, (start_x, start_y, jnp.zeros((), jnp.int32)), source.shape
        )
    next_x = passed_along(face_x[:1], "gx", -1)
    next_y = passed_along(face_y[:, :1], "gy", -1)
    lower_row = jnp.zeros_like(next_x)
    lower_col = jnp.zeros_like(next_y)
    padded_x = jnp.pad(
        jnp.concatenate((lower_row, face_x, next_x), axis=0), ((0, 0), (1, 1), (0, 0))
    )
    padded_y = jnp.pad(
        jnp.concatenate((lower_col, face_y, next_y), axis=1), ((1, 1), (0, 0), (0, 0))
    )

    def smoother(values, starting):
        return sweep_pair_narrow(values, source, padded_x, padded_y, face_z, starting)

    iterate = smoother(iterate, zero_start)
    applied, diagonal = stencil(field_rim(iterate), padded_x, padded_y, face_z)
    coarse_src = restrict(source - applied)
    coarse_x, coarse_y, coarse_z = coarsen_faces(face_x, face_y, face_z)
    correction = descend(
        grid_level + 1,
        jnp.zeros_like(coarse_src),
        coarse_src,
        coarse_x,
        coarse_y,
        coarse_z,
        True,
        gather_level,
    )
    iterate = iterate + prolong(correction)
    return smoother(iterate, False)


def fits(nx, ny, nz, devices_x, devices_y):
    cells = devices_x * nx * devices_y * ny * nz // 8
    even = devices_x % 8 == 0 and devices_y % 4 == 0
    even = even and devices_x & (devices_x - 1) == 0 and devices_y & (devices_y - 1) == 0
    return cells <= 2**18 and even and (nx, ny, nz) == (16, 16, LANES)


def local(source_term, initial_guess, face_x, face_y, face_z):
    if fits(*source_term.shape, lax.axis_size("gx"), lax.axis_size("gy")):
        return fused_cycle(source_term, initial_guess, face_x, face_y, face_z)
    gather_level = 4
    return descend(0, initial_guess, source_term, face_x, face_y, face_z, False, gather_level)


def solution(mesh):
    placed = (P("gx", "gy", None),) * 5
    return jax.shard_map(
        local, mesh=mesh, in_specs=placed, out_specs=P("gx", "gy", None), check_vma=False
    )
```

```python
import functools

import jax
import jax.numpy as jnp
from jax import lax
from jax.experimental import pallas as pl
from jax.experimental.pallas import tpu as pltpu
from jax.sharding import PartitionSpec as P

LEVELS = 6
OMEGA = 0.8
LANES = 128
RIM = 4
EDGE = 3
PAD = 8
BLOCK_ROWS = 24
F32 = jnp.float32

V, F, FX, FY, ZL, ZH, W, D = range(8)
SLOTS = (F, V, FX, FY, ZL)
X_LAYERS = (2, 3, 3, 2, 2)
Y_LAYERS = (2, 3, 2, 3, 2)


def lanes_of(shape):
    return lax.broadcasted_iota(jnp.int32, shape, len(shape) - 1)


def rows_of(shape):
    return lax.broadcasted_iota(jnp.int32, shape, len(shape) - 2)


def roll_lanes(values, step):
    return pltpu.roll(values, step % LANES, values.ndim - 1)


def roll_rows(values, step):
    return pltpu.roll(values, step % values.shape[-2], values.ndim - 2)


def exact_dot(left, right):
    return jnp.dot(left, right, precision=lax.Precision.HIGHEST, preferred_element_type=F32)


def compact(depth, part, even_only=False):
    source = lax.broadcasted_iota(jnp.int32, (LANES, LANES), 0)
    target = lax.broadcasted_iota(jnp.int32, (LANES, LANES), 1)
    half = depth // 2
    hit = target == (source // depth * 2 + part) * half + source % depth // 2
    if even_only:
        hit = hit & (source % 2 == 0)
    return jnp.where(hit, 1.0, 0.0).astype(F32)


def expand(depth, part):
    target = lax.broadcasted_iota(jnp.int32, (LANES, LANES), 0)
    source = lax.broadcasted_iota(jnp.int32, (LANES, LANES), 1)
    half = depth // 2
    hit = target == (source // depth * 2 + part) * half + source % depth // 2
    return jnp.where(hit, 1.0, 0.0).astype(F32)


def merge_lanes(values, depth, even_only=False):
    count, rows, _ = values.shape
    half = count // 2
    flat = values.reshape(2, half * rows, LANES)
    out = exact_dot(flat[0], compact(depth, 0, even_only))
    out = out + exact_dot(flat[1], compact(depth, 1, even_only))
    return out.reshape(half, rows, LANES)


def even_rows(ref, rows):
    return ref[:, pl.ds(0, rows // 2, stride=2), :]


def odd_rows(ref, rows):
    return ref[:, pl.ds(1, rows // 2, stride=2), :]


HALF = LANES // 2


def low_half(values):
    return jnp.where(lanes_of(values.shape) < HALF, values, 0.0)


def two_in_one(first, second):
    return first + roll_lanes(second, HALF)


def one_of_two(values):
    return low_half(values), low_half(roll_lanes(values, HALF))


def x_rows(nx, ny):
    return sum(X_LAYERS) * ny, 3 * RIM // 2 * (ny // 2)


def y_rows(nx, ny):
    return sum(Y_LAYERS) * (nx + 2 * EDGE), 3 * (nx // 2 + 2 * RIM) // 2 * RIM


def x_place(index, layer, ny):
    return pl.ds((sum(X_LAYERS[:index]) + layer) * ny, ny)


def y_place(index, slab, slabs):
    return pl.ds(sum(Y_LAYERS[:index]) * slabs + slab * Y_LAYERS[index], Y_LAYERS[index])


def start_pack(*refs):
    fields, (own, x_low, x_high, faces, tmp, done) = refs[:5], refs[5:]
    copies = [pltpu.make_async_copy(ref, own.at[index], done.at[index]) for index, ref in enumerate(fields)]
    for copy in copies:
        copy.start()
    nx, ny = own.shape[1:3]
    for index, copy in enumerate(copies):
        copy.wait()
        for layer in range(X_LAYERS[index]):
            x_low[x_place(index, layer, ny)] = own[index, layer]
            x_high[x_place(index, layer, ny)] = own[index, nx - X_LAYERS[index] + layer]
    fx, fy, fz = own.at[2], own.at[3], own.at[4]
    halve = compact(LANES, 0)

    def stored(index, values, matrix):
        count, rows, _ = values.shape
        flat = exact_dot(values.reshape(count * rows, LANES), matrix)
        faces[index] = 0.25 * flat.reshape(count, rows, LANES)

    tmp[...] = pair_slabs(fx)[0]
    stored(0, even_rows(tmp, ny) + odd_rows(tmp, ny), halve)
    first, second = pair_slabs(fy)
    tmp[...] = first + second
    stored(1, even_rows(tmp, ny), halve)
    first, second = pair_slabs(fz)
    tmp[...] = first + second
    stored(2, even_rows(tmp, ny) + odd_rows(tmp, ny), compact(LANES, 0, True))
    base = x_rows(nx, ny)[0]
    coarse_rows = ny // 2
    for face in range(3):
        for layer in range(RIM // 2):
            rows = pl.ds(base + (face * (RIM // 2) + layer) * coarse_rows, coarse_rows)
            top = nx // 2 - RIM + layer
            x_low[rows] = two_in_one(faces[face, layer], faces[face, layer + RIM // 2])
            x_high[rows] = two_in_one(faces[face, top], faces[face, top + RIM // 2])


def pair_slabs(ref):
    count = ref.shape[0]
    values = ref[...].reshape((count // 2, 2) + ref.shape[1:])
    return values[:, 0], values[:, 1]


def wide_slab(slab, from_low, own, from_high):
    count = own.shape[0]
    if slab < RIM:
        return from_low(slab)
    if slab < RIM + count:
        return own[slab - RIM]
    return from_high(slab - RIM - count)


def rim_slab(ref, base, rows, layer):
    place = pl.ds(base + layer % (RIM // 2) * rows, rows)
    return one_of_two(ref[place])[layer // (RIM // 2)]


def pack_y(own, faces, x_low, x_high, low, high):
    coarse_x, coarse_y = faces.shape[1:3]
    nx, ny = 2 * coarse_x, 2 * coarse_y
    slabs = nx + 2 * EDGE
    for index in range(5):
        width, layers = Y_LAYERS[index], X_LAYERS[index]
        for out, start in ((low, 0), (high, ny - width)):
            for slab in range(nx):
                out[y_place(index, EDGE + slab, slabs)] = own[index, slab, start : start + width]
            for layer in range(EDGE):
                near, far = layer + layers - EDGE, layer
                rows = pl.ds(x_place(index, max(near, 0), ny).start + start, width)
                out[y_place(index, layer, slabs)] = x_low[rows]
                rows = pl.ds(x_place(index, min(far, layers - 1), ny).start + start, width)
                out[y_place(index, EDGE + nx + layer, slabs)] = x_high[rows]
    base_x, base_y = x_rows(nx, ny)[0], y_rows(nx, ny)[0]
    half = (coarse_x + 2 * RIM) // 2
    for face in range(3):
        place = base_x + face * (RIM // 2) * coarse_y
        slabs = [
            wide_slab(
                slab,
                lambda layer: rim_slab(x_low, place, coarse_y, layer),
                faces.at[face],
                lambda layer: rim_slab(x_high, place, coarse_y, layer),
            )
            for slab in range(2 * half)
        ]
        for slab in range(half):
            both = two_in_one(slabs[slab], slabs[slab + half])
            rows = pl.ds(base_y + (face * half + slab) * RIM, RIM)
            low[rows] = both[:RIM]
            high[rows] = both[coarse_y - RIM :]


def fold_four(slabs, even_only=False):
    out = None
    for part in range(2):
        term = exact_dot(two_in_one(slabs[part], slabs[2 + part]), compact(HALF, part, even_only))
        out = term if out is None else out + term
    return out


def coarse_faces(faces, out, tmp):
    rows = faces.shape[2]
    coarse = rows // 2
    fx, fy, fz = faces.at[0], faces.at[1], faces.at[2]
    tmp[...] = pair_slabs(fx)[0]
    x = even_rows(tmp, rows) + odd_rows(tmp, rows)
    first, second = pair_slabs(fy)
    tmp[...] = first + second
    y = even_rows(tmp, rows)
    first, second = pair_slabs(fz)
    tmp[...] = first + second
    z = even_rows(tmp, rows) + odd_rows(tmp, rows)
    out[...] = jnp.zeros(out.shape, F32)
    out[:coarse] = 0.25 * fold_four([x[i] for i in range(4)])
    out[coarse : 2 * coarse] = 0.25 * fold_four([y[i] for i in range(4)])
    out[2 * coarse : 3 * coarse] = 0.25 * fold_four([z[i] for i in range(4)], True)


def weighted(lev, src, slab, start, rows, f=None):
    here = pl.ds(start, rows)
    below = pl.ds(start - 1, rows)
    above = pl.ds(start + 1, rows)
    v = src[slab, here]
    f = lev.at[F] if f is None else f
    x = lev[FX, slab, here] * src[slab - 1, here] + lev[FX, slab + 1, here] * src[slab + 1, here]
    y = lev[FY, slab, here] * src[slab, below] + lev[FY, slab, above] * src[slab, above]
    z = lev[ZL, slab, here] * roll_lanes(v, 1) + lev[ZH, slab, here] * roll_lanes(v, -1)
    total = ((x + y) + f[slab, here]) + z
    return v, total


def swept(lev, src, slab, start, rows, f=None):
    v, total = weighted(lev, src, slab, start, rows, f)
    return (1.0 - OMEGA) * v + lev[W, slab, pl.ds(start, rows)] * total


def set_weights(lev, slab, start, rows, depth, inside=None):
    here = pl.ds(start, rows)
    fz = lev[ZL, slab, here]
    z = lanes_of(fz.shape) % depth
    upper = jnp.where(z == depth - 1, 0.0, roll_lanes(fz, -1))
    diagonal = lev[FX, slab, here] + lev[FX, slab + 1, here]
    diagonal = diagonal + lev[FY, slab, here] + lev[FY, slab, pl.ds(start + 1, rows)] + fz + upper
    valid = diagonal > 0.0
    if inside is not None:
        valid = valid & inside
    lev[ZL, slab, here] = jnp.where(z == 0, 0.0, fz)
    lev[ZH, slab, here] = upper
    lev[D, slab, here] = diagonal
    lev[W, slab, here] = jnp.where(valid, OMEGA / jnp.where(valid, diagonal, 1.0), 0.0)


def run(count, body):
    for index in range(count):
        body(index)


def clear_pads(ref, rows):
    for start in (0, RIM + rows):
        ref[:, start : start + RIM] = jnp.zeros((ref.shape[0], RIM, LANES), F32)


def level_down(axes, own, faces, coefficients, x_low, x_high, y_low, y_high, *refs):
    top, mid, chunk, v_low, v_high, other, tmp, one, two = refs
    nx, ny = own.shape[1:3]
    slabs, rows = nx + 2 * EDGE, ny + 2 * RIM
    me_x, me_y = lax.axis_index(axes[0]), lax.axis_index(axes[1])
    inner = pl.ds(PAD, ny)
    for index, slot in enumerate(SLOTS):
        layers, width = X_LAYERS[index], Y_LAYERS[index]
        top[slot, :, :PAD] = jnp.zeros((slabs, PAD, LANES), F32)
        top[slot, :, PAD + ny :] = jnp.zeros((slabs, PAD, LANES), F32)
        top[slot, EDGE : EDGE + nx, inner] = own[index]
        for layer in range(EDGE):
            if layer < layers:
                top[slot, EDGE - layers + layer, inner] = x_low[x_place(index, layer, ny)]
                top[slot, EDGE + nx + layer, inner] = x_high[x_place(index, layer, ny)]
            else:
                top[slot, EDGE - 1 - layer, inner] = jnp.zeros((ny, LANES), F32)
                top[slot, EDGE + nx + layer, inner] = jnp.zeros((ny, LANES), F32)
        for slab in range(slabs):
            top[slot, slab, PAD - width : PAD] = y_low[y_place(index, slab, slabs)]
            top[slot, slab, PAD + ny : PAD + ny + width] = y_high[y_place(index, slab, slabs)]
    clear_pads(other, rows)
    row_inside = (rows_of((rows, LANES)) >= RIM) | (me_y > 0)
    main = pl.ds(RIM, rows)
    start_v = top.at[V]

    def first(index):
        slab = index + 1
        inside = row_inside & ((slab >= EDGE) | (me_x > 0))
        set_weights(top, slab, RIM, rows, LANES, inside)
        other[slab, main] = swept(top, start_v, slab, RIM, rows)

    run(slabs - 2, first)

    def second(index):
        slab = index + 2
        top[V, slab, main] = swept(top, other, slab, RIM, rows)

    run(slabs - 4, second)

    def rest(slab):
        v, total = weighted(top, top.at[V], slab, PAD, ny)
        return total - top[D, slab, inner] * v

    def residual(index):
        slab = EDGE + 2 * index
        tmp[index] = rest(slab) + rest(slab + 1)

    run(nx // 2, residual)

    coarse_x, coarse_y = nx // 2, ny // 2
    slabs, rows = coarse_x + 2 * RIM, coarse_y + 2 * RIM
    half = slabs // 2
    inner = pl.ds(2 * RIM, coarse_y)
    main = pl.ds(RIM, rows)
    base_x, base_y = x_rows(nx, ny)[0], y_rows(nx, ny)[0]
    for face, slot in enumerate((FX, FY, ZL)):
        clear_pads(mid.at[slot], rows)
        mid[slot, RIM : RIM + coarse_x, inner] = faces[face]
        place = base_x + face * (RIM // 2) * coarse_y
        for layer in range(RIM):
            mid[slot, layer, inner] = rim_slab(x_low, place, coarse_y, layer)
            mid[slot, RIM + coarse_x + layer, inner] = rim_slab(x_high, place, coarse_y, layer)
        for slab in range(half):
            place = pl.ds(base_y + (face * half + slab) * RIM, RIM)
            for message, row in ((y_low, RIM), (y_high, 2 * RIM + coarse_y)):
                pair = one_of_two(message[place])
                mid[slot, slab, row : row + RIM] = pair[0]
                mid[slot, slab + half, row : row + RIM] = pair[1]
    row_inside = (rows_of((rows, LANES)) >= RIM) | (me_y > 0)
    for slab in range(slabs - 1):
        inside = row_inside & (me_x > 0) if slab < RIM else row_inside
        set_weights(mid, slab, RIM, rows, HALF, inside)

    source = even_rows(tmp, ny) + odd_rows(tmp, ny)
    source = 0.5 * exact_dot(source.reshape(coarse_x * coarse_y, LANES), compact(LANES, 0))
    for ref in (mid.at[F], mid.at[V], one):
        ref[...] = jnp.zeros(ref.shape, F32)
    mid[F, RIM : RIM + coarse_x, inner] = source.reshape(coarse_x, coarse_y, LANES)
    for slab in range(RIM, RIM + coarse_x):
        mid[V, slab, inner] = mid[W, slab, inner] * mid[F, slab, inner]
    for layer in range(RIM // 2):
        near, far = RIM + layer, coarse_x + layer
        v_low[layer * coarse_y : (layer + 1) * coarse_y] = two_in_one(
            mid[V, near, inner], mid[V, near + RIM // 2, inner]
        )
        v_high[layer * coarse_y : (layer + 1) * coarse_y] = two_in_one(
            mid[V, far, inner], mid[V, far + RIM // 2, inner]
        )
    base = RIM // 2 * coarse_y
    for layer in range(2):
        place = pl.ds(base + layer * ny, ny)
        v_low[place] = top[V, EDGE + layer, pl.ds(PAD, ny)]
        v_high[place] = top[V, EDGE + nx - 2 + layer, pl.ds(PAD, ny)]
    for slab in range(RIM - 1, RIM + coarse_x + 1):
        one[slab, main] = swept(mid, mid.at[V], slab, RIM, rows)

    def rest_1(slab):
        v, total = weighted(mid, one, slab, RIM, rows)
        return total - mid[D, slab, main] * v

    two[...] = jnp.zeros(two.shape, F32)
    for pair in range(1, half - 1):
        two[pair] = rest_1(2 * pair) + rest_1(2 * pair + 1)
    pieces = even_rows(two, rows) + odd_rows(two, rows)
    coarse_rows, quarter_rows = rows // 2, rows // 4
    chunk[:coarse_rows] = 0.5 * fold_four([pieces[1 + i] for i in range(4)])
    rest_of = [pieces[5 + i // 2][i % 2 * quarter_rows :][:quarter_rows] for i in range(4)]
    chunk[coarse_rows : coarse_rows + quarter_rows] = 0.5 * fold_four(rest_of)
    chunk[coarse_rows + quarter_rows :] = coefficients[:BLOCK_ROWS - coarse_rows - quarter_rows]


def pack_v(top, mid, x_low, x_high, low, high):
    slabs = mid.shape[1]
    coarse_x = slabs - 2 * RIM
    coarse_y = mid.shape[2] - 4 * RIM
    half = slabs // 2
    own = mid[V, RIM : RIM + coarse_x, 2 * RIM : 2 * RIM + coarse_y]
    values = [
        wide_slab(
            slab,
            lambda layer: rim_slab(x_low, 0, coarse_y, layer),
            own,
            lambda layer: rim_slab(x_high, 0, coarse_y, layer),
        )
        for slab in range(slabs)
    ]
    for slab in range(half):
        both = two_in_one(values[slab], values[slab + half])
        low[slab * RIM : (slab + 1) * RIM] = both[:RIM]
        high[slab * RIM : (slab + 1) * RIM] = both[coarse_y - RIM :]
    nx, ny = 2 * coarse_x, 2 * coarse_y
    base_x, base_y = RIM // 2 * coarse_y, half * RIM
    for out, start in ((low, 0), (high, ny - 2)):
        for layer in range(2):
            rows = pl.ds(base_x + layer * ny + start, 2)
            out[pl.ds(base_y + 2 * layer, 2)] = x_low[rows]
            out[pl.ds(base_y + 2 * (2 + nx + layer), 2)] = x_high[rows]
        for slab in range(nx):
            out[pl.ds(base_y + 2 * (2 + slab), 2)] = top[V, EDGE + slab, pl.ds(PAD + start, 2)]


def stack_blocks(count, blocks, *refs):
    for index in range(blocks):
        refs[count][index] = refs[index][...]
    for index in range(blocks, count):
        if index + 1 - blocks < len(refs) - count:
            refs[count + 1 + index - blocks][...] = refs[index][...]


def pair_rows(values, stride):
    return values + roll_rows(values, -stride)


def pair_lanes(values, stride):
    return values + roll_lanes(values, -stride)


class Listed:
    def __init__(self, fx, fy, fz, stride, depth):
        self.fx, self.fy, self.fz, self.stride, self.depth = fx, fy, fz, stride, depth
        shape = fx[0].shape
        rows = shape[0]
        row, lane = rows_of(shape), lanes_of(shape)
        z = lane % depth
        count = self.count = len(fx)
        self.x_high = [
            fx[s + 1] if s + 1 < count else jnp.where(lane < LANES - depth, roll_lanes(fx[0], -depth), 0.0)
            for s in range(count)
        ]
        self.x_low = [fx[s] if s > 0 else jnp.where(lane >= depth, fx[0], 0.0) for s in range(count)]
        self.y_high = [jnp.where(row < rows - stride, roll_rows(f, -stride), 0.0) for f in fy]
        self.y_low = [jnp.where(row >= stride, f, 0.0) for f in fy]
        self.z_high = [jnp.where(z < depth - stride, roll_lanes(f, -stride), 0.0) for f in fz]
        self.z_low = [jnp.where(z >= stride, f, 0.0) for f in fz]
        self.d = [
            fx[s] + self.x_high[s] + fy[s] + self.y_high[s] + fz[s] + self.z_high[s] for s in range(count)
        ]
        self.w = [jnp.where(d > 0.0, OMEGA / jnp.where(d > 0.0, d, 1.0), 0.0) for d in self.d]

    def weighted(self, v, f):
        count = self.count
        out = []
        for s in range(count):
            low = v[s - 1] if s > 0 else roll_lanes(v[count - 1], self.depth)
            high = v[s + 1] if s + 1 < count else roll_lanes(v[0], -self.depth)
            x = self.x_low[s] * low + self.x_high[s] * high
            y = self.y_low[s] * roll_rows(v[s], self.stride) + self.y_high[s] * roll_rows(v[s], -self.stride)
            z = self.z_low[s] * roll_lanes(v[s], self.stride) + self.z_high[s] * roll_lanes(v[s], -self.stride)
            total = (f[s] + y) + (x + z)
            out.append(total)
        return out

    def sweep(self, v, f):
        totals = self.weighted(v, f)
        return [(1.0 - OMEGA) * v[s] + self.w[s] * totals[s] for s in range(self.count)]

    def sweeps(self, count, f):
        folded = [
            [w * c for w, c in zip(self.w, coefficients)]
            for coefficients in (self.x_low, self.x_high, self.y_low, self.y_high, self.z_low, self.z_high)
        ]
        scaled = self.start(f)
        slabs = self.count

        def step(index, v):
            out = []
            for s in range(slabs):
                low = v[s - 1] if s > 0 else roll_lanes(v[slabs - 1], self.depth)
                high = v[s + 1] if s + 1 < slabs else roll_lanes(v[0], -self.depth)
                x = folded[0][s] * low + folded[1][s] * high
                y = folded[2][s] * roll_rows(v[s], self.stride) + folded[3][s] * roll_rows(v[s], -self.stride)
                z = folded[4][s] * roll_lanes(v[s], self.stride) + folded[5][s] * roll_lanes(v[s], -self.stride)
                out.append((((1.0 - OMEGA) * v[s] + scaled[s]) + y) + (x + z))
            return out

        return lax.fori_loop(1, count, step, scaled)

    def start(self, f):
        return [self.w[s] * f[s] for s in range(self.count)]

    def residual(self, v, f):
        totals = self.weighted(v, f)
        return [totals[s] - self.d[s] * v[s] for s in range(self.count)]

    def kept(self):
        shape = self.fx[0].shape
        step = 2 * self.stride
        return (rows_of(shape) % step == 0) & (lanes_of(shape) % step == 0)

    def coarser(self):
        keep, stride = self.kept(), self.stride
        half = range(self.count // 2)

        def kept(values):
            return jnp.where(keep, 0.25 * values, 0.0)

        fx = [kept(pair_lanes(pair_rows(self.fx[2 * s], stride), stride)) for s in half]
        fy = [kept(pair_lanes(self.fy[2 * s] + self.fy[2 * s + 1], stride)) for s in half]
        fz = [kept(pair_rows(self.fz[2 * s] + self.fz[2 * s + 1], stride)) for s in half]
        return Listed(fx, fy, fz, 2 * stride, self.depth)

    def restrict(self, r):
        keep, stride = self.kept(), self.stride
        return [
            jnp.where(keep, 0.5 * pair_lanes(pair_rows(r[2 * s] + r[2 * s + 1], stride), stride), 0.0)
            for s in range(self.count // 2)
        ]

    def prolong(self, e):
        out = []
        for values in e:
            values = values + roll_rows(values, self.stride)
            values = values + roll_lanes(values, self.stride)
            out += [values, values]
        return out


def listed_cycle(levels, sweeps, f):
    level = levels[0]
    if len(levels) == 1:
        return level.sweeps(sweeps, f)
    v = level.sweep(level.start(f), f)
    e = listed_cycle(levels[1:], sweeps, level.restrict(level.residual(v, f)))
    v = [a + b for a, b in zip(v, level.prolong(e))]
    return level.sweep(level.sweep(v, f), f)


def level_two(axes, grid, sweeps, shape, pieces, out, wide, tall):
    devices_x, devices_y = grid
    me_x, me_y = lax.axis_index(axes[0]), lax.axis_index(axes[1])
    own_x, own_y = shape
    quarter = LANES // 4
    reach = RIM // 2
    blocks = 4
    count = devices_x * own_x // blocks
    rows = devices_y * own_y
    main = pl.ds(PAD, rows)
    window = own_y + RIM

    def piece(gx, gy):
        slow, far = (me_x // 2) ^ (gx // 2), (me_y // 2) ^ (gy // 2)
        return ((me_y + gy) % 2, (me_x + gx) % 2 * (devices_y // 2) + far, slow)

    for ref in (wide, tall):
        ref[...] = jnp.zeros(ref.shape, F32)
    lane = lanes_of((window, LANES))
    for gy in range(devices_y):
        sums = [None] * count
        for gx in range(devices_x):
            where = piece(gx, gy)
            first = pieces[where + (pl.ds(0, window),)]
            second = pieces[where + (pl.ds(window, window // 2),)]
            for local in range(1, 2 * blocks - 1):
                x = own_x * gx - reach + local
                if not 0 <= x < devices_x * own_x:
                    continue
                block, slab = x // count, x % count
                if local <= blocks:
                    moved = roll_lanes(first, (block - local + 1) * quarter)
                else:
                    at = 2 * (local - blocks - 1)
                    halves = [roll_lanes(second, (block - at - odd) * quarter) for odd in range(2)]
                    moved = jnp.concatenate(halves)
                moved = jnp.where(lane // quarter == block, moved, 0.0)
                sums[slab] = moved if sums[slab] is None else sums[slab] + moved
        place = pl.ds(PAD + own_y * gy - reach, window)
        for slab in range(count):
            tall[slab, place] = tall[slab, place] + sums[slab]
    f = [tall[slab, main] for slab in range(count)]

    lane = lanes_of((rows, LANES))
    for gx in range(devices_x):
        for gy in range(devices_y):
            where = piece(gx, gy)
            for face in range(3):
                values = pieces[where + (pl.ds(window + window // 2 + face * own_y, own_y),)]
                wide[face, gx, gy * own_y : (gy + 1) * own_y] = values
    faces = []
    for face in range(3):
        slabs = [None] * count
        for gx in range(devices_x):
            values = wide[face, gx]
            for local in range(own_x):
                x = own_x * gx + local
                block, slab = x // count, x % count
                moved = roll_lanes(values, (block - local) * quarter)
                moved = jnp.where(lane // quarter == block, moved, 0.0)
                slabs[slab] = moved if slabs[slab] is None else slabs[slab] + moved
        faces.append(slabs)
    levels = [Listed(*faces, 1, quarter)]
    while len(levels) < LEVELS - 2:
        levels.append(levels[-1].coarser())
    e = listed_cycle(levels, sweeps, f)

    for slab in range(count):
        out[reach + slab, main] = e[slab]
    for slab in range(reach):
        out[slab, main] = jnp.where(lane < quarter, 0.0, roll_lanes(e[count - reach + slab], quarter))
        out[reach + count + slab, main] = jnp.where(
            lane >= LANES - quarter, 0.0, roll_lanes(e[slab], -quarter)
        )
    out[:, :PAD] = jnp.zeros((count + 2 * reach, PAD, LANES), F32)
    out[:, PAD + rows :] = jnp.zeros((count + 2 * reach, PAD, LANES), F32)


def level_up(axes, grid, coarse, top, mid, x_low, x_high, y_low, y_high, out, one, two, right, post, up):
    devices_x, devices_y = grid
    me_x, me_y = lax.axis_index(axes[0]), lax.axis_index(axes[1])
    coarse_x, coarse_y = mid.shape[1] - 2 * RIM, mid.shape[2] - 4 * RIM
    own_x, own_y = coarse_x // 2, coarse_y // 2
    quarter = LANES // 4
    reach = RIM // 2
    window = own_y + RIM

    slabs, high = coarse_x + 2 * RIM, coarse_y + 2 * RIM
    half = slabs // 2
    inner = pl.ds(2 * RIM, coarse_y)
    body = pl.ds(RIM, high)
    one[...] = mid[V]
    clear_pads(two, high)
    for layer in range(RIM):
        one[layer, inner] = rim_slab(x_low, 0, coarse_y, layer)
        one[RIM + coarse_x + layer, inner] = rim_slab(x_high, 0, coarse_y, layer)
    for slab in range(half):
        place = pl.ds(slab * RIM, RIM)
        for message, row in ((y_low, RIM), (y_high, 2 * RIM + coarse_y)):
            pair = one_of_two(message[place])
            one[slab, row : row + RIM] = pair[0]
            one[slab + half, row : row + RIM] = pair[1]
    row = rows_of((high, LANES))
    own_row = (row >= RIM) & (row < RIM + coarse_y)
    for slab in range(1, slabs - 1):
        f_rim = one[slab, body] * mid[D, slab, body] * (1.0 / OMEGA)
        if RIM <= slab < RIM + coarse_x:
            f_rim = jnp.where(own_row, mid[F, slab, body], f_rim)
        right[slab, body] = f_rim
        two[slab, body] = swept(mid, one, slab, RIM, high, right)

    per_block = (coarse.shape[0] - 2 * reach) // own_x
    base = me_x % per_block * own_x
    mine = None
    for gy in range(devices_y):
        place = pl.ds(PAD + gy * own_y - reach, window)
        values = jnp.where(me_y == gy, coarse[pl.ds(base, half), place, :], 0.0)
        mine = values if mine is None else mine + values
    source = lax.broadcasted_iota(jnp.int32, (LANES, LANES), 0)
    target = lax.broadcasted_iota(jnp.int32, (LANES, LANES), 1)
    hit = (source == me_x // per_block * quarter + target // 2) & (target < HALF)
    fine = exact_dot(mine.reshape(half * window, LANES), jnp.where(hit, 1.0, 0.0).astype(F32))
    fine = fine.reshape(half, window, LANES)
    for odd in range(2):
        up[:half, pl.ds(odd, window, stride=2), :] = fine
    for pair in range(half):
        for slab in (2 * pair, 2 * pair + 1):
            if 1 <= slab < slabs - 1:
                two[slab, body] = two[slab, body] + up[pair, :high]
    for slab in range(2, slabs - 2):
        one[slab, body] = swept(mid, two, slab, RIM, high, right)
    for slab in range(3, slabs - 3):
        two[slab, body] = swept(mid, one, slab, RIM, high, right)

    nx, ny = out.shape[:2]
    steps = coarse_x + 2
    fine_rows = ny + 2 * RIM
    e = two[RIM - 1 : RIM - 1 + steps, body]
    fine = exact_dot(e.reshape(steps * high, LANES), expand(LANES, 0)).reshape(steps, high, LANES)
    fine = fine[:, reach : reach + fine_rows // 2]
    for odd in range(2):
        up[:, pl.ds(odd, fine_rows // 2, stride=2), :] = fine
    body = pl.ds(RIM, fine_rows)
    for slot in (0, 1):
        clear_pads(post.at[slot], fine_rows)
    inner = pl.ds(PAD, ny)
    post[0, EDGE : EDGE + nx, inner] = top[V, EDGE : EDGE + nx, inner]
    base_x, base_y = RIM // 2 * coarse_y, half * RIM
    for layer in range(2):
        place = pl.ds(base_x + layer * ny, ny)
        post[0, EDGE - 2 + layer, inner] = x_low[place]
        post[0, EDGE + nx + layer, inner] = x_high[place]
    for slab in range(nx + 4):
        place = pl.ds(base_y + 2 * slab, 2)
        post[0, slab + EDGE - 2, RIM:PAD] = jnp.zeros((RIM, LANES), F32)
        post[0, slab + EDGE - 2, PAD + ny : PAD + ny + RIM] = jnp.zeros((RIM, LANES), F32)
        post[0, slab + EDGE - 2, PAD - 2 : PAD] = y_low[place]
        post[0, slab + EDGE - 2, PAD + ny : PAD + ny + 2] = y_high[place]

    def raise_level(index):
        for slab in (EDGE - 2 + 2 * index, EDGE - 1 + 2 * index):
            post[0, slab, body] = post[0, slab, body] + up[index]

    run(steps, raise_level)

    def fifth(index):
        slab = EDGE - 1 + index
        post[1, slab, body] = swept(top, post.at[0], slab, RIM, fine_rows)

    run(nx + 2, fifth)

    def sixth(index):
        out[index] = swept(top, post.at[1], EDGE + index, PAD, ny)

    run(nx, sixth)


IN_VMEM = pl.BlockSpec(memory_space=pltpu.VMEM)


def call(kernel, outs, scratch=(), from_hbm=False):
    ins = pl.BlockSpec(memory_space=pl.ANY) if from_hbm else IN_VMEM

    def launch(*args):
        if from_hbm:
            args = [pltpu.with_memory_space_constraint(arg, pltpu.HBM) for arg in args]
        return pl.pallas_call(
            kernel,
            out_shape=[pltpu.VMEM(shape, F32) for shape in outs],
            in_specs=[ins] * len(args),
            out_specs=[IN_VMEM] * len(outs),
            scratch_shapes=[pltpu.VMEM(s, F32) if isinstance(s, tuple) else s for s in scratch],
            compiler_params=pltpu.CompilerParams(vmem_limit_bytes=24 * 2**20),
        )(*args)

    return launch


def pair_route(axis):
    return [(i, i ^ 1) for i in range(lax.axis_size(axis))]


def swap_route(axis):
    count = lax.axis_size(axis)
    return [(i, (i + 1 ^ 1) - 1) for i in range(1, count - 1)]


def by_partner(low, high, axis):
    odd = lax.axis_index(axis) % 2 == 1
    return jnp.where(odd, low, high), jnp.where(odd, high, low)


def from_sides(low, high, axis):
    pair, swap = by_partner(low, high, axis)
    pair = lax.ppermute(pair, axis, pair_route(axis))
    swap = lax.ppermute(swap, axis, swap_route(axis))
    return by_partner(pair, swap, axis)


def passed_round(block, axis, stride):
    count = lax.axis_size(axis)
    return [block] + [
        lax.ppermute(block, axis, [(i, i ^ distance) for i in range(count)])
        for distance in range(stride, count, stride)
    ]


def passed_across(block, rider):
    count, size = lax.axis_size("gx"), lax.axis_size("gy")
    rows = block.shape[0]
    blocks = [block]
    for side in range(2):
        for distance in range(0, size, 2):
            route = [
                (x * size + y, (x ^ side) * size + (y ^ distance)) for x in range(count) for y in range(size)
            ]
            if side == 1 and distance == 0:
                both = lax.ppermute(jnp.concatenate((block, rider)), ("gx", "gy"), route)
                blocks.append(both[:rows])
                rider = both[rows:]
            elif distance > 0:
                blocks.append(lax.ppermute(block, ("gx", "gy"), route))
    return blocks, rider


def fused_cycle(*fields):
    axes = ("gx", "gy")
    devices_x, devices_y = lax.axis_size("gx"), lax.axis_size("gy")
    nx, ny, nz = fields[0].shape
    coarse_x, coarse_y = nx // 2, ny // 2
    x_shape = (sum(x_rows(nx, ny)), LANES)
    y_shape = (sum(y_rows(nx, ny)), LANES)
    own, x_low, x_high, faces = call(
        start_pack,
        [(5, nx, ny, nz), x_shape, x_shape, (3, coarse_x, coarse_y, LANES)],
        [(coarse_x, ny, LANES), pltpu.SemaphoreType.DMA((5,))],
        True,
    )(*fields)
    x_low, x_high = from_sides(x_low, x_high, "gx")
    (coefficients,) = call(coarse_faces, [(16, LANES)], [(coarse_x // 2, coarse_y, LANES)])(faces)
    y_low, y_high = call(pack_y, [y_shape] * 2)(own, faces, x_low, x_high)
    y_low, y_high = from_sides(y_low, y_high, "gy")
    stack = (nx + 2 * EDGE, ny + 4 * RIM, LANES)
    stack_1 = (coarse_x + 2 * RIM, coarse_y + 4 * RIM, LANES)
    half = stack_1[0] // 2
    v_shape = (RIM // 2 * coarse_y + 2 * ny, LANES)
    w_shape = (half * RIM + 2 * (nx + 4), LANES)
    top, mid, chunk, v_low, v_high = call(
        functools.partial(level_down, axes),
        [(D + 1,) + stack, (D + 1,) + stack_1, (BLOCK_ROWS, LANES), v_shape, v_shape],
        [stack, (nx // 2, ny, LANES), stack_1, (half, coarse_y + 2 * RIM, LANES)],
    )(own, faces, coefficients, x_low, x_high, y_low, y_high)

    blocks = passed_round(chunk, "gx", 2)
    slow = (len(blocks),) + chunk.shape
    pieces, v_low, v_high = call(
        functools.partial(stack_blocks, len(blocks) + 2, len(blocks)), [slow, v_shape, v_shape]
    )(*blocks, v_low, v_high)
    pair, swap = by_partner(v_low, v_high, "gx")
    swap = lax.ppermute(swap, "gx", swap_route("gx"))
    blocks, pair = passed_across(pieces.reshape(-1, LANES), pair)
    v_low, v_high = by_partner(pair, swap, "gx")
    w_low, w_high = call(pack_v, [w_shape] * 2)(top, mid, v_low, v_high)
    pair, swap = by_partner(w_low, w_high, "gy")
    message = jnp.concatenate(blocks + [pair])
    swap = lax.ppermute(swap, "gy", swap_route("gy"))
    other = lax.ppermute(message, "gy", pair_route("gy"))
    rows = message.shape[0] - w_shape[0]
    pieces = jnp.stack((message[:rows], other[:rows])).reshape((2, len(blocks)) + slow)
    w_low, w_high = by_partner(other[rows:], swap, "gy")
    count = devices_x * nx // 16
    rows = devices_y * ny // 4
    grid = (devices_x, devices_y)
    coarsest = (devices_x * nx >> LEVELS - 1, devices_y * ny >> LEVELS - 1)
    wide = (count + RIM, rows + 2 * PAD, LANES)
    (coarse,) = call(
        functools.partial(level_two, axes, grid, 4 * max(coarsest), (nx // 4, ny // 4)),
        [wide],
        [(3, devices_x, rows, LANES), wide],
    )(pieces)
    return pl.pallas_call(
        functools.partial(level_up, axes, grid),
        out_shape=jax.ShapeDtypeStruct((nx, ny, nz), F32),
        in_specs=[IN_VMEM] * 7,
        out_specs=IN_VMEM,
        scratch_shapes=[
            pltpu.VMEM(shape, F32)
            for shape in (stack_1, stack_1, stack_1, (2,) + stack, (coarse_x + 2, ny + 2 * RIM, LANES))
        ],
        compiler_params=pltpu.CompilerParams(vmem_limit_bytes=24 * 2**20),
    )(coarse, top, mid, v_low, v_high, w_low, w_high)


def with_halo(block, sides, width):
    for axis, dim in sides:
        count = lax.axis_size(axis)
        forward = [(i, i + 1) for i in range(count - 1)]
        backward = [(target, source) for source, target in forward]
        low = lax.ppermute(
            lax.slice_in_dim(block, block.shape[dim] - width, None, axis=dim), axis, forward
        )
        high = lax.ppermute(lax.slice_in_dim(block, 0, width, axis=dim), axis, backward)
        block = jnp.concatenate([low, block, high], axis=dim)
    return block


def passed_along(block, axis, distance):
    devices = range(lax.axis_size(axis))
    route = [(i - distance, i) for i in devices if i - distance in devices]
    return lax.ppermute(block, axis, route)


def stencil(padded, padded_x, padded_y, face_z):
    center = padded[1:-1, 1:-1]
    zero_plane = jnp.zeros(center.shape[:2] + (1,), center.dtype)
    above_face = jnp.concatenate((face_z[:, :, 1:], zero_plane), axis=2)
    below_z = jnp.concatenate((zero_plane, center[:, :, :-1]), axis=2)
    above_z = jnp.concatenate((center[:, :, 1:], zero_plane), axis=2)
    lower_x = padded_x[1:-1, 1:-1]
    upper_x = padded_x[2:, 1:-1]
    lower_y = padded_y[1:-1, 1:-1]
    upper_y = padded_y[1:-1, 2:]
    applied = lower_x * (center - padded[:-2, 1:-1]) + upper_x * (center - padded[2:, 1:-1])
    applied = (
        applied + lower_y * (center - padded[1:-1, :-2]) + upper_y * (center - padded[1:-1, 2:])
    )
    applied = applied + face_z * (center - below_z) + above_face * (center - above_z)
    diagonal = lower_x + upper_x + lower_y + upper_y + face_z + above_face
    return (applied, diagonal)


def jacobi_sweep(padded, source, padded_x, padded_y, face_z):
    applied, diagonal = stencil(padded, padded_x, padded_y, face_z)
    return padded[1:-1, 1:-1] + OMEGA * (source - applied) / diagonal


def pad_plane(values, width):
    return jnp.pad(values, ((width, width), (width, width), (0, 0)))


def restrict(residual):
    shape = residual.shape
    blocks = residual.reshape(shape[0] // 2, 2, shape[1] // 2, 2, shape[2] // 2, 2)
    return 4.0 * jnp.mean(blocks, axis=(1, 3, 5))


def coarsen_faces(face_x, face_y, face_z):
    shape = face_x.shape
    blocks = (shape[0] // 2, 2, shape[1] // 2, 2, shape[2] // 2, 2)
    coarse_x = jnp.mean(face_x.reshape(blocks)[:, 0], axis=(2, 4))
    coarse_y = jnp.mean(face_y.reshape(blocks)[:, :, :, 0], axis=(1, 4))
    coarse_z = jnp.mean(face_z.reshape(blocks)[..., 0], axis=(1, 3))
    return (coarse_x, coarse_y, coarse_z)


def prolong(coarse):
    return jnp.repeat(jnp.repeat(jnp.repeat(coarse, 2, axis=0), 2, axis=1), 2, axis=2)


def local_cycle(grid_level, iterate, source, face_x, face_y, face_z):
    padded_x = pad_plane(face_x, 1)
    padded_y = pad_plane(face_y, 1)
    if grid_level == LEVELS - 1:
        count = 4 * max(iterate.shape[0], iterate.shape[1])

        def one_sweep(index, values):
            return jacobi_sweep(pad_plane(values, 1), source, padded_x, padded_y, face_z)

        return lax.fori_loop(0, count, one_sweep, iterate)
    for sweep_index in range(2):
        iterate = jacobi_sweep(pad_plane(iterate, 1), source, padded_x, padded_y, face_z)
    applied, diagonal = stencil(pad_plane(iterate, 1), padded_x, padded_y, face_z)
    coarse_src = restrict(source - applied)
    coarse_x, coarse_y, coarse_z = coarsen_faces(face_x, face_y, face_z)
    correction = local_cycle(
        grid_level + 1, jnp.zeros_like(coarse_src), coarse_src, coarse_x, coarse_y, coarse_z
    )
    iterate = iterate + prolong(correction)
    for sweep_index in range(2):
        iterate = jacobi_sweep(pad_plane(iterate, 1), source, padded_x, padded_y, face_z)
    return iterate


def field_rim(iterate):
    return with_halo(iterate, (("gx", 0), ("gy", 1)), 1)


def sweep_pair_narrow(iterate, source, padded_x, padded_y, face_z, zero_start):
    for sweep_index in range(2):
        if sweep_index == 0 and zero_start:
            padded = pad_plane(iterate, 1)
        else:
            padded = field_rim(iterate)
        iterate = jacobi_sweep(padded, source, padded_x, padded_y, face_z)
    return iterate


def descend(grid_level, iterate, source, face_x, face_y, face_z, zero_start, gather_level):
    if grid_level == gather_level:
        pieces = (
            lax.all_gather(source, "gy", axis=1, tiled=True),
            lax.all_gather(face_x, "gy", axis=1, tiled=True),
            lax.all_gather(face_y, "gy", axis=1, tiled=True),
            lax.all_gather(face_z, "gy", axis=1, tiled=True),
        )
        gathered = (
            lax.all_gather(pieces[0], "gx", axis=0, tiled=True),
            lax.all_gather(pieces[1], "gx", axis=0, tiled=True),
            lax.all_gather(pieces[2], "gx", axis=0, tiled=True),
            lax.all_gather(pieces[3], "gx", axis=0, tiled=True),
        )
        correction = local_cycle(
            grid_level,
            jnp.zeros_like(gathered[0]),
            gathered[0],
            gathered[1],
            gathered[2],
            gathered[3],
        )
        start_x = lax.axis_index("gx") * source.shape[0]
        start_y = lax.axis_index("gy") * source.shape[1]
        return lax.dynamic_slice(
            correction, (start_x, start_y, jnp.zeros((), jnp.int32)), source.shape
        )
    next_x = passed_along(face_x[:1], "gx", -1)
    next_y = passed_along(face_y[:, :1], "gy", -1)
    lower_row = jnp.zeros_like(next_x)
    lower_col = jnp.zeros_like(next_y)
    padded_x = jnp.pad(
        jnp.concatenate((lower_row, face_x, next_x), axis=0), ((0, 0), (1, 1), (0, 0))
    )
    padded_y = jnp.pad(
        jnp.concatenate((lower_col, face_y, next_y), axis=1), ((1, 1), (0, 0), (0, 0))
    )

    def smoother(values, starting):
        return sweep_pair_narrow(values, source, padded_x, padded_y, face_z, starting)

    iterate = smoother(iterate, zero_start)
    applied, diagonal = stencil(field_rim(iterate), padded_x, padded_y, face_z)
    coarse_src = restrict(source - applied)
    coarse_x, coarse_y, coarse_z = coarsen_faces(face_x, face_y, face_z)
    correction = descend(
        grid_level + 1,
        jnp.zeros_like(coarse_src),
        coarse_src,
        coarse_x,
        coarse_y,
        coarse_z,
        True,
        gather_level,
    )
    iterate = iterate + prolong(correction)
    return smoother(iterate, False)


def fits(nx, ny, nz, devices_x, devices_y):
    cells = devices_x * nx * devices_y * ny * nz // 8
    even = devices_x % 8 == 0 and devices_y % 4 == 0
    even = even and devices_x & (devices_x - 1) == 0 and devices_y & (devices_y - 1) == 0
    return cells <= 2**18 and even and (nx, ny, nz) == (16, 16, LANES)


def local(source_term, initial_guess, face_x, face_y, face_z):
    if fits(*source_term.shape, lax.axis_size("gx"), lax.axis_size("gy")):
        return fused_cycle(source_term, initial_guess, face_x, face_y, face_z)
    gather_level = 4
    return descend(0, initial_guess, source_term, face_x, face_y, face_z, False, gather_level)


def solution(mesh):
    placed = (P("gx", "gy", None),) * 5
    return jax.shard_map(
        local, mesh=mesh, in_specs=placed, out_specs=P("gx", "gy", None), check_vma=False
    )
```

```python
import functools

import jax
import jax.numpy as jnp
from jax import lax
from jax.experimental import pallas as pl
from jax.experimental.pallas import tpu as pltpu
from jax.sharding import PartitionSpec as P

LEVELS = 6
OMEGA = 0.8
LANES = 128
RIM = 4
EDGE = 3
PAD = 8
BLOCK_ROWS = 24
F32 = jnp.float32

V, F, FX, FY, ZL, ZH, W, D = range(8)
SLOTS = (F, V, FX, FY, ZL)
X_LAYERS = (2, 3, 3, 2, 2)
Y_LAYERS = (2, 3, 2, 3, 2)
Y_REACH = (1, 2, 2, 2, 1)


def lanes_of(shape):
    return lax.broadcasted_iota(jnp.int32, shape, len(shape) - 1)


def rows_of(shape):
    return lax.broadcasted_iota(jnp.int32, shape, len(shape) - 2)


def roll_lanes(values, step):
    return pltpu.roll(values, step % LANES, values.ndim - 1)


def roll_rows(values, step):
    return pltpu.roll(values, step % values.shape[-2], values.ndim - 2)


def exact_dot(left, right):
    return jnp.dot(left, right, precision=lax.Precision.HIGHEST, preferred_element_type=F32)


def compact(depth, part, even_only=False):
    source = lax.broadcasted_iota(jnp.int32, (LANES, LANES), 0)
    target = lax.broadcasted_iota(jnp.int32, (LANES, LANES), 1)
    half = depth // 2
    hit = target == (source // depth * 2 + part) * half + source % depth // 2
    if even_only:
        hit = hit & (source % 2 == 0)
    return jnp.where(hit, 1.0, 0.0).astype(F32)


def expand(depth, part):
    target = lax.broadcasted_iota(jnp.int32, (LANES, LANES), 0)
    source = lax.broadcasted_iota(jnp.int32, (LANES, LANES), 1)
    half = depth // 2
    hit = target == (source // depth * 2 + part) * half + source % depth // 2
    return jnp.where(hit, 1.0, 0.0).astype(F32)


def merge_lanes(values, depth, even_only=False):
    count, rows, _ = values.shape
    half = count // 2
    flat = values.reshape(2, half * rows, LANES)
    out = exact_dot(flat[0], compact(depth, 0, even_only))
    out = out + exact_dot(flat[1], compact(depth, 1, even_only))
    return out.reshape(half, rows, LANES)


def even_rows(ref, rows):
    return ref[:, pl.ds(0, rows // 2, stride=2), :]


def odd_rows(ref, rows):
    return ref[:, pl.ds(1, rows // 2, stride=2), :]


HALF = LANES // 2


def low_half(values):
    return jnp.where(lanes_of(values.shape) < HALF, values, 0.0)


def two_in_one(first, second):
    return first + roll_lanes(second, HALF)


def one_of_two(values):
    return low_half(values), low_half(roll_lanes(values, HALF))


def x_rows(nx, ny):
    return sum(X_LAYERS) * ny, 3 * RIM // 2 * (ny // 2)


def y_rows(nx, ny):
    fine = sum(layers * (nx + 2 * reach) for layers, reach in zip(Y_LAYERS, Y_REACH))
    return fine, 3 * (nx // 2 + 2 * RIM) // 2 * RIM


def x_place(index, layer, ny):
    return pl.ds((sum(X_LAYERS[:index]) + layer) * ny, ny)


def y_place(index, slab, nx):
    before = zip(Y_LAYERS[:index], Y_REACH[:index])
    start = sum(layers * (nx + 2 * reach) for layers, reach in before)
    return pl.ds(start + (Y_REACH[index] + slab) * Y_LAYERS[index], Y_LAYERS[index])


def start_pack(*refs):
    fields, (own, x_low, x_high, faces, tmp, done) = refs[:5], refs[5:]
    copies = [pltpu.make_async_copy(ref, own.at[index], done.at[index]) for index, ref in enumerate(fields)]
    for copy in copies:
        copy.start()
    nx, ny = own.shape[1:3]
    for index, copy in enumerate(copies):
        copy.wait()
        for layer in range(X_LAYERS[index]):
            x_low[x_place(index, layer, ny)] = own[index, layer]
            x_high[x_place(index, layer, ny)] = own[index, nx - X_LAYERS[index] + layer]
    fx, fy, fz = own.at[2], own.at[3], own.at[4]
    halve = compact(LANES, 0)

    def stored(index, values, matrix):
        count, rows, _ = values.shape
        flat = exact_dot(values.reshape(count * rows, LANES), matrix)
        faces[index] = 0.25 * flat.reshape(count, rows, LANES)

    tmp[...] = pair_slabs(fx)[0]
    stored(0, even_rows(tmp, ny) + odd_rows(tmp, ny), halve)
    first, second = pair_slabs(fy)
    tmp[...] = first + second
    stored(1, even_rows(tmp, ny), halve)
    first, second = pair_slabs(fz)
    tmp[...] = first + second
    stored(2, even_rows(tmp, ny) + odd_rows(tmp, ny), compact(LANES, 0, True))
    base = x_rows(nx, ny)[0]
    coarse_rows = ny // 2
    for face in range(3):
        for layer in range(RIM // 2):
            rows = pl.ds(base + (face * (RIM // 2) + layer) * coarse_rows, coarse_rows)
            top = nx // 2 - RIM + layer
            x_low[rows] = two_in_one(faces[face, layer], faces[face, layer + RIM // 2])
            x_high[rows] = two_in_one(faces[face, top], faces[face, top + RIM // 2])


def pair_slabs(ref):
    count = ref.shape[0]
    values = ref[...].reshape((count // 2, 2) + ref.shape[1:])
    return values[:, 0], values[:, 1]


def wide_slab(slab, from_low, own, from_high):
    count = own.shape[0]
    if slab < RIM:
        return from_low(slab)
    if slab < RIM + count:
        return own[slab - RIM]
    return from_high(slab - RIM - count)


def rim_slab(ref, base, rows, layer):
    place = pl.ds(base + layer % (RIM // 2) * rows, rows)
    return one_of_two(ref[place])[layer // (RIM // 2)]


def pack_y(own, faces, x_low, x_high, low, high):
    coarse_x, coarse_y = faces.shape[1:3]
    nx, ny = 2 * coarse_x, 2 * coarse_y
    for index in range(5):
        width, layers, reach = Y_LAYERS[index], X_LAYERS[index], Y_REACH[index]
        for out, start in ((low, 0), (high, ny - width)):
            for slab in range(nx):
                out[y_place(index, slab, nx)] = own[index, slab, start : start + width]
            for layer in range(reach):
                rows = pl.ds(x_place(index, layers - reach + layer, ny).start + start, width)
                out[y_place(index, layer - reach, nx)] = x_low[rows]
                rows = pl.ds(x_place(index, layer, ny).start + start, width)
                out[y_place(index, nx + layer, nx)] = x_high[rows]
    base_x, base_y = x_rows(nx, ny)[0], y_rows(nx, ny)[0]
    half = (coarse_x + 2 * RIM) // 2
    for face in range(3):
        place = base_x + face * (RIM // 2) * coarse_y
        slabs = [
            wide_slab(
                slab,
                lambda layer: rim_slab(x_low, place, coarse_y, layer),
                faces.at[face],
                lambda layer: rim_slab(x_high, place, coarse_y, layer),
            )
            for slab in range(2 * half)
        ]
        for slab in range(half):
            both = two_in_one(slabs[slab], slabs[slab + half])
            rows = pl.ds(base_y + (face * half + slab) * RIM, RIM)
            low[rows] = both[:RIM]
            high[rows] = both[coarse_y - RIM :]


def fold_four(slabs, even_only=False):
    out = None
    for part in range(2):
        term = exact_dot(two_in_one(slabs[part], slabs[2 + part]), compact(HALF, part, even_only))
        out = term if out is None else out + term
    return out


def coarse_faces(faces, out, tmp):
    rows = faces.shape[2]
    coarse = rows // 2
    fx, fy, fz = faces.at[0], faces.at[1], faces.at[2]
    tmp[...] = pair_slabs(fx)[0]
    x = even_rows(tmp, rows) + odd_rows(tmp, rows)
    first, second = pair_slabs(fy)
    tmp[...] = first + second
    y = even_rows(tmp, rows)
    first, second = pair_slabs(fz)
    tmp[...] = first + second
    z = even_rows(tmp, rows) + odd_rows(tmp, rows)
    out[...] = jnp.zeros(out.shape, F32)
    out[:coarse] = 0.25 * fold_four([x[i] for i in range(4)])
    out[coarse : 2 * coarse] = 0.25 * fold_four([y[i] for i in range(4)])
    out[2 * coarse : 3 * coarse] = 0.25 * fold_four([z[i] for i in range(4)], True)


def weighted(lev, src, slab, start, rows, f=None):
    here = pl.ds(start, rows)
    below = pl.ds(start - 1, rows)
    above = pl.ds(start + 1, rows)
    v = src[slab, here]
    f = lev.at[F] if f is None else f
    x = lev[FX, slab, here] * src[slab - 1, here] + lev[FX, slab + 1, here] * src[slab + 1, here]
    y = lev[FY, slab, here] * src[slab, below] + lev[FY, slab, above] * src[slab, above]
    z = lev[ZL, slab, here] * roll_lanes(v, 1) + lev[ZH, slab, here] * roll_lanes(v, -1)
    total = ((x + y) + f[slab, here]) + z
    return v, total


def swept(lev, src, slab, start, rows, f=None):
    v, total = weighted(lev, src, slab, start, rows, f)
    return (1.0 - OMEGA) * v + lev[W, slab, pl.ds(start, rows)] * total


def set_weights(lev, slab, start, rows, depth, inside=None):
    here = pl.ds(start, rows)
    fz = lev[ZL, slab, here]
    z = lanes_of(fz.shape) % depth
    upper = jnp.where(z == depth - 1, 0.0, roll_lanes(fz, -1))
    diagonal = lev[FX, slab, here] + lev[FX, slab + 1, here]
    diagonal = diagonal + lev[FY, slab, here] + lev[FY, slab, pl.ds(start + 1, rows)] + fz + upper
    valid = diagonal > 0.0
    if inside is not None:
        valid = valid & inside
    lev[ZL, slab, here] = jnp.where(z == 0, 0.0, fz)
    lev[ZH, slab, here] = upper
    lev[D, slab, here] = diagonal
    lev[W, slab, here] = jnp.where(valid, OMEGA / jnp.where(valid, diagonal, 1.0), 0.0)


def run(count, body):
    for index in range(count):
        body(index)


def clear_pads(ref, rows):
    for start in (0, RIM + rows):
        ref[:, start : start + RIM] = jnp.zeros((ref.shape[0], RIM, LANES), F32)


def level_down(axes, own, faces, coefficients, x_low, x_high, y_low, y_high, *refs):
    top, mid, chunk, v_low, v_high, other, tmp, one, two = refs
    nx, ny = own.shape[1:3]
    slabs, rows = nx + 2 * EDGE, ny + 2 * RIM
    me_x, me_y = lax.axis_index(axes[0]), lax.axis_index(axes[1])
    inner = pl.ds(PAD, ny)
    for index, slot in enumerate(SLOTS):
        layers, width = X_LAYERS[index], Y_LAYERS[index]
        top[slot, :, :PAD] = jnp.zeros((slabs, PAD, LANES), F32)
        top[slot, :, PAD + ny :] = jnp.zeros((slabs, PAD, LANES), F32)
        top[slot, EDGE : EDGE + nx, inner] = own[index]
        for layer in range(EDGE):
            if layer < layers:
                top[slot, EDGE - layers + layer, inner] = x_low[x_place(index, layer, ny)]
                top[slot, EDGE + nx + layer, inner] = x_high[x_place(index, layer, ny)]
            else:
                top[slot, EDGE - 1 - layer, inner] = jnp.zeros((ny, LANES), F32)
                top[slot, EDGE + nx + layer, inner] = jnp.zeros((ny, LANES), F32)
        for slab in range(-Y_REACH[index], nx + Y_REACH[index]):
            top[slot, EDGE + slab, PAD - width : PAD] = y_low[y_place(index, slab, nx)]
            top[slot, EDGE + slab, PAD + ny : PAD + ny + width] = y_high[y_place(index, slab, nx)]
    clear_pads(other, rows)
    row_inside = (rows_of((rows, LANES)) >= RIM) | (me_y > 0)
    main = pl.ds(RIM, rows)
    start_v = top.at[V]

    def first(index):
        slab = index + 1
        inside = row_inside & ((slab >= EDGE) | (me_x > 0))
        set_weights(top, slab, RIM, rows, LANES, inside)
        other[slab, main] = swept(top, start_v, slab, RIM, rows)

    run(slabs - 2, first)

    def second(index):
        slab = index + 2
        top[V, slab, main] = swept(top, other, slab, RIM, rows)

    run(slabs - 4, second)

    def rest(slab):
        v, total = weighted(top, top.at[V], slab, PAD, ny)
        return total - top[D, slab, inner] * v

    def residual(index):
        slab = EDGE + 2 * index
        tmp[index] = rest(slab) + rest(slab + 1)

    run(nx // 2, residual)

    coarse_x, coarse_y = nx // 2, ny // 2
    slabs, rows = coarse_x + 2 * RIM, coarse_y + 2 * RIM
    half = slabs // 2
    inner = pl.ds(2 * RIM, coarse_y)
    main = pl.ds(RIM, rows)
    base_x, base_y = x_rows(nx, ny)[0], y_rows(nx, ny)[0]
    for face, slot in enumerate((FX, FY, ZL)):
        clear_pads(mid.at[slot], rows)
        mid[slot, RIM : RIM + coarse_x, inner] = faces[face]
        place = base_x + face * (RIM // 2) * coarse_y
        for layer in range(RIM):
            mid[slot, layer, inner] = rim_slab(x_low, place, coarse_y, layer)
            mid[slot, RIM + coarse_x + layer, inner] = rim_slab(x_high, place, coarse_y, layer)
        for slab in range(half):
            place = pl.ds(base_y + (face * half + slab) * RIM, RIM)
            for message, row in ((y_low, RIM), (y_high, 2 * RIM + coarse_y)):
                pair = one_of_two(message[place])
                mid[slot, slab, row : row + RIM] = pair[0]
                mid[slot, slab + half, row : row + RIM] = pair[1]
    row_inside = (rows_of((rows, LANES)) >= RIM) | (me_y > 0)
    for slab in range(slabs - 1):
        inside = row_inside & (me_x > 0) if slab < RIM else row_inside
        set_weights(mid, slab, RIM, rows, HALF, inside)

    source = even_rows(tmp, ny) + odd_rows(tmp, ny)
    source = 0.5 * exact_dot(source.reshape(coarse_x * coarse_y, LANES), compact(LANES, 0))
    for ref in (mid.at[F], mid.at[V], one):
        ref[...] = jnp.zeros(ref.shape, F32)
    mid[F, RIM : RIM + coarse_x, inner] = source.reshape(coarse_x, coarse_y, LANES)
    for slab in range(RIM, RIM + coarse_x):
        mid[V, slab, inner] = mid[W, slab, inner] * mid[F, slab, inner]
    for layer in range(RIM // 2):
        near, far = RIM + layer, coarse_x + layer
        v_low[layer * coarse_y : (layer + 1) * coarse_y] = two_in_one(
            mid[V, near, inner], mid[V, near + RIM // 2, inner]
        )
        v_high[layer * coarse_y : (layer + 1) * coarse_y] = two_in_one(
            mid[V, far, inner], mid[V, far + RIM // 2, inner]
        )
    base = RIM // 2 * coarse_y
    for layer in range(2):
        place = pl.ds(base + layer * ny, ny)
        v_low[place] = top[V, EDGE + layer, pl.ds(PAD, ny)]
        v_high[place] = top[V, EDGE + nx - 2 + layer, pl.ds(PAD, ny)]
    for slab in range(RIM - 1, RIM + coarse_x + 1):
        one[slab, main] = swept(mid, mid.at[V], slab, RIM, rows)

    def rest_1(slab):
        v, total = weighted(mid, one, slab, RIM, rows)
        return total - mid[D, slab, main] * v

    two[...] = jnp.zeros(two.shape, F32)
    for pair in range(1, half - 1):
        two[pair] = rest_1(2 * pair) + rest_1(2 * pair + 1)
    pieces = even_rows(two, rows) + odd_rows(two, rows)
    coarse_rows, quarter_rows = rows // 2, rows // 4
    chunk[:coarse_rows] = 0.5 * fold_four([pieces[1 + i] for i in range(4)])
    rest_of = [pieces[5 + i // 2][i % 2 * quarter_rows :][:quarter_rows] for i in range(4)]
    chunk[coarse_rows : coarse_rows + quarter_rows] = 0.5 * fold_four(rest_of)
    chunk[coarse_rows + quarter_rows :] = coefficients[:BLOCK_ROWS - coarse_rows - quarter_rows]


def pack_v(top, mid, x_low, x_high, low, high):
    slabs = mid.shape[1]
    coarse_x = slabs - 2 * RIM
    coarse_y = mid.shape[2] - 4 * RIM
    half = slabs // 2
    own = mid[V, RIM : RIM + coarse_x, 2 * RIM : 2 * RIM + coarse_y]
    values = [
        wide_slab(
            slab,
            lambda layer: rim_slab(x_low, 0, coarse_y, layer),
            own,
            lambda layer: rim_slab(x_high, 0, coarse_y, layer),
        )
        for slab in range(slabs)
    ]
    for slab in range(half):
        both = two_in_one(values[slab], values[slab + half])
        low[slab * RIM : (slab + 1) * RIM] = both[:RIM]
        high[slab * RIM : (slab + 1) * RIM] = both[coarse_y - RIM :]
    nx, ny = 2 * coarse_x, 2 * coarse_y
    base_x, base_y = RIM // 2 * coarse_y, half * RIM
    for out, start in ((low, 0), (high, ny - 2)):
        for layer in range(2):
            rows = pl.ds(base_x + layer * ny + start, 2)
            out[pl.ds(base_y + 2 * layer, 2)] = x_low[rows]
            out[pl.ds(base_y + 2 * (2 + nx + layer), 2)] = x_high[rows]
        for slab in range(nx):
            out[pl.ds(base_y + 2 * (2 + slab), 2)] = top[V, EDGE + slab, pl.ds(PAD + start, 2)]


def stack_blocks(*refs):
    for index, ref in enumerate(refs[:-3]):
        refs[-1][index] = ref[...]


def pair_rows(values, stride):
    return values + roll_rows(values, -stride)


def pair_lanes(values, stride):
    return values + roll_lanes(values, -stride)


class Listed:
    def __init__(self, fx, fy, fz, stride, depth):
        self.fx, self.fy, self.fz, self.stride, self.depth = fx, fy, fz, stride, depth
        shape = fx[0].shape
        rows = shape[0]
        row, lane = rows_of(shape), lanes_of(shape)
        z = lane % depth
        count = self.count = len(fx)
        self.x_high = [
            fx[s + 1] if s + 1 < count else jnp.where(lane < LANES - depth, roll_lanes(fx[0], -depth), 0.0)
            for s in range(count)
        ]
        self.x_low = [fx[s] if s > 0 else jnp.where(lane >= depth, fx[0], 0.0) for s in range(count)]
        self.y_high = [jnp.where(row < rows - stride, roll_rows(f, -stride), 0.0) for f in fy]
        self.y_low = [jnp.where(row >= stride, f, 0.0) for f in fy]
        self.z_high = [jnp.where(z < depth - stride, roll_lanes(f, -stride), 0.0) for f in fz]
        self.z_low = [jnp.where(z >= stride, f, 0.0) for f in fz]
        self.d = [
            fx[s] + self.x_high[s] + fy[s] + self.y_high[s] + fz[s] + self.z_high[s] for s in range(count)
        ]
        self.w = [jnp.where(d > 0.0, OMEGA / jnp.where(d > 0.0, d, 1.0), 0.0) for d in self.d]

    def weighted(self, v, f):
        count = self.count
        out = []
        for s in range(count):
            low = v[s - 1] if s > 0 else roll_lanes(v[count - 1], self.depth)
            high = v[s + 1] if s + 1 < count else roll_lanes(v[0], -self.depth)
            x = self.x_low[s] * low + self.x_high[s] * high
            y = self.y_low[s] * roll_rows(v[s], self.stride) + self.y_high[s] * roll_rows(v[s], -self.stride)
            z = self.z_low[s] * roll_lanes(v[s], self.stride) + self.z_high[s] * roll_lanes(v[s], -self.stride)
            total = (f[s] + y) + (x + z)
            out.append(total)
        return out

    def sweep(self, v, f):
        totals = self.weighted(v, f)
        return [(1.0 - OMEGA) * v[s] + self.w[s] * totals[s] for s in range(self.count)]

    def sweeps(self, count, f):
        folded = [
            [w * c for w, c in zip(self.w, coefficients)]
            for coefficients in (self.x_low, self.x_high, self.y_low, self.y_high, self.z_low, self.z_high)
        ]
        scaled = self.start(f)
        slabs = self.count

        def step(index, v):
            out = []
            for s in range(slabs):
                low = v[s - 1] if s > 0 else roll_lanes(v[slabs - 1], self.depth)
                high = v[s + 1] if s + 1 < slabs else roll_lanes(v[0], -self.depth)
                x = folded[0][s] * low + folded[1][s] * high
                y = folded[2][s] * roll_rows(v[s], self.stride) + folded[3][s] * roll_rows(v[s], -self.stride)
                z = folded[4][s] * roll_lanes(v[s], self.stride) + folded[5][s] * roll_lanes(v[s], -self.stride)
                out.append((((1.0 - OMEGA) * v[s] + scaled[s]) + y) + (x + z))
            return out

        return lax.fori_loop(1, count, step, scaled)

    def start(self, f):
        return [self.w[s] * f[s] for s in range(self.count)]

    def residual(self, v, f):
        totals = self.weighted(v, f)
        return [totals[s] - self.d[s] * v[s] for s in range(self.count)]

    def kept(self):
        shape = self.fx[0].shape
        step = 2 * self.stride
        return (rows_of(shape) % step == 0) & (lanes_of(shape) % step == 0)

    def coarser(self):
        keep, stride = self.kept(), self.stride
        half = range(self.count // 2)

        def kept(values):
            return jnp.where(keep, 0.25 * values, 0.0)

        fx = [kept(pair_lanes(pair_rows(self.fx[2 * s], stride), stride)) for s in half]
        fy = [kept(pair_lanes(self.fy[2 * s] + self.fy[2 * s + 1], stride)) for s in half]
        fz = [kept(pair_rows(self.fz[2 * s] + self.fz[2 * s + 1], stride)) for s in half]
        return Listed(fx, fy, fz, 2 * stride, self.depth)

    def restrict(self, r):
        keep, stride = self.kept(), self.stride
        return [
            jnp.where(keep, 0.5 * pair_lanes(pair_rows(r[2 * s] + r[2 * s + 1], stride), stride), 0.0)
            for s in range(self.count // 2)
        ]

    def prolong(self, e):
        out = []
        for values in e:
            values = values + roll_rows(values, self.stride)
            values = values + roll_lanes(values, self.stride)
            out += [values, values]
        return out


def listed_cycle(levels, sweeps, f):
    level = levels[0]
    if len(levels) == 1:
        return level.sweeps(sweeps, f)
    v = level.sweep(level.start(f), f)
    e = listed_cycle(levels[1:], sweeps, level.restrict(level.residual(v, f)))
    v = [a + b for a, b in zip(v, level.prolong(e))]
    return level.sweep(level.sweep(v, f), f)


def level_two(axes, grid, sweeps, shape, pieces, out, wide, tall):
    devices_x, devices_y = grid
    me_x, me_y = lax.axis_index(axes[0]), lax.axis_index(axes[1])
    own_x, own_y = shape
    quarter = LANES // 4
    reach = RIM // 2
    blocks = 4
    count = devices_x * own_x // blocks
    rows = devices_y * own_y
    main = pl.ds(PAD, rows)
    window = own_y + RIM

    def piece(gx, gy):
        slow, far = (me_x // 2) ^ (gx // 2), (me_y // 2) ^ (gy // 2)
        return ((me_y + gy) % 2, (me_x + gx) % 2 * (devices_y // 2) + far, slow)

    for ref in (wide, tall):
        ref[...] = jnp.zeros(ref.shape, F32)
    lane = lanes_of((window, LANES))
    for gy in range(devices_y):
        sums = [None] * count
        for gx in range(devices_x):
            where = piece(gx, gy)
            first = pieces[where + (pl.ds(0, window),)]
            second = pieces[where + (pl.ds(window, window // 2),)]
            for local in range(1, 2 * blocks - 1):
                x = own_x * gx - reach + local
                if not 0 <= x < devices_x * own_x:
                    continue
                block, slab = x // count, x % count
                if local <= blocks:
                    moved = roll_lanes(first, (block - local + 1) * quarter)
                else:
                    at = 2 * (local - blocks - 1)
                    halves = [roll_lanes(second, (block - at - odd) * quarter) for odd in range(2)]
                    moved = jnp.concatenate(halves)
                moved = jnp.where(lane // quarter == block, moved, 0.0)
                sums[slab] = moved if sums[slab] is None else sums[slab] + moved
        place = pl.ds(PAD + own_y * gy - reach, window)
        for slab in range(count):
            tall[slab, place] = tall[slab, place] + sums[slab]
    f = [tall[slab, main] for slab in range(count)]

    lane = lanes_of((rows, LANES))
    for gx in range(devices_x):
        for gy in range(devices_y):
            where = piece(gx, gy)
            for face in range(3):
                values = pieces[where + (pl.ds(window + window // 2 + face * own_y, own_y),)]
                wide[face, gx, gy * own_y : (gy + 1) * own_y] = values
    faces = []
    for face in range(3):
        slabs = [None] * count
        for gx in range(devices_x):
            values = wide[face, gx]
            for local in range(own_x):
                x = own_x * gx + local
                block, slab = x // count, x % count
                moved = roll_lanes(values, (block - local) * quarter)
                moved = jnp.where(lane // quarter == block, moved, 0.0)
                slabs[slab] = moved if slabs[slab] is None else slabs[slab] + moved
        faces.append(slabs)
    levels = [Listed(*faces, 1, quarter)]
    while len(levels) < LEVELS - 2:
        levels.append(levels[-1].coarser())
    e = listed_cycle(levels, sweeps, f)

    for slab in range(count):
        out[reach + slab, main] = e[slab]
    for slab in range(reach):
        out[slab, main] = jnp.where(lane < quarter, 0.0, roll_lanes(e[count - reach + slab], quarter))
        out[reach + count + slab, main] = jnp.where(
            lane >= LANES - quarter, 0.0, roll_lanes(e[slab], -quarter)
        )
    out[:, :PAD] = jnp.zeros((count + 2 * reach, PAD, LANES), F32)
    out[:, PAD + rows :] = jnp.zeros((count + 2 * reach, PAD, LANES), F32)


def level_up(axes, grid, coarse, top, mid, x_low, x_high, y_low, y_high, out, one, two, right, post, up):
    devices_x, devices_y = grid
    me_x, me_y = lax.axis_index(axes[0]), lax.axis_index(axes[1])
    coarse_x, coarse_y = mid.shape[1] - 2 * RIM, mid.shape[2] - 4 * RIM
    own_x, own_y = coarse_x // 2, coarse_y // 2
    quarter = LANES // 4
    reach = RIM // 2
    window = own_y + RIM

    slabs, high = coarse_x + 2 * RIM, coarse_y + 2 * RIM
    half = slabs // 2
    inner = pl.ds(2 * RIM, coarse_y)
    body = pl.ds(RIM, high)
    one[...] = mid[V]
    clear_pads(two, high)
    for layer in range(RIM):
        one[layer, inner] = rim_slab(x_low, 0, coarse_y, layer)
        one[RIM + coarse_x + layer, inner] = rim_slab(x_high, 0, coarse_y, layer)
    for slab in range(half):
        place = pl.ds(slab * RIM, RIM)
        for message, row in ((y_low, RIM), (y_high, 2 * RIM + coarse_y)):
            pair = one_of_two(message[place])
            one[slab, row : row + RIM] = pair[0]
            one[slab + half, row : row + RIM] = pair[1]
    row = rows_of((high, LANES))
    own_row = (row >= RIM) & (row < RIM + coarse_y)
    for slab in range(1, slabs - 1):
        f_rim = one[slab, body] * mid[D, slab, body] * (1.0 / OMEGA)
        if RIM <= slab < RIM + coarse_x:
            f_rim = jnp.where(own_row, mid[F, slab, body], f_rim)
        right[slab, body] = f_rim
        two[slab, body] = swept(mid, one, slab, RIM, high, right)

    per_block = (coarse.shape[0] - 2 * reach) // own_x
    base = me_x % per_block * own_x
    mine = None
    for gy in range(devices_y):
        place = pl.ds(PAD + gy * own_y - reach, window)
        values = jnp.where(me_y == gy, coarse[pl.ds(base, half), place, :], 0.0)
        mine = values if mine is None else mine + values
    source = lax.broadcasted_iota(jnp.int32, (LANES, LANES), 0)
    target = lax.broadcasted_iota(jnp.int32, (LANES, LANES), 1)
    hit = (source == me_x // per_block * quarter + target // 2) & (target < HALF)
    fine = exact_dot(mine.reshape(half * window, LANES), jnp.where(hit, 1.0, 0.0).astype(F32))
    fine = fine.reshape(half, window, LANES)
    for odd in range(2):
        up[:half, pl.ds(odd, window, stride=2), :] = fine
    for pair in range(half):
        for slab in (2 * pair, 2 * pair + 1):
            if 1 <= slab < slabs - 1:
                two[slab, body] = two[slab, body] + up[pair, :high]
    for slab in range(2, slabs - 2):
        one[slab, body] = swept(mid, two, slab, RIM, high, right)
    for slab in range(3, slabs - 3):
        two[slab, body] = swept(mid, one, slab, RIM, high, right)

    nx, ny = out.shape[:2]
    steps = coarse_x + 2
    fine_rows = ny + 2 * RIM
    e = two[RIM - 1 : RIM - 1 + steps, body]
    fine = exact_dot(e.reshape(steps * high, LANES), expand(LANES, 0)).reshape(steps, high, LANES)
    fine = fine[:, reach : reach + fine_rows // 2]
    for odd in range(2):
        up[:, pl.ds(odd, fine_rows // 2, stride=2), :] = fine
    body = pl.ds(RIM, fine_rows)
    for slot in (0, 1):
        clear_pads(post.at[slot], fine_rows)
    inner = pl.ds(PAD, ny)
    post[0, EDGE : EDGE + nx, inner] = top[V, EDGE : EDGE + nx, inner]
    base_x, base_y = RIM // 2 * coarse_y, half * RIM
    for layer in range(2):
        place = pl.ds(base_x + layer * ny, ny)
        post[0, EDGE - 2 + layer, inner] = x_low[place]
        post[0, EDGE + nx + layer, inner] = x_high[place]
    for slab in range(nx + 4):
        place = pl.ds(base_y + 2 * slab, 2)
        post[0, slab + EDGE - 2, RIM:PAD] = jnp.zeros((RIM, LANES), F32)
        post[0, slab + EDGE - 2, PAD + ny : PAD + ny + RIM] = jnp.zeros((RIM, LANES), F32)
        post[0, slab + EDGE - 2, PAD - 2 : PAD] = y_low[place]
        post[0, slab + EDGE - 2, PAD + ny : PAD + ny + 2] = y_high[place]

    def raise_level(index):
        for slab in (EDGE - 2 + 2 * index, EDGE - 1 + 2 * index):
            post[0, slab, body] = post[0, slab, body] + up[index]

    run(steps, raise_level)

    def fifth(index):
        slab = EDGE - 1 + index
        post[1, slab, body] = swept(top, post.at[0], slab, RIM, fine_rows)

    run(nx + 2, fifth)

    def sixth(index):
        out[index] = swept(top, post.at[1], EDGE + index, PAD, ny)

    run(nx, sixth)


IN_VMEM = pl.BlockSpec(memory_space=pltpu.VMEM)


def call(kernel, outs, scratch=(), from_hbm=False):
    ins = pl.BlockSpec(memory_space=pl.ANY) if from_hbm else IN_VMEM

    def launch(*args):
        if from_hbm:
            args = [pltpu.with_memory_space_constraint(arg, pltpu.HBM) for arg in args]
        return pl.pallas_call(
            kernel,
            out_shape=[pltpu.VMEM(shape, F32) for shape in outs],
            in_specs=[ins] * len(args),
            out_specs=[IN_VMEM] * len(outs),
            scratch_shapes=[pltpu.VMEM(s, F32) if isinstance(s, tuple) else s for s in scratch],
            compiler_params=pltpu.CompilerParams(vmem_limit_bytes=24 * 2**20),
        )(*args)

    return launch


def pair_route(axis):
    return [(i, i ^ 1) for i in range(lax.axis_size(axis))]


def swap_route(axis):
    count = lax.axis_size(axis)
    return [(i, (i + 1 ^ 1) - 1) for i in range(1, count - 1)]


def by_partner(low, high, axis):
    odd = lax.axis_index(axis) % 2 == 1
    return jnp.where(odd, low, high), jnp.where(odd, high, low)


def from_sides(low, high, axis):
    pair, swap = by_partner(low, high, axis)
    pair = lax.ppermute(pair, axis, pair_route(axis))
    swap = lax.ppermute(swap, axis, swap_route(axis))
    return by_partner(pair, swap, axis)


def passed_round(block, axis, stride):
    count = lax.axis_size(axis)
    return [block] + [
        lax.ppermute(block, axis, [(i, i ^ distance) for i in range(count)])
        for distance in range(stride, count, stride)
    ]


def passed_across(block):
    count, size = lax.axis_size("gx"), lax.axis_size("gy")
    blocks = []
    for side in range(2):
        for distance in range(0, size, 2):
            route = [
                (x * size + y, (x ^ side) * size + (y ^ distance)) for x in range(count) for y in range(size)
            ]
            moved = side + distance > 0
            blocks.append(lax.ppermute(block, ("gx", "gy"), route) if moved else block)
    return blocks


def fused_cycle(*fields):
    axes = ("gx", "gy")
    devices_x, devices_y = lax.axis_size("gx"), lax.axis_size("gy")
    nx, ny, nz = fields[0].shape
    coarse_x, coarse_y = nx // 2, ny // 2
    x_shape = (sum(x_rows(nx, ny)), LANES)
    y_shape = (sum(y_rows(nx, ny)), LANES)
    own, x_low, x_high, faces = call(
        start_pack,
        [(5, nx, ny, nz), x_shape, x_shape, (3, coarse_x, coarse_y, LANES)],
        [(coarse_x, ny, LANES), pltpu.SemaphoreType.DMA((5,))],
        True,
    )(*fields)
    x_low, x_high = from_sides(x_low, x_high, "gx")
    (coefficients,) = call(coarse_faces, [(16, LANES)], [(coarse_x // 2, coarse_y, LANES)])(faces)
    y_low, y_high = call(pack_y, [y_shape] * 2)(own, faces, x_low, x_high)
    y_low, y_high = from_sides(y_low, y_high, "gy")
    stack = (nx + 2 * EDGE, ny + 4 * RIM, LANES)
    stack_1 = (coarse_x + 2 * RIM, coarse_y + 4 * RIM, LANES)
    half = stack_1[0] // 2
    v_shape = (RIM // 2 * coarse_y + 2 * ny, LANES)
    w_shape = (half * RIM + 2 * (nx + 4), LANES)
    top, mid, chunk, v_low, v_high = call(
        functools.partial(level_down, axes),
        [(D + 1,) + stack, (D + 1,) + stack_1, (BLOCK_ROWS, LANES), v_shape, v_shape],
        [stack, (nx // 2, ny, LANES), stack_1, (half, coarse_y + 2 * RIM, LANES)],
    )(own, faces, coefficients, x_low, x_high, y_low, y_high)

    blocks = passed_round(chunk, "gx", 2)
    v_low, v_high = from_sides(v_low, v_high, "gx")
    slow = (len(blocks),) + chunk.shape
    (pieces,) = call(stack_blocks, [slow])(*blocks, v_low, v_high)
    blocks = passed_across(pieces.reshape(-1, LANES))
    w_low, w_high = call(pack_v, [w_shape] * 2)(top, mid, v_low, v_high)
    pair, swap = by_partner(w_low, w_high, "gy")
    message = jnp.concatenate(blocks + [pair])
    swap = lax.ppermute(swap, "gy", swap_route("gy"))
    other = lax.ppermute(message, "gy", pair_route("gy"))
    rows = message.shape[0] - w_shape[0]
    pieces = jnp.stack((message[:rows], other[:rows])).reshape((2, len(blocks)) + slow)
    w_low, w_high = by_partner(other[rows:], swap, "gy")
    count = devices_x * nx // 16
    rows = devices_y * ny // 4
    grid = (devices_x, devices_y)
    coarsest = (devices_x * nx >> LEVELS - 1, devices_y * ny >> LEVELS - 1)
    wide = (count + RIM, rows + 2 * PAD, LANES)
    (coarse,) = call(
        functools.partial(level_two, axes, grid, 4 * max(coarsest), (nx // 4, ny // 4)),
        [wide],
        [(3, devices_x, rows, LANES), wide],
    )(pieces)
    return pl.pallas_call(
        functools.partial(level_up, axes, grid),
        out_shape=jax.ShapeDtypeStruct((nx, ny, nz), F32),
        in_specs=[IN_VMEM] * 7,
        out_specs=IN_VMEM,
        scratch_shapes=[
            pltpu.VMEM(shape, F32)
            for shape in (stack_1, stack_1, stack_1, (2,) + stack, (coarse_x + 2, ny + 2 * RIM, LANES))
        ],
        compiler_params=pltpu.CompilerParams(vmem_limit_bytes=24 * 2**20),
    )(coarse, top, mid, v_low, v_high, w_low, w_high)


def with_halo(block, sides, width):
    for axis, dim in sides:
        count = lax.axis_size(axis)
        forward = [(i, i + 1) for i in range(count - 1)]
        backward = [(target, source) for source, target in forward]
        low = lax.ppermute(
            lax.slice_in_dim(block, block.shape[dim] - width, None, axis=dim), axis, forward
        )
        high = lax.ppermute(lax.slice_in_dim(block, 0, width, axis=dim), axis, backward)
        block = jnp.concatenate([low, block, high], axis=dim)
    return block


def passed_along(block, axis, distance):
    devices = range(lax.axis_size(axis))
    route = [(i - distance, i) for i in devices if i - distance in devices]
    return lax.ppermute(block, axis, route)


def stencil(padded, padded_x, padded_y, face_z):
    center = padded[1:-1, 1:-1]
    zero_plane = jnp.zeros(center.shape[:2] + (1,), center.dtype)
    above_face = jnp.concatenate((face_z[:, :, 1:], zero_plane), axis=2)
    below_z = jnp.concatenate((zero_plane, center[:, :, :-1]), axis=2)
    above_z = jnp.concatenate((center[:, :, 1:], zero_plane), axis=2)
    lower_x = padded_x[1:-1, 1:-1]
    upper_x = padded_x[2:, 1:-1]
    lower_y = padded_y[1:-1, 1:-1]
    upper_y = padded_y[1:-1, 2:]
    applied = lower_x * (center - padded[:-2, 1:-1]) + upper_x * (center - padded[2:, 1:-1])
    applied = (
        applied + lower_y * (center - padded[1:-1, :-2]) + upper_y * (center - padded[1:-1, 2:])
    )
    applied = applied + face_z * (center - below_z) + above_face * (center - above_z)
    diagonal = lower_x + upper_x + lower_y + upper_y + face_z + above_face
    return (applied, diagonal)


def jacobi_sweep(padded, source, padded_x, padded_y, face_z):
    applied, diagonal = stencil(padded, padded_x, padded_y, face_z)
    return padded[1:-1, 1:-1] + OMEGA * (source - applied) / diagonal


def pad_plane(values, width):
    return jnp.pad(values, ((width, width), (width, width), (0, 0)))


def restrict(residual):
    shape = residual.shape
    blocks = residual.reshape(shape[0] // 2, 2, shape[1] // 2, 2, shape[2] // 2, 2)
    return 4.0 * jnp.mean(blocks, axis=(1, 3, 5))


def coarsen_faces(face_x, face_y, face_z):
    shape = face_x.shape
    blocks = (shape[0] // 2, 2, shape[1] // 2, 2, shape[2] // 2, 2)
    coarse_x = jnp.mean(face_x.reshape(blocks)[:, 0], axis=(2, 4))
    coarse_y = jnp.mean(face_y.reshape(blocks)[:, :, :, 0], axis=(1, 4))
    coarse_z = jnp.mean(face_z.reshape(blocks)[..., 0], axis=(1, 3))
    return (coarse_x, coarse_y, coarse_z)


def prolong(coarse):
    return jnp.repeat(jnp.repeat(jnp.repeat(coarse, 2, axis=0), 2, axis=1), 2, axis=2)


def local_cycle(grid_level, iterate, source, face_x, face_y, face_z):
    padded_x = pad_plane(face_x, 1)
    padded_y = pad_plane(face_y, 1)
    if grid_level == LEVELS - 1:
        count = 4 * max(iterate.shape[0], iterate.shape[1])

        def one_sweep(index, values):
            return jacobi_sweep(pad_plane(values, 1), source, padded_x, padded_y, face_z)

        return lax.fori_loop(0, count, one_sweep, iterate)
    for sweep_index in range(2):
        iterate = jacobi_sweep(pad_plane(iterate, 1), source, padded_x, padded_y, face_z)
    applied, diagonal = stencil(pad_plane(iterate, 1), padded_x, padded_y, face_z)
    coarse_src = restrict(source - applied)
    coarse_x, coarse_y, coarse_z = coarsen_faces(face_x, face_y, face_z)
    correction = local_cycle(
        grid_level + 1, jnp.zeros_like(coarse_src), coarse_src, coarse_x, coarse_y, coarse_z
    )
    iterate = iterate + prolong(correction)
    for sweep_index in range(2):
        iterate = jacobi_sweep(pad_plane(iterate, 1), source, padded_x, padded_y, face_z)
    return iterate


def field_rim(iterate):
    return with_halo(iterate, (("gx", 0), ("gy", 1)), 1)


def sweep_pair_narrow(iterate, source, padded_x, padded_y, face_z, zero_start):
    for sweep_index in range(2):
        if sweep_index == 0 and zero_start:
            padded = pad_plane(iterate, 1)
        else:
            padded = field_rim(iterate)
        iterate = jacobi_sweep(padded, source, padded_x, padded_y, face_z)
    return iterate


def descend(grid_level, iterate, source, face_x, face_y, face_z, zero_start, gather_level):
    if grid_level == gather_level:
        pieces = (
            lax.all_gather(source, "gy", axis=1, tiled=True),
            lax.all_gather(face_x, "gy", axis=1, tiled=True),
            lax.all_gather(face_y, "gy", axis=1, tiled=True),
            lax.all_gather(face_z, "gy", axis=1, tiled=True),
        )
        gathered = (
            lax.all_gather(pieces[0], "gx", axis=0, tiled=True),
            lax.all_gather(pieces[1], "gx", axis=0, tiled=True),
            lax.all_gather(pieces[2], "gx", axis=0, tiled=True),
            lax.all_gather(pieces[3], "gx", axis=0, tiled=True),
        )
        correction = local_cycle(
            grid_level,
            jnp.zeros_like(gathered[0]),
            gathered[0],
            gathered[1],
            gathered[2],
            gathered[3],
        )
        start_x = lax.axis_index("gx") * source.shape[0]
        start_y = lax.axis_index("gy") * source.shape[1]
        return lax.dynamic_slice(
            correction, (start_x, start_y, jnp.zeros((), jnp.int32)), source.shape
        )
    next_x = passed_along(face_x[:1], "gx", -1)
    next_y = passed_along(face_y[:, :1], "gy", -1)
    lower_row = jnp.zeros_like(next_x)
    lower_col = jnp.zeros_like(next_y)
    padded_x = jnp.pad(
        jnp.concatenate((lower_row, face_x, next_x), axis=0), ((0, 0), (1, 1), (0, 0))
    )
    padded_y = jnp.pad(
        jnp.concatenate((lower_col, face_y, next_y), axis=1), ((1, 1), (0, 0), (0, 0))
    )

    def smoother(values, starting):
        return sweep_pair_narrow(values, source, padded_x, padded_y, face_z, starting)

    iterate = smoother(iterate, zero_start)
    applied, diagonal = stencil(field_rim(iterate), padded_x, padded_y, face_z)
    coarse_src = restrict(source - applied)
    coarse_x, coarse_y, coarse_z = coarsen_faces(face_x, face_y, face_z)
    correction = descend(
        grid_level + 1,
        jnp.zeros_like(coarse_src),
        coarse_src,
        coarse_x,
        coarse_y,
        coarse_z,
        True,
        gather_level,
    )
    iterate = iterate + prolong(correction)
    return smoother(iterate, False)


def fits(nx, ny, nz, devices_x, devices_y):
    cells = devices_x * nx * devices_y * ny * nz // 8
    even = devices_x % 8 == 0 and devices_y % 4 == 0
    even = even and devices_x & (devices_x - 1) == 0 and devices_y & (devices_y - 1) == 0
    return cells <= 2**18 and even and (nx, ny, nz) == (16, 16, LANES)


def local(source_term, initial_guess, face_x, face_y, face_z):
    if fits(*source_term.shape, lax.axis_size("gx"), lax.axis_size("gy")):
        return fused_cycle(source_term, initial_guess, face_x, face_y, face_z)
    gather_level = 4
    return descend(0, initial_guess, source_term, face_x, face_y, face_z, False, gather_level)


def solution(mesh):
    placed = (P("gx", "gy", None),) * 5
    return jax.shard_map(
        local, mesh=mesh, in_specs=placed, out_specs=P("gx", "gy", None), check_vma=False
    )
```

```python
import functools

import jax
import jax.numpy as jnp
from jax import lax
from jax.experimental import pallas as pl
from jax.experimental.pallas import tpu as pltpu
from jax.sharding import PartitionSpec as P

LEVELS = 6
OMEGA = 0.8
LANES = 128
RIM = 4
EDGE = 3
PAD = 8
BLOCK_ROWS = 24
F32 = jnp.float32

V, F, FX, FY, ZL, ZH, W, D = range(8)
SLOTS = (F, V, FX, FY, ZL)
X_LAYERS = (2, 3, 3, 2, 2)
Y_LAYERS = (2, 3, 2, 3, 2)
Y_REACH = (1, 2, 2, 2, 1)


def lanes_of(shape):
    return lax.broadcasted_iota(jnp.int32, shape, len(shape) - 1)


def rows_of(shape):
    return lax.broadcasted_iota(jnp.int32, shape, len(shape) - 2)


def roll_lanes(values, step):
    return pltpu.roll(values, step % LANES, values.ndim - 1)


def roll_rows(values, step):
    return pltpu.roll(values, step % values.shape[-2], values.ndim - 2)


def exact_dot(left, right):
    return jnp.dot(left, right, precision=lax.Precision.HIGHEST, preferred_element_type=F32)


def compact(depth, part, even_only=False):
    source = lax.broadcasted_iota(jnp.int32, (LANES, LANES), 0)
    target = lax.broadcasted_iota(jnp.int32, (LANES, LANES), 1)
    half = depth // 2
    hit = target == (source // depth * 2 + part) * half + source % depth // 2
    if even_only:
        hit = hit & (source % 2 == 0)
    return jnp.where(hit, 1.0, 0.0).astype(F32)


def expand(depth, part):
    target = lax.broadcasted_iota(jnp.int32, (LANES, LANES), 0)
    source = lax.broadcasted_iota(jnp.int32, (LANES, LANES), 1)
    half = depth // 2
    hit = target == (source // depth * 2 + part) * half + source % depth // 2
    return jnp.where(hit, 1.0, 0.0).astype(F32)


def merge_lanes(values, depth, even_only=False):
    count, rows, _ = values.shape
    half = count // 2
    flat = values.reshape(2, half * rows, LANES)
    out = exact_dot(flat[0], compact(depth, 0, even_only))
    out = out + exact_dot(flat[1], compact(depth, 1, even_only))
    return out.reshape(half, rows, LANES)


def even_rows(ref, rows):
    return ref[:, pl.ds(0, rows // 2, stride=2), :]


def odd_rows(ref, rows):
    return ref[:, pl.ds(1, rows // 2, stride=2), :]


HALF = LANES // 2


def low_half(values):
    return jnp.where(lanes_of(values.shape) < HALF, values, 0.0)


def two_in_one(first, second):
    return first + roll_lanes(second, HALF)


def one_of_two(values):
    return low_half(values), low_half(roll_lanes(values, HALF))


def x_rows(nx, ny):
    return sum(X_LAYERS) * ny


def y_rows(nx, ny):
    return sum(layers * (nx + 2 * reach) for layers, reach in zip(Y_LAYERS, Y_REACH))


def rim_rows_x(nx, ny):
    slab = RIM // 2 * (ny // 2)
    return slab, 2 * ny, 3 * slab


def rim_rows_y(nx, ny):
    slabs = (nx // 2 + 2 * RIM) // 2 * RIM
    return slabs, 2 * (nx + 4), 3 * slabs


def x_place(index, layer, ny):
    return pl.ds((sum(X_LAYERS[:index]) + layer) * ny, ny)


def y_place(index, slab, nx):
    before = zip(Y_LAYERS[:index], Y_REACH[:index])
    start = sum(layers * (nx + 2 * reach) for layers, reach in before)
    return pl.ds(start + (Y_REACH[index] + slab) * Y_LAYERS[index], Y_LAYERS[index])


def start_pack(*refs):
    fields, (own, x_low, x_high, done) = refs[:5], refs[5:]
    copies = [pltpu.make_async_copy(ref, own.at[index], done.at[index]) for index, ref in enumerate(fields)]
    for copy in copies:
        copy.start()
    nx, ny = own.shape[1:3]
    for index, copy in enumerate(copies):
        copy.wait()
        for layer in range(X_LAYERS[index]):
            x_low[x_place(index, layer, ny)] = own[index, layer]
            x_high[x_place(index, layer, ny)] = own[index, nx - X_LAYERS[index] + layer]


def pair_slabs(ref):
    count = ref.shape[0]
    values = ref[...].reshape((count // 2, 2) + ref.shape[1:])
    return values[:, 0], values[:, 1]


def wide_slab(slab, from_low, own, from_high):
    count = own.shape[0]
    if slab < RIM:
        return from_low(slab)
    if slab < RIM + count:
        return own[slab - RIM]
    return from_high(slab - RIM - count)


def rim_slab(ref, base, rows, layer):
    place = pl.ds(base + layer % (RIM // 2) * rows, rows)
    return one_of_two(ref[place])[layer // (RIM // 2)]


def pack_y(own, x_low, x_high, low, high):
    nx, ny = own.shape[1:3]
    for index in range(5):
        width, layers, reach = Y_LAYERS[index], X_LAYERS[index], Y_REACH[index]
        for out, start in ((low, 0), (high, ny - width)):
            for slab in range(nx):
                out[y_place(index, slab, nx)] = own[index, slab, start : start + width]
            for layer in range(reach):
                rows = pl.ds(x_place(index, layers - reach + layer, ny).start + start, width)
                out[y_place(index, layer - reach, nx)] = x_low[rows]
                rows = pl.ds(x_place(index, layer, ny).start + start, width)
                out[y_place(index, nx + layer, nx)] = x_high[rows]


def fold_four(slabs, even_only=False):
    out = None
    for part in range(2):
        term = exact_dot(two_in_one(slabs[part], slabs[2 + part]), compact(HALF, part, even_only))
        out = term if out is None else out + term
    return out


def coarse_slab_sums(ref_x, ref_y, ref_z, count, first, tmp):
    extra = tmp.shape[0]
    rows = tmp.shape[1]
    for index in range(extra):
        tmp[index] = ref_x[first + 2 * index]
    x = even_rows(tmp, rows) + odd_rows(tmp, rows)
    for index in range(count):
        tmp[index] = ref_y[first + 2 * index] + ref_y[first + 2 * index + 1]
    y = even_rows(tmp, rows)[:count]
    for index in range(count):
        tmp[index] = ref_z[first + 2 * index] + ref_z[first + 2 * index + 1]
    return x, y, (even_rows(tmp, rows) + odd_rows(tmp, rows))[:count]


def halved(values, even_only=False):
    count, rows, _ = values.shape
    flat = exact_dot(values.reshape(count * rows, LANES), compact(LANES, 0, even_only))
    return 0.25 * flat.reshape(count, rows, LANES)


def coarse_faces(own, faces, out, fine, tmp):
    x, y, z = coarse_slab_sums(own.at[2], own.at[3], own.at[4], own.shape[1] // 2, 0, fine)
    faces[0] = halved(x)
    faces[1] = halved(y)
    faces[2] = halved(z, True)
    rows = faces.shape[2]
    coarse = rows // 2
    fx, fy, fz = faces.at[0], faces.at[1], faces.at[2]
    tmp[...] = pair_slabs(fx)[0]
    x = even_rows(tmp, rows) + odd_rows(tmp, rows)
    first, second = pair_slabs(fy)
    tmp[...] = first + second
    y = even_rows(tmp, rows)
    first, second = pair_slabs(fz)
    tmp[...] = first + second
    z = even_rows(tmp, rows) + odd_rows(tmp, rows)
    out[...] = jnp.zeros(out.shape, F32)
    out[:coarse] = 0.25 * fold_four([x[i] for i in range(4)])
    out[coarse : 2 * coarse] = 0.25 * fold_four([y[i] for i in range(4)])
    out[2 * coarse : 3 * coarse] = 0.25 * fold_four([z[i] for i in range(4)], True)


def weighted(lev, src, slab, start, rows, f=None):
    here = pl.ds(start, rows)
    below = pl.ds(start - 1, rows)
    above = pl.ds(start + 1, rows)
    v = src[slab, here]
    f = lev.at[F] if f is None else f
    x = lev[FX, slab, here] * src[slab - 1, here] + lev[FX, slab + 1, here] * src[slab + 1, here]
    y = lev[FY, slab, here] * src[slab, below] + lev[FY, slab, above] * src[slab, above]
    z = lev[ZL, slab, here] * roll_lanes(v, 1) + lev[ZH, slab, here] * roll_lanes(v, -1)
    total = ((x + y) + f[slab, here]) + z
    return v, total


def swept(lev, src, slab, start, rows, f=None):
    v, total = weighted(lev, src, slab, start, rows, f)
    return (1.0 - OMEGA) * v + lev[W, slab, pl.ds(start, rows)] * total


def set_weights(lev, slab, start, rows, depth, inside=None):
    here = pl.ds(start, rows)
    fz = lev[ZL, slab, here]
    z = lanes_of(fz.shape) % depth
    upper = jnp.where(z == depth - 1, 0.0, roll_lanes(fz, -1))
    diagonal = lev[FX, slab, here] + lev[FX, slab + 1, here]
    diagonal = diagonal + lev[FY, slab, here] + lev[FY, slab, pl.ds(start + 1, rows)] + fz + upper
    valid = diagonal > 0.0
    if inside is not None:
        valid = valid & inside
    lev[ZL, slab, here] = jnp.where(z == 0, 0.0, fz)
    lev[ZH, slab, here] = upper
    lev[D, slab, here] = diagonal
    lev[W, slab, here] = jnp.where(valid, OMEGA / jnp.where(valid, diagonal, 1.0), 0.0)


def run(count, body):
    for index in range(count):
        body(index)


def clear_pads(ref, rows):
    for start in (0, RIM + rows):
        ref[:, start : start + RIM] = jnp.zeros((ref.shape[0], RIM, LANES), F32)


def level_down(axes, own, faces, coefficients, x_low, x_high, y_low, y_high, *refs):
    top, kept, chunk, v_low, v_high, other, tmp, one, two, mid, wide = refs
    nx, ny = own.shape[1:3]
    slabs, rows = nx + 2 * EDGE, ny + 2 * RIM
    me_x, me_y = lax.axis_index(axes[0]), lax.axis_index(axes[1])
    inner = pl.ds(PAD, ny)
    for index, slot in enumerate(SLOTS):
        layers, width = X_LAYERS[index], Y_LAYERS[index]
        top[slot, :, :PAD] = jnp.zeros((slabs, PAD, LANES), F32)
        top[slot, :, PAD + ny :] = jnp.zeros((slabs, PAD, LANES), F32)
        top[slot, EDGE : EDGE + nx, inner] = own[index]
        for layer in range(EDGE):
            if layer < layers:
                top[slot, EDGE - layers + layer, inner] = x_low[x_place(index, layer, ny)]
                top[slot, EDGE + nx + layer, inner] = x_high[x_place(index, layer, ny)]
            else:
                top[slot, EDGE - 1 - layer, inner] = jnp.zeros((ny, LANES), F32)
                top[slot, EDGE + nx + layer, inner] = jnp.zeros((ny, LANES), F32)
        for slab in range(-Y_REACH[index], nx + Y_REACH[index]):
            top[slot, EDGE + slab, PAD - width : PAD] = y_low[y_place(index, slab, nx)]
            top[slot, EDGE + slab, PAD + ny : PAD + ny + width] = y_high[y_place(index, slab, nx)]
    clear_pads(other, rows)

    coarse_x, coarse_y = nx // 2, ny // 2
    near = RIM - 1
    for slot in (FX, FY, ZL, ZH, W, D):
        mid[slot] = jnp.zeros(mid.shape[1:], F32)
    x, y, z = coarse_slab_sums(top.at[FX], top.at[FY], top.at[ZL], coarse_x + 2, EDGE - 2, wide)
    mid[FX, near : near + coarse_x + 3, RIM : 3 * RIM + coarse_y] = halved(x)
    mid[FY, near : near + coarse_x + 2, RIM : 3 * RIM + coarse_y] = halved(y)
    mid[ZL, near : near + coarse_x + 2, RIM : 3 * RIM + coarse_y] = halved(z, True)

    row_inside = (rows_of((rows, LANES)) >= RIM) | (me_y > 0)
    main = pl.ds(RIM, rows)
    start_v = top.at[V]

    def first(index):
        slab = index + 1
        inside = row_inside & ((slab >= EDGE) | (me_x > 0))
        set_weights(top, slab, RIM, rows, LANES, inside)
        other[slab, main] = swept(top, start_v, slab, RIM, rows)

    run(slabs - 2, first)

    def second(index):
        slab = index + 2
        top[V, slab, main] = swept(top, other, slab, RIM, rows)

    run(slabs - 4, second)

    def rest(slab):
        v, total = weighted(top, top.at[V], slab, PAD, ny)
        return total - top[D, slab, inner] * v

    def residual(index):
        slab = EDGE + 2 * index
        tmp[index] = rest(slab) + rest(slab + 1)

    run(nx // 2, residual)

    slabs, rows = coarse_x + 2 * RIM, coarse_y + 2 * RIM
    half = slabs // 2
    inner = pl.ds(2 * RIM, coarse_y)
    main = pl.ds(RIM, rows)
    row_inside = (rows_of((rows, LANES)) >= RIM) | (me_y > 0)
    for slab in range(near, near + coarse_x + 2):
        inside = row_inside & (me_x > 0) if slab < RIM else row_inside
        set_weights(mid, slab, RIM, rows, HALF, inside)

    source = even_rows(tmp, ny) + odd_rows(tmp, ny)
    source = 0.5 * exact_dot(source.reshape(coarse_x * coarse_y, LANES), compact(LANES, 0))
    for ref in (mid.at[F], mid.at[V], one):
        ref[...] = jnp.zeros(ref.shape, F32)
    mid[F, RIM : RIM + coarse_x, inner] = source.reshape(coarse_x, coarse_y, LANES)
    for slab in range(RIM, RIM + coarse_x):
        mid[V, slab, inner] = mid[W, slab, inner] * mid[F, slab, inner]
    for layer in range(RIM // 2):
        near, far = RIM + layer, coarse_x + layer
        v_low[layer * coarse_y : (layer + 1) * coarse_y] = two_in_one(
            mid[V, near, inner], mid[V, near + RIM // 2, inner]
        )
        v_high[layer * coarse_y : (layer + 1) * coarse_y] = two_in_one(
            mid[V, far, inner], mid[V, far + RIM // 2, inner]
        )
    kept[0] = mid[F, RIM : RIM + coarse_x, inner]
    kept[1] = mid[V, RIM : RIM + coarse_x, inner]
    base, after, _ = rim_rows_x(nx, ny)
    pairs = RIM // 2
    for face in range(3):
        for layer in range(pairs):
            place = pl.ds(base + after + (face * pairs + layer) * coarse_y, coarse_y)
            far = coarse_x - RIM + layer
            v_low[place] = two_in_one(faces[face, layer], faces[face, layer + pairs])
            v_high[place] = two_in_one(faces[face, far], faces[face, far + pairs])
    for layer in range(2):
        place = pl.ds(base + layer * ny, ny)
        v_low[place] = top[V, EDGE + layer, pl.ds(PAD, ny)]
        v_high[place] = top[V, EDGE + nx - 2 + layer, pl.ds(PAD, ny)]
    for slab in range(RIM - 1, RIM + coarse_x + 1):
        one[slab, main] = swept(mid, mid.at[V], slab, RIM, rows)

    def rest_1(slab):
        v, total = weighted(mid, one, slab, RIM, rows)
        return total - mid[D, slab, main] * v

    two[...] = jnp.zeros(two.shape, F32)
    for pair in range(1, half - 1):
        two[pair] = rest_1(2 * pair) + rest_1(2 * pair + 1)
    pieces = even_rows(two, rows) + odd_rows(two, rows)
    coarse_rows, quarter_rows = rows // 2, rows // 4
    chunk[:coarse_rows] = 0.5 * fold_four([pieces[1 + i] for i in range(4)])
    rest_of = [pieces[5 + i // 2][i % 2 * quarter_rows :][:quarter_rows] for i in range(4)]
    chunk[coarse_rows : coarse_rows + quarter_rows] = 0.5 * fold_four(rest_of)
    chunk[coarse_rows + quarter_rows :] = coefficients[:BLOCK_ROWS - coarse_rows - quarter_rows]


def pack_v(top, kept, faces, x_low, x_high, low, high):
    coarse_x, coarse_y = faces.shape[1:3]
    nx, ny = 2 * coarse_x, 2 * coarse_y
    slabs = coarse_x + 2 * RIM
    half = slabs // 2
    sizes_x, sizes_y = rim_rows_x(nx, ny), rim_rows_y(nx, ny)

    def folded(own, place_x, place_y):
        values = [
            wide_slab(
                slab,
                lambda layer: rim_slab(x_low, place_x, coarse_y, layer),
                own,
                lambda layer: rim_slab(x_high, place_x, coarse_y, layer),
            )
            for slab in range(slabs)
        ]
        for slab in range(half):
            both = two_in_one(values[slab], values[slab + half])
            rows = pl.ds(place_y + slab * RIM, RIM)
            low[rows] = both[:RIM]
            high[rows] = both[coarse_y - RIM :]

    folded(kept.at[1], 0, 0)
    for face in range(3):
        folded(
            faces.at[face],
            sizes_x[0] + sizes_x[1] + face * sizes_x[0],
            sizes_y[0] + sizes_y[1] + face * sizes_y[0],
        )
    base_x, base_y = sizes_x[0], sizes_y[0]
    for out, start in ((low, 0), (high, ny - 2)):
        for layer in range(2):
            rows = pl.ds(base_x + layer * ny + start, 2)
            out[pl.ds(base_y + 2 * layer, 2)] = x_low[rows]
            out[pl.ds(base_y + 2 * (2 + nx + layer), 2)] = x_high[rows]
        for slab in range(nx):
            out[pl.ds(base_y + 2 * (2 + slab), 2)] = top[V, EDGE + slab, pl.ds(PAD + start, 2)]


def stack_blocks(*refs):
    for index, ref in enumerate(refs[:-3]):
        refs[-1][index] = ref[...]


def pair_rows(values, stride):
    return values + roll_rows(values, -stride)


def pair_lanes(values, stride):
    return values + roll_lanes(values, -stride)


class Listed:
    def __init__(self, fx, fy, fz, stride, depth):
        self.fx, self.fy, self.fz, self.stride, self.depth = fx, fy, fz, stride, depth
        shape = fx[0].shape
        rows = shape[0]
        row, lane = rows_of(shape), lanes_of(shape)
        z = lane % depth
        count = self.count = len(fx)
        self.x_high = [
            fx[s + 1] if s + 1 < count else jnp.where(lane < LANES - depth, roll_lanes(fx[0], -depth), 0.0)
            for s in range(count)
        ]
        self.x_low = [fx[s] if s > 0 else jnp.where(lane >= depth, fx[0], 0.0) for s in range(count)]
        self.y_high = [jnp.where(row < rows - stride, roll_rows(f, -stride), 0.0) for f in fy]
        self.y_low = [jnp.where(row >= stride, f, 0.0) for f in fy]
        self.z_high = [jnp.where(z < depth - stride, roll_lanes(f, -stride), 0.0) for f in fz]
        self.z_low = [jnp.where(z >= stride, f, 0.0) for f in fz]
        self.d = [
            fx[s] + self.x_high[s] + fy[s] + self.y_high[s] + fz[s] + self.z_high[s] for s in range(count)
        ]
        self.w = [jnp.where(d > 0.0, OMEGA / jnp.where(d > 0.0, d, 1.0), 0.0) for d in self.d]

    def weighted(self, v, f):
        count = self.count
        out = []
        for s in range(count):
            low = v[s - 1] if s > 0 else roll_lanes(v[count - 1], self.depth)
            high = v[s + 1] if s + 1 < count else roll_lanes(v[0], -self.depth)
            x = self.x_low[s] * low + self.x_high[s] * high
            y = self.y_low[s] * roll_rows(v[s], self.stride) + self.y_high[s] * roll_rows(v[s], -self.stride)
            z = self.z_low[s] * roll_lanes(v[s], self.stride) + self.z_high[s] * roll_lanes(v[s], -self.stride)
            total = (f[s] + y) + (x + z)
            out.append(total)
        return out

    def sweep(self, v, f):
        totals = self.weighted(v, f)
        return [(1.0 - OMEGA) * v[s] + self.w[s] * totals[s] for s in range(self.count)]

    def sweeps(self, count, f):
        folded = [
            [w * c for w, c in zip(self.w, coefficients)]
            for coefficients in (self.x_low, self.x_high, self.y_low, self.y_high, self.z_low, self.z_high)
        ]
        scaled = self.start(f)
        slabs = self.count

        def step(index, v):
            out = []
            for s in range(slabs):
                low = v[s - 1] if s > 0 else roll_lanes(v[slabs - 1], self.depth)
                high = v[s + 1] if s + 1 < slabs else roll_lanes(v[0], -self.depth)
                x = folded[0][s] * low + folded[1][s] * high
                y = folded[2][s] * roll_rows(v[s], self.stride) + folded[3][s] * roll_rows(v[s], -self.stride)
                z = folded[4][s] * roll_lanes(v[s], self.stride) + folded[5][s] * roll_lanes(v[s], -self.stride)
                out.append((((1.0 - OMEGA) * v[s] + scaled[s]) + y) + (x + z))
            return out

        return lax.fori_loop(1, count, step, scaled)

    def start(self, f):
        return [self.w[s] * f[s] for s in range(self.count)]

    def residual(self, v, f):
        totals = self.weighted(v, f)
        return [totals[s] - self.d[s] * v[s] for s in range(self.count)]

    def kept(self):
        shape = self.fx[0].shape
        step = 2 * self.stride
        return (rows_of(shape) % step == 0) & (lanes_of(shape) % step == 0)

    def coarser(self):
        keep, stride = self.kept(), self.stride
        half = range(self.count // 2)

        def kept(values):
            return jnp.where(keep, 0.25 * values, 0.0)

        fx = [kept(pair_lanes(pair_rows(self.fx[2 * s], stride), stride)) for s in half]
        fy = [kept(pair_lanes(self.fy[2 * s] + self.fy[2 * s + 1], stride)) for s in half]
        fz = [kept(pair_rows(self.fz[2 * s] + self.fz[2 * s + 1], stride)) for s in half]
        return Listed(fx, fy, fz, 2 * stride, self.depth)

    def restrict(self, r):
        keep, stride = self.kept(), self.stride
        return [
            jnp.where(keep, 0.5 * pair_lanes(pair_rows(r[2 * s] + r[2 * s + 1], stride), stride), 0.0)
            for s in range(self.count // 2)
        ]

    def prolong(self, e):
        out = []
        for values in e:
            values = values + roll_rows(values, self.stride)
            values = values + roll_lanes(values, self.stride)
            out += [values, values]
        return out


def listed_cycle(levels, sweeps, f):
    level = levels[0]
    if len(levels) == 1:
        return level.sweeps(sweeps, f)
    v = level.sweep(level.start(f), f)
    e = listed_cycle(levels[1:], sweeps, level.restrict(level.residual(v, f)))
    v = [a + b for a, b in zip(v, level.prolong(e))]
    return level.sweep(level.sweep(v, f), f)


def level_two(axes, grid, sweeps, shape, pieces, out, wide, tall):
    devices_x, devices_y = grid
    me_x, me_y = lax.axis_index(axes[0]), lax.axis_index(axes[1])
    own_x, own_y = shape
    quarter = LANES // 4
    reach = RIM // 2
    blocks = 4
    count = devices_x * own_x // blocks
    rows = devices_y * own_y
    main = pl.ds(PAD, rows)
    window = own_y + RIM

    def piece(gx, gy):
        slow, far = (me_x // 2) ^ (gx // 2), (me_y // 2) ^ (gy // 2)
        return ((me_y + gy) % 2, (me_x + gx) % 2 * (devices_y // 2) + far, slow)

    for ref in (wide, tall):
        ref[...] = jnp.zeros(ref.shape, F32)
    lane = lanes_of((window, LANES))
    for gy in range(devices_y):
        sums = [None] * count
        for gx in range(devices_x):
            where = piece(gx, gy)
            first = pieces[where + (pl.ds(0, window),)]
            second = pieces[where + (pl.ds(window, window // 2),)]
            for local in range(1, 2 * blocks - 1):
                x = own_x * gx - reach + local
                if not 0 <= x < devices_x * own_x:
                    continue
                block, slab = x // count, x % count
                if local <= blocks:
                    moved = roll_lanes(first, (block - local + 1) * quarter)
                else:
                    at = 2 * (local - blocks - 1)
                    halves = [roll_lanes(second, (block - at - odd) * quarter) for odd in range(2)]
                    moved = jnp.concatenate(halves)
                moved = jnp.where(lane // quarter == block, moved, 0.0)
                sums[slab] = moved if sums[slab] is None else sums[slab] + moved
        place = pl.ds(PAD + own_y * gy - reach, window)
        for slab in range(count):
            tall[slab, place] = tall[slab, place] + sums[slab]
    f = [tall[slab, main] for slab in range(count)]

    lane = lanes_of((rows, LANES))
    for gx in range(devices_x):
        for gy in range(devices_y):
            where = piece(gx, gy)
            for face in range(3):
                values = pieces[where + (pl.ds(window + window // 2 + face * own_y, own_y),)]
                wide[face, gx, gy * own_y : (gy + 1) * own_y] = values
    faces = []
    for face in range(3):
        slabs = [None] * count
        for gx in range(devices_x):
            values = wide[face, gx]
            for local in range(own_x):
                x = own_x * gx + local
                block, slab = x // count, x % count
                moved = roll_lanes(values, (block - local) * quarter)
                moved = jnp.where(lane // quarter == block, moved, 0.0)
                slabs[slab] = moved if slabs[slab] is None else slabs[slab] + moved
        faces.append(slabs)
    levels = [Listed(*faces, 1, quarter)]
    while len(levels) < LEVELS - 2:
        levels.append(levels[-1].coarser())
    e = listed_cycle(levels, sweeps, f)

    for slab in range(count):
        out[reach + slab, main] = e[slab]
    for slab in range(reach):
        out[slab, main] = jnp.where(lane < quarter, 0.0, roll_lanes(e[count - reach + slab], quarter))
        out[reach + count + slab, main] = jnp.where(
            lane >= LANES - quarter, 0.0, roll_lanes(e[slab], -quarter)
        )
    out[:, :PAD] = jnp.zeros((count + 2 * reach, PAD, LANES), F32)
    out[:, PAD + rows :] = jnp.zeros((count + 2 * reach, PAD, LANES), F32)


def level_up(axes, grid, coarse, top, kept, faces, x_low, x_high, y_low, y_high, *refs):
    out, mid, one, two, right, post, up = refs
    devices_x, devices_y = grid
    me_x, me_y = lax.axis_index(axes[0]), lax.axis_index(axes[1])
    coarse_x, coarse_y = faces.shape[1:3]
    nx, ny = out.shape[:2]
    own_x, own_y = coarse_x // 2, coarse_y // 2
    quarter = LANES // 4
    reach = RIM // 2
    window = own_y + RIM

    slabs, high = coarse_x + 2 * RIM, coarse_y + 2 * RIM
    half = slabs // 2
    inner = pl.ds(2 * RIM, coarse_y)
    body = pl.ds(RIM, high)
    sizes_x, sizes_y = rim_rows_x(nx, ny), rim_rows_y(nx, ny)
    for face, slot in enumerate((FX, FY, ZL)):
        clear_pads(mid.at[slot], high)
        mid[slot, RIM : RIM + coarse_x, inner] = faces[face]
        place_x = sizes_x[0] + sizes_x[1] + face * sizes_x[0]
        place_y = sizes_y[0] + sizes_y[1] + face * sizes_y[0]
        for layer in range(RIM):
            mid[slot, layer, inner] = rim_slab(x_low, place_x, coarse_y, layer)
            mid[slot, RIM + coarse_x + layer, inner] = rim_slab(x_high, place_x, coarse_y, layer)
        for slab in range(half):
            place = pl.ds(place_y + slab * RIM, RIM)
            for message, row in ((y_low, RIM), (y_high, 2 * RIM + coarse_y)):
                pair = one_of_two(message[place])
                mid[slot, slab, row : row + RIM] = pair[0]
                mid[slot, slab + half, row : row + RIM] = pair[1]
    row_inside = (rows_of((high, LANES)) >= RIM) | (me_y > 0)
    for slab in range(slabs - 1):
        inside = row_inside & (me_x > 0) if slab < RIM else row_inside
        set_weights(mid, slab, RIM, high, HALF, inside)
    clear_pads(one, high)
    clear_pads(right, high)
    clear_pads(two, high)
    one[RIM : RIM + coarse_x, inner] = kept[1]
    right[RIM : RIM + coarse_x, inner] = kept[0]
    for layer in range(RIM):
        one[layer, inner] = rim_slab(x_low, 0, coarse_y, layer)
        one[RIM + coarse_x + layer, inner] = rim_slab(x_high, 0, coarse_y, layer)
    for slab in range(half):
        place = pl.ds(slab * RIM, RIM)
        for message, row in ((y_low, RIM), (y_high, 2 * RIM + coarse_y)):
            pair = one_of_two(message[place])
            one[slab, row : row + RIM] = pair[0]
            one[slab + half, row : row + RIM] = pair[1]
    row = rows_of((high, LANES))
    own_row = (row >= RIM) & (row < RIM + coarse_y)
    for slab in range(1, slabs - 1):
        f_rim = one[slab, body] * mid[D, slab, body] * (1.0 / OMEGA)
        if RIM <= slab < RIM + coarse_x:
            f_rim = jnp.where(own_row, right[slab, body], f_rim)
        right[slab, body] = f_rim
        two[slab, body] = swept(mid, one, slab, RIM, high, right)

    per_block = (coarse.shape[0] - 2 * reach) // own_x
    base = me_x % per_block * own_x
    mine = None
    for gy in range(devices_y):
        place = pl.ds(PAD + gy * own_y - reach, window)
        values = jnp.where(me_y == gy, coarse[pl.ds(base, half), place, :], 0.0)
        mine = values if mine is None else mine + values
    source = lax.broadcasted_iota(jnp.int32, (LANES, LANES), 0)
    target = lax.broadcasted_iota(jnp.int32, (LANES, LANES), 1)
    hit = (source == me_x // per_block * quarter + target // 2) & (target < HALF)
    fine = exact_dot(mine.reshape(half * window, LANES), jnp.where(hit, 1.0, 0.0).astype(F32))
    fine = fine.reshape(half, window, LANES)
    for odd in range(2):
        up[:half, pl.ds(odd, window, stride=2), :] = fine
    for pair in range(half):
        for slab in (2 * pair, 2 * pair + 1):
            if 1 <= slab < slabs - 1:
                two[slab, body] = two[slab, body] + up[pair, :high]
    for slab in range(2, slabs - 2):
        one[slab, body] = swept(mid, two, slab, RIM, high, right)
    for slab in range(3, slabs - 3):
        two[slab, body] = swept(mid, one, slab, RIM, high, right)

    steps = coarse_x + 2
    fine_rows = ny + 2 * RIM
    e = two[RIM - 1 : RIM - 1 + steps, body]
    fine = exact_dot(e.reshape(steps * high, LANES), expand(LANES, 0)).reshape(steps, high, LANES)
    fine = fine[:, reach : reach + fine_rows // 2]
    for odd in range(2):
        up[:, pl.ds(odd, fine_rows // 2, stride=2), :] = fine
    body = pl.ds(RIM, fine_rows)
    for slot in (0, 1):
        clear_pads(post.at[slot], fine_rows)
    inner = pl.ds(PAD, ny)
    post[0, EDGE : EDGE + nx, inner] = top[V, EDGE : EDGE + nx, inner]
    base_x, base_y = RIM // 2 * coarse_y, half * RIM
    for layer in range(2):
        place = pl.ds(base_x + layer * ny, ny)
        post[0, EDGE - 2 + layer, inner] = x_low[place]
        post[0, EDGE + nx + layer, inner] = x_high[place]
    for slab in range(nx + 4):
        place = pl.ds(base_y + 2 * slab, 2)
        post[0, slab + EDGE - 2, RIM:PAD] = jnp.zeros((RIM, LANES), F32)
        post[0, slab + EDGE - 2, PAD + ny : PAD + ny + RIM] = jnp.zeros((RIM, LANES), F32)
        post[0, slab + EDGE - 2, PAD - 2 : PAD] = y_low[place]
        post[0, slab + EDGE - 2, PAD + ny : PAD + ny + 2] = y_high[place]

    def raise_level(index):
        for slab in (EDGE - 2 + 2 * index, EDGE - 1 + 2 * index):
            post[0, slab, body] = post[0, slab, body] + up[index]

    run(steps, raise_level)

    def fifth(index):
        slab = EDGE - 1 + index
        post[1, slab, body] = swept(top, post.at[0], slab, RIM, fine_rows)

    run(nx + 2, fifth)

    def sixth(index):
        out[index] = swept(top, post.at[1], EDGE + index, PAD, ny)

    run(nx, sixth)


IN_VMEM = pl.BlockSpec(memory_space=pltpu.VMEM)


def call(kernel, outs, scratch=(), from_hbm=False):
    ins = pl.BlockSpec(memory_space=pl.ANY) if from_hbm else IN_VMEM

    def launch(*args):
        if from_hbm:
            args = [pltpu.with_memory_space_constraint(arg, pltpu.HBM) for arg in args]
        return pl.pallas_call(
            kernel,
            out_shape=[pltpu.VMEM(shape, F32) for shape in outs],
            in_specs=[ins] * len(args),
            out_specs=[IN_VMEM] * len(outs),
            scratch_shapes=[pltpu.VMEM(s, F32) if isinstance(s, tuple) else s for s in scratch],
            compiler_params=pltpu.CompilerParams(vmem_limit_bytes=24 * 2**20),
        )(*args)

    return launch


def pair_route(axis):
    return [(i, i ^ 1) for i in range(lax.axis_size(axis))]


def swap_route(axis):
    count = lax.axis_size(axis)
    return [(i, (i + 1 ^ 1) - 1) for i in range(1, count - 1)]


def by_partner(low, high, axis):
    odd = lax.axis_index(axis) % 2 == 1
    return jnp.where(odd, low, high), jnp.where(odd, high, low)


def from_sides(low, high, axis):
    pair, swap = by_partner(low, high, axis)
    pair = lax.ppermute(pair, axis, pair_route(axis))
    swap = lax.ppermute(swap, axis, swap_route(axis))
    return by_partner(pair, swap, axis)


def passed_round(block, axis, stride):
    count = lax.axis_size(axis)
    return [block] + [
        lax.ppermute(block, axis, [(i, i ^ distance) for i in range(count)])
        for distance in range(stride, count, stride)
    ]


def passed_across(block):
    count, size = lax.axis_size("gx"), lax.axis_size("gy")
    blocks = []
    for side in range(2):
        for distance in range(0, size, 2):
            route = [
                (x * size + y, (x ^ side) * size + (y ^ distance)) for x in range(count) for y in range(size)
            ]
            moved = side + distance > 0
            blocks.append(lax.ppermute(block, ("gx", "gy"), route) if moved else block)
    return blocks


def fused_cycle(*fields):
    axes = ("gx", "gy")
    devices_x, devices_y = lax.axis_size("gx"), lax.axis_size("gy")
    nx, ny, nz = fields[0].shape
    coarse_x, coarse_y = nx // 2, ny // 2
    x_shape, y_shape = (x_rows(nx, ny), LANES), (y_rows(nx, ny), LANES)
    own, x_low, x_high = call(
        start_pack, [(5, nx, ny, nz), x_shape, x_shape], [pltpu.SemaphoreType.DMA((5,))], True
    )(*fields)
    x_low, x_high = from_sides(x_low, x_high, "gx")
    faces, coefficients = call(
        coarse_faces,
        [(3, coarse_x, coarse_y, LANES), (16, LANES)],
        [(coarse_x, ny, LANES), (coarse_x // 2, coarse_y, LANES)],
    )(own)
    y_low, y_high = call(pack_y, [y_shape] * 2)(own, x_low, x_high)
    y_low, y_high = from_sides(y_low, y_high, "gy")
    stack = (nx + 2 * EDGE, ny + 4 * RIM, LANES)
    stack_1 = (coarse_x + 2 * RIM, coarse_y + 4 * RIM, LANES)
    half = stack_1[0] // 2
    v_shape = (sum(rim_rows_x(nx, ny)), LANES)
    w_shape = (sum(rim_rows_y(nx, ny)), LANES)
    top, kept, chunk, v_low, v_high = call(
        functools.partial(level_down, axes),
        [(D + 1,) + stack, (2, coarse_x, coarse_y, LANES), (BLOCK_ROWS, LANES), v_shape, v_shape],
        [
            stack,
            (nx // 2, ny, LANES),
            stack_1,
            (half, coarse_y + 2 * RIM, LANES),
            (D + 1,) + stack_1,
            (coarse_x + 3,) + stack[1:],
        ],
    )(own, faces, coefficients, x_low, x_high, y_low, y_high)

    blocks = passed_round(chunk, "gx", 2)
    v_low, v_high = from_sides(v_low, v_high, "gx")
    slow = (len(blocks),) + chunk.shape
    (pieces,) = call(stack_blocks, [slow])(*blocks, v_low, v_high)
    blocks = passed_across(pieces.reshape(-1, LANES))
    w_low, w_high = call(pack_v, [w_shape] * 2)(top, kept, faces, v_low, v_high)
    pair, swap = by_partner(w_low, w_high, "gy")
    message = jnp.concatenate(blocks + [pair])
    swap = lax.ppermute(swap, "gy", swap_route("gy"))
    other = lax.ppermute(message, "gy", pair_route("gy"))
    rows = message.shape[0] - w_shape[0]
    pieces = jnp.stack((message[:rows], other[:rows])).reshape((2, len(blocks)) + slow)
    w_low, w_high = by_partner(other[rows:], swap, "gy")
    count = devices_x * nx // 16
    rows = devices_y * ny // 4
    grid = (devices_x, devices_y)
    coarsest = (devices_x * nx >> LEVELS - 1, devices_y * ny >> LEVELS - 1)
    wide = (count + RIM, rows + 2 * PAD, LANES)
    (coarse,) = call(
        functools.partial(level_two, axes, grid, 4 * max(coarsest), (nx // 4, ny // 4)),
        [wide],
        [(3, devices_x, rows, LANES), wide],
    )(pieces)
    return pl.pallas_call(
        functools.partial(level_up, axes, grid),
        out_shape=jax.ShapeDtypeStruct((nx, ny, nz), F32),
        in_specs=[IN_VMEM] * 8,
        out_specs=IN_VMEM,
        scratch_shapes=[
            pltpu.VMEM(shape, F32)
            for shape in ((D + 1,) + stack_1, stack_1, stack_1, stack_1, (2,) + stack, (coarse_x + 2, ny + 2 * RIM, LANES))
        ],
        compiler_params=pltpu.CompilerParams(vmem_limit_bytes=24 * 2**20),
    )(coarse, top, kept, faces, v_low, v_high, w_low, w_high)


def with_halo(block, sides, width):
    for axis, dim in sides:
        count = lax.axis_size(axis)
        forward = [(i, i + 1) for i in range(count - 1)]
        backward = [(target, source) for source, target in forward]
        low = lax.ppermute(
            lax.slice_in_dim(block, block.shape[dim] - width, None, axis=dim), axis, forward
        )
        high = lax.ppermute(lax.slice_in_dim(block, 0, width, axis=dim), axis, backward)
        block = jnp.concatenate([low, block, high], axis=dim)
    return block


def passed_along(block, axis, distance):
    devices = range(lax.axis_size(axis))
    route = [(i - distance, i) for i in devices if i - distance in devices]
    return lax.ppermute(block, axis, route)


def stencil(padded, padded_x, padded_y, face_z):
    center = padded[1:-1, 1:-1]
    zero_plane = jnp.zeros(center.shape[:2] + (1,), center.dtype)
    above_face = jnp.concatenate((face_z[:, :, 1:], zero_plane), axis=2)
    below_z = jnp.concatenate((zero_plane, center[:, :, :-1]), axis=2)
    above_z = jnp.concatenate((center[:, :, 1:], zero_plane), axis=2)
    lower_x = padded_x[1:-1, 1:-1]
    upper_x = padded_x[2:, 1:-1]
    lower_y = padded_y[1:-1, 1:-1]
    upper_y = padded_y[1:-1, 2:]
    applied = lower_x * (center - padded[:-2, 1:-1]) + upper_x * (center - padded[2:, 1:-1])
    applied = (
        applied + lower_y * (center - padded[1:-1, :-2]) + upper_y * (center - padded[1:-1, 2:])
    )
    applied = applied + face_z * (center - below_z) + above_face * (center - above_z)
    diagonal = lower_x + upper_x + lower_y + upper_y + face_z + above_face
    return (applied, diagonal)


def jacobi_sweep(padded, source, padded_x, padded_y, face_z):
    applied, diagonal = stencil(padded, padded_x, padded_y, face_z)
    return padded[1:-1, 1:-1] + OMEGA * (source - applied) / diagonal


def pad_plane(values, width):
    return jnp.pad(values, ((width, width), (width, width), (0, 0)))


def restrict(residual):
    shape = residual.shape
    blocks = residual.reshape(shape[0] // 2, 2, shape[1] // 2, 2, shape[2] // 2, 2)
    return 4.0 * jnp.mean(blocks, axis=(1, 3, 5))


def coarsen_faces(face_x, face_y, face_z):
    shape = face_x.shape
    blocks = (shape[0] // 2, 2, shape[1] // 2, 2, shape[2] // 2, 2)
    coarse_x = jnp.mean(face_x.reshape(blocks)[:, 0], axis=(2, 4))
    coarse_y = jnp.mean(face_y.reshape(blocks)[:, :, :, 0], axis=(1, 4))
    coarse_z = jnp.mean(face_z.reshape(blocks)[..., 0], axis=(1, 3))
    return (coarse_x, coarse_y, coarse_z)


def prolong(coarse):
    return jnp.repeat(jnp.repeat(jnp.repeat(coarse, 2, axis=0), 2, axis=1), 2, axis=2)


def local_cycle(grid_level, iterate, source, face_x, face_y, face_z):
    padded_x = pad_plane(face_x, 1)
    padded_y = pad_plane(face_y, 1)
    if grid_level == LEVELS - 1:
        count = 4 * max(iterate.shape[0], iterate.shape[1])

        def one_sweep(index, values):
            return jacobi_sweep(pad_plane(values, 1), source, padded_x, padded_y, face_z)

        return lax.fori_loop(0, count, one_sweep, iterate)
    for sweep_index in range(2):
        iterate = jacobi_sweep(pad_plane(iterate, 1), source, padded_x, padded_y, face_z)
    applied, diagonal = stencil(pad_plane(iterate, 1), padded_x, padded_y, face_z)
    coarse_src = restrict(source - applied)
    coarse_x, coarse_y, coarse_z = coarsen_faces(face_x, face_y, face_z)
    correction = local_cycle(
        grid_level + 1, jnp.zeros_like(coarse_src), coarse_src, coarse_x, coarse_y, coarse_z
    )
    iterate = iterate + prolong(correction)
    for sweep_index in range(2):
        iterate = jacobi_sweep(pad_plane(iterate, 1), source, padded_x, padded_y, face_z)
    return iterate


def field_rim(iterate):
    return with_halo(iterate, (("gx", 0), ("gy", 1)), 1)


def sweep_pair_narrow(iterate, source, padded_x, padded_y, face_z, zero_start):
    for sweep_index in range(2):
        if sweep_index == 0 and zero_start:
            padded = pad_plane(iterate, 1)
        else:
            padded = field_rim(iterate)
        iterate = jacobi_sweep(padded, source, padded_x, padded_y, face_z)
    return iterate


def descend(grid_level, iterate, source, face_x, face_y, face_z, zero_start, gather_level):
    if grid_level == gather_level:
        pieces = (
            lax.all_gather(source, "gy", axis=1, tiled=True),
            lax.all_gather(face_x, "gy", axis=1, tiled=True),
            lax.all_gather(face_y, "gy", axis=1, tiled=True),
            lax.all_gather(face_z, "gy", axis=1, tiled=True),
        )
        gathered = (
            lax.all_gather(pieces[0], "gx", axis=0, tiled=True),
            lax.all_gather(pieces[1], "gx", axis=0, tiled=True),
            lax.all_gather(pieces[2], "gx", axis=0, tiled=True),
            lax.all_gather(pieces[3], "gx", axis=0, tiled=True),
        )
        correction = local_cycle(
            grid_level,
            jnp.zeros_like(gathered[0]),
            gathered[0],
            gathered[1],
            gathered[2],
            gathered[3],
        )
        start_x = lax.axis_index("gx") * source.shape[0]
        start_y = lax.axis_index("gy") * source.shape[1]
        return lax.dynamic_slice(
            correction, (start_x, start_y, jnp.zeros((), jnp.int32)), source.shape
        )
    next_x = passed_along(face_x[:1], "gx", -1)
    next_y = passed_along(face_y[:, :1], "gy", -1)
    lower_row = jnp.zeros_like(next_x)
    lower_col = jnp.zeros_like(next_y)
    padded_x = jnp.pad(
        jnp.concatenate((lower_row, face_x, next_x), axis=0), ((0, 0), (1, 1), (0, 0))
    )
    padded_y = jnp.pad(
        jnp.concatenate((lower_col, face_y, next_y), axis=1), ((1, 1), (0, 0), (0, 0))
    )

    def smoother(values, starting):
        return sweep_pair_narrow(values, source, padded_x, padded_y, face_z, starting)

    iterate = smoother(iterate, zero_start)
    applied, diagonal = stencil(field_rim(iterate), padded_x, padded_y, face_z)
    coarse_src = restrict(source - applied)
    coarse_x, coarse_y, coarse_z = coarsen_faces(face_x, face_y, face_z)
    correction = descend(
        grid_level + 1,
        jnp.zeros_like(coarse_src),
        coarse_src,
        coarse_x,
        coarse_y,
        coarse_z,
        True,
        gather_level,
    )
    iterate = iterate + prolong(correction)
    return smoother(iterate, False)


def fits(nx, ny, nz, devices_x, devices_y):
    cells = devices_x * nx * devices_y * ny * nz // 8
    even = devices_x % 8 == 0 and devices_y % 4 == 0
    even = even and devices_x & (devices_x - 1) == 0 and devices_y & (devices_y - 1) == 0
    return cells <= 2**18 and even and (nx, ny, nz) == (16, 16, LANES)


def local(source_term, initial_guess, face_x, face_y, face_z):
    if fits(*source_term.shape, lax.axis_size("gx"), lax.axis_size("gy")):
        return fused_cycle(source_term, initial_guess, face_x, face_y, face_z)
    gather_level = 4
    return descend(0, initial_guess, source_term, face_x, face_y, face_z, False, gather_level)


def solution(mesh):
    placed = (P("gx", "gy", None),) * 5
    return jax.shard_map(
        local, mesh=mesh, in_specs=placed, out_specs=P("gx", "gy", None), check_vma=False
    )
```

```python
import functools

import jax
import jax.numpy as jnp
from jax import lax
from jax.experimental import pallas as pl
from jax.experimental.pallas import tpu as pltpu
from jax.sharding import PartitionSpec as P

LEVELS = 6
OMEGA = 0.8
LANES = 128
RIM = 4
EDGE = 3
PAD = 8
BLOCK_ROWS = 24
F32 = jnp.float32

V, F, FX, FY, ZL, ZH, W, D = range(8)
SLOTS = (F, V, FX, FY, ZL)
X_LAYERS = (2, 3, 3, 2, 2)
Y_LAYERS = (2, 3, 2, 3, 2)
Y_REACH = (1, 2, 2, 2, 1)


def lanes_of(shape):
    return lax.broadcasted_iota(jnp.int32, shape, len(shape) - 1)


def rows_of(shape):
    return lax.broadcasted_iota(jnp.int32, shape, len(shape) - 2)


def roll_lanes(values, step):
    return pltpu.roll(values, step % LANES, values.ndim - 1)


def roll_rows(values, step):
    return pltpu.roll(values, step % values.shape[-2], values.ndim - 2)


def exact_dot(left, right):
    return jnp.dot(left, right, precision=lax.Precision.HIGHEST, preferred_element_type=F32)


def compact(depth, part, even_only=False):
    source = lax.broadcasted_iota(jnp.int32, (LANES, LANES), 0)
    target = lax.broadcasted_iota(jnp.int32, (LANES, LANES), 1)
    half = depth // 2
    hit = target == (source // depth * 2 + part) * half + source % depth // 2
    if even_only:
        hit = hit & (source % 2 == 0)
    return jnp.where(hit, 1.0, 0.0).astype(F32)


def expand(depth, part):
    target = lax.broadcasted_iota(jnp.int32, (LANES, LANES), 0)
    source = lax.broadcasted_iota(jnp.int32, (LANES, LANES), 1)
    half = depth // 2
    hit = target == (source // depth * 2 + part) * half + source % depth // 2
    return jnp.where(hit, 1.0, 0.0).astype(F32)


def merge_lanes(values, depth, even_only=False):
    count, rows, _ = values.shape
    half = count // 2
    flat = values.reshape(2, half * rows, LANES)
    out = exact_dot(flat[0], compact(depth, 0, even_only))
    out = out + exact_dot(flat[1], compact(depth, 1, even_only))
    return out.reshape(half, rows, LANES)


def even_rows(ref, rows):
    return ref[:, pl.ds(0, rows // 2, stride=2), :]


def odd_rows(ref, rows):
    return ref[:, pl.ds(1, rows // 2, stride=2), :]


HALF = LANES // 2


def low_half(values):
    return jnp.where(lanes_of(values.shape) < HALF, values, 0.0)


def two_in_one(first, second):
    return first + roll_lanes(second, HALF)


def one_of_two(values):
    return low_half(values), low_half(roll_lanes(values, HALF))


def x_rows(nx, ny):
    return sum(X_LAYERS) * ny


def y_rows(nx, ny):
    return sum(layers * (nx + 2 * reach) for layers, reach in zip(Y_LAYERS, Y_REACH))


def rim_rows_x(nx, ny):
    slab = RIM // 2 * (ny // 2)
    return slab, 2 * ny, 3 * slab


def rim_rows_y(nx, ny):
    slabs = (nx // 2 + 2 * RIM) // 2 * RIM
    return slabs, 2 * (nx + 4), 3 * slabs


def x_place(index, layer, ny):
    return pl.ds((sum(X_LAYERS[:index]) + layer) * ny, ny)


def y_place(index, slab, nx):
    before = zip(Y_LAYERS[:index], Y_REACH[:index])
    start = sum(layers * (nx + 2 * reach) for layers, reach in before)
    return pl.ds(start + (Y_REACH[index] + slab) * Y_LAYERS[index], Y_LAYERS[index])


def start_pack(*refs):
    fields, (own, x_low, x_high, done) = refs[:5], refs[5:]
    copies = [pltpu.make_async_copy(ref, own.at[index], done.at[index]) for index, ref in enumerate(fields)]
    for copy in copies:
        copy.start()
    nx, ny = own.shape[1:3]
    for index, copy in enumerate(copies):
        copy.wait()
        for layer in range(X_LAYERS[index]):
            x_low[x_place(index, layer, ny)] = own[index, layer]
            x_high[x_place(index, layer, ny)] = own[index, nx - X_LAYERS[index] + layer]


def pair_slabs(ref):
    count = ref.shape[0]
    values = ref[...].reshape((count // 2, 2) + ref.shape[1:])
    return values[:, 0], values[:, 1]


def wide_slab(slab, from_low, own, from_high):
    count = own.shape[0]
    if slab < RIM:
        return from_low(slab)
    if slab < RIM + count:
        return own[slab - RIM]
    return from_high(slab - RIM - count)


def rim_slab(ref, base, rows, layer):
    place = pl.ds(base + layer % (RIM // 2) * rows, rows)
    return one_of_two(ref[place])[layer // (RIM // 2)]


def pack_y(own, x_low, x_high, low, high):
    nx, ny = own.shape[1:3]
    for index in range(5):
        width, layers, reach = Y_LAYERS[index], X_LAYERS[index], Y_REACH[index]
        for out, start in ((low, 0), (high, ny - width)):
            for slab in range(nx):
                out[y_place(index, slab, nx)] = own[index, slab, start : start + width]
            for layer in range(reach):
                rows = pl.ds(x_place(index, layers - reach + layer, ny).start + start, width)
                out[y_place(index, layer - reach, nx)] = x_low[rows]
                rows = pl.ds(x_place(index, layer, ny).start + start, width)
                out[y_place(index, nx + layer, nx)] = x_high[rows]


def fold_four(slabs, even_only=False):
    out = None
    for part in range(2):
        term = exact_dot(two_in_one(slabs[part], slabs[2 + part]), compact(HALF, part, even_only))
        out = term if out is None else out + term
    return out


def coarse_slab_sums(ref_x, ref_y, ref_z, count, first, tmp):
    extra = tmp.shape[0]
    rows = tmp.shape[1]
    for index in range(extra):
        tmp[index] = ref_x[first + 2 * index]
    x = even_rows(tmp, rows) + odd_rows(tmp, rows)
    for index in range(count):
        tmp[index] = ref_y[first + 2 * index] + ref_y[first + 2 * index + 1]
    y = even_rows(tmp, rows)[:count]
    for index in range(count):
        tmp[index] = ref_z[first + 2 * index] + ref_z[first + 2 * index + 1]
    return x, y, (even_rows(tmp, rows) + odd_rows(tmp, rows))[:count]


def halved(values, even_only=False):
    count, rows, _ = values.shape
    flat = exact_dot(values.reshape(count * rows, LANES), compact(LANES, 0, even_only))
    return 0.25 * flat.reshape(count, rows, LANES)


def coarse_faces(own, faces, out, fine, tmp):
    x, y, z = coarse_slab_sums(own.at[2], own.at[3], own.at[4], own.shape[1] // 2, 0, fine)
    faces[0] = halved(x)
    faces[1] = halved(y)
    faces[2] = halved(z, True)
    rows = faces.shape[2]
    coarse = rows // 2
    fx, fy, fz = faces.at[0], faces.at[1], faces.at[2]
    tmp[...] = pair_slabs(fx)[0]
    x = even_rows(tmp, rows) + odd_rows(tmp, rows)
    first, second = pair_slabs(fy)
    tmp[...] = first + second
    y = even_rows(tmp, rows)
    first, second = pair_slabs(fz)
    tmp[...] = first + second
    z = even_rows(tmp, rows) + odd_rows(tmp, rows)
    out[...] = jnp.zeros(out.shape, F32)
    out[:coarse] = 0.25 * fold_four([x[i] for i in range(4)])
    out[coarse : 2 * coarse] = 0.25 * fold_four([y[i] for i in range(4)])
    out[2 * coarse : 3 * coarse] = 0.25 * fold_four([z[i] for i in range(4)], True)


def weighted(lev, src, slab, start, rows, f=None):
    here = pl.ds(start, rows)
    below = pl.ds(start - 1, rows)
    above = pl.ds(start + 1, rows)
    v = src[slab, here]
    f = lev.at[F] if f is None else f
    x = lev[FX, slab, here] * src[slab - 1, here] + lev[FX, slab + 1, here] * src[slab + 1, here]
    y = lev[FY, slab, here] * src[slab, below] + lev[FY, slab, above] * src[slab, above]
    z = lev[ZL, slab, here] * roll_lanes(v, 1) + lev[ZH, slab, here] * roll_lanes(v, -1)
    total = ((x + y) + f[slab, here]) + z
    return v, total


def swept(lev, src, slab, start, rows, f=None):
    v, total = weighted(lev, src, slab, start, rows, f)
    return (1.0 - OMEGA) * v + lev[W, slab, pl.ds(start, rows)] * total


def set_weights(lev, slab, start, rows, depth, inside=None):
    here = pl.ds(start, rows)
    fz = lev[ZL, slab, here]
    z = lanes_of(fz.shape) % depth
    upper = jnp.where(z == depth - 1, 0.0, roll_lanes(fz, -1))
    diagonal = lev[FX, slab, here] + lev[FX, slab + 1, here]
    diagonal = diagonal + lev[FY, slab, here] + lev[FY, slab, pl.ds(start + 1, rows)] + fz + upper
    valid = diagonal > 0.0
    if inside is not None:
        valid = valid & inside
    lev[ZL, slab, here] = jnp.where(z == 0, 0.0, fz)
    lev[ZH, slab, here] = upper
    lev[D, slab, here] = diagonal
    lev[W, slab, here] = jnp.where(valid, OMEGA / jnp.where(valid, diagonal, 1.0), 0.0)


def run(count, body):
    for index in range(count):
        body(index)


def clear_pads(ref, rows):
    for start in (0, RIM + rows):
        ref[:, start : start + RIM] = jnp.zeros((ref.shape[0], RIM, LANES), F32)


def level_down(axes, own, faces, coefficients, x_low, x_high, y_low, y_high, *refs):
    top, kept, chunk, v_low, v_high, other, tmp, one, two, mid, wide = refs
    nx, ny = own.shape[1:3]
    slabs, rows = nx + 2 * EDGE, ny + 2 * RIM
    me_x, me_y = lax.axis_index(axes[0]), lax.axis_index(axes[1])
    inner = pl.ds(PAD, ny)
    for index, slot in enumerate(SLOTS):
        layers, width = X_LAYERS[index], Y_LAYERS[index]
        top[slot, :, :PAD] = jnp.zeros((slabs, PAD, LANES), F32)
        top[slot, :, PAD + ny :] = jnp.zeros((slabs, PAD, LANES), F32)
        top[slot, EDGE : EDGE + nx, inner] = own[index]
        for layer in range(EDGE):
            if layer < layers:
                top[slot, EDGE - layers + layer, inner] = x_low[x_place(index, layer, ny)]
                top[slot, EDGE + nx + layer, inner] = x_high[x_place(index, layer, ny)]
            else:
                top[slot, EDGE - 1 - layer, inner] = jnp.zeros((ny, LANES), F32)
                top[slot, EDGE + nx + layer, inner] = jnp.zeros((ny, LANES), F32)
        for slab in range(-Y_REACH[index], nx + Y_REACH[index]):
            top[slot, EDGE + slab, PAD - width : PAD] = y_low[y_place(index, slab, nx)]
            top[slot, EDGE + slab, PAD + ny : PAD + ny + width] = y_high[y_place(index, slab, nx)]
    clear_pads(other, rows)

    coarse_x, coarse_y = nx // 2, ny // 2
    near = RIM - 1
    for slot in (FX, FY, ZL, ZH, W, D):
        mid[slot] = jnp.zeros(mid.shape[1:], F32)
    x, y, z = coarse_slab_sums(top.at[FX], top.at[FY], top.at[ZL], coarse_x + 2, EDGE - 2, wide)
    mid[FX, near : near + coarse_x + 3, RIM : 3 * RIM + coarse_y] = halved(x)
    mid[FY, near : near + coarse_x + 2, RIM : 3 * RIM + coarse_y] = halved(y)
    mid[ZL, near : near + coarse_x + 2, RIM : 3 * RIM + coarse_y] = halved(z, True)

    row_inside = (rows_of((rows, LANES)) >= RIM) | (me_y > 0)
    main = pl.ds(RIM, rows)
    start_v = top.at[V]

    def first(index):
        slab = index + 1
        inside = row_inside & ((slab >= EDGE) | (me_x > 0))
        set_weights(top, slab, RIM, rows, LANES, inside)
        other[slab, main] = swept(top, start_v, slab, RIM, rows)

    run(slabs - 2, first)

    def second(index):
        slab = index + 2
        top[V, slab, main] = swept(top, other, slab, RIM, rows)

    run(slabs - 4, second)

    def rest(slab):
        v, total = weighted(top, top.at[V], slab, PAD, ny)
        return total - top[D, slab, inner] * v

    def residual(index):
        slab = EDGE + 2 * index
        tmp[index] = rest(slab) + rest(slab + 1)

    run(nx // 2, residual)

    slabs, rows = coarse_x + 2 * RIM, coarse_y + 2 * RIM
    half = slabs // 2
    inner = pl.ds(2 * RIM, coarse_y)
    main = pl.ds(RIM, rows)
    row_inside = (rows_of((rows, LANES)) >= RIM) | (me_y > 0)
    for slab in range(near, near + coarse_x + 2):
        inside = row_inside & (me_x > 0) if slab < RIM else row_inside
        set_weights(mid, slab, RIM, rows, HALF, inside)

    source = even_rows(tmp, ny) + odd_rows(tmp, ny)
    source = 0.5 * exact_dot(source.reshape(coarse_x * coarse_y, LANES), compact(LANES, 0))
    for ref in (mid.at[F], mid.at[V], one):
        ref[...] = jnp.zeros(ref.shape, F32)
    mid[F, RIM : RIM + coarse_x, inner] = source.reshape(coarse_x, coarse_y, LANES)
    for slab in range(RIM, RIM + coarse_x):
        mid[V, slab, inner] = mid[W, slab, inner] * mid[F, slab, inner]
    for layer in range(RIM // 2):
        near, far = RIM + layer, coarse_x + layer
        v_low[layer * coarse_y : (layer + 1) * coarse_y] = two_in_one(
            mid[V, near, inner], mid[V, near + RIM // 2, inner]
        )
        v_high[layer * coarse_y : (layer + 1) * coarse_y] = two_in_one(
            mid[V, far, inner], mid[V, far + RIM // 2, inner]
        )
    kept[0] = mid[F, RIM : RIM + coarse_x, inner]
    kept[1] = mid[V, RIM : RIM + coarse_x, inner]
    base, after, _ = rim_rows_x(nx, ny)
    pairs = RIM // 2
    for face in range(3):
        for layer in range(pairs):
            place = pl.ds(base + after + (face * pairs + layer) * coarse_y, coarse_y)
            far = coarse_x - RIM + layer
            v_low[place] = two_in_one(faces[face, layer], faces[face, layer + pairs])
            v_high[place] = two_in_one(faces[face, far], faces[face, far + pairs])
    for layer in range(2):
        place = pl.ds(base + layer * ny, ny)
        v_low[place] = top[V, EDGE + layer, pl.ds(PAD, ny)]
        v_high[place] = top[V, EDGE + nx - 2 + layer, pl.ds(PAD, ny)]
    for slab in range(RIM - 1, RIM + coarse_x + 1):
        one[slab, main] = swept(mid, mid.at[V], slab, RIM, rows)

    def rest_1(slab):
        v, total = weighted(mid, one, slab, RIM, rows)
        return total - mid[D, slab, main] * v

    two[...] = jnp.zeros(two.shape, F32)
    for pair in range(1, half - 1):
        two[pair] = rest_1(2 * pair) + rest_1(2 * pair + 1)
    pieces = even_rows(two, rows) + odd_rows(two, rows)
    coarse_rows, quarter_rows = rows // 2, rows // 4
    chunk[:coarse_rows] = 0.5 * fold_four([pieces[1 + i] for i in range(4)])
    rest_of = [pieces[5 + i // 2][i % 2 * quarter_rows :][:quarter_rows] for i in range(4)]
    chunk[coarse_rows : coarse_rows + quarter_rows] = 0.5 * fold_four(rest_of)
    chunk[coarse_rows + quarter_rows :] = coefficients[:BLOCK_ROWS - coarse_rows - quarter_rows]


def pack_v(top, kept, faces, x_low, x_high, low, high):
    coarse_x, coarse_y = faces.shape[1:3]
    nx, ny = 2 * coarse_x, 2 * coarse_y
    slabs = coarse_x + 2 * RIM
    half = slabs // 2
    sizes_x, sizes_y = rim_rows_x(nx, ny), rim_rows_y(nx, ny)

    def folded(own, place_x, place_y):
        values = [
            wide_slab(
                slab,
                lambda layer: rim_slab(x_low, place_x, coarse_y, layer),
                own,
                lambda layer: rim_slab(x_high, place_x, coarse_y, layer),
            )
            for slab in range(slabs)
        ]
        for slab in range(half):
            both = two_in_one(values[slab], values[slab + half])
            rows = pl.ds(place_y + slab * RIM, RIM)
            low[rows] = both[:RIM]
            high[rows] = both[coarse_y - RIM :]

    folded(kept.at[1], 0, 0)
    for face in range(3):
        folded(
            faces.at[face],
            sizes_x[0] + sizes_x[1] + face * sizes_x[0],
            sizes_y[0] + sizes_y[1] + face * sizes_y[0],
        )
    base_x, base_y = sizes_x[0], sizes_y[0]
    for out, start in ((low, 0), (high, ny - 2)):
        for layer in range(2):
            rows = pl.ds(base_x + layer * ny + start, 2)
            out[pl.ds(base_y + 2 * layer, 2)] = x_low[rows]
            out[pl.ds(base_y + 2 * (2 + nx + layer), 2)] = x_high[rows]
        for slab in range(nx):
            out[pl.ds(base_y + 2 * (2 + slab), 2)] = top[V, EDGE + slab, pl.ds(PAD + start, 2)]


def stack_blocks(*refs):
    for index, ref in enumerate(refs[:-3]):
        refs[-1][index] = ref[...]


def join_blocks(*refs):
    start = 0
    for ref in refs[:-2]:
        refs[-1][start : start + ref.shape[0]] = ref[...]
        start += ref.shape[0]


def pair_rows(values, stride):
    return values + roll_rows(values, -stride)


def pair_lanes(values, stride):
    return values + roll_lanes(values, -stride)


class Listed:
    def __init__(self, fx, fy, fz, stride, depth):
        self.fx, self.fy, self.fz, self.stride, self.depth = fx, fy, fz, stride, depth
        shape = fx[0].shape
        rows = shape[0]
        row, lane = rows_of(shape), lanes_of(shape)
        z = lane % depth
        count = self.count = len(fx)
        self.x_high = [
            fx[s + 1] if s + 1 < count else jnp.where(lane < LANES - depth, roll_lanes(fx[0], -depth), 0.0)
            for s in range(count)
        ]
        self.x_low = [fx[s] if s > 0 else jnp.where(lane >= depth, fx[0], 0.0) for s in range(count)]
        self.y_high = [jnp.where(row < rows - stride, roll_rows(f, -stride), 0.0) for f in fy]
        self.y_low = [jnp.where(row >= stride, f, 0.0) for f in fy]
        self.z_high = [jnp.where(z < depth - stride, roll_lanes(f, -stride), 0.0) for f in fz]
        self.z_low = [jnp.where(z >= stride, f, 0.0) for f in fz]
        self.d = [
            fx[s] + self.x_high[s] + fy[s] + self.y_high[s] + fz[s] + self.z_high[s] for s in range(count)
        ]
        self.w = [jnp.where(d > 0.0, OMEGA / jnp.where(d > 0.0, d, 1.0), 0.0) for d in self.d]

    def weighted(self, v, f):
        count = self.count
        out = []
        for s in range(count):
            low = v[s - 1] if s > 0 else roll_lanes(v[count - 1], self.depth)
            high = v[s + 1] if s + 1 < count else roll_lanes(v[0], -self.depth)
            x = self.x_low[s] * low + self.x_high[s] * high
            y = self.y_low[s] * roll_rows(v[s], self.stride) + self.y_high[s] * roll_rows(v[s], -self.stride)
            z = self.z_low[s] * roll_lanes(v[s], self.stride) + self.z_high[s] * roll_lanes(v[s], -self.stride)
            total = (f[s] + y) + (x + z)
            out.append(total)
        return out

    def sweep(self, v, f):
        totals = self.weighted(v, f)
        return [(1.0 - OMEGA) * v[s] + self.w[s] * totals[s] for s in range(self.count)]

    def sweeps(self, count, f):
        folded = [
            [w * c for w, c in zip(self.w, coefficients)]
            for coefficients in (self.x_low, self.x_high, self.y_low, self.y_high, self.z_low, self.z_high)
        ]
        scaled = self.start(f)
        slabs = self.count

        def step(v):
            out = []
            for s in range(slabs):
                low = v[s - 1] if s > 0 else roll_lanes(v[slabs - 1], self.depth)
                high = v[s + 1] if s + 1 < slabs else roll_lanes(v[0], -self.depth)
                x = folded[0][s] * low + folded[1][s] * high
                y = folded[2][s] * roll_rows(v[s], self.stride) + folded[3][s] * roll_rows(v[s], -self.stride)
                z = folded[4][s] * roll_lanes(v[s], self.stride) + folded[5][s] * roll_lanes(v[s], -self.stride)
                out.append((((1.0 - OMEGA) * v[s] + scaled[s]) + y) + (x + z))
            return out

        v = scaled
        for _ in range(count - 1):
            v = step(v)
        return v

    def start(self, f):
        return [self.w[s] * f[s] for s in range(self.count)]

    def residual(self, v, f):
        totals = self.weighted(v, f)
        return [totals[s] - self.d[s] * v[s] for s in range(self.count)]

    def kept(self):
        shape = self.fx[0].shape
        step = 2 * self.stride
        return (rows_of(shape) % step == 0) & (lanes_of(shape) % step == 0)

    def coarser(self):
        keep, stride = self.kept(), self.stride
        half = range(self.count // 2)

        def kept(values):
            return jnp.where(keep, 0.25 * values, 0.0)

        fx = [kept(pair_lanes(pair_rows(self.fx[2 * s], stride), stride)) for s in half]
        fy = [kept(pair_lanes(self.fy[2 * s] + self.fy[2 * s + 1], stride)) for s in half]
        fz = [kept(pair_rows(self.fz[2 * s] + self.fz[2 * s + 1], stride)) for s in half]
        return Listed(fx, fy, fz, 2 * stride, self.depth)

    def restrict(self, r):
        keep, stride = self.kept(), self.stride
        return [
            jnp.where(keep, 0.5 * pair_lanes(pair_rows(r[2 * s] + r[2 * s + 1], stride), stride), 0.0)
            for s in range(self.count // 2)
        ]

    def prolong(self, e):
        out = []
        for values in e:
            values = values + roll_rows(values, self.stride)
            values = values + roll_lanes(values, self.stride)
            out += [values, values]
        return out


def listed_cycle(levels, sweeps, f):
    level = levels[0]
    if len(levels) == 1:
        return level.sweeps(sweeps, f)
    v = level.sweep(level.start(f), f)
    e = listed_cycle(levels[1:], sweeps, level.restrict(level.residual(v, f)))
    v = [a + b for a, b in zip(v, level.prolong(e))]
    return level.sweep(level.sweep(v, f), f)


def level_two(axes, grid, sweeps, shape, pieces, out, wide, tall):
    devices_x, devices_y = grid
    me_x, me_y = lax.axis_index(axes[0]), lax.axis_index(axes[1])
    own_x, own_y = shape
    quarter = LANES // 4
    reach = RIM // 2
    blocks = 4
    count = devices_x * own_x // blocks
    rows = devices_y * own_y
    main = pl.ds(PAD, rows)
    window = own_y + RIM

    def piece(gx, gy):
        slow, far = (me_x // 2) ^ (gx // 2), (me_y // 2) ^ (gy // 2)
        return ((me_y + gy) % 2, (me_x + gx) % 2 * (devices_y // 2) + far, slow)

    for ref in (wide, tall):
        ref[...] = jnp.zeros(ref.shape, F32)
    lane = lanes_of((window, LANES))
    for gy in range(devices_y):
        sums = [None] * count
        for gx in range(devices_x):
            where = piece(gx, gy)
            first = pieces[where + (pl.ds(0, window),)]
            second = pieces[where + (pl.ds(window, window // 2),)]
            for local in range(1, 2 * blocks - 1):
                x = own_x * gx - reach + local
                if not 0 <= x < devices_x * own_x:
                    continue
                block, slab = x // count, x % count
                if local <= blocks:
                    moved = roll_lanes(first, (block - local + 1) * quarter)
                else:
                    at = 2 * (local - blocks - 1)
                    halves = [roll_lanes(second, (block - at - odd) * quarter) for odd in range(2)]
                    moved = jnp.concatenate(halves)
                moved = jnp.where(lane // quarter == block, moved, 0.0)
                sums[slab] = moved if sums[slab] is None else sums[slab] + moved
        place = pl.ds(PAD + own_y * gy - reach, window)
        for slab in range(count):
            tall[slab, place] = tall[slab, place] + sums[slab]
    f = [tall[slab, main] for slab in range(count)]

    lane = lanes_of((rows, LANES))
    for gx in range(devices_x):
        for gy in range(devices_y):
            where = piece(gx, gy)
            for face in range(3):
                values = pieces[where + (pl.ds(window + window // 2 + face * own_y, own_y),)]
                wide[face, gx, gy * own_y : (gy + 1) * own_y] = values
    faces = []
    for face in range(3):
        slabs = [None] * count
        for gx in range(devices_x):
            values = wide[face, gx]
            for local in range(own_x):
                x = own_x * gx + local
                block, slab = x // count, x % count
                moved = roll_lanes(values, (block - local) * quarter)
                moved = jnp.where(lane // quarter == block, moved, 0.0)
                slabs[slab] = moved if slabs[slab] is None else slabs[slab] + moved
        faces.append(slabs)
    levels = [Listed(*faces, 1, quarter)]
    while len(levels) < LEVELS - 2:
        levels.append(levels[-1].coarser())
    e = listed_cycle(levels, sweeps, f)

    for slab in range(count):
        out[reach + slab, main] = e[slab]
    for slab in range(reach):
        out[slab, main] = jnp.where(lane < quarter, 0.0, roll_lanes(e[count - reach + slab], quarter))
        out[reach + count + slab, main] = jnp.where(
            lane >= LANES - quarter, 0.0, roll_lanes(e[slab], -quarter)
        )
    out[:, :PAD] = jnp.zeros((count + 2 * reach, PAD, LANES), F32)
    out[:, PAD + rows :] = jnp.zeros((count + 2 * reach, PAD, LANES), F32)


def level_up(axes, grid, coarse, top, kept, faces, x_low, x_high, y_low, y_high, *refs):
    out, mid, one, two, right, post, up = refs
    devices_x, devices_y = grid
    me_x, me_y = lax.axis_index(axes[0]), lax.axis_index(axes[1])
    coarse_x, coarse_y = faces.shape[1:3]
    nx, ny = out.shape[:2]
    own_x, own_y = coarse_x // 2, coarse_y // 2
    quarter = LANES // 4
    reach = RIM // 2
    window = own_y + RIM

    slabs, high = coarse_x + 2 * RIM, coarse_y + 2 * RIM
    half = slabs // 2
    inner = pl.ds(2 * RIM, coarse_y)
    body = pl.ds(RIM, high)
    sizes_x, sizes_y = rim_rows_x(nx, ny), rim_rows_y(nx, ny)
    for face, slot in enumerate((FX, FY, ZL)):
        clear_pads(mid.at[slot], high)
        mid[slot, RIM : RIM + coarse_x, inner] = faces[face]
        place_x = sizes_x[0] + sizes_x[1] + face * sizes_x[0]
        place_y = sizes_y[0] + sizes_y[1] + face * sizes_y[0]
        for layer in range(RIM):
            mid[slot, layer, inner] = rim_slab(x_low, place_x, coarse_y, layer)
            mid[slot, RIM + coarse_x + layer, inner] = rim_slab(x_high, place_x, coarse_y, layer)
        for slab in range(half):
            place = pl.ds(place_y + slab * RIM, RIM)
            for message, row in ((y_low, RIM), (y_high, 2 * RIM + coarse_y)):
                pair = one_of_two(message[place])
                mid[slot, slab, row : row + RIM] = pair[0]
                mid[slot, slab + half, row : row + RIM] = pair[1]
    row_inside = (rows_of((high, LANES)) >= RIM) | (me_y > 0)
    for slab in range(slabs - 1):
        inside = row_inside & (me_x > 0) if slab < RIM else row_inside
        set_weights(mid, slab, RIM, high, HALF, inside)
    clear_pads(one, high)
    clear_pads(right, high)
    clear_pads(two, high)
    one[RIM : RIM + coarse_x, inner] = kept[1]
    right[RIM : RIM + coarse_x, inner] = kept[0]
    for layer in range(RIM):
        one[layer, inner] = rim_slab(x_low, 0, coarse_y, layer)
        one[RIM + coarse_x + layer, inner] = rim_slab(x_high, 0, coarse_y, layer)
    for slab in range(half):
        place = pl.ds(slab * RIM, RIM)
        for message, row in ((y_low, RIM), (y_high, 2 * RIM + coarse_y)):
            pair = one_of_two(message[place])
            one[slab, row : row + RIM] = pair[0]
            one[slab + half, row : row + RIM] = pair[1]
    row = rows_of((high, LANES))
    own_row = (row >= RIM) & (row < RIM + coarse_y)
    for slab in range(1, slabs - 1):
        f_rim = one[slab, body] * mid[D, slab, body] * (1.0 / OMEGA)
        if RIM <= slab < RIM + coarse_x:
            f_rim = jnp.where(own_row, right[slab, body], f_rim)
        right[slab, body] = f_rim
        two[slab, body] = swept(mid, one, slab, RIM, high, right)

    per_block = (coarse.shape[0] - 2 * reach) // own_x
    base = me_x % per_block * own_x
    mine = None
    for gy in range(devices_y):
        place = pl.ds(PAD + gy * own_y - reach, window)
        values = jnp.where(me_y == gy, coarse[pl.ds(base, half), place, :], 0.0)
        mine = values if mine is None else mine + values
    source = lax.broadcasted_iota(jnp.int32, (LANES, LANES), 0)
    target = lax.broadcasted_iota(jnp.int32, (LANES, LANES), 1)
    hit = (source == me_x // per_block * quarter + target // 2) & (target < HALF)
    fine = exact_dot(mine.reshape(half * window, LANES), jnp.where(hit, 1.0, 0.0).astype(F32))
    fine = fine.reshape(half, window, LANES)
    for odd in range(2):
        up[:half, pl.ds(odd, window, stride=2), :] = fine
    for pair in range(half):
        for slab in (2 * pair, 2 * pair + 1):
            if 1 <= slab < slabs - 1:
                two[slab, body] = two[slab, body] + up[pair, :high]
    for slab in range(2, slabs - 2):
        one[slab, body] = swept(mid, two, slab, RIM, high, right)
    for slab in range(3, slabs - 3):
        two[slab, body] = swept(mid, one, slab, RIM, high, right)

    steps = coarse_x + 2
    fine_rows = ny + 2 * RIM
    e = two[RIM - 1 : RIM - 1 + steps, body]
    fine = exact_dot(e.reshape(steps * high, LANES), expand(LANES, 0)).reshape(steps, high, LANES)
    fine = fine[:, reach : reach + fine_rows // 2]
    for odd in range(2):
        up[:, pl.ds(odd, fine_rows // 2, stride=2), :] = fine
    body = pl.ds(RIM, fine_rows)
    for slot in (0, 1):
        clear_pads(post.at[slot], fine_rows)
    inner = pl.ds(PAD, ny)
    post[0, EDGE : EDGE + nx, inner] = top[V, EDGE : EDGE + nx, inner]
    base_x, base_y = RIM // 2 * coarse_y, half * RIM
    for layer in range(2):
        place = pl.ds(base_x + layer * ny, ny)
        post[0, EDGE - 2 + layer, inner] = x_low[place]
        post[0, EDGE + nx + layer, inner] = x_high[place]
    for slab in range(nx + 4):
        place = pl.ds(base_y + 2 * slab, 2)
        post[0, slab + EDGE - 2, RIM:PAD] = jnp.zeros((RIM, LANES), F32)
        post[0, slab + EDGE - 2, PAD + ny : PAD + ny + RIM] = jnp.zeros((RIM, LANES), F32)
        post[0, slab + EDGE - 2, PAD - 2 : PAD] = y_low[place]
        post[0, slab + EDGE - 2, PAD + ny : PAD + ny + 2] = y_high[place]

    def raise_level(index):
        for slab in (EDGE - 2 + 2 * index, EDGE - 1 + 2 * index):
            post[0, slab, body] = post[0, slab, body] + up[index]

    run(steps, raise_level)

    def fifth(index):
        slab = EDGE - 1 + index
        post[1, slab, body] = swept(top, post.at[0], slab, RIM, fine_rows)

    run(nx + 2, fifth)

    def sixth(index):
        out[index] = swept(top, post.at[1], EDGE + index, PAD, ny)

    run(nx, sixth)


IN_VMEM = pl.BlockSpec(memory_space=pltpu.VMEM)


def call(kernel, outs, scratch=(), from_hbm=False):
    ins = pl.BlockSpec(memory_space=pl.ANY) if from_hbm else IN_VMEM

    def launch(*args):
        if from_hbm:
            args = [pltpu.with_memory_space_constraint(arg, pltpu.HBM) for arg in args]
        return pl.pallas_call(
            kernel,
            out_shape=[pltpu.VMEM(shape, F32) for shape in outs],
            in_specs=[ins] * len(args),
            out_specs=[IN_VMEM] * len(outs),
            scratch_shapes=[pltpu.VMEM(s, F32) if isinstance(s, tuple) else s for s in scratch],
            compiler_params=pltpu.CompilerParams(vmem_limit_bytes=24 * 2**20),
        )(*args)

    return launch


def pair_route(axis):
    return [(i, i ^ 1) for i in range(lax.axis_size(axis))]


def swap_route(axis):
    count = lax.axis_size(axis)
    return [(i, (i + 1 ^ 1) - 1) for i in range(1, count - 1)]


def by_partner(low, high, axis):
    odd = lax.axis_index(axis) % 2 == 1
    return jnp.where(odd, low, high), jnp.where(odd, high, low)


def from_sides(low, high, axis):
    pair, swap = by_partner(low, high, axis)
    pair = lax.ppermute(pair, axis, pair_route(axis))
    swap = lax.ppermute(swap, axis, swap_route(axis))
    return by_partner(pair, swap, axis)


def passed_round(block, axis, stride):
    count = lax.axis_size(axis)
    return [block] + [
        lax.ppermute(block, axis, [(i, i ^ distance) for i in range(count)])
        for distance in range(stride, count, stride)
    ]


def passed_across(block):
    count, size = lax.axis_size("gx"), lax.axis_size("gy")
    blocks = []
    for side in range(2):
        for distance in range(0, size, 2):
            route = [
                (x * size + y, (x ^ side) * size + (y ^ distance)) for x in range(count) for y in range(size)
            ]
            moved = side + distance > 0
            blocks.append(lax.ppermute(block, ("gx", "gy"), route) if moved else block)
    return blocks


def fused_cycle(*fields):
    axes = ("gx", "gy")
    devices_x, devices_y = lax.axis_size("gx"), lax.axis_size("gy")
    nx, ny, nz = fields[0].shape
    coarse_x, coarse_y = nx // 2, ny // 2
    x_shape, y_shape = (x_rows(nx, ny), LANES), (y_rows(nx, ny), LANES)
    own, x_low, x_high = call(
        start_pack, [(5, nx, ny, nz), x_shape, x_shape], [pltpu.SemaphoreType.DMA((5,))], True
    )(*fields)
    x_low, x_high = from_sides(x_low, x_high, "gx")
    faces, coefficients = call(
        coarse_faces,
        [(3, coarse_x, coarse_y, LANES), (16, LANES)],
        [(coarse_x, ny, LANES), (coarse_x // 2, coarse_y, LANES)],
    )(own)
    y_low, y_high = call(pack_y, [y_shape] * 2)(own, x_low, x_high)
    y_low, y_high = from_sides(y_low, y_high, "gy")
    stack = (nx + 2 * EDGE, ny + 4 * RIM, LANES)
    stack_1 = (coarse_x + 2 * RIM, coarse_y + 4 * RIM, LANES)
    half = stack_1[0] // 2
    v_shape = (sum(rim_rows_x(nx, ny)), LANES)
    w_shape = (sum(rim_rows_y(nx, ny)), LANES)
    top, kept, chunk, v_low, v_high = call(
        functools.partial(level_down, axes),
        [(D + 1,) + stack, (2, coarse_x, coarse_y, LANES), (BLOCK_ROWS, LANES), v_shape, v_shape],
        [
            stack,
            (nx // 2, ny, LANES),
            stack_1,
            (half, coarse_y + 2 * RIM, LANES),
            (D + 1,) + stack_1,
            (coarse_x + 3,) + stack[1:],
        ],
    )(own, faces, coefficients, x_low, x_high, y_low, y_high)

    blocks = passed_round(chunk, "gx", 2)
    v_low, v_high = from_sides(v_low, v_high, "gx")
    slow = (len(blocks),) + chunk.shape
    (pieces,) = call(stack_blocks, [slow])(*blocks, v_low, v_high)
    blocks = passed_across(pieces.reshape(-1, LANES))
    w_low, w_high = call(pack_v, [w_shape] * 2)(top, kept, faces, v_low, v_high)
    pair, swap = by_partner(w_low, w_high, "gy")
    swap = lax.ppermute(swap, "gy", swap_route("gy"))
    rows = sum(block.shape[0] for block in blocks) + w_shape[0]
    (message,) = call(join_blocks, [(rows, LANES)])(*blocks, pair, swap)
    other = lax.ppermute(message, "gy", pair_route("gy"))
    rows = message.shape[0] - w_shape[0]
    pieces = jnp.stack((message[:rows], other[:rows])).reshape((2, len(blocks)) + slow)
    w_low, w_high = by_partner(other[rows:], swap, "gy")
    count = devices_x * nx // 16
    rows = devices_y * ny // 4
    grid = (devices_x, devices_y)
    coarsest = (devices_x * nx >> LEVELS - 1, devices_y * ny >> LEVELS - 1)
    wide = (count + RIM, rows + 2 * PAD, LANES)
    (coarse,) = call(
        functools.partial(level_two, axes, grid, 4 * max(coarsest), (nx // 4, ny // 4)),
        [wide],
        [(3, devices_x, rows, LANES), wide],
    )(pieces)
    return pl.pallas_call(
        functools.partial(level_up, axes, grid),
        out_shape=jax.ShapeDtypeStruct((nx, ny, nz), F32),
        in_specs=[IN_VMEM] * 8,
        out_specs=IN_VMEM,
        scratch_shapes=[
            pltpu.VMEM(shape, F32)
            for shape in ((D + 1,) + stack_1, stack_1, stack_1, stack_1, (2,) + stack, (coarse_x + 2, ny + 2 * RIM, LANES))
        ],
        compiler_params=pltpu.CompilerParams(vmem_limit_bytes=24 * 2**20),
    )(coarse, top, kept, faces, v_low, v_high, w_low, w_high)


def with_halo(block, sides, width):
    for axis, dim in sides:
        count = lax.axis_size(axis)
        forward = [(i, i + 1) for i in range(count - 1)]
        backward = [(target, source) for source, target in forward]
        low = lax.ppermute(
            lax.slice_in_dim(block, block.shape[dim] - width, None, axis=dim), axis, forward
        )
        high = lax.ppermute(lax.slice_in_dim(block, 0, width, axis=dim), axis, backward)
        block = jnp.concatenate([low, block, high], axis=dim)
    return block


def passed_along(block, axis, distance):
    devices = range(lax.axis_size(axis))
    route = [(i - distance, i) for i in devices if i - distance in devices]
    return lax.ppermute(block, axis, route)


def stencil(padded, padded_x, padded_y, face_z):
    center = padded[1:-1, 1:-1]
    zero_plane = jnp.zeros(center.shape[:2] + (1,), center.dtype)
    above_face = jnp.concatenate((face_z[:, :, 1:], zero_plane), axis=2)
    below_z = jnp.concatenate((zero_plane, center[:, :, :-1]), axis=2)
    above_z = jnp.concatenate((center[:, :, 1:], zero_plane), axis=2)
    lower_x = padded_x[1:-1, 1:-1]
    upper_x = padded_x[2:, 1:-1]
    lower_y = padded_y[1:-1, 1:-1]
    upper_y = padded_y[1:-1, 2:]
    applied = lower_x * (center - padded[:-2, 1:-1]) + upper_x * (center - padded[2:, 1:-1])
    applied = (
        applied + lower_y * (center - padded[1:-1, :-2]) + upper_y * (center - padded[1:-1, 2:])
    )
    applied = applied + face_z * (center - below_z) + above_face * (center - above_z)
    diagonal = lower_x + upper_x + lower_y + upper_y + face_z + above_face
    return (applied, diagonal)


def jacobi_sweep(padded, source, padded_x, padded_y, face_z):
    applied, diagonal = stencil(padded, padded_x, padded_y, face_z)
    return padded[1:-1, 1:-1] + OMEGA * (source - applied) / diagonal


def pad_plane(values, width):
    return jnp.pad(values, ((width, width), (width, width), (0, 0)))


def restrict(residual):
    shape = residual.shape
    blocks = residual.reshape(shape[0] // 2, 2, shape[1] // 2, 2, shape[2] // 2, 2)
    return 4.0 * jnp.mean(blocks, axis=(1, 3, 5))


def coarsen_faces(face_x, face_y, face_z):
    shape = face_x.shape
    blocks = (shape[0] // 2, 2, shape[1] // 2, 2, shape[2] // 2, 2)
    coarse_x = jnp.mean(face_x.reshape(blocks)[:, 0], axis=(2, 4))
    coarse_y = jnp.mean(face_y.reshape(blocks)[:, :, :, 0], axis=(1, 4))
    coarse_z = jnp.mean(face_z.reshape(blocks)[..., 0], axis=(1, 3))
    return (coarse_x, coarse_y, coarse_z)


def prolong(coarse):
    return jnp.repeat(jnp.repeat(jnp.repeat(coarse, 2, axis=0), 2, axis=1), 2, axis=2)


def local_cycle(grid_level, iterate, source, face_x, face_y, face_z):
    padded_x = pad_plane(face_x, 1)
    padded_y = pad_plane(face_y, 1)
    if grid_level == LEVELS - 1:
        count = 4 * max(iterate.shape[0], iterate.shape[1])

        def one_sweep(index, values):
            return jacobi_sweep(pad_plane(values, 1), source, padded_x, padded_y, face_z)

        return lax.fori_loop(0, count, one_sweep, iterate)
    for sweep_index in range(2):
        iterate = jacobi_sweep(pad_plane(iterate, 1), source, padded_x, padded_y, face_z)
    applied, diagonal = stencil(pad_plane(iterate, 1), padded_x, padded_y, face_z)
    coarse_src = restrict(source - applied)
    coarse_x, coarse_y, coarse_z = coarsen_faces(face_x, face_y, face_z)
    correction = local_cycle(
        grid_level + 1, jnp.zeros_like(coarse_src), coarse_src, coarse_x, coarse_y, coarse_z
    )
    iterate = iterate + prolong(correction)
    for sweep_index in range(2):
        iterate = jacobi_sweep(pad_plane(iterate, 1), source, padded_x, padded_y, face_z)
    return iterate


def field_rim(iterate):
    return with_halo(iterate, (("gx", 0), ("gy", 1)), 1)


def sweep_pair_narrow(iterate, source, padded_x, padded_y, face_z, zero_start):
    for sweep_index in range(2):
        if sweep_index == 0 and zero_start:
            padded = pad_plane(iterate, 1)
        else:
            padded = field_rim(iterate)
        iterate = jacobi_sweep(padded, source, padded_x, padded_y, face_z)
    return iterate


def descend(grid_level, iterate, source, face_x, face_y, face_z, zero_start, gather_level):
    if grid_level == gather_level:
        pieces = (
            lax.all_gather(source, "gy", axis=1, tiled=True),
            lax.all_gather(face_x, "gy", axis=1, tiled=True),
            lax.all_gather(face_y, "gy", axis=1, tiled=True),
            lax.all_gather(face_z, "gy", axis=1, tiled=True),
        )
        gathered = (
            lax.all_gather(pieces[0], "gx", axis=0, tiled=True),
            lax.all_gather(pieces[1], "gx", axis=0, tiled=True),
            lax.all_gather(pieces[2], "gx", axis=0, tiled=True),
            lax.all_gather(pieces[3], "gx", axis=0, tiled=True),
        )
        correction = local_cycle(
            grid_level,
            jnp.zeros_like(gathered[0]),
            gathered[0],
            gathered[1],
            gathered[2],
            gathered[3],
        )
        start_x = lax.axis_index("gx") * source.shape[0]
        start_y = lax.axis_index("gy") * source.shape[1]
        return lax.dynamic_slice(
            correction, (start_x, start_y, jnp.zeros((), jnp.int32)), source.shape
        )
    next_x = passed_along(face_x[:1], "gx", -1)
    next_y = passed_along(face_y[:, :1], "gy", -1)
    lower_row = jnp.zeros_like(next_x)
    lower_col = jnp.zeros_like(next_y)
    padded_x = jnp.pad(
        jnp.concatenate((lower_row, face_x, next_x), axis=0), ((0, 0), (1, 1), (0, 0))
    )
    padded_y = jnp.pad(
        jnp.concatenate((lower_col, face_y, next_y), axis=1), ((1, 1), (0, 0), (0, 0))
    )

    def smoother(values, starting):
        return sweep_pair_narrow(values, source, padded_x, padded_y, face_z, starting)

    iterate = smoother(iterate, zero_start)
    applied, diagonal = stencil(field_rim(iterate), padded_x, padded_y, face_z)
    coarse_src = restrict(source - applied)
    coarse_x, coarse_y, coarse_z = coarsen_faces(face_x, face_y, face_z)
    correction = descend(
        grid_level + 1,
        jnp.zeros_like(coarse_src),
        coarse_src,
        coarse_x,
        coarse_y,
        coarse_z,
        True,
        gather_level,
    )
    iterate = iterate + prolong(correction)
    return smoother(iterate, False)


def fits(nx, ny, nz, devices_x, devices_y):
    cells = devices_x * nx * devices_y * ny * nz // 8
    even = devices_x % 8 == 0 and devices_y % 4 == 0
    even = even and devices_x & (devices_x - 1) == 0 and devices_y & (devices_y - 1) == 0
    return cells <= 2**18 and even and (nx, ny, nz) == (16, 16, LANES)


def local(source_term, initial_guess, face_x, face_y, face_z):
    if fits(*source_term.shape, lax.axis_size("gx"), lax.axis_size("gy")):
        return fused_cycle(source_term, initial_guess, face_x, face_y, face_z)
    gather_level = 4
    return descend(0, initial_guess, source_term, face_x, face_y, face_z, False, gather_level)


def solution(mesh):
    placed = (P("gx", "gy", None),) * 5
    return jax.shard_map(
        local, mesh=mesh, in_specs=placed, out_specs=P("gx", "gy", None), check_vma=False
    )
```

```python
import functools

import jax
import jax.numpy as jnp
from jax import lax
from jax.experimental import pallas as pl
from jax.experimental.pallas import tpu as pltpu
from jax.sharding import PartitionSpec as P

LEVELS = 6
OMEGA = 0.8
LANES = 128
RIM = 4
EDGE = 3
PAD = 8
BLOCK_ROWS = 24
F32 = jnp.float32

V, F, FX, FY, ZL, ZH, W, D = range(8)
SLOTS = (F, V, FX, FY, ZL)
X_LAYERS = (2, 3, 3, 2, 2)
Y_LAYERS = (2, 3, 2, 3, 2)
Y_REACH = (1, 2, 2, 2, 1)


def lanes_of(shape):
    return lax.broadcasted_iota(jnp.int32, shape, len(shape) - 1)


def rows_of(shape):
    return lax.broadcasted_iota(jnp.int32, shape, len(shape) - 2)


def roll_lanes(values, step):
    return pltpu.roll(values, step % LANES, values.ndim - 1)


def roll_rows(values, step):
    return pltpu.roll(values, step % values.shape[-2], values.ndim - 2)


def exact_dot(left, right):
    return jnp.dot(left, right, precision=lax.Precision.HIGHEST, preferred_element_type=F32)


def compact(depth, part, even_only=False):
    source = lax.broadcasted_iota(jnp.int32, (LANES, LANES), 0)
    target = lax.broadcasted_iota(jnp.int32, (LANES, LANES), 1)
    half = depth // 2
    hit = target == (source // depth * 2 + part) * half + source % depth // 2
    if even_only:
        hit = hit & (source % 2 == 0)
    return jnp.where(hit, 1.0, 0.0).astype(F32)


def expand(depth, part):
    target = lax.broadcasted_iota(jnp.int32, (LANES, LANES), 0)
    source = lax.broadcasted_iota(jnp.int32, (LANES, LANES), 1)
    half = depth // 2
    hit = target == (source // depth * 2 + part) * half + source % depth // 2
    return jnp.where(hit, 1.0, 0.0).astype(F32)


def merge_lanes(values, depth, even_only=False):
    count, rows, _ = values.shape
    half = count // 2
    flat = values.reshape(2, half * rows, LANES)
    out = exact_dot(flat[0], compact(depth, 0, even_only))
    out = out + exact_dot(flat[1], compact(depth, 1, even_only))
    return out.reshape(half, rows, LANES)


def even_rows(ref, rows):
    return ref[:, pl.ds(0, rows // 2, stride=2), :]


def odd_rows(ref, rows):
    return ref[:, pl.ds(1, rows // 2, stride=2), :]


HALF = LANES // 2


def low_half(values):
    return jnp.where(lanes_of(values.shape) < HALF, values, 0.0)


def two_in_one(first, second):
    return first + roll_lanes(second, HALF)


def one_of_two(values):
    return low_half(values), low_half(roll_lanes(values, HALF))


def x_rows(nx, ny):
    return sum(X_LAYERS) * ny


def y_rows(nx, ny):
    return sum(layers * (nx + 2 * reach) for layers, reach in zip(Y_LAYERS, Y_REACH))


def rim_rows_x(nx, ny):
    slab = RIM // 2 * (ny // 2)
    return slab, 2 * ny, 3 * slab


def rim_rows_y(nx, ny):
    slabs = (nx // 2 + 2 * RIM) // 2 * RIM
    return slabs, 2 * (nx + 4), 3 * slabs


def x_place(index, layer, ny):
    return pl.ds((sum(X_LAYERS[:index]) + layer) * ny, ny)


def y_place(index, slab, nx):
    before = zip(Y_LAYERS[:index], Y_REACH[:index])
    start = sum(layers * (nx + 2 * reach) for layers, reach in before)
    return pl.ds(start + (Y_REACH[index] + slab) * Y_LAYERS[index], Y_LAYERS[index])


def start_pack(*refs):
    fields, (own, x_low, x_high, done) = refs[:5], refs[5:]
    copies = [pltpu.make_async_copy(ref, own.at[index], done.at[index]) for index, ref in enumerate(fields)]
    for copy in copies:
        copy.start()
    nx, ny = own.shape[1:3]
    for index, copy in enumerate(copies):
        copy.wait()
        for layer in range(X_LAYERS[index]):
            x_low[x_place(index, layer, ny)] = own[index, layer]
            x_high[x_place(index, layer, ny)] = own[index, nx - X_LAYERS[index] + layer]


def pair_slabs(ref):
    count = ref.shape[0]
    values = ref[...].reshape((count // 2, 2) + ref.shape[1:])
    return values[:, 0], values[:, 1]


def wide_slab(slab, from_low, own, from_high):
    count = own.shape[0]
    if slab < RIM:
        return from_low(slab)
    if slab < RIM + count:
        return own[slab - RIM]
    return from_high(slab - RIM - count)


def rim_slab(ref, base, rows, layer):
    place = pl.ds(base + layer % (RIM // 2) * rows, rows)
    return one_of_two(ref[place])[layer // (RIM // 2)]


def pack_y(own, x_low, x_high, low, high):
    nx, ny = own.shape[1:3]
    for index in range(5):
        width, layers, reach = Y_LAYERS[index], X_LAYERS[index], Y_REACH[index]
        for out, start in ((low, 0), (high, ny - width)):
            for slab in range(nx):
                out[y_place(index, slab, nx)] = own[index, slab, start : start + width]
            for layer in range(reach):
                rows = pl.ds(x_place(index, layers - reach + layer, ny).start + start, width)
                out[y_place(index, layer - reach, nx)] = x_low[rows]
                rows = pl.ds(x_place(index, layer, ny).start + start, width)
                out[y_place(index, nx + layer, nx)] = x_high[rows]


def fold_four(slabs, even_only=False):
    out = None
    for part in range(2):
        term = exact_dot(two_in_one(slabs[part], slabs[2 + part]), compact(HALF, part, even_only))
        out = term if out is None else out + term
    return out


def coarse_slab_sums(ref_x, ref_y, ref_z, count, first, tmp):
    extra = tmp.shape[0]
    rows = tmp.shape[1]
    for index in range(extra):
        tmp[index] = ref_x[first + 2 * index]
    x = even_rows(tmp, rows) + odd_rows(tmp, rows)
    for index in range(count):
        tmp[index] = ref_y[first + 2 * index] + ref_y[first + 2 * index + 1]
    y = even_rows(tmp, rows)[:count]
    for index in range(count):
        tmp[index] = ref_z[first + 2 * index] + ref_z[first + 2 * index + 1]
    return x, y, (even_rows(tmp, rows) + odd_rows(tmp, rows))[:count]


def halved(values, even_only=False):
    count, rows, _ = values.shape
    flat = exact_dot(values.reshape(count * rows, LANES), compact(LANES, 0, even_only))
    return 0.25 * flat.reshape(count, rows, LANES)


def coarse_faces(own, faces, out, fine, tmp):
    x, y, z = coarse_slab_sums(own.at[2], own.at[3], own.at[4], own.shape[1] // 2, 0, fine)
    faces[0] = halved(x)
    faces[1] = halved(y)
    faces[2] = halved(z, True)
    rows = faces.shape[2]
    coarse = rows // 2
    fx, fy, fz = faces.at[0], faces.at[1], faces.at[2]
    tmp[...] = pair_slabs(fx)[0]
    x = even_rows(tmp, rows) + odd_rows(tmp, rows)
    first, second = pair_slabs(fy)
    tmp[...] = first + second
    y = even_rows(tmp, rows)
    first, second = pair_slabs(fz)
    tmp[...] = first + second
    z = even_rows(tmp, rows) + odd_rows(tmp, rows)
    out[...] = jnp.zeros(out.shape, F32)
    out[:coarse] = 0.25 * fold_four([x[i] for i in range(4)])
    out[coarse : 2 * coarse] = 0.25 * fold_four([y[i] for i in range(4)])
    out[2 * coarse : 3 * coarse] = 0.25 * fold_four([z[i] for i in range(4)], True)


def weighted(lev, src, slab, start, rows, f=None):
    here = pl.ds(start, rows)
    below = pl.ds(start - 1, rows)
    above = pl.ds(start + 1, rows)
    v = src[slab, here]
    f = lev.at[F] if f is None else f
    x = lev[FX, slab, here] * src[slab - 1, here] + lev[FX, slab + 1, here] * src[slab + 1, here]
    y = lev[FY, slab, here] * src[slab, below] + lev[FY, slab, above] * src[slab, above]
    z = lev[ZL, slab, here] * roll_lanes(v, 1) + lev[ZH, slab, here] * roll_lanes(v, -1)
    total = ((x + y) + f[slab, here]) + z
    return v, total


def swept(lev, src, slab, start, rows, f=None):
    v, total = weighted(lev, src, slab, start, rows, f)
    return (1.0 - OMEGA) * v + lev[W, slab, pl.ds(start, rows)] * total


def set_weights(lev, slab, start, rows, depth, inside=None):
    here = pl.ds(start, rows)
    fz = lev[ZL, slab, here]
    z = lanes_of(fz.shape) % depth
    upper = jnp.where(z == depth - 1, 0.0, roll_lanes(fz, -1))
    diagonal = lev[FX, slab, here] + lev[FX, slab + 1, here]
    diagonal = diagonal + lev[FY, slab, here] + lev[FY, slab, pl.ds(start + 1, rows)] + fz + upper
    valid = diagonal > 0.0
    if inside is not None:
        valid = valid & inside
    lev[ZL, slab, here] = jnp.where(z == 0, 0.0, fz)
    lev[ZH, slab, here] = upper
    lev[D, slab, here] = diagonal
    lev[W, slab, here] = jnp.where(valid, OMEGA / jnp.where(valid, diagonal, 1.0), 0.0)


def run(count, body):
    for index in range(count):
        body(index)


def clear_pads(ref, rows):
    for start in (0, RIM + rows):
        ref[:, start : start + RIM] = jnp.zeros((ref.shape[0], RIM, LANES), F32)


def level_down(axes, own, faces, coefficients, x_low, x_high, y_low, y_high, *refs):
    top, kept, chunk, v_low, v_high, other, tmp, one, two, mid, wide = refs
    nx, ny = own.shape[1:3]
    slabs, rows = nx + 2 * EDGE, ny + 2 * RIM
    me_x, me_y = lax.axis_index(axes[0]), lax.axis_index(axes[1])
    inner = pl.ds(PAD, ny)
    for index, slot in enumerate(SLOTS):
        layers, width = X_LAYERS[index], Y_LAYERS[index]
        top[slot, :, :PAD] = jnp.zeros((slabs, PAD, LANES), F32)
        top[slot, :, PAD + ny :] = jnp.zeros((slabs, PAD, LANES), F32)
        top[slot, EDGE : EDGE + nx, inner] = own[index]
        for layer in range(EDGE):
            if layer < layers:
                top[slot, EDGE - layers + layer, inner] = x_low[x_place(index, layer, ny)]
                top[slot, EDGE + nx + layer, inner] = x_high[x_place(index, layer, ny)]
            else:
                top[slot, EDGE - 1 - layer, inner] = jnp.zeros((ny, LANES), F32)
                top[slot, EDGE + nx + layer, inner] = jnp.zeros((ny, LANES), F32)
        for slab in range(-Y_REACH[index], nx + Y_REACH[index]):
            top[slot, EDGE + slab, PAD - width : PAD] = y_low[y_place(index, slab, nx)]
            top[slot, EDGE + slab, PAD + ny : PAD + ny + width] = y_high[y_place(index, slab, nx)]
    clear_pads(other, rows)

    coarse_x, coarse_y = nx // 2, ny // 2
    near = RIM - 1
    for slot in (FX, FY, ZL, ZH, W, D):
        mid[slot] = jnp.zeros(mid.shape[1:], F32)
    x, y, z = coarse_slab_sums(top.at[FX], top.at[FY], top.at[ZL], coarse_x + 2, EDGE - 2, wide)
    mid[FX, near : near + coarse_x + 3, RIM : 3 * RIM + coarse_y] = halved(x)
    mid[FY, near : near + coarse_x + 2, RIM : 3 * RIM + coarse_y] = halved(y)
    mid[ZL, near : near + coarse_x + 2, RIM : 3 * RIM + coarse_y] = halved(z, True)

    row_inside = (rows_of((rows, LANES)) >= RIM) | (me_y > 0)
    main = pl.ds(RIM, rows)
    start_v = top.at[V]

    def first(index):
        slab = index + 1
        inside = row_inside & ((slab >= EDGE) | (me_x > 0))
        set_weights(top, slab, RIM, rows, LANES, inside)
        other[slab, main] = swept(top, start_v, slab, RIM, rows)

    run(slabs - 2, first)

    def second(index):
        slab = index + 2
        top[V, slab, main] = swept(top, other, slab, RIM, rows)

    run(slabs - 4, second)

    def rest(slab):
        v, total = weighted(top, top.at[V], slab, PAD, ny)
        return total - top[D, slab, inner] * v

    def residual(index):
        slab = EDGE + 2 * index
        tmp[index] = rest(slab) + rest(slab + 1)

    run(nx // 2, residual)

    slabs, rows = coarse_x + 2 * RIM, coarse_y + 2 * RIM
    half = slabs // 2
    inner = pl.ds(2 * RIM, coarse_y)
    main = pl.ds(RIM, rows)
    row_inside = (rows_of((rows, LANES)) >= RIM) | (me_y > 0)
    for slab in range(near, near + coarse_x + 2):
        inside = row_inside & (me_x > 0) if slab < RIM else row_inside
        set_weights(mid, slab, RIM, rows, HALF, inside)

    source = even_rows(tmp, ny) + odd_rows(tmp, ny)
    source = 0.5 * exact_dot(source.reshape(coarse_x * coarse_y, LANES), compact(LANES, 0))
    for ref in (mid.at[F], mid.at[V], one):
        ref[...] = jnp.zeros(ref.shape, F32)
    mid[F, RIM : RIM + coarse_x, inner] = source.reshape(coarse_x, coarse_y, LANES)
    for slab in range(RIM, RIM + coarse_x):
        mid[V, slab, inner] = mid[W, slab, inner] * mid[F, slab, inner]
    for layer in range(RIM // 2):
        near, far = RIM + layer, coarse_x + layer
        v_low[layer * coarse_y : (layer + 1) * coarse_y] = two_in_one(
            mid[V, near, inner], mid[V, near + RIM // 2, inner]
        )
        v_high[layer * coarse_y : (layer + 1) * coarse_y] = two_in_one(
            mid[V, far, inner], mid[V, far + RIM // 2, inner]
        )
    kept[0] = mid[F, RIM : RIM + coarse_x, inner]
    kept[1] = mid[V, RIM : RIM + coarse_x, inner]
    base, after, _ = rim_rows_x(nx, ny)
    pairs = RIM // 2
    for face in range(3):
        for layer in range(pairs):
            place = pl.ds(base + after + (face * pairs + layer) * coarse_y, coarse_y)
            far = coarse_x - RIM + layer
            v_low[place] = two_in_one(faces[face, layer], faces[face, layer + pairs])
            v_high[place] = two_in_one(faces[face, far], faces[face, far + pairs])
    for layer in range(2):
        place = pl.ds(base + layer * ny, ny)
        v_low[place] = top[V, EDGE + layer, pl.ds(PAD, ny)]
        v_high[place] = top[V, EDGE + nx - 2 + layer, pl.ds(PAD, ny)]
    for slab in range(RIM - 1, RIM + coarse_x + 1):
        one[slab, main] = swept(mid, mid.at[V], slab, RIM, rows)

    def rest_1(slab):
        v, total = weighted(mid, one, slab, RIM, rows)
        return total - mid[D, slab, main] * v

    two[...] = jnp.zeros(two.shape, F32)
    for pair in range(1, half - 1):
        two[pair] = rest_1(2 * pair) + rest_1(2 * pair + 1)
    pieces = even_rows(two, rows) + odd_rows(two, rows)
    coarse_rows, quarter_rows = rows // 2, rows // 4
    chunk[:coarse_rows] = 0.5 * fold_four([pieces[1 + i] for i in range(4)])
    rest_of = [pieces[5 + i // 2][i % 2 * quarter_rows :][:quarter_rows] for i in range(4)]
    chunk[coarse_rows : coarse_rows + quarter_rows] = 0.5 * fold_four(rest_of)
    chunk[coarse_rows + quarter_rows :] = coefficients[:BLOCK_ROWS - coarse_rows - quarter_rows]


def pack_v(top, kept, faces, x_low, x_high, _, low, high):
    coarse_x, coarse_y = faces.shape[1:3]
    nx, ny = 2 * coarse_x, 2 * coarse_y
    slabs = coarse_x + 2 * RIM
    half = slabs // 2
    sizes_x, sizes_y = rim_rows_x(nx, ny), rim_rows_y(nx, ny)

    def folded(own, place_x, place_y):
        values = [
            wide_slab(
                slab,
                lambda layer: rim_slab(x_low, place_x, coarse_y, layer),
                own,
                lambda layer: rim_slab(x_high, place_x, coarse_y, layer),
            )
            for slab in range(slabs)
        ]
        for slab in range(half):
            both = two_in_one(values[slab], values[slab + half])
            rows = pl.ds(place_y + slab * RIM, RIM)
            low[rows] = both[:RIM]
            high[rows] = both[coarse_y - RIM :]

    folded(kept.at[1], 0, 0)
    for face in range(3):
        folded(
            faces.at[face],
            sizes_x[0] + sizes_x[1] + face * sizes_x[0],
            sizes_y[0] + sizes_y[1] + face * sizes_y[0],
        )
    base_x, base_y = sizes_x[0], sizes_y[0]
    for out, start in ((low, 0), (high, ny - 2)):
        for layer in range(2):
            rows = pl.ds(base_x + layer * ny + start, 2)
            out[pl.ds(base_y + 2 * layer, 2)] = x_low[rows]
            out[pl.ds(base_y + 2 * (2 + nx + layer), 2)] = x_high[rows]
        for slab in range(nx):
            out[pl.ds(base_y + 2 * (2 + slab), 2)] = top[V, EDGE + slab, pl.ds(PAD + start, 2)]


def stack_blocks(*refs):
    for index, ref in enumerate(refs[:-3]):
        refs[-1][index] = ref[...]


def join_blocks(*refs):
    start = 0
    for ref in refs[:-2]:
        refs[-1][start : start + ref.shape[0]] = ref[...]
        start += ref.shape[0]


def pair_rows(values, stride):
    return values + roll_rows(values, -stride)


def pair_lanes(values, stride):
    return values + roll_lanes(values, -stride)


class Listed:
    def __init__(self, fx, fy, fz, stride, depth):
        self.fx, self.fy, self.fz, self.stride, self.depth = fx, fy, fz, stride, depth
        shape = fx[0].shape
        rows = shape[0]
        row, lane = rows_of(shape), lanes_of(shape)
        z = lane % depth
        count = self.count = len(fx)
        self.x_high = [
            fx[s + 1] if s + 1 < count else jnp.where(lane < LANES - depth, roll_lanes(fx[0], -depth), 0.0)
            for s in range(count)
        ]
        self.x_low = [fx[s] if s > 0 else jnp.where(lane >= depth, fx[0], 0.0) for s in range(count)]
        self.y_high = [jnp.where(row < rows - stride, roll_rows(f, -stride), 0.0) for f in fy]
        self.y_low = [jnp.where(row >= stride, f, 0.0) for f in fy]
        self.z_high = [jnp.where(z < depth - stride, roll_lanes(f, -stride), 0.0) for f in fz]
        self.z_low = [jnp.where(z >= stride, f, 0.0) for f in fz]
        self.d = [
            fx[s] + self.x_high[s] + fy[s] + self.y_high[s] + fz[s] + self.z_high[s] for s in range(count)
        ]
        self.w = [jnp.where(d > 0.0, OMEGA / jnp.where(d > 0.0, d, 1.0), 0.0) for d in self.d]

    def weighted(self, v, f):
        count = self.count
        out = []
        for s in range(count):
            low = v[s - 1] if s > 0 else roll_lanes(v[count - 1], self.depth)
            high = v[s + 1] if s + 1 < count else roll_lanes(v[0], -self.depth)
            x = self.x_low[s] * low + self.x_high[s] * high
            y = self.y_low[s] * roll_rows(v[s], self.stride) + self.y_high[s] * roll_rows(v[s], -self.stride)
            z = self.z_low[s] * roll_lanes(v[s], self.stride) + self.z_high[s] * roll_lanes(v[s], -self.stride)
            total = (f[s] + y) + (x + z)
            out.append(total)
        return out

    def sweep(self, v, f):
        totals = self.weighted(v, f)
        return [(1.0 - OMEGA) * v[s] + self.w[s] * totals[s] for s in range(self.count)]

    def sweeps(self, count, f):
        folded = [
            [w * c for w, c in zip(self.w, coefficients)]
            for coefficients in (self.x_low, self.x_high, self.y_low, self.y_high, self.z_low, self.z_high)
        ]
        scaled = self.start(f)
        slabs = self.count

        def step(v):
            out = []
            for s in range(slabs):
                low = v[s - 1] if s > 0 else roll_lanes(v[slabs - 1], self.depth)
                high = v[s + 1] if s + 1 < slabs else roll_lanes(v[0], -self.depth)
                x = folded[0][s] * low + folded[1][s] * high
                y = folded[2][s] * roll_rows(v[s], self.stride) + folded[3][s] * roll_rows(v[s], -self.stride)
                z = folded[4][s] * roll_lanes(v[s], self.stride) + folded[5][s] * roll_lanes(v[s], -self.stride)
                out.append((((1.0 - OMEGA) * v[s] + scaled[s]) + y) + (x + z))
            return out

        v = scaled
        for _ in range(count - 1):
            v = step(v)
        return v

    def start(self, f):
        return [self.w[s] * f[s] for s in range(self.count)]

    def residual(self, v, f):
        totals = self.weighted(v, f)
        return [totals[s] - self.d[s] * v[s] for s in range(self.count)]

    def kept(self):
        shape = self.fx[0].shape
        step = 2 * self.stride
        return (rows_of(shape) % step == 0) & (lanes_of(shape) % step == 0)

    def coarser(self):
        keep, stride = self.kept(), self.stride
        half = range(self.count // 2)

        def kept(values):
            return jnp.where(keep, 0.25 * values, 0.0)

        fx = [kept(pair_lanes(pair_rows(self.fx[2 * s], stride), stride)) for s in half]
        fy = [kept(pair_lanes(self.fy[2 * s] + self.fy[2 * s + 1], stride)) for s in half]
        fz = [kept(pair_rows(self.fz[2 * s] + self.fz[2 * s + 1], stride)) for s in half]
        return Listed(fx, fy, fz, 2 * stride, self.depth)

    def restrict(self, r):
        keep, stride = self.kept(), self.stride
        return [
            jnp.where(keep, 0.5 * pair_lanes(pair_rows(r[2 * s] + r[2 * s + 1], stride), stride), 0.0)
            for s in range(self.count // 2)
        ]

    def prolong(self, e):
        out = []
        for values in e:
            values = values + roll_rows(values, self.stride)
            values = values + roll_lanes(values, self.stride)
            out += [values, values]
        return out


def listed_cycle(levels, sweeps, f):
    level = levels[0]
    if len(levels) == 1:
        return level.sweeps(sweeps, f)
    v = level.sweep(level.start(f), f)
    e = listed_cycle(levels[1:], sweeps, level.restrict(level.residual(v, f)))
    v = [a + b for a, b in zip(v, level.prolong(e))]
    return level.sweep(level.sweep(v, f), f)


def level_two(axes, grid, sweeps, shape, pieces, out, wide, tall):
    devices_x, devices_y = grid
    me_x, me_y = lax.axis_index(axes[0]), lax.axis_index(axes[1])
    own_x, own_y = shape
    quarter = LANES // 4
    reach = RIM // 2
    blocks = 4
    count = devices_x * own_x // blocks
    rows = devices_y * own_y
    main = pl.ds(PAD, rows)
    window = own_y + RIM

    def piece(gx, gy):
        slow, far = (me_x // 2) ^ (gx // 2), (me_y // 2) ^ (gy // 2)
        return ((me_y + gy) % 2, (me_x + gx) % 2 * (devices_y // 2) + far, slow)

    for ref in (wide, tall):
        ref[...] = jnp.zeros(ref.shape, F32)
    lane = lanes_of((window, LANES))
    for gy in range(devices_y):
        sums = [None] * count
        for gx in range(devices_x):
            where = piece(gx, gy)
            first = pieces[where + (pl.ds(0, window),)]
            second = pieces[where + (pl.ds(window, window // 2),)]
            for local in range(1, 2 * blocks - 1):
                x = own_x * gx - reach + local
                if not 0 <= x < devices_x * own_x:
                    continue
                block, slab = x // count, x % count
                if local <= blocks:
                    moved = roll_lanes(first, (block - local + 1) * quarter)
                else:
                    at = 2 * (local - blocks - 1)
                    halves = [roll_lanes(second, (block - at - odd) * quarter) for odd in range(2)]
                    moved = jnp.concatenate(halves)
                moved = jnp.where(lane // quarter == block, moved, 0.0)
                sums[slab] = moved if sums[slab] is None else sums[slab] + moved
        place = pl.ds(PAD + own_y * gy - reach, window)
        for slab in range(count):
            tall[slab, place] = tall[slab, place] + sums[slab]
    f = [tall[slab, main] for slab in range(count)]

    lane = lanes_of((rows, LANES))
    for gx in range(devices_x):
        for gy in range(devices_y):
            where = piece(gx, gy)
            for face in range(3):
                values = pieces[where + (pl.ds(window + window // 2 + face * own_y, own_y),)]
                wide[face, gx, gy * own_y : (gy + 1) * own_y] = values
    faces = []
    for face in range(3):
        slabs = [None] * count
        for gx in range(devices_x):
            values = wide[face, gx]
            for local in range(own_x):
                x = own_x * gx + local
                block, slab = x // count, x % count
                moved = roll_lanes(values, (block - local) * quarter)
                moved = jnp.where(lane // quarter == block, moved, 0.0)
                slabs[slab] = moved if slabs[slab] is None else slabs[slab] + moved
        faces.append(slabs)
    levels = [Listed(*faces, 1, quarter)]
    while len(levels) < LEVELS - 2:
        levels.append(levels[-1].coarser())
    e = listed_cycle(levels, sweeps, f)

    for slab in range(count):
        out[reach + slab, main] = e[slab]
    for slab in range(reach):
        out[slab, main] = jnp.where(lane < quarter, 0.0, roll_lanes(e[count - reach + slab], quarter))
        out[reach + count + slab, main] = jnp.where(
            lane >= LANES - quarter, 0.0, roll_lanes(e[slab], -quarter)
        )
    out[:, :PAD] = jnp.zeros((count + 2 * reach, PAD, LANES), F32)
    out[:, PAD + rows :] = jnp.zeros((count + 2 * reach, PAD, LANES), F32)


def level_up(axes, grid, coarse, top, kept, faces, x_low, x_high, y_low, y_high, *refs):
    out, mid, one, two, right, post, up = refs
    devices_x, devices_y = grid
    me_x, me_y = lax.axis_index(axes[0]), lax.axis_index(axes[1])
    coarse_x, coarse_y = faces.shape[1:3]
    nx, ny = out.shape[:2]
    own_x, own_y = coarse_x // 2, coarse_y // 2
    quarter = LANES // 4
    reach = RIM // 2
    window = own_y + RIM

    slabs, high = coarse_x + 2 * RIM, coarse_y + 2 * RIM
    half = slabs // 2
    inner = pl.ds(2 * RIM, coarse_y)
    body = pl.ds(RIM, high)
    sizes_x, sizes_y = rim_rows_x(nx, ny), rim_rows_y(nx, ny)
    for face, slot in enumerate((FX, FY, ZL)):
        clear_pads(mid.at[slot], high)
        mid[slot, RIM : RIM + coarse_x, inner] = faces[face]
        place_x = sizes_x[0] + sizes_x[1] + face * sizes_x[0]
        place_y = sizes_y[0] + sizes_y[1] + face * sizes_y[0]
        for layer in range(RIM):
            mid[slot, layer, inner] = rim_slab(x_low, place_x, coarse_y, layer)
            mid[slot, RIM + coarse_x + layer, inner] = rim_slab(x_high, place_x, coarse_y, layer)
        for slab in range(half):
            place = pl.ds(place_y + slab * RIM, RIM)
            for message, row in ((y_low, RIM), (y_high, 2 * RIM + coarse_y)):
                pair = one_of_two(message[place])
                mid[slot, slab, row : row + RIM] = pair[0]
                mid[slot, slab + half, row : row + RIM] = pair[1]
    row_inside = (rows_of((high, LANES)) >= RIM) | (me_y > 0)
    for slab in range(slabs - 1):
        inside = row_inside & (me_x > 0) if slab < RIM else row_inside
        set_weights(mid, slab, RIM, high, HALF, inside)
    clear_pads(one, high)
    clear_pads(right, high)
    clear_pads(two, high)
    one[RIM : RIM + coarse_x, inner] = kept[1]
    right[RIM : RIM + coarse_x, inner] = kept[0]
    for layer in range(RIM):
        one[layer, inner] = rim_slab(x_low, 0, coarse_y, layer)
        one[RIM + coarse_x + layer, inner] = rim_slab(x_high, 0, coarse_y, layer)
    for slab in range(half):
        place = pl.ds(slab * RIM, RIM)
        for message, row in ((y_low, RIM), (y_high, 2 * RIM + coarse_y)):
            pair = one_of_two(message[place])
            one[slab, row : row + RIM] = pair[0]
            one[slab + half, row : row + RIM] = pair[1]
    row = rows_of((high, LANES))
    own_row = (row >= RIM) & (row < RIM + coarse_y)
    for slab in range(1, slabs - 1):
        f_rim = one[slab, body] * mid[D, slab, body] * (1.0 / OMEGA)
        if RIM <= slab < RIM + coarse_x:
            f_rim = jnp.where(own_row, right[slab, body], f_rim)
        right[slab, body] = f_rim
        two[slab, body] = swept(mid, one, slab, RIM, high, right)

    per_block = (coarse.shape[0] - 2 * reach) // own_x
    base = me_x % per_block * own_x
    mine = None
    for gy in range(devices_y):
        place = pl.ds(PAD + gy * own_y - reach, window)
        values = jnp.where(me_y == gy, coarse[pl.ds(base, half), place, :], 0.0)
        mine = values if mine is None else mine + values
    source = lax.broadcasted_iota(jnp.int32, (LANES, LANES), 0)
    target = lax.broadcasted_iota(jnp.int32, (LANES, LANES), 1)
    hit = (source == me_x // per_block * quarter + target // 2) & (target < HALF)
    fine = exact_dot(mine.reshape(half * window, LANES), jnp.where(hit, 1.0, 0.0).astype(F32))
    fine = fine.reshape(half, window, LANES)
    for odd in range(2):
        up[:half, pl.ds(odd, window, stride=2), :] = fine
    for pair in range(half):
        for slab in (2 * pair, 2 * pair + 1):
            if 1 <= slab < slabs - 1:
                two[slab, body] = two[slab, body] + up[pair, :high]
    for slab in range(2, slabs - 2):
        one[slab, body] = swept(mid, two, slab, RIM, high, right)
    for slab in range(3, slabs - 3):
        two[slab, body] = swept(mid, one, slab, RIM, high, right)

    steps = coarse_x + 2
    fine_rows = ny + 2 * RIM
    e = two[RIM - 1 : RIM - 1 + steps, body]
    fine = exact_dot(e.reshape(steps * high, LANES), expand(LANES, 0)).reshape(steps, high, LANES)
    fine = fine[:, reach : reach + fine_rows // 2]
    for odd in range(2):
        up[:, pl.ds(odd, fine_rows // 2, stride=2), :] = fine
    body = pl.ds(RIM, fine_rows)
    for slot in (0, 1):
        clear_pads(post.at[slot], fine_rows)
    inner = pl.ds(PAD, ny)
    post[0, EDGE : EDGE + nx, inner] = top[V, EDGE : EDGE + nx, inner]
    base_x, base_y = RIM // 2 * coarse_y, half * RIM
    for layer in range(2):
        place = pl.ds(base_x + layer * ny, ny)
        post[0, EDGE - 2 + layer, inner] = x_low[place]
        post[0, EDGE + nx + layer, inner] = x_high[place]
    for slab in range(nx + 4):
        place = pl.ds(base_y + 2 * slab, 2)
        post[0, slab + EDGE - 2, RIM:PAD] = jnp.zeros((RIM, LANES), F32)
        post[0, slab + EDGE - 2, PAD + ny : PAD + ny + RIM] = jnp.zeros((RIM, LANES), F32)
        post[0, slab + EDGE - 2, PAD - 2 : PAD] = y_low[place]
        post[0, slab + EDGE - 2, PAD + ny : PAD + ny + 2] = y_high[place]

    def raise_level(index):
        for slab in (EDGE - 2 + 2 * index, EDGE - 1 + 2 * index):
            post[0, slab, body] = post[0, slab, body] + up[index]

    run(steps, raise_level)

    def fifth(index):
        slab = EDGE - 1 + index
        post[1, slab, body] = swept(top, post.at[0], slab, RIM, fine_rows)

    run(nx + 2, fifth)

    def sixth(index):
        out[index] = swept(top, post.at[1], EDGE + index, PAD, ny)

    run(nx, sixth)


IN_VMEM = pl.BlockSpec(memory_space=pltpu.VMEM)


def call(kernel, outs, scratch=(), from_hbm=False):
    ins = pl.BlockSpec(memory_space=pl.ANY) if from_hbm else IN_VMEM

    def launch(*args):
        if from_hbm:
            args = [pltpu.with_memory_space_constraint(arg, pltpu.HBM) for arg in args]
        return pl.pallas_call(
            kernel,
            out_shape=[pltpu.VMEM(shape, F32) for shape in outs],
            in_specs=[ins] * len(args),
            out_specs=[IN_VMEM] * len(outs),
            scratch_shapes=[pltpu.VMEM(s, F32) if isinstance(s, tuple) else s for s in scratch],
            compiler_params=pltpu.CompilerParams(vmem_limit_bytes=24 * 2**20),
        )(*args)

    return launch


def pair_route(axis):
    return [(i, i ^ 1) for i in range(lax.axis_size(axis))]


def swap_route(axis):
    count = lax.axis_size(axis)
    return [(i, (i + 1 ^ 1) - 1) for i in range(1, count - 1)]


def by_partner(low, high, axis):
    odd = lax.axis_index(axis) % 2 == 1
    return jnp.where(odd, low, high), jnp.where(odd, high, low)


def from_sides(low, high, axis):
    pair, swap = by_partner(low, high, axis)
    pair = lax.ppermute(pair, axis, pair_route(axis))
    swap = lax.ppermute(swap, axis, swap_route(axis))
    return by_partner(pair, swap, axis)


def passed_round(block, axis, stride):
    count = lax.axis_size(axis)
    return [block] + [
        lax.ppermute(block, axis, [(i, i ^ distance) for i in range(count)])
        for distance in range(stride, count, stride)
    ]


def passed_across(block):
    count, size = lax.axis_size("gx"), lax.axis_size("gy")
    blocks = []
    for side in range(2):
        for distance in range(0, size, 2):
            route = [
                (x * size + y, (x ^ side) * size + (y ^ distance)) for x in range(count) for y in range(size)
            ]
            moved = side + distance > 0
            blocks.append(lax.ppermute(block, ("gx", "gy"), route) if moved else block)
    return blocks


def fused_cycle(*fields):
    axes = ("gx", "gy")
    devices_x, devices_y = lax.axis_size("gx"), lax.axis_size("gy")
    nx, ny, nz = fields[0].shape
    coarse_x, coarse_y = nx // 2, ny // 2
    x_shape, y_shape = (x_rows(nx, ny), LANES), (y_rows(nx, ny), LANES)
    own, x_low, x_high = call(
        start_pack, [(5, nx, ny, nz), x_shape, x_shape], [pltpu.SemaphoreType.DMA((5,))], True
    )(*fields)
    x_low, x_high = from_sides(x_low, x_high, "gx")
    faces, coefficients = call(
        coarse_faces,
        [(3, coarse_x, coarse_y, LANES), (16, LANES)],
        [(coarse_x, ny, LANES), (coarse_x // 2, coarse_y, LANES)],
    )(own)
    y_low, y_high = call(pack_y, [y_shape] * 2)(own, x_low, x_high)
    y_low, y_high = from_sides(y_low, y_high, "gy")
    stack = (nx + 2 * EDGE, ny + 4 * RIM, LANES)
    stack_1 = (coarse_x + 2 * RIM, coarse_y + 4 * RIM, LANES)
    half = stack_1[0] // 2
    v_shape = (sum(rim_rows_x(nx, ny)), LANES)
    w_shape = (sum(rim_rows_y(nx, ny)), LANES)
    top, kept, chunk, v_low, v_high = call(
        functools.partial(level_down, axes),
        [(D + 1,) + stack, (2, coarse_x, coarse_y, LANES), (BLOCK_ROWS, LANES), v_shape, v_shape],
        [
            stack,
            (nx // 2, ny, LANES),
            stack_1,
            (half, coarse_y + 2 * RIM, LANES),
            (D + 1,) + stack_1,
            (coarse_x + 3,) + stack[1:],
        ],
    )(own, faces, coefficients, x_low, x_high, y_low, y_high)

    blocks = passed_round(chunk, "gx", 2)
    v_low, v_high = from_sides(v_low, v_high, "gx")
    slow = (len(blocks),) + chunk.shape
    (pieces,) = call(stack_blocks, [slow])(*blocks, v_low, v_high)
    blocks = passed_across(pieces.reshape(-1, LANES))
    w_low, w_high = call(pack_v, [w_shape] * 2)(top, kept, faces, v_low, v_high, pieces)
    pair, swap = by_partner(w_low, w_high, "gy")
    swap = lax.ppermute(swap, "gy", swap_route("gy"))
    rows = sum(block.shape[0] for block in blocks) + w_shape[0]
    (message,) = call(join_blocks, [(rows, LANES)])(*blocks, pair, swap)
    other = lax.ppermute(message, "gy", pair_route("gy"))
    rows = message.shape[0] - w_shape[0]
    pieces = jnp.stack((message[:rows], other[:rows])).reshape((2, len(blocks)) + slow)
    w_low, w_high = by_partner(other[rows:], swap, "gy")
    count = devices_x * nx // 16
    rows = devices_y * ny // 4
    grid = (devices_x, devices_y)
    coarsest = (devices_x * nx >> LEVELS - 1, devices_y * ny >> LEVELS - 1)
    wide = (count + RIM, rows + 2 * PAD, LANES)
    (coarse,) = call(
        functools.partial(level_two, axes, grid, 4 * max(coarsest), (nx // 4, ny // 4)),
        [wide],
        [(3, devices_x, rows, LANES), wide],
    )(pieces)
    return pl.pallas_call(
        functools.partial(level_up, axes, grid),
        out_shape=jax.ShapeDtypeStruct((nx, ny, nz), F32),
        in_specs=[IN_VMEM] * 8,
        out_specs=IN_VMEM,
        scratch_shapes=[
            pltpu.VMEM(shape, F32)
            for shape in ((D + 1,) + stack_1, stack_1, stack_1, stack_1, (2,) + stack, (coarse_x + 2, ny + 2 * RIM, LANES))
        ],
        compiler_params=pltpu.CompilerParams(vmem_limit_bytes=24 * 2**20),
    )(coarse, top, kept, faces, v_low, v_high, w_low, w_high)


def with_halo(block, sides, width):
    for axis, dim in sides:
        count = lax.axis_size(axis)
        forward = [(i, i + 1) for i in range(count - 1)]
        backward = [(target, source) for source, target in forward]
        low = lax.ppermute(
            lax.slice_in_dim(block, block.shape[dim] - width, None, axis=dim), axis, forward
        )
        high = lax.ppermute(lax.slice_in_dim(block, 0, width, axis=dim), axis, backward)
        block = jnp.concatenate([low, block, high], axis=dim)
    return block


def passed_along(block, axis, distance):
    devices = range(lax.axis_size(axis))
    route = [(i - distance, i) for i in devices if i - distance in devices]
    return lax.ppermute(block, axis, route)


def stencil(padded, padded_x, padded_y, face_z):
    center = padded[1:-1, 1:-1]
    zero_plane = jnp.zeros(center.shape[:2] + (1,), center.dtype)
    above_face = jnp.concatenate((face_z[:, :, 1:], zero_plane), axis=2)
    below_z = jnp.concatenate((zero_plane, center[:, :, :-1]), axis=2)
    above_z = jnp.concatenate((center[:, :, 1:], zero_plane), axis=2)
    lower_x = padded_x[1:-1, 1:-1]
    upper_x = padded_x[2:, 1:-1]
    lower_y = padded_y[1:-1, 1:-1]
    upper_y = padded_y[1:-1, 2:]
    applied = lower_x * (center - padded[:-2, 1:-1]) + upper_x * (center - padded[2:, 1:-1])
    applied = (
        applied + lower_y * (center - padded[1:-1, :-2]) + upper_y * (center - padded[1:-1, 2:])
    )
    applied = applied + face_z * (center - below_z) + above_face * (center - above_z)
    diagonal = lower_x + upper_x + lower_y + upper_y + face_z + above_face
    return (applied, diagonal)


def jacobi_sweep(padded, source, padded_x, padded_y, face_z):
    applied, diagonal = stencil(padded, padded_x, padded_y, face_z)
    return padded[1:-1, 1:-1] + OMEGA * (source - applied) / diagonal


def pad_plane(values, width):
    return jnp.pad(values, ((width, width), (width, width), (0, 0)))


def restrict(residual):
    shape = residual.shape
    blocks = residual.reshape(shape[0] // 2, 2, shape[1] // 2, 2, shape[2] // 2, 2)
    return 4.0 * jnp.mean(blocks, axis=(1, 3, 5))


def coarsen_faces(face_x, face_y, face_z):
    shape = face_x.shape
    blocks = (shape[0] // 2, 2, shape[1] // 2, 2, shape[2] // 2, 2)
    coarse_x = jnp.mean(face_x.reshape(blocks)[:, 0], axis=(2, 4))
    coarse_y = jnp.mean(face_y.reshape(blocks)[:, :, :, 0], axis=(1, 4))
    coarse_z = jnp.mean(face_z.reshape(blocks)[..., 0], axis=(1, 3))
    return (coarse_x, coarse_y, coarse_z)


def prolong(coarse):
    return jnp.repeat(jnp.repeat(jnp.repeat(coarse, 2, axis=0), 2, axis=1), 2, axis=2)


def local_cycle(grid_level, iterate, source, face_x, face_y, face_z):
    padded_x = pad_plane(face_x, 1)
    padded_y = pad_plane(face_y, 1)
    if grid_level == LEVELS - 1:
        count = 4 * max(iterate.shape[0], iterate.shape[1])

        def one_sweep(index, values):
            return jacobi_sweep(pad_plane(values, 1), source, padded_x, padded_y, face_z)

        return lax.fori_loop(0, count, one_sweep, iterate)
    for sweep_index in range(2):
        iterate = jacobi_sweep(pad_plane(iterate, 1), source, padded_x, padded_y, face_z)
    applied, diagonal = stencil(pad_plane(iterate, 1), padded_x, padded_y, face_z)
    coarse_src = restrict(source - applied)
    coarse_x, coarse_y, coarse_z = coarsen_faces(face_x, face_y, face_z)
    correction = local_cycle(
        grid_level + 1, jnp.zeros_like(coarse_src), coarse_src, coarse_x, coarse_y, coarse_z
    )
    iterate = iterate + prolong(correction)
    for sweep_index in range(2):
        iterate = jacobi_sweep(pad_plane(iterate, 1), source, padded_x, padded_y, face_z)
    return iterate


def field_rim(iterate):
    return with_halo(iterate, (("gx", 0), ("gy", 1)), 1)


def sweep_pair_narrow(iterate, source, padded_x, padded_y, face_z, zero_start):
    for sweep_index in range(2):
        if sweep_index == 0 and zero_start:
            padded = pad_plane(iterate, 1)
        else:
            padded = field_rim(iterate)
        iterate = jacobi_sweep(padded, source, padded_x, padded_y, face_z)
    return iterate


def descend(grid_level, iterate, source, face_x, face_y, face_z, zero_start, gather_level):
    if grid_level == gather_level:
        pieces = (
            lax.all_gather(source, "gy", axis=1, tiled=True),
            lax.all_gather(face_x, "gy", axis=1, tiled=True),
            lax.all_gather(face_y, "gy", axis=1, tiled=True),
            lax.all_gather(face_z, "gy", axis=1, tiled=True),
        )
        gathered = (
            lax.all_gather(pieces[0], "gx", axis=0, tiled=True),
            lax.all_gather(pieces[1], "gx", axis=0, tiled=True),
            lax.all_gather(pieces[2], "gx", axis=0, tiled=True),
            lax.all_gather(pieces[3], "gx", axis=0, tiled=True),
        )
        correction = local_cycle(
            grid_level,
            jnp.zeros_like(gathered[0]),
            gathered[0],
            gathered[1],
            gathered[2],
            gathered[3],
        )
        start_x = lax.axis_index("gx") * source.shape[0]
        start_y = lax.axis_index("gy") * source.shape[1]
        return lax.dynamic_slice(
            correction, (start_x, start_y, jnp.zeros((), jnp.int32)), source.shape
        )
    next_x = passed_along(face_x[:1], "gx", -1)
    next_y = passed_along(face_y[:, :1], "gy", -1)
    lower_row = jnp.zeros_like(next_x)
    lower_col = jnp.zeros_like(next_y)
    padded_x = jnp.pad(
        jnp.concatenate((lower_row, face_x, next_x), axis=0), ((0, 0), (1, 1), (0, 0))
    )
    padded_y = jnp.pad(
        jnp.concatenate((lower_col, face_y, next_y), axis=1), ((1, 1), (0, 0), (0, 0))
    )

    def smoother(values, starting):
        return sweep_pair_narrow(values, source, padded_x, padded_y, face_z, starting)

    iterate = smoother(iterate, zero_start)
    applied, diagonal = stencil(field_rim(iterate), padded_x, padded_y, face_z)
    coarse_src = restrict(source - applied)
    coarse_x, coarse_y, coarse_z = coarsen_faces(face_x, face_y, face_z)
    correction = descend(
        grid_level + 1,
        jnp.zeros_like(coarse_src),
        coarse_src,
        coarse_x,
        coarse_y,
        coarse_z,
        True,
        gather_level,
    )
    iterate = iterate + prolong(correction)
    return smoother(iterate, False)


def fits(nx, ny, nz, devices_x, devices_y):
    cells = devices_x * nx * devices_y * ny * nz // 8
    even = devices_x % 8 == 0 and devices_y % 4 == 0
    even = even and devices_x & (devices_x - 1) == 0 and devices_y & (devices_y - 1) == 0
    return cells <= 2**18 and even and (nx, ny, nz) == (16, 16, LANES)


def local(source_term, initial_guess, face_x, face_y, face_z):
    if fits(*source_term.shape, lax.axis_size("gx"), lax.axis_size("gy")):
        return fused_cycle(source_term, initial_guess, face_x, face_y, face_z)
    gather_level = 4
    return descend(0, initial_guess, source_term, face_x, face_y, face_z, False, gather_level)


def solution(mesh):
    placed = (P("gx", "gy", None),) * 5
    return jax.shard_map(
        local, mesh=mesh, in_specs=placed, out_specs=P("gx", "gy", None), check_vma=False
    )
```

```python
import functools

import jax
import jax.numpy as jnp
from jax import lax
from jax.experimental import pallas as pl
from jax.experimental.pallas import tpu as pltpu
from jax.sharding import PartitionSpec as P

LEVELS = 6
OMEGA = 0.8
LANES = 128
RIM = 4
EDGE = 3
PAD = 8
BLOCK_ROWS = 24
F32 = jnp.float32

V, F, FX, FY, ZL, ZH, W, D = range(8)
SLOTS = (F, V, FX, FY, ZL)
X_LAYERS = (2, 3, 3, 2, 2)
Y_LAYERS = (2, 3, 2, 3, 2)
Y_REACH = (1, 2, 2, 2, 1)


def lanes_of(shape):
    return lax.broadcasted_iota(jnp.int32, shape, len(shape) - 1)


def rows_of(shape):
    return lax.broadcasted_iota(jnp.int32, shape, len(shape) - 2)


def roll_lanes(values, step):
    return pltpu.roll(values, step % LANES, values.ndim - 1)


def roll_rows(values, step):
    return pltpu.roll(values, step % values.shape[-2], values.ndim - 2)


def exact_dot(left, right):
    return jnp.dot(left, right, precision=lax.Precision.HIGHEST, preferred_element_type=F32)


def compact(depth, part, even_only=False):
    source = lax.broadcasted_iota(jnp.int32, (LANES, LANES), 0)
    target = lax.broadcasted_iota(jnp.int32, (LANES, LANES), 1)
    half = depth // 2
    hit = target == (source // depth * 2 + part) * half + source % depth // 2
    if even_only:
        hit = hit & (source % 2 == 0)
    return jnp.where(hit, 1.0, 0.0).astype(F32)


def expand(depth, part):
    target = lax.broadcasted_iota(jnp.int32, (LANES, LANES), 0)
    source = lax.broadcasted_iota(jnp.int32, (LANES, LANES), 1)
    half = depth // 2
    hit = target == (source // depth * 2 + part) * half + source % depth // 2
    return jnp.where(hit, 1.0, 0.0).astype(F32)


def merge_lanes(values, depth, even_only=False):
    count, rows, _ = values.shape
    half = count // 2
    flat = values.reshape(2, half * rows, LANES)
    out = exact_dot(flat[0], compact(depth, 0, even_only))
    out = out + exact_dot(flat[1], compact(depth, 1, even_only))
    return out.reshape(half, rows, LANES)


def even_rows(ref, rows):
    return ref[:, pl.ds(0, rows // 2, stride=2), :]


def odd_rows(ref, rows):
    return ref[:, pl.ds(1, rows // 2, stride=2), :]


HALF = LANES // 2


def low_half(values):
    return jnp.where(lanes_of(values.shape) < HALF, values, 0.0)


def two_in_one(first, second):
    return first + roll_lanes(second, HALF)


def one_of_two(values):
    return low_half(values), low_half(roll_lanes(values, HALF))


def x_rows(nx, ny):
    return sum(X_LAYERS) * ny


def y_rows(nx, ny):
    return sum(layers * (nx + 2 * reach) for layers, reach in zip(Y_LAYERS, Y_REACH))


def rim_rows_x(nx, ny):
    slab = RIM // 2 * (ny // 2)
    return slab, 2 * ny, 3 * slab


def rim_rows_y(nx, ny):
    slabs = (nx // 2 + 2 * RIM) // 2 * RIM
    return slabs, 2 * (nx + 4), 3 * slabs


def x_place(index, layer, ny):
    return pl.ds((sum(X_LAYERS[:index]) + layer) * ny, ny)


def y_place(index, slab, nx):
    before = zip(Y_LAYERS[:index], Y_REACH[:index])
    start = sum(layers * (nx + 2 * reach) for layers, reach in before)
    return pl.ds(start + (Y_REACH[index] + slab) * Y_LAYERS[index], Y_LAYERS[index])


def start_pack(*refs):
    fields, (own, x_low, x_high, done) = refs[:5], refs[5:]
    copies = [pltpu.make_async_copy(ref, own.at[index], done.at[index]) for index, ref in enumerate(fields)]
    for copy in copies:
        copy.start()
    nx, ny = own.shape[1:3]
    for index, copy in enumerate(copies):
        copy.wait()
        for layer in range(X_LAYERS[index]):
            x_low[x_place(index, layer, ny)] = own[index, layer]
            x_high[x_place(index, layer, ny)] = own[index, nx - X_LAYERS[index] + layer]


def pair_slabs(ref):
    count = ref.shape[0]
    values = ref[...].reshape((count // 2, 2) + ref.shape[1:])
    return values[:, 0], values[:, 1]


def wide_slab(slab, from_low, own, from_high):
    count = own.shape[0]
    if slab < RIM:
        return from_low(slab)
    if slab < RIM + count:
        return own[slab - RIM]
    return from_high(slab - RIM - count)


def rim_slab(ref, base, rows, layer):
    place = pl.ds(base + layer % (RIM // 2) * rows, rows)
    return one_of_two(ref[place])[layer // (RIM // 2)]


def pack_y(own, x_low, x_high, low, high):
    nx, ny = own.shape[1:3]
    for index in range(5):
        width, layers, reach = Y_LAYERS[index], X_LAYERS[index], Y_REACH[index]
        for out, start in ((low, 0), (high, ny - width)):
            for slab in range(nx):
                out[y_place(index, slab, nx)] = own[index, slab, start : start + width]
            for layer in range(reach):
                rows = pl.ds(x_place(index, layers - reach + layer, ny).start + start, width)
                out[y_place(index, layer - reach, nx)] = x_low[rows]
                rows = pl.ds(x_place(index, layer, ny).start + start, width)
                out[y_place(index, nx + layer, nx)] = x_high[rows]


def fold_four(slabs, even_only=False):
    out = None
    for part in range(2):
        term = exact_dot(two_in_one(slabs[part], slabs[2 + part]), compact(HALF, part, even_only))
        out = term if out is None else out + term
    return out


def coarse_slab_sums(ref_x, ref_y, ref_z, count, first, tmp):
    extra = tmp.shape[0]
    rows = tmp.shape[1]
    for index in range(extra):
        tmp[index] = ref_x[first + 2 * index]
    x = even_rows(tmp, rows) + odd_rows(tmp, rows)
    for index in range(count):
        tmp[index] = ref_y[first + 2 * index] + ref_y[first + 2 * index + 1]
    y = even_rows(tmp, rows)[:count]
    for index in range(count):
        tmp[index] = ref_z[first + 2 * index] + ref_z[first + 2 * index + 1]
    return x, y, (even_rows(tmp, rows) + odd_rows(tmp, rows))[:count]


def halved(values, even_only=False):
    count, rows, _ = values.shape
    flat = exact_dot(values.reshape(count * rows, LANES), compact(LANES, 0, even_only))
    return 0.25 * flat.reshape(count, rows, LANES)


def coarse_faces(own, faces, out, fine, tmp):
    x, y, z = coarse_slab_sums(own.at[2], own.at[3], own.at[4], own.shape[1] // 2, 0, fine)
    faces[0] = halved(x)
    faces[1] = halved(y)
    faces[2] = halved(z, True)
    rows = faces.shape[2]
    coarse = rows // 2
    fx, fy, fz = faces.at[0], faces.at[1], faces.at[2]
    tmp[...] = pair_slabs(fx)[0]
    x = even_rows(tmp, rows) + odd_rows(tmp, rows)
    first, second = pair_slabs(fy)
    tmp[...] = first + second
    y = even_rows(tmp, rows)
    first, second = pair_slabs(fz)
    tmp[...] = first + second
    z = even_rows(tmp, rows) + odd_rows(tmp, rows)
    out[...] = jnp.zeros(out.shape, F32)
    out[:coarse] = 0.25 * fold_four([x[i] for i in range(4)])
    out[coarse : 2 * coarse] = 0.25 * fold_four([y[i] for i in range(4)])
    out[2 * coarse : 3 * coarse] = 0.25 * fold_four([z[i] for i in range(4)], True)


def weighted(lev, src, slab, start, rows, f=None):
    here = pl.ds(start, rows)
    below = pl.ds(start - 1, rows)
    above = pl.ds(start + 1, rows)
    v = src[slab, here]
    f = lev.at[F] if f is None else f
    x = lev[FX, slab, here] * src[slab - 1, here] + lev[FX, slab + 1, here] * src[slab + 1, here]
    y = lev[FY, slab, here] * src[slab, below] + lev[FY, slab, above] * src[slab, above]
    z = lev[ZL, slab, here] * roll_lanes(v, 1) + lev[ZH, slab, here] * roll_lanes(v, -1)
    total = ((x + y) + f[slab, here]) + z
    return v, total


def swept(lev, src, slab, start, rows, f=None):
    v, total = weighted(lev, src, slab, start, rows, f)
    return (1.0 - OMEGA) * v + lev[W, slab, pl.ds(start, rows)] * total


def set_weights(lev, slab, start, rows, depth, inside=None):
    here = pl.ds(start, rows)
    fz = lev[ZL, slab, here]
    z = lanes_of(fz.shape) % depth
    upper = jnp.where(z == depth - 1, 0.0, roll_lanes(fz, -1))
    diagonal = lev[FX, slab, here] + lev[FX, slab + 1, here]
    diagonal = diagonal + lev[FY, slab, here] + lev[FY, slab, pl.ds(start + 1, rows)] + fz + upper
    valid = diagonal > 0.0
    if inside is not None:
        valid = valid & inside
    lev[ZL, slab, here] = jnp.where(z == 0, 0.0, fz)
    lev[ZH, slab, here] = upper
    lev[D, slab, here] = diagonal
    lev[W, slab, here] = jnp.where(valid, OMEGA / jnp.where(valid, diagonal, 1.0), 0.0)


def run(count, body):
    for index in range(count):
        body(index)


def clear_pads(ref, rows):
    for start in (0, RIM + rows):
        ref[:, start : start + RIM] = jnp.zeros((ref.shape[0], RIM, LANES), F32)


def level_down(axes, own, faces, coefficients, x_low, x_high, y_low, y_high, *refs):
    top, kept, chunk, v_low, v_high, other, tmp, one, two, mid, wide = refs
    nx, ny = own.shape[1:3]
    slabs, rows = nx + 2 * EDGE, ny + 2 * RIM
    me_x, me_y = lax.axis_index(axes[0]), lax.axis_index(axes[1])
    inner = pl.ds(PAD, ny)
    for index, slot in enumerate(SLOTS):
        layers, width = X_LAYERS[index], Y_LAYERS[index]
        top[slot, :, :PAD] = jnp.zeros((slabs, PAD, LANES), F32)
        top[slot, :, PAD + ny :] = jnp.zeros((slabs, PAD, LANES), F32)
        top[slot, EDGE : EDGE + nx, inner] = own[index]
        for layer in range(EDGE):
            if layer < layers:
                top[slot, EDGE - layers + layer, inner] = x_low[x_place(index, layer, ny)]
                top[slot, EDGE + nx + layer, inner] = x_high[x_place(index, layer, ny)]
            else:
                top[slot, EDGE - 1 - layer, inner] = jnp.zeros((ny, LANES), F32)
                top[slot, EDGE + nx + layer, inner] = jnp.zeros((ny, LANES), F32)
        for slab in range(-Y_REACH[index], nx + Y_REACH[index]):
            top[slot, EDGE + slab, PAD - width : PAD] = y_low[y_place(index, slab, nx)]
            top[slot, EDGE + slab, PAD + ny : PAD + ny + width] = y_high[y_place(index, slab, nx)]
    clear_pads(other, rows)

    coarse_x, coarse_y = nx // 2, ny // 2
    near = RIM - 1
    for slot in (FX, FY, ZL, ZH, W, D):
        mid[slot] = jnp.zeros(mid.shape[1:], F32)
    x, y, z = coarse_slab_sums(top.at[FX], top.at[FY], top.at[ZL], coarse_x + 2, EDGE - 2, wide)
    mid[FX, near : near + coarse_x + 3, RIM : 3 * RIM + coarse_y] = halved(x)
    mid[FY, near : near + coarse_x + 2, RIM : 3 * RIM + coarse_y] = halved(y)
    mid[ZL, near : near + coarse_x + 2, RIM : 3 * RIM + coarse_y] = halved(z, True)

    row_inside = (rows_of((rows, LANES)) >= RIM) | (me_y > 0)
    main = pl.ds(RIM, rows)
    start_v = top.at[V]

    def first(index):
        slab = index + 1
        inside = row_inside & ((slab >= EDGE) | (me_x > 0))
        set_weights(top, slab, RIM, rows, LANES, inside)
        other[slab, main] = swept(top, start_v, slab, RIM, rows)

    run(slabs - 2, first)

    def second(index):
        slab = index + 2
        top[V, slab, main] = swept(top, other, slab, RIM, rows)

    run(slabs - 4, second)

    def rest(slab):
        v, total = weighted(top, top.at[V], slab, PAD, ny)
        return total - top[D, slab, inner] * v

    def residual(index):
        slab = EDGE + 2 * index
        tmp[index] = rest(slab) + rest(slab + 1)

    run(nx // 2, residual)

    slabs, rows = coarse_x + 2 * RIM, coarse_y + 2 * RIM
    half = slabs // 2
    inner = pl.ds(2 * RIM, coarse_y)
    main = pl.ds(RIM, rows)
    row_inside = (rows_of((rows, LANES)) >= RIM) | (me_y > 0)
    for slab in range(near, near + coarse_x + 2):
        inside = row_inside & (me_x > 0) if slab < RIM else row_inside
        set_weights(mid, slab, RIM, rows, HALF, inside)

    source = even_rows(tmp, ny) + odd_rows(tmp, ny)
    source = 0.5 * exact_dot(source.reshape(coarse_x * coarse_y, LANES), compact(LANES, 0))
    for ref in (mid.at[F], mid.at[V], one):
        ref[...] = jnp.zeros(ref.shape, F32)
    mid[F, RIM : RIM + coarse_x, inner] = source.reshape(coarse_x, coarse_y, LANES)
    for slab in range(RIM, RIM + coarse_x):
        mid[V, slab, inner] = mid[W, slab, inner] * mid[F, slab, inner]
    for layer in range(RIM // 2):
        near, far = RIM + layer, coarse_x + layer
        v_low[layer * coarse_y : (layer + 1) * coarse_y] = two_in_one(
            mid[V, near, inner], mid[V, near + RIM // 2, inner]
        )
        v_high[layer * coarse_y : (layer + 1) * coarse_y] = two_in_one(
            mid[V, far, inner], mid[V, far + RIM // 2, inner]
        )
    kept[0] = mid[F, RIM : RIM + coarse_x, inner]
    kept[1] = mid[V, RIM : RIM + coarse_x, inner]
    base, after, _ = rim_rows_x(nx, ny)
    pairs = RIM // 2
    for face in range(3):
        for layer in range(pairs):
            place = pl.ds(base + after + (face * pairs + layer) * coarse_y, coarse_y)
            far = coarse_x - RIM + layer
            v_low[place] = two_in_one(faces[face, layer], faces[face, layer + pairs])
            v_high[place] = two_in_one(faces[face, far], faces[face, far + pairs])
    for layer in range(2):
        place = pl.ds(base + layer * ny, ny)
        v_low[place] = top[V, EDGE + layer, pl.ds(PAD, ny)]
        v_high[place] = top[V, EDGE + nx - 2 + layer, pl.ds(PAD, ny)]
    for slab in range(RIM - 1, RIM + coarse_x + 1):
        one[slab, main] = swept(mid, mid.at[V], slab, RIM, rows)

    def rest_1(slab):
        v, total = weighted(mid, one, slab, RIM, rows)
        return total - mid[D, slab, main] * v

    two[...] = jnp.zeros(two.shape, F32)
    for pair in range(1, half - 1):
        two[pair] = rest_1(2 * pair) + rest_1(2 * pair + 1)
    pieces = even_rows(two, rows) + odd_rows(two, rows)
    coarse_rows, quarter_rows = rows // 2, rows // 4
    chunk[:coarse_rows] = 0.5 * fold_four([pieces[1 + i] for i in range(4)])
    rest_of = [pieces[5 + i // 2][i % 2 * quarter_rows :][:quarter_rows] for i in range(4)]
    chunk[coarse_rows : coarse_rows + quarter_rows] = 0.5 * fold_four(rest_of)
    chunk[coarse_rows + quarter_rows :] = coefficients[:BLOCK_ROWS - coarse_rows - quarter_rows]


def pack_v(top, kept, faces, x_low, x_high, low, high):
    coarse_x, coarse_y = faces.shape[1:3]
    nx, ny = 2 * coarse_x, 2 * coarse_y
    slabs = coarse_x + 2 * RIM
    half = slabs // 2
    sizes_x, sizes_y = rim_rows_x(nx, ny), rim_rows_y(nx, ny)

    def folded(own, place_x, place_y):
        values = [
            wide_slab(
                slab,
                lambda layer: rim_slab(x_low, place_x, coarse_y, layer),
                own,
                lambda layer: rim_slab(x_high, place_x, coarse_y, layer),
            )
            for slab in range(slabs)
        ]
        for slab in range(half):
            both = two_in_one(values[slab], values[slab + half])
            rows = pl.ds(place_y + slab * RIM, RIM)
            low[rows] = both[:RIM]
            high[rows] = both[coarse_y - RIM :]

    folded(kept.at[1], 0, 0)
    for face in range(3):
        folded(
            faces.at[face],
            sizes_x[0] + sizes_x[1] + face * sizes_x[0],
            sizes_y[0] + sizes_y[1] + face * sizes_y[0],
        )
    base_x, base_y = sizes_x[0], sizes_y[0]
    for out, start in ((low, 0), (high, ny - 2)):
        for layer in range(2):
            rows = pl.ds(base_x + layer * ny + start, 2)
            out[pl.ds(base_y + 2 * layer, 2)] = x_low[rows]
            out[pl.ds(base_y + 2 * (2 + nx + layer), 2)] = x_high[rows]
        for slab in range(nx):
            out[pl.ds(base_y + 2 * (2 + slab), 2)] = top[V, EDGE + slab, pl.ds(PAD + start, 2)]


def hand_on(first, second, _, first_out, second_out):
    first_out[...] = first[...]
    second_out[...] = second[...]


def stack_blocks(*refs):
    for index, ref in enumerate(refs[:-3]):
        refs[-1][index] = ref[...]


def pair_rows(values, stride):
    return values + roll_rows(values, -stride)


def pair_lanes(values, stride):
    return values + roll_lanes(values, -stride)


class Listed:
    def __init__(self, fx, fy, fz, stride, depth):
        self.fx, self.fy, self.fz, self.stride, self.depth = fx, fy, fz, stride, depth
        shape = fx[0].shape
        rows = shape[0]
        row, lane = rows_of(shape), lanes_of(shape)
        z = lane % depth
        count = self.count = len(fx)
        self.x_high = [
            fx[s + 1] if s + 1 < count else jnp.where(lane < LANES - depth, roll_lanes(fx[0], -depth), 0.0)
            for s in range(count)
        ]
        self.x_low = [fx[s] if s > 0 else jnp.where(lane >= depth, fx[0], 0.0) for s in range(count)]
        self.y_high = [jnp.where(row < rows - stride, roll_rows(f, -stride), 0.0) for f in fy]
        self.y_low = [jnp.where(row >= stride, f, 0.0) for f in fy]
        self.z_high = [jnp.where(z < depth - stride, roll_lanes(f, -stride), 0.0) for f in fz]
        self.z_low = [jnp.where(z >= stride, f, 0.0) for f in fz]
        self.d = [
            fx[s] + self.x_high[s] + fy[s] + self.y_high[s] + fz[s] + self.z_high[s] for s in range(count)
        ]
        self.w = [jnp.where(d > 0.0, OMEGA / jnp.where(d > 0.0, d, 1.0), 0.0) for d in self.d]

    def weighted(self, v, f):
        count = self.count
        out = []
        for s in range(count):
            low = v[s - 1] if s > 0 else roll_lanes(v[count - 1], self.depth)
            high = v[s + 1] if s + 1 < count else roll_lanes(v[0], -self.depth)
            x = self.x_low[s] * low + self.x_high[s] * high
            y = self.y_low[s] * roll_rows(v[s], self.stride) + self.y_high[s] * roll_rows(v[s], -self.stride)
            z = self.z_low[s] * roll_lanes(v[s], self.stride) + self.z_high[s] * roll_lanes(v[s], -self.stride)
            total = (f[s] + y) + (x + z)
            out.append(total)
        return out

    def sweep(self, v, f):
        totals = self.weighted(v, f)
        return [(1.0 - OMEGA) * v[s] + self.w[s] * totals[s] for s in range(self.count)]

    def sweeps(self, count, f):
        folded = [
            [w * c for w, c in zip(self.w, coefficients)]
            for coefficients in (self.x_low, self.x_high, self.y_low, self.y_high, self.z_low, self.z_high)
        ]
        scaled = self.start(f)
        slabs = self.count

        def step(index, v):
            out = []
            for s in range(slabs):
                low = v[s - 1] if s > 0 else roll_lanes(v[slabs - 1], self.depth)
                high = v[s + 1] if s + 1 < slabs else roll_lanes(v[0], -self.depth)
                x = folded[0][s] * low + folded[1][s] * high
                y = folded[2][s] * roll_rows(v[s], self.stride) + folded[3][s] * roll_rows(v[s], -self.stride)
                z = folded[4][s] * roll_lanes(v[s], self.stride) + folded[5][s] * roll_lanes(v[s], -self.stride)
                out.append((((1.0 - OMEGA) * v[s] + scaled[s]) + y) + (x + z))
            return out

        return lax.fori_loop(1, count, step, scaled)

    def start(self, f):
        return [self.w[s] * f[s] for s in range(self.count)]

    def residual(self, v, f):
        totals = self.weighted(v, f)
        return [totals[s] - self.d[s] * v[s] for s in range(self.count)]

    def kept(self):
        shape = self.fx[0].shape
        step = 2 * self.stride
        return (rows_of(shape) % step == 0) & (lanes_of(shape) % step == 0)

    def coarser(self):
        keep, stride = self.kept(), self.stride
        half = range(self.count // 2)

        def kept(values):
            return jnp.where(keep, 0.25 * values, 0.0)

        fx = [kept(pair_lanes(pair_rows(self.fx[2 * s], stride), stride)) for s in half]
        fy = [kept(pair_lanes(self.fy[2 * s] + self.fy[2 * s + 1], stride)) for s in half]
        fz = [kept(pair_rows(self.fz[2 * s] + self.fz[2 * s + 1], stride)) for s in half]
        return Listed(fx, fy, fz, 2 * stride, self.depth)

    def restrict(self, r):
        keep, stride = self.kept(), self.stride
        return [
            jnp.where(keep, 0.5 * pair_lanes(pair_rows(r[2 * s] + r[2 * s + 1], stride), stride), 0.0)
            for s in range(self.count // 2)
        ]

    def prolong(self, e):
        out = []
        for values in e:
            values = values + roll_rows(values, self.stride)
            values = values + roll_lanes(values, self.stride)
            out += [values, values]
        return out


def listed_cycle(levels, sweeps, f):
    level = levels[0]
    if len(levels) == 1:
        return level.sweeps(sweeps, f)
    v = level.sweep(level.start(f), f)
    e = listed_cycle(levels[1:], sweeps, level.restrict(level.residual(v, f)))
    v = [a + b for a, b in zip(v, level.prolong(e))]
    return level.sweep(level.sweep(v, f), f)


def level_two(axes, grid, sweeps, shape, pieces, out, wide, tall):
    devices_x, devices_y = grid
    me_x, me_y = lax.axis_index(axes[0]), lax.axis_index(axes[1])
    own_x, own_y = shape
    quarter = LANES // 4
    reach = RIM // 2
    blocks = 4
    count = devices_x * own_x // blocks
    rows = devices_y * own_y
    main = pl.ds(PAD, rows)
    window = own_y + RIM

    def piece(gx, gy):
        slow, far = (me_x // 2) ^ (gx // 2), (me_y // 2) ^ (gy // 2)
        return ((me_y + gy) % 2, (me_x + gx) % 2 * (devices_y // 2) + far, slow)

    for ref in (wide, tall):
        ref[...] = jnp.zeros(ref.shape, F32)
    lane = lanes_of((window, LANES))
    for gy in range(devices_y):
        sums = [None] * count
        for gx in range(devices_x):
            where = piece(gx, gy)
            first = pieces[where + (pl.ds(0, window),)]
            second = pieces[where + (pl.ds(window, window // 2),)]
            for local in range(1, 2 * blocks - 1):
                x = own_x * gx - reach + local
                if not 0 <= x < devices_x * own_x:
                    continue
                block, slab = x // count, x % count
                if local <= blocks:
                    moved = roll_lanes(first, (block - local + 1) * quarter)
                else:
                    at = 2 * (local - blocks - 1)
                    halves = [roll_lanes(second, (block - at - odd) * quarter) for odd in range(2)]
                    moved = jnp.concatenate(halves)
                moved = jnp.where(lane // quarter == block, moved, 0.0)
                sums[slab] = moved if sums[slab] is None else sums[slab] + moved
        place = pl.ds(PAD + own_y * gy - reach, window)
        for slab in range(count):
            tall[slab, place] = tall[slab, place] + sums[slab]
    f = [tall[slab, main] for slab in range(count)]

    lane = lanes_of((rows, LANES))
    for gx in range(devices_x):
        for gy in range(devices_y):
            where = piece(gx, gy)
            for face in range(3):
                values = pieces[where + (pl.ds(window + window // 2 + face * own_y, own_y),)]
                wide[face, gx, gy * own_y : (gy + 1) * own_y] = values
    faces = []
    for face in range(3):
        slabs = [None] * count
        for gx in range(devices_x):
            values = wide[face, gx]
            for local in range(own_x):
                x = own_x * gx + local
                block, slab = x // count, x % count
                moved = roll_lanes(values, (block - local) * quarter)
                moved = jnp.where(lane // quarter == block, moved, 0.0)
                slabs[slab] = moved if slabs[slab] is None else slabs[slab] + moved
        faces.append(slabs)
    levels = [Listed(*faces, 1, quarter)]
    while len(levels) < LEVELS - 2:
        levels.append(levels[-1].coarser())
    e = listed_cycle(levels, sweeps, f)

    for slab in range(count):
        out[reach + slab, main] = e[slab]
    for slab in range(reach):
        out[slab, main] = jnp.where(lane < quarter, 0.0, roll_lanes(e[count - reach + slab], quarter))
        out[reach + count + slab, main] = jnp.where(
            lane >= LANES - quarter, 0.0, roll_lanes(e[slab], -quarter)
        )
    out[:, :PAD] = jnp.zeros((count + 2 * reach, PAD, LANES), F32)
    out[:, PAD + rows :] = jnp.zeros((count + 2 * reach, PAD, LANES), F32)


def level_up(axes, grid, coarse, top, kept, faces, x_low, x_high, y_low, y_high, *refs):
    out, mid, one, two, right, post, up = refs
    devices_x, devices_y = grid
    me_x, me_y = lax.axis_index(axes[0]), lax.axis_index(axes[1])
    coarse_x, coarse_y = faces.shape[1:3]
    nx, ny = out.shape[:2]
    own_x, own_y = coarse_x // 2, coarse_y // 2
    quarter = LANES // 4
    reach = RIM // 2
    window = own_y + RIM

    slabs, high = coarse_x + 2 * RIM, coarse_y + 2 * RIM
    half = slabs // 2
    inner = pl.ds(2 * RIM, coarse_y)
    body = pl.ds(RIM, high)
    sizes_x, sizes_y = rim_rows_x(nx, ny), rim_rows_y(nx, ny)
    for face, slot in enumerate((FX, FY, ZL)):
        clear_pads(mid.at[slot], high)
        mid[slot, RIM : RIM + coarse_x, inner] = faces[face]
        place_x = sizes_x[0] + sizes_x[1] + face * sizes_x[0]
        place_y = sizes_y[0] + sizes_y[1] + face * sizes_y[0]
        for layer in range(RIM):
            mid[slot, layer, inner] = rim_slab(x_low, place_x, coarse_y, layer)
            mid[slot, RIM + coarse_x + layer, inner] = rim_slab(x_high, place_x, coarse_y, layer)
        for slab in range(half):
            place = pl.ds(place_y + slab * RIM, RIM)
            for message, row in ((y_low, RIM), (y_high, 2 * RIM + coarse_y)):
                pair = one_of_two(message[place])
                mid[slot, slab, row : row + RIM] = pair[0]
                mid[slot, slab + half, row : row + RIM] = pair[1]
    row_inside = (rows_of((high, LANES)) >= RIM) | (me_y > 0)
    for slab in range(slabs - 1):
        inside = row_inside & (me_x > 0) if slab < RIM else row_inside
        set_weights(mid, slab, RIM, high, HALF, inside)
    clear_pads(one, high)
    clear_pads(right, high)
    clear_pads(two, high)
    one[RIM : RIM + coarse_x, inner] = kept[1]
    right[RIM : RIM + coarse_x, inner] = kept[0]
    for layer in range(RIM):
        one[layer, inner] = rim_slab(x_low, 0, coarse_y, layer)
        one[RIM + coarse_x + layer, inner] = rim_slab(x_high, 0, coarse_y, layer)
    for slab in range(half):
        place = pl.ds(slab * RIM, RIM)
        for message, row in ((y_low, RIM), (y_high, 2 * RIM + coarse_y)):
            pair = one_of_two(message[place])
            one[slab, row : row + RIM] = pair[0]
            one[slab + half, row : row + RIM] = pair[1]
    row = rows_of((high, LANES))
    own_row = (row >= RIM) & (row < RIM + coarse_y)
    for slab in range(1, slabs - 1):
        f_rim = one[slab, body] * mid[D, slab, body] * (1.0 / OMEGA)
        if RIM <= slab < RIM + coarse_x:
            f_rim = jnp.where(own_row, right[slab, body], f_rim)
        right[slab, body] = f_rim
        two[slab, body] = swept(mid, one, slab, RIM, high, right)

    per_block = (coarse.shape[0] - 2 * reach) // own_x
    base = me_x % per_block * own_x
    mine = None
    for gy in range(devices_y):
        place = pl.ds(PAD + gy * own_y - reach, window)
        values = jnp.where(me_y == gy, coarse[pl.ds(base, half), place, :], 0.0)
        mine = values if mine is None else mine + values
    source = lax.broadcasted_iota(jnp.int32, (LANES, LANES), 0)
    target = lax.broadcasted_iota(jnp.int32, (LANES, LANES), 1)
    hit = (source == me_x // per_block * quarter + target // 2) & (target < HALF)
    fine = exact_dot(mine.reshape(half * window, LANES), jnp.where(hit, 1.0, 0.0).astype(F32))
    fine = fine.reshape(half, window, LANES)
    for odd in range(2):
        up[:half, pl.ds(odd, window, stride=2), :] = fine
    for pair in range(half):
        for slab in (2 * pair, 2 * pair + 1):
            if 1 <= slab < slabs - 1:
                two[slab, body] = two[slab, body] + up[pair, :high]
    for slab in range(2, slabs - 2):
        one[slab, body] = swept(mid, two, slab, RIM, high, right)
    for slab in range(3, slabs - 3):
        two[slab, body] = swept(mid, one, slab, RIM, high, right)

    steps = coarse_x + 2
    fine_rows = ny + 2 * RIM
    e = two[RIM - 1 : RIM - 1 + steps, body]
    fine = exact_dot(e.reshape(steps * high, LANES), expand(LANES, 0)).reshape(steps, high, LANES)
    fine = fine[:, reach : reach + fine_rows // 2]
    for odd in range(2):
        up[:, pl.ds(odd, fine_rows // 2, stride=2), :] = fine
    body = pl.ds(RIM, fine_rows)
    for slot in (0, 1):
        clear_pads(post.at[slot], fine_rows)
    inner = pl.ds(PAD, ny)
    post[0, EDGE : EDGE + nx, inner] = top[V, EDGE : EDGE + nx, inner]
    base_x, base_y = RIM // 2 * coarse_y, half * RIM
    for layer in range(2):
        place = pl.ds(base_x + layer * ny, ny)
        post[0, EDGE - 2 + layer, inner] = x_low[place]
        post[0, EDGE + nx + layer, inner] = x_high[place]
    for slab in range(nx + 4):
        place = pl.ds(base_y + 2 * slab, 2)
        post[0, slab + EDGE - 2, RIM:PAD] = jnp.zeros((RIM, LANES), F32)
        post[0, slab + EDGE - 2, PAD + ny : PAD + ny + RIM] = jnp.zeros((RIM, LANES), F32)
        post[0, slab + EDGE - 2, PAD - 2 : PAD] = y_low[place]
        post[0, slab + EDGE - 2, PAD + ny : PAD + ny + 2] = y_high[place]

    def raise_level(index):
        for slab in (EDGE - 2 + 2 * index, EDGE - 1 + 2 * index):
            post[0, slab, body] = post[0, slab, body] + up[index]

    run(steps, raise_level)

    def fifth(index):
        slab = EDGE - 1 + index
        post[1, slab, body] = swept(top, post.at[0], slab, RIM, fine_rows)

    run(nx + 2, fifth)

    def sixth(index):
        out[index] = swept(top, post.at[1], EDGE + index, PAD, ny)

    run(nx, sixth)


IN_VMEM = pl.BlockSpec(memory_space=pltpu.VMEM)


def call(kernel, outs, scratch=(), from_hbm=False):
    ins = pl.BlockSpec(memory_space=pl.ANY) if from_hbm else IN_VMEM

    def launch(*args):
        if from_hbm:
            args = [pltpu.with_memory_space_constraint(arg, pltpu.HBM) for arg in args]
        return pl.pallas_call(
            kernel,
            out_shape=[pltpu.VMEM(shape, F32) for shape in outs],
            in_specs=[ins] * len(args),
            out_specs=[IN_VMEM] * len(outs),
            scratch_shapes=[pltpu.VMEM(s, F32) if isinstance(s, tuple) else s for s in scratch],
            compiler_params=pltpu.CompilerParams(vmem_limit_bytes=24 * 2**20),
        )(*args)

    return launch


def pair_route(axis):
    return [(i, i ^ 1) for i in range(lax.axis_size(axis))]


def swap_route(axis):
    count = lax.axis_size(axis)
    return [(i, (i + 1 ^ 1) - 1) for i in range(1, count - 1)]


def by_partner(low, high, axis):
    odd = lax.axis_index(axis) % 2 == 1
    return jnp.where(odd, low, high), jnp.where(odd, high, low)


def from_sides(low, high, axis):
    pair, swap = by_partner(low, high, axis)
    pair = lax.ppermute(pair, axis, pair_route(axis))
    swap = lax.ppermute(swap, axis, swap_route(axis))
    return by_partner(pair, swap, axis)


def passed_round(block, axis, stride):
    count = lax.axis_size(axis)
    return [block] + [
        lax.ppermute(block, axis, [(i, i ^ distance) for i in range(count)])
        for distance in range(stride, count, stride)
    ]


def passed_across(block):
    count, size = lax.axis_size("gx"), lax.axis_size("gy")
    blocks = []
    for side in range(2):
        for distance in range(0, size, 2):
            route = [
                (x * size + y, (x ^ side) * size + (y ^ distance)) for x in range(count) for y in range(size)
            ]
            moved = side + distance > 0
            blocks.append(lax.ppermute(block, ("gx", "gy"), route) if moved else block)
    return blocks


def fused_cycle(*fields):
    axes = ("gx", "gy")
    devices_x, devices_y = lax.axis_size("gx"), lax.axis_size("gy")
    nx, ny, nz = fields[0].shape
    coarse_x, coarse_y = nx // 2, ny // 2
    x_shape, y_shape = (x_rows(nx, ny), LANES), (y_rows(nx, ny), LANES)
    own, x_low, x_high = call(
        start_pack, [(5, nx, ny, nz), x_shape, x_shape], [pltpu.SemaphoreType.DMA((5,))], True
    )(*fields)
    x_low, x_high = from_sides(x_low, x_high, "gx")
    faces, coefficients = call(
        coarse_faces,
        [(3, coarse_x, coarse_y, LANES), (16, LANES)],
        [(coarse_x, ny, LANES), (coarse_x // 2, coarse_y, LANES)],
    )(own)
    y_low, y_high = call(pack_y, [y_shape] * 2)(own, x_low, x_high)
    y_low, y_high = from_sides(y_low, y_high, "gy")
    stack = (nx + 2 * EDGE, ny + 4 * RIM, LANES)
    stack_1 = (coarse_x + 2 * RIM, coarse_y + 4 * RIM, LANES)
    half = stack_1[0] // 2
    v_shape = (sum(rim_rows_x(nx, ny)), LANES)
    w_shape = (sum(rim_rows_y(nx, ny)), LANES)
    top, kept, chunk, v_low, v_high = call(
        functools.partial(level_down, axes),
        [(D + 1,) + stack, (2, coarse_x, coarse_y, LANES), (BLOCK_ROWS, LANES), v_shape, v_shape],
        [
            stack,
            (nx // 2, ny, LANES),
            stack_1,
            (half, coarse_y + 2 * RIM, LANES),
            (D + 1,) + stack_1,
            (coarse_x + 3,) + stack[1:],
        ],
    )(own, faces, coefficients, x_low, x_high, y_low, y_high)

    blocks = passed_round(chunk, "gx", 2)
    v_low, v_high = call(hand_on, [v_shape, v_shape])(v_low, v_high, blocks[1])
    v_low, v_high = from_sides(v_low, v_high, "gx")
    slow = (len(blocks),) + chunk.shape
    (pieces,) = call(stack_blocks, [slow])(*blocks, v_low, v_high)
    blocks = passed_across(pieces.reshape(-1, LANES))
    w_low, w_high = call(pack_v, [w_shape] * 2)(top, kept, faces, v_low, v_high)
    pair, swap = by_partner(w_low, w_high, "gy")
    message = jnp.concatenate(blocks + [pair])
    swap = lax.ppermute(swap, "gy", swap_route("gy"))
    other = lax.ppermute(message, "gy", pair_route("gy"))
    rows = message.shape[0] - w_shape[0]
    pieces = jnp.stack((message[:rows], other[:rows])).reshape((2, len(blocks)) + slow)
    w_low, w_high = by_partner(other[rows:], swap, "gy")
    count = devices_x * nx // 16
    rows = devices_y * ny // 4
    grid = (devices_x, devices_y)
    coarsest = (devices_x * nx >> LEVELS - 1, devices_y * ny >> LEVELS - 1)
    wide = (count + RIM, rows + 2 * PAD, LANES)
    (coarse,) = call(
        functools.partial(level_two, axes, grid, 4 * max(coarsest), (nx // 4, ny // 4)),
        [wide],
        [(3, devices_x, rows, LANES), wide],
    )(pieces)
    return pl.pallas_call(
        functools.partial(level_up, axes, grid),
        out_shape=jax.ShapeDtypeStruct((nx, ny, nz), F32),
        in_specs=[IN_VMEM] * 8,
        out_specs=IN_VMEM,
        scratch_shapes=[
            pltpu.VMEM(shape, F32)
            for shape in ((D + 1,) + stack_1, stack_1, stack_1, stack_1, (2,) + stack, (coarse_x + 2, ny + 2 * RIM, LANES))
        ],
        compiler_params=pltpu.CompilerParams(vmem_limit_bytes=24 * 2**20),
    )(coarse, top, kept, faces, v_low, v_high, w_low, w_high)


def with_halo(block, sides, width):
    for axis, dim in sides:
        count = lax.axis_size(axis)
        forward = [(i, i + 1) for i in range(count - 1)]
        backward = [(target, source) for source, target in forward]
        low = lax.ppermute(
            lax.slice_in_dim(block, block.shape[dim] - width, None, axis=dim), axis, forward
        )
        high = lax.ppermute(lax.slice_in_dim(block, 0, width, axis=dim), axis, backward)
        block = jnp.concatenate([low, block, high], axis=dim)
    return block


def passed_along(block, axis, distance):
    devices = range(lax.axis_size(axis))
    route = [(i - distance, i) for i in devices if i - distance in devices]
    return lax.ppermute(block, axis, route)


def stencil(padded, padded_x, padded_y, face_z):
    center = padded[1:-1, 1:-1]
    zero_plane = jnp.zeros(center.shape[:2] + (1,), center.dtype)
    above_face = jnp.concatenate((face_z[:, :, 1:], zero_plane), axis=2)
    below_z = jnp.concatenate((zero_plane, center[:, :, :-1]), axis=2)
    above_z = jnp.concatenate((center[:, :, 1:], zero_plane), axis=2)
    lower_x = padded_x[1:-1, 1:-1]
    upper_x = padded_x[2:, 1:-1]
    lower_y = padded_y[1:-1, 1:-1]
    upper_y = padded_y[1:-1, 2:]
    applied = lower_x * (center - padded[:-2, 1:-1]) + upper_x * (center - padded[2:, 1:-1])
    applied = (
        applied + lower_y * (center - padded[1:-1, :-2]) + upper_y * (center - padded[1:-1, 2:])
    )
    applied = applied + face_z * (center - below_z) + above_face * (center - above_z)
    diagonal = lower_x + upper_x + lower_y + upper_y + face_z + above_face
    return (applied, diagonal)


def jacobi_sweep(padded, source, padded_x, padded_y, face_z):
    applied, diagonal = stencil(padded, padded_x, padded_y, face_z)
    return padded[1:-1, 1:-1] + OMEGA * (source - applied) / diagonal


def pad_plane(values, width):
    return jnp.pad(values, ((width, width), (width, width), (0, 0)))


def restrict(residual):
    shape = residual.shape
    blocks = residual.reshape(shape[0] // 2, 2, shape[1] // 2, 2, shape[2] // 2, 2)
    return 4.0 * jnp.mean(blocks, axis=(1, 3, 5))


def coarsen_faces(face_x, face_y, face_z):
    shape = face_x.shape
    blocks = (shape[0] // 2, 2, shape[1] // 2, 2, shape[2] // 2, 2)
    coarse_x = jnp.mean(face_x.reshape(blocks)[:, 0], axis=(2, 4))
    coarse_y = jnp.mean(face_y.reshape(blocks)[:, :, :, 0], axis=(1, 4))
    coarse_z = jnp.mean(face_z.reshape(blocks)[..., 0], axis=(1, 3))
    return (coarse_x, coarse_y, coarse_z)


def prolong(coarse):
    return jnp.repeat(jnp.repeat(jnp.repeat(coarse, 2, axis=0), 2, axis=1), 2, axis=2)


def local_cycle(grid_level, iterate, source, face_x, face_y, face_z):
    padded_x = pad_plane(face_x, 1)
    padded_y = pad_plane(face_y, 1)
    if grid_level == LEVELS - 1:
        count = 4 * max(iterate.shape[0], iterate.shape[1])

        def one_sweep(index, values):
            return jacobi_sweep(pad_plane(values, 1), source, padded_x, padded_y, face_z)

        return lax.fori_loop(0, count, one_sweep, iterate)
    for sweep_index in range(2):
        iterate = jacobi_sweep(pad_plane(iterate, 1), source, padded_x, padded_y, face_z)
    applied, diagonal = stencil(pad_plane(iterate, 1), padded_x, padded_y, face_z)
    coarse_src = restrict(source - applied)
    coarse_x, coarse_y, coarse_z = coarsen_faces(face_x, face_y, face_z)
    correction = local_cycle(
        grid_level + 1, jnp.zeros_like(coarse_src), coarse_src, coarse_x, coarse_y, coarse_z
    )
    iterate = iterate + prolong(correction)
    for sweep_index in range(2):
        iterate = jacobi_sweep(pad_plane(iterate, 1), source, padded_x, padded_y, face_z)
    return iterate


def field_rim(iterate):
    return with_halo(iterate, (("gx", 0), ("gy", 1)), 1)


def sweep_pair_narrow(iterate, source, padded_x, padded_y, face_z, zero_start):
    for sweep_index in range(2):
        if sweep_index == 0 and zero_start:
            padded = pad_plane(iterate, 1)
        else:
            padded = field_rim(iterate)
        iterate = jacobi_sweep(padded, source, padded_x, padded_y, face_z)
    return iterate


def descend(grid_level, iterate, source, face_x, face_y, face_z, zero_start, gather_level):
    if grid_level == gather_level:
        pieces = (
            lax.all_gather(source, "gy", axis=1, tiled=True),
            lax.all_gather(face_x, "gy", axis=1, tiled=True),
            lax.all_gather(face_y, "gy", axis=1, tiled=True),
            lax.all_gather(face_z, "gy", axis=1, tiled=True),
        )
        gathered = (
            lax.all_gather(pieces[0], "gx", axis=0, tiled=True),
            lax.all_gather(pieces[1], "gx", axis=0, tiled=True),
            lax.all_gather(pieces[2], "gx", axis=0, tiled=True),
            lax.all_gather(pieces[3], "gx", axis=0, tiled=True),
        )
        correction = local_cycle(
            grid_level,
            jnp.zeros_like(gathered[0]),
            gathered[0],
            gathered[1],
            gathered[2],
            gathered[3],
        )
        start_x = lax.axis_index("gx") * source.shape[0]
        start_y = lax.axis_index("gy") * source.shape[1]
        return lax.dynamic_slice(
            correction, (start_x, start_y, jnp.zeros((), jnp.int32)), source.shape
        )
    next_x = passed_along(face_x[:1], "gx", -1)
    next_y = passed_along(face_y[:, :1], "gy", -1)
    lower_row = jnp.zeros_like(next_x)
    lower_col = jnp.zeros_like(next_y)
    padded_x = jnp.pad(
        jnp.concatenate((lower_row, face_x, next_x), axis=0), ((0, 0), (1, 1), (0, 0))
    )
    padded_y = jnp.pad(
        jnp.concatenate((lower_col, face_y, next_y), axis=1), ((1, 1), (0, 0), (0, 0))
    )

    def smoother(values, starting):
        return sweep_pair_narrow(values, source, padded_x, padded_y, face_z, starting)

    iterate = smoother(iterate, zero_start)
    applied, diagonal = stencil(field_rim(iterate), padded_x, padded_y, face_z)
    coarse_src = restrict(source - applied)
    coarse_x, coarse_y, coarse_z = coarsen_faces(face_x, face_y, face_z)
    correction = descend(
        grid_level + 1,
        jnp.zeros_like(coarse_src),
        coarse_src,
        coarse_x,
        coarse_y,
        coarse_z,
        True,
        gather_level,
    )
    iterate = iterate + prolong(correction)
    return smoother(iterate, False)


def fits(nx, ny, nz, devices_x, devices_y):
    cells = devices_x * nx * devices_y * ny * nz // 8
    even = devices_x % 8 == 0 and devices_y % 4 == 0
    even = even and devices_x & (devices_x - 1) == 0 and devices_y & (devices_y - 1) == 0
    return cells <= 2**18 and even and (nx, ny, nz) == (16, 16, LANES)


def local(source_term, initial_guess, face_x, face_y, face_z):
    if fits(*source_term.shape, lax.axis_size("gx"), lax.axis_size("gy")):
        return fused_cycle(source_term, initial_guess, face_x, face_y, face_z)
    gather_level = 4
    return descend(0, initial_guess, source_term, face_x, face_y, face_z, False, gather_level)


def solution(mesh):
    placed = (P("gx", "gy", None),) * 5
    return jax.shard_map(
        local, mesh=mesh, in_specs=placed, out_specs=P("gx", "gy", None), check_vma=False
    )
```

```python
import functools

import jax
import jax.numpy as jnp
from jax import lax
from jax.experimental import pallas as pl
from jax.experimental.pallas import tpu as pltpu
from jax.sharding import PartitionSpec as P

LEVELS = 6
OMEGA = 0.8
LANES = 128
RIM = 4
EDGE = 3
PAD = 8
BLOCK_ROWS = 24
F32 = jnp.float32

V, F, FX, FY, ZL, ZH, W, D = range(8)
SLOTS = (F, V, FX, FY, ZL)
X_LAYERS = (2, 3, 3, 2, 2)
Y_LAYERS = (2, 3, 2, 3, 2)
Y_REACH = (1, 2, 2, 2, 1)


def lanes_of(shape):
    return lax.broadcasted_iota(jnp.int32, shape, len(shape) - 1)


def rows_of(shape):
    return lax.broadcasted_iota(jnp.int32, shape, len(shape) - 2)


def roll_lanes(values, step):
    return pltpu.roll(values, step % LANES, values.ndim - 1)


def roll_rows(values, step):
    return pltpu.roll(values, step % values.shape[-2], values.ndim - 2)


def exact_dot(left, right):
    return jnp.dot(left, right, precision=lax.Precision.HIGHEST, preferred_element_type=F32)


def compact(depth, part, even_only=False):
    source = lax.broadcasted_iota(jnp.int32, (LANES, LANES), 0)
    target = lax.broadcasted_iota(jnp.int32, (LANES, LANES), 1)
    half = depth // 2
    hit = target == (source // depth * 2 + part) * half + source % depth // 2
    if even_only:
        hit = hit & (source % 2 == 0)
    return jnp.where(hit, 1.0, 0.0).astype(F32)


def expand(depth, part):
    target = lax.broadcasted_iota(jnp.int32, (LANES, LANES), 0)
    source = lax.broadcasted_iota(jnp.int32, (LANES, LANES), 1)
    half = depth // 2
    hit = target == (source // depth * 2 + part) * half + source % depth // 2
    return jnp.where(hit, 1.0, 0.0).astype(F32)


def merge_lanes(values, depth, even_only=False):
    count, rows, _ = values.shape
    half = count // 2
    flat = values.reshape(2, half * rows, LANES)
    out = exact_dot(flat[0], compact(depth, 0, even_only))
    out = out + exact_dot(flat[1], compact(depth, 1, even_only))
    return out.reshape(half, rows, LANES)


def even_rows(ref, rows):
    return ref[:, pl.ds(0, rows // 2, stride=2), :]


def odd_rows(ref, rows):
    return ref[:, pl.ds(1, rows // 2, stride=2), :]


HALF = LANES // 2


def low_half(values):
    return jnp.where(lanes_of(values.shape) < HALF, values, 0.0)


def two_in_one(first, second):
    return first + roll_lanes(second, HALF)


def one_of_two(values):
    return low_half(values), low_half(roll_lanes(values, HALF))


def x_rows(nx, ny):
    return sum(X_LAYERS) * ny


def y_rows(nx, ny):
    return sum(layers * (nx + 2 * reach) for layers, reach in zip(Y_LAYERS, Y_REACH))


def rim_rows_x(nx, ny):
    slab = RIM // 2 * (ny // 2)
    return slab, 2 * ny, 3 * slab


def rim_rows_y(nx, ny):
    slabs = (nx // 2 + 2 * RIM) // 2 * RIM
    return slabs, 2 * (nx + 4), 3 * slabs


def x_place(index, layer, ny):
    return pl.ds((sum(X_LAYERS[:index]) + layer) * ny, ny)


def y_place(index, slab, nx):
    before = zip(Y_LAYERS[:index], Y_REACH[:index])
    start = sum(layers * (nx + 2 * reach) for layers, reach in before)
    return pl.ds(start + (Y_REACH[index] + slab) * Y_LAYERS[index], Y_LAYERS[index])


def start_pack(*refs):
    fields, (own, x_low, x_high, done) = refs[:5], refs[5:]
    copies = [pltpu.make_async_copy(ref, own.at[index], done.at[index]) for index, ref in enumerate(fields)]
    for copy in copies:
        copy.start()
    nx, ny = own.shape[1:3]
    for index, copy in enumerate(copies):
        copy.wait()
        for layer in range(X_LAYERS[index]):
            x_low[x_place(index, layer, ny)] = own[index, layer]
            x_high[x_place(index, layer, ny)] = own[index, nx - X_LAYERS[index] + layer]


def pair_slabs(ref):
    count = ref.shape[0]
    values = ref[...].reshape((count // 2, 2) + ref.shape[1:])
    return values[:, 0], values[:, 1]


def wide_slab(slab, from_low, own, from_high):
    count = own.shape[0]
    if slab < RIM:
        return from_low(slab)
    if slab < RIM + count:
        return own[slab - RIM]
    return from_high(slab - RIM - count)


def rim_slab(ref, base, rows, layer):
    place = pl.ds(base + layer % (RIM // 2) * rows, rows)
    return one_of_two(ref[place])[layer // (RIM // 2)]


def pack_y(own, x_low, x_high, low, high):
    nx, ny = own.shape[1:3]
    for index in range(5):
        width, layers, reach = Y_LAYERS[index], X_LAYERS[index], Y_REACH[index]
        for out, start in ((low, 0), (high, ny - width)):
            for slab in range(nx):
                out[y_place(index, slab, nx)] = own[index, slab, start : start + width]
            for layer in range(reach):
                rows = pl.ds(x_place(index, layers - reach + layer, ny).start + start, width)
                out[y_place(index, layer - reach, nx)] = x_low[rows]
                rows = pl.ds(x_place(index, layer, ny).start + start, width)
                out[y_place(index, nx + layer, nx)] = x_high[rows]


def fold_four(slabs, even_only=False):
    out = None
    for part in range(2):
        term = exact_dot(two_in_one(slabs[part], slabs[2 + part]), compact(HALF, part, even_only))
        out = term if out is None else out + term
    return out


def coarse_slab_sums(ref_x, ref_y, ref_z, count, first, tmp):
    extra = tmp.shape[0]
    rows = tmp.shape[1]
    for index in range(extra):
        tmp[index] = ref_x[first + 2 * index]
    x = even_rows(tmp, rows) + odd_rows(tmp, rows)
    for index in range(count):
        tmp[index] = ref_y[first + 2 * index] + ref_y[first + 2 * index + 1]
    y = even_rows(tmp, rows)[:count]
    for index in range(count):
        tmp[index] = ref_z[first + 2 * index] + ref_z[first + 2 * index + 1]
    return x, y, (even_rows(tmp, rows) + odd_rows(tmp, rows))[:count]


def halved(values, even_only=False):
    count, rows, _ = values.shape
    flat = exact_dot(values.reshape(count * rows, LANES), compact(LANES, 0, even_only))
    return 0.25 * flat.reshape(count, rows, LANES)


def coarse_faces(own, faces, out, fine, tmp):
    x, y, z = coarse_slab_sums(own.at[2], own.at[3], own.at[4], own.shape[1] // 2, 0, fine)
    faces[0] = halved(x)
    faces[1] = halved(y)
    faces[2] = halved(z, True)
    rows = faces.shape[2]
    coarse = rows // 2
    fx, fy, fz = faces.at[0], faces.at[1], faces.at[2]
    tmp[...] = pair_slabs(fx)[0]
    x = even_rows(tmp, rows) + odd_rows(tmp, rows)
    first, second = pair_slabs(fy)
    tmp[...] = first + second
    y = even_rows(tmp, rows)
    first, second = pair_slabs(fz)
    tmp[...] = first + second
    z = even_rows(tmp, rows) + odd_rows(tmp, rows)
    out[...] = jnp.zeros(out.shape, F32)
    out[:coarse] = 0.25 * fold_four([x[i] for i in range(4)])
    out[coarse : 2 * coarse] = 0.25 * fold_four([y[i] for i in range(4)])
    out[2 * coarse : 3 * coarse] = 0.25 * fold_four([z[i] for i in range(4)], True)


def weighted(lev, src, slab, start, rows, f=None):
    here = pl.ds(start, rows)
    below = pl.ds(start - 1, rows)
    above = pl.ds(start + 1, rows)
    v = src[slab, here]
    f = lev.at[F] if f is None else f
    x = lev[FX, slab, here] * src[slab - 1, here] + lev[FX, slab + 1, here] * src[slab + 1, here]
    y = lev[FY, slab, here] * src[slab, below] + lev[FY, slab, above] * src[slab, above]
    z = lev[ZL, slab, here] * roll_lanes(v, 1) + lev[ZH, slab, here] * roll_lanes(v, -1)
    total = ((x + y) + f[slab, here]) + z
    return v, total


def swept(lev, src, slab, start, rows, f=None):
    v, total = weighted(lev, src, slab, start, rows, f)
    return (1.0 - OMEGA) * v + lev[W, slab, pl.ds(start, rows)] * total


def set_weights(lev, slab, start, rows, depth, inside=None):
    here = pl.ds(start, rows)
    fz = lev[ZL, slab, here]
    z = lanes_of(fz.shape) % depth
    upper = jnp.where(z == depth - 1, 0.0, roll_lanes(fz, -1))
    diagonal = lev[FX, slab, here] + lev[FX, slab + 1, here]
    diagonal = diagonal + lev[FY, slab, here] + lev[FY, slab, pl.ds(start + 1, rows)] + fz + upper
    valid = diagonal > 0.0
    if inside is not None:
        valid = valid & inside
    lev[ZL, slab, here] = jnp.where(z == 0, 0.0, fz)
    lev[ZH, slab, here] = upper
    lev[D, slab, here] = diagonal
    lev[W, slab, here] = jnp.where(valid, OMEGA / jnp.where(valid, diagonal, 1.0), 0.0)


def run(count, body):
    for index in range(count):
        body(index)


def clear_pads(ref, rows):
    for start in (0, RIM + rows):
        ref[:, start : start + RIM] = jnp.zeros((ref.shape[0], RIM, LANES), F32)


def level_down(axes, own, faces, coefficients, x_low, x_high, y_low, y_high, *refs):
    top, kept, chunk, v_low, v_high, other, tmp, one, two, mid, wide = refs
    nx, ny = own.shape[1:3]
    slabs, rows = nx + 2 * EDGE, ny + 2 * RIM
    me_x, me_y = lax.axis_index(axes[0]), lax.axis_index(axes[1])
    inner = pl.ds(PAD, ny)
    for index, slot in enumerate(SLOTS):
        layers, width = X_LAYERS[index], Y_LAYERS[index]
        top[slot, :, :PAD] = jnp.zeros((slabs, PAD, LANES), F32)
        top[slot, :, PAD + ny :] = jnp.zeros((slabs, PAD, LANES), F32)
        top[slot, EDGE : EDGE + nx, inner] = own[index]
        for layer in range(EDGE):
            if layer < layers:
                top[slot, EDGE - layers + layer, inner] = x_low[x_place(index, layer, ny)]
                top[slot, EDGE + nx + layer, inner] = x_high[x_place(index, layer, ny)]
            else:
                top[slot, EDGE - 1 - layer, inner] = jnp.zeros((ny, LANES), F32)
                top[slot, EDGE + nx + layer, inner] = jnp.zeros((ny, LANES), F32)
        for slab in range(-Y_REACH[index], nx + Y_REACH[index]):
            top[slot, EDGE + slab, PAD - width : PAD] = y_low[y_place(index, slab, nx)]
            top[slot, EDGE + slab, PAD + ny : PAD + ny + width] = y_high[y_place(index, slab, nx)]
    clear_pads(other, rows)

    coarse_x, coarse_y = nx // 2, ny // 2
    near = RIM - 1
    for slot in (FX, FY, ZL, ZH, W, D):
        mid[slot] = jnp.zeros(mid.shape[1:], F32)
    x, y, z = coarse_slab_sums(top.at[FX], top.at[FY], top.at[ZL], coarse_x + 2, EDGE - 2, wide)
    mid[FX, near : near + coarse_x + 3, RIM : 3 * RIM + coarse_y] = halved(x)
    mid[FY, near : near + coarse_x + 2, RIM : 3 * RIM + coarse_y] = halved(y)
    mid[ZL, near : near + coarse_x + 2, RIM : 3 * RIM + coarse_y] = halved(z, True)

    row_inside = (rows_of((rows, LANES)) >= RIM) | (me_y > 0)
    main = pl.ds(RIM, rows)
    start_v = top.at[V]

    def first(index):
        slab = index + 1
        inside = row_inside & ((slab >= EDGE) | (me_x > 0))
        set_weights(top, slab, RIM, rows, LANES, inside)
        other[slab, main] = swept(top, start_v, slab, RIM, rows)

    run(slabs - 2, first)

    def second(index):
        slab = index + 2
        top[V, slab, main] = swept(top, other, slab, RIM, rows)

    run(slabs - 4, second)

    def rest(slab):
        v, total = weighted(top, top.at[V], slab, PAD, ny)
        return total - top[D, slab, inner] * v

    def residual(index):
        slab = EDGE + 2 * index
        tmp[index] = rest(slab) + rest(slab + 1)

    run(nx // 2, residual)

    slabs, rows = coarse_x + 2 * RIM, coarse_y + 2 * RIM
    half = slabs // 2
    inner = pl.ds(2 * RIM, coarse_y)
    main = pl.ds(RIM, rows)
    row_inside = (rows_of((rows, LANES)) >= RIM) | (me_y > 0)
    for slab in range(near, near + coarse_x + 2):
        inside = row_inside & (me_x > 0) if slab < RIM else row_inside
        set_weights(mid, slab, RIM, rows, HALF, inside)

    source = even_rows(tmp, ny) + odd_rows(tmp, ny)
    source = 0.5 * exact_dot(source.reshape(coarse_x * coarse_y, LANES), compact(LANES, 0))
    for ref in (mid.at[F], mid.at[V], one):
        ref[...] = jnp.zeros(ref.shape, F32)
    mid[F, RIM : RIM + coarse_x, inner] = source.reshape(coarse_x, coarse_y, LANES)
    for slab in range(RIM, RIM + coarse_x):
        mid[V, slab, inner] = mid[W, slab, inner] * mid[F, slab, inner]
    for layer in range(RIM // 2):
        near, far = RIM + layer, coarse_x + layer
        v_low[layer * coarse_y : (layer + 1) * coarse_y] = two_in_one(
            mid[V, near, inner], mid[V, near + RIM // 2, inner]
        )
        v_high[layer * coarse_y : (layer + 1) * coarse_y] = two_in_one(
            mid[V, far, inner], mid[V, far + RIM // 2, inner]
        )
    kept[0] = mid[F, RIM : RIM + coarse_x, inner]
    kept[1] = mid[V, RIM : RIM + coarse_x, inner]
    base, after, _ = rim_rows_x(nx, ny)
    pairs = RIM // 2
    for face in range(3):
        for layer in range(pairs):
            place = pl.ds(base + after + (face * pairs + layer) * coarse_y, coarse_y)
            far = coarse_x - RIM + layer
            v_low[place] = two_in_one(faces[face, layer], faces[face, layer + pairs])
            v_high[place] = two_in_one(faces[face, far], faces[face, far + pairs])
    for layer in range(2):
        place = pl.ds(base + layer * ny, ny)
        v_low[place] = top[V, EDGE + layer, pl.ds(PAD, ny)]
        v_high[place] = top[V, EDGE + nx - 2 + layer, pl.ds(PAD, ny)]
    for slab in range(RIM - 1, RIM + coarse_x + 1):
        one[slab, main] = swept(mid, mid.at[V], slab, RIM, rows)

    def rest_1(slab):
        v, total = weighted(mid, one, slab, RIM, rows)
        return total - mid[D, slab, main] * v

    two[...] = jnp.zeros(two.shape, F32)
    for pair in range(1, half - 1):
        two[pair] = rest_1(2 * pair) + rest_1(2 * pair + 1)
    pieces = even_rows(two, rows) + odd_rows(two, rows)
    coarse_rows, quarter_rows = rows // 2, rows // 4
    chunk[:coarse_rows] = 0.5 * fold_four([pieces[1 + i] for i in range(4)])
    rest_of = [pieces[5 + i // 2][i % 2 * quarter_rows :][:quarter_rows] for i in range(4)]
    chunk[coarse_rows : coarse_rows + quarter_rows] = 0.5 * fold_four(rest_of)
    chunk[coarse_rows + quarter_rows :] = coefficients[:BLOCK_ROWS - coarse_rows - quarter_rows]
    block = me_x // (lax.axis_size(axes[0]) // 4)
    values = chunk[...]
    for turn in range(1, 4):
        chunk[...] = jnp.where(block == turn, roll_lanes(values, turn * (LANES // 4)), chunk[...])


def pack_v(top, kept, faces, x_low, x_high, low, high):
    coarse_x, coarse_y = faces.shape[1:3]
    nx, ny = 2 * coarse_x, 2 * coarse_y
    slabs = coarse_x + 2 * RIM
    half = slabs // 2
    sizes_x, sizes_y = rim_rows_x(nx, ny), rim_rows_y(nx, ny)

    def folded(own, place_x, place_y):
        values = [
            wide_slab(
                slab,
                lambda layer: rim_slab(x_low, place_x, coarse_y, layer),
                own,
                lambda layer: rim_slab(x_high, place_x, coarse_y, layer),
            )
            for slab in range(slabs)
        ]
        for slab in range(half):
            both = two_in_one(values[slab], values[slab + half])
            rows = pl.ds(place_y + slab * RIM, RIM)
            low[rows] = both[:RIM]
            high[rows] = both[coarse_y - RIM :]

    folded(kept.at[1], 0, 0)
    for face in range(3):
        folded(
            faces.at[face],
            sizes_x[0] + sizes_x[1] + face * sizes_x[0],
            sizes_y[0] + sizes_y[1] + face * sizes_y[0],
        )
    base_x, base_y = sizes_x[0], sizes_y[0]
    for out, start in ((low, 0), (high, ny - 2)):
        for layer in range(2):
            rows = pl.ds(base_x + layer * ny + start, 2)
            out[pl.ds(base_y + 2 * layer, 2)] = x_low[rows]
            out[pl.ds(base_y + 2 * (2 + nx + layer), 2)] = x_high[rows]
        for slab in range(nx):
            out[pl.ds(base_y + 2 * (2 + slab), 2)] = top[V, EDGE + slab, pl.ds(PAD + start, 2)]


def stack_blocks(*refs):
    for index, ref in enumerate(refs[:-3]):
        refs[-1][index] = ref[...]


def pair_rows(values, stride):
    return values + roll_rows(values, -stride)


def pair_lanes(values, stride):
    return values + roll_lanes(values, -stride)


class Listed:
    def __init__(self, fx, fy, fz, stride, depth):
        self.fx, self.fy, self.fz, self.stride, self.depth = fx, fy, fz, stride, depth
        shape = fx[0].shape
        rows = shape[0]
        row, lane = rows_of(shape), lanes_of(shape)
        z = lane % depth
        count = self.count = len(fx)
        self.x_high = [
            fx[s + 1] if s + 1 < count else jnp.where(lane < LANES - depth, roll_lanes(fx[0], -depth), 0.0)
            for s in range(count)
        ]
        self.x_low = [fx[s] if s > 0 else jnp.where(lane >= depth, fx[0], 0.0) for s in range(count)]
        self.y_high = [jnp.where(row < rows - stride, roll_rows(f, -stride), 0.0) for f in fy]
        self.y_low = [jnp.where(row >= stride, f, 0.0) for f in fy]
        self.z_high = [jnp.where(z < depth - stride, roll_lanes(f, -stride), 0.0) for f in fz]
        self.z_low = [jnp.where(z >= stride, f, 0.0) for f in fz]
        self.d = [
            fx[s] + self.x_high[s] + fy[s] + self.y_high[s] + fz[s] + self.z_high[s] for s in range(count)
        ]
        self.w = [jnp.where(d > 0.0, OMEGA / jnp.where(d > 0.0, d, 1.0), 0.0) for d in self.d]

    def weighted(self, v, f):
        count = self.count
        out = []
        for s in range(count):
            low = v[s - 1] if s > 0 else roll_lanes(v[count - 1], self.depth)
            high = v[s + 1] if s + 1 < count else roll_lanes(v[0], -self.depth)
            x = self.x_low[s] * low + self.x_high[s] * high
            y = self.y_low[s] * roll_rows(v[s], self.stride) + self.y_high[s] * roll_rows(v[s], -self.stride)
            z = self.z_low[s] * roll_lanes(v[s], self.stride) + self.z_high[s] * roll_lanes(v[s], -self.stride)
            total = (f[s] + y) + (x + z)
            out.append(total)
        return out

    def sweep(self, v, f):
        totals = self.weighted(v, f)
        return [(1.0 - OMEGA) * v[s] + self.w[s] * totals[s] for s in range(self.count)]

    def sweeps(self, count, f):
        folded = [
            [w * c for w, c in zip(self.w, coefficients)]
            for coefficients in (self.x_low, self.x_high, self.y_low, self.y_high, self.z_low, self.z_high)
        ]
        scaled = self.start(f)
        slabs = self.count

        def step(index, v):
            out = []
            for s in range(slabs):
                low = v[s - 1] if s > 0 else roll_lanes(v[slabs - 1], self.depth)
                high = v[s + 1] if s + 1 < slabs else roll_lanes(v[0], -self.depth)
                x = folded[0][s] * low + folded[1][s] * high
                y = folded[2][s] * roll_rows(v[s], self.stride) + folded[3][s] * roll_rows(v[s], -self.stride)
                z = folded[4][s] * roll_lanes(v[s], self.stride) + folded[5][s] * roll_lanes(v[s], -self.stride)
                out.append((((1.0 - OMEGA) * v[s] + scaled[s]) + y) + (x + z))
            return out

        return lax.fori_loop(1, count, step, scaled)

    def start(self, f):
        return [self.w[s] * f[s] for s in range(self.count)]

    def residual(self, v, f):
        totals = self.weighted(v, f)
        return [totals[s] - self.d[s] * v[s] for s in range(self.count)]

    def kept(self):
        shape = self.fx[0].shape
        step = 2 * self.stride
        return (rows_of(shape) % step == 0) & (lanes_of(shape) % step == 0)

    def coarser(self):
        keep, stride = self.kept(), self.stride
        half = range(self.count // 2)

        def kept(values):
            return jnp.where(keep, 0.25 * values, 0.0)

        fx = [kept(pair_lanes(pair_rows(self.fx[2 * s], stride), stride)) for s in half]
        fy = [kept(pair_lanes(self.fy[2 * s] + self.fy[2 * s + 1], stride)) for s in half]
        fz = [kept(pair_rows(self.fz[2 * s] + self.fz[2 * s + 1], stride)) for s in half]
        return Listed(fx, fy, fz, 2 * stride, self.depth)

    def restrict(self, r):
        keep, stride = self.kept(), self.stride
        return [
            jnp.where(keep, 0.5 * pair_lanes(pair_rows(r[2 * s] + r[2 * s + 1], stride), stride), 0.0)
            for s in range(self.count // 2)
        ]

    def prolong(self, e):
        out = []
        for values in e:
            values = values + roll_rows(values, self.stride)
            values = values + roll_lanes(values, self.stride)
            out += [values, values]
        return out


def listed_cycle(levels, sweeps, f):
    level = levels[0]
    if len(levels) == 1:
        return level.sweeps(sweeps, f)
    v = level.sweep(level.start(f), f)
    e = listed_cycle(levels[1:], sweeps, level.restrict(level.residual(v, f)))
    v = [a + b for a, b in zip(v, level.prolong(e))]
    return level.sweep(level.sweep(v, f), f)


def level_two(axes, grid, sweeps, shape, pieces, out, wide, tall):
    devices_x, devices_y = grid
    me_x, me_y = lax.axis_index(axes[0]), lax.axis_index(axes[1])
    own_x, own_y = shape
    quarter = LANES // 4
    reach = RIM // 2
    blocks = 4
    count = devices_x * own_x // blocks
    rows = devices_y * own_y
    main = pl.ds(PAD, rows)
    window = own_y + RIM

    def piece(gx, gy):
        slow, far = (me_x // 2) ^ (gx // 2), (me_y // 2) ^ (gy // 2)
        return ((me_y + gy) % 2, (me_x + gx) % 2 * (devices_y // 2) + far, slow)

    for ref in (wide, tall):
        ref[...] = jnp.zeros(ref.shape, F32)
    per_block = count // own_x

    def merged(values, shift, turn):
        at = lanes_of(values[0].shape) // quarter
        out = values[0]
        for block in range(1, blocks):
            out = jnp.where(at == (shift + block) % blocks, values[block], out)
        return roll_lanes(out, (turn - shift) * quarter)

    lane = lanes_of((window, LANES))
    for gy in range(devices_y):
        sums = [None] * count
        for turn in range(per_block):
            where = [piece(block * per_block + turn, gy) for block in range(blocks)]
            first = [pieces[at + (pl.ds(0, window),)] for at in where]
            second = [pieces[at + (pl.ds(window, window // 2),)] for at in where]
            for local in range(1, 2 * blocks - 1):
                offset = own_x * turn - reach + local
                over, slab = offset // count, offset % count
                if local <= blocks:
                    moved = merged(first, local - 1, over)
                else:
                    at = 2 * (local - blocks - 1)
                    moved = jnp.concatenate([merged(second, at + odd, over) for odd in range(2)])
                if over < 0:
                    moved = jnp.where(lane // quarter == blocks - 1, 0.0, moved)
                elif over > 0:
                    moved = jnp.where(lane // quarter == 0, 0.0, moved)
                sums[slab] = moved if sums[slab] is None else sums[slab] + moved
        place = pl.ds(PAD + own_y * gy - reach, window)
        for slab in range(count):
            tall[slab, place] = tall[slab, place] + sums[slab]
    f = [tall[slab, main] for slab in range(count)]

    lane = lanes_of((rows, LANES))
    for gx in range(devices_x):
        for gy in range(devices_y):
            where = piece(gx, gy)
            for face in range(3):
                values = pieces[where + (pl.ds(window + window // 2 + face * own_y, own_y),)]
                wide[face, gx, gy * own_y : (gy + 1) * own_y] = values
    faces = []
    for face in range(3):
        slabs = []
        for turn in range(per_block):
            values = [wide[face, block * per_block + turn] for block in range(blocks)]
            slabs += [merged(values, local, 0) for local in range(own_x)]
        faces.append(slabs)
    levels = [Listed(*faces, 1, quarter)]
    while len(levels) < LEVELS - 2:
        levels.append(levels[-1].coarser())
    e = listed_cycle(levels, sweeps, f)

    for slab in range(count):
        out[reach + slab, main] = e[slab]
    for slab in range(reach):
        out[slab, main] = jnp.where(lane < quarter, 0.0, roll_lanes(e[count - reach + slab], quarter))
        out[reach + count + slab, main] = jnp.where(
            lane >= LANES - quarter, 0.0, roll_lanes(e[slab], -quarter)
        )
    out[:, :PAD] = jnp.zeros((count + 2 * reach, PAD, LANES), F32)
    out[:, PAD + rows :] = jnp.zeros((count + 2 * reach, PAD, LANES), F32)


def level_up(axes, grid, coarse, top, kept, faces, x_low, x_high, y_low, y_high, *refs):
    out, mid, one, two, right, post, up = refs
    devices_x, devices_y = grid
    me_x, me_y = lax.axis_index(axes[0]), lax.axis_index(axes[1])
    coarse_x, coarse_y = faces.shape[1:3]
    nx, ny = out.shape[:2]
    own_x, own_y = coarse_x // 2, coarse_y // 2
    quarter = LANES // 4
    reach = RIM // 2
    window = own_y + RIM

    slabs, high = coarse_x + 2 * RIM, coarse_y + 2 * RIM
    half = slabs // 2
    inner = pl.ds(2 * RIM, coarse_y)
    body = pl.ds(RIM, high)
    sizes_x, sizes_y = rim_rows_x(nx, ny), rim_rows_y(nx, ny)
    for face, slot in enumerate((FX, FY, ZL)):
        clear_pads(mid.at[slot], high)
        mid[slot, RIM : RIM + coarse_x, inner] = faces[face]
        place_x = sizes_x[0] + sizes_x[1] + face * sizes_x[0]
        place_y = sizes_y[0] + sizes_y[1] + face * sizes_y[0]
        for layer in range(RIM):
            mid[slot, layer, inner] = rim_slab(x_low, place_x, coarse_y, layer)
            mid[slot, RIM + coarse_x + layer, inner] = rim_slab(x_high, place_x, coarse_y, layer)
        for slab in range(half):
            place = pl.ds(place_y + slab * RIM, RIM)
            for message, row in ((y_low, RIM), (y_high, 2 * RIM + coarse_y)):
                pair = one_of_two(message[place])
                mid[slot, slab, row : row + RIM] = pair[0]
                mid[slot, slab + half, row : row + RIM] = pair[1]
    row_inside = (rows_of((high, LANES)) >= RIM) | (me_y > 0)
    for slab in range(slabs - 1):
        inside = row_inside & (me_x > 0) if slab < RIM else row_inside
        set_weights(mid, slab, RIM, high, HALF, inside)
    clear_pads(one, high)
    clear_pads(right, high)
    clear_pads(two, high)
    one[RIM : RIM + coarse_x, inner] = kept[1]
    right[RIM : RIM + coarse_x, inner] = kept[0]
    for layer in range(RIM):
        one[layer, inner] = rim_slab(x_low, 0, coarse_y, layer)
        one[RIM + coarse_x + layer, inner] = rim_slab(x_high, 0, coarse_y, layer)
    for slab in range(half):
        place = pl.ds(slab * RIM, RIM)
        for message, row in ((y_low, RIM), (y_high, 2 * RIM + coarse_y)):
            pair = one_of_two(message[place])
            one[slab, row : row + RIM] = pair[0]
            one[slab + half, row : row + RIM] = pair[1]
    row = rows_of((high, LANES))
    own_row = (row >= RIM) & (row < RIM + coarse_y)
    for slab in range(1, slabs - 1):
        f_rim = one[slab, body] * mid[D, slab, body] * (1.0 / OMEGA)
        if RIM <= slab < RIM + coarse_x:
            f_rim = jnp.where(own_row, right[slab, body], f_rim)
        right[slab, body] = f_rim
        two[slab, body] = swept(mid, one, slab, RIM, high, right)

    per_block = (coarse.shape[0] - 2 * reach) // own_x
    base = me_x % per_block * own_x
    mine = None
    for gy in range(devices_y):
        place = pl.ds(PAD + gy * own_y - reach, window)
        values = jnp.where(me_y == gy, coarse[pl.ds(base, half), place, :], 0.0)
        mine = values if mine is None else mine + values
    source = lax.broadcasted_iota(jnp.int32, (LANES, LANES), 0)
    target = lax.broadcasted_iota(jnp.int32, (LANES, LANES), 1)
    hit = (source == me_x // per_block * quarter + target // 2) & (target < HALF)
    fine = exact_dot(mine.reshape(half * window, LANES), jnp.where(hit, 1.0, 0.0).astype(F32))
    fine = fine.reshape(half, window, LANES)
    for odd in range(2):
        up[:half, pl.ds(odd, window, stride=2), :] = fine
    for pair in range(half):
        for slab in (2 * pair, 2 * pair + 1):
            if 1 <= slab < slabs - 1:
                two[slab, body] = two[slab, body] + up[pair, :high]
    for slab in range(2, slabs - 2):
        one[slab, body] = swept(mid, two, slab, RIM, high, right)
    for slab in range(3, slabs - 3):
        two[slab, body] = swept(mid, one, slab, RIM, high, right)

    steps = coarse_x + 2
    fine_rows = ny + 2 * RIM
    e = two[RIM - 1 : RIM - 1 + steps, body]
    fine = exact_dot(e.reshape(steps * high, LANES), expand(LANES, 0)).reshape(steps, high, LANES)
    fine = fine[:, reach : reach + fine_rows // 2]
    for odd in range(2):
        up[:, pl.ds(odd, fine_rows // 2, stride=2), :] = fine
    body = pl.ds(RIM, fine_rows)
    for slot in (0, 1):
        clear_pads(post.at[slot], fine_rows)
    inner = pl.ds(PAD, ny)
    post[0, EDGE : EDGE + nx, inner] = top[V, EDGE : EDGE + nx, inner]
    base_x, base_y = RIM // 2 * coarse_y, half * RIM
    for layer in range(2):
        place = pl.ds(base_x + layer * ny, ny)
        post[0, EDGE - 2 + layer, inner] = x_low[place]
        post[0, EDGE + nx + layer, inner] = x_high[place]
    for slab in range(nx + 4):
        place = pl.ds(base_y + 2 * slab, 2)
        post[0, slab + EDGE - 2, RIM:PAD] = jnp.zeros((RIM, LANES), F32)
        post[0, slab + EDGE - 2, PAD + ny : PAD + ny + RIM] = jnp.zeros((RIM, LANES), F32)
        post[0, slab + EDGE - 2, PAD - 2 : PAD] = y_low[place]
        post[0, slab + EDGE - 2, PAD + ny : PAD + ny + 2] = y_high[place]

    def raise_level(index):
        for slab in (EDGE - 2 + 2 * index, EDGE - 1 + 2 * index):
            post[0, slab, body] = post[0, slab, body] + up[index]

    run(steps, raise_level)

    def fifth(index):
        slab = EDGE - 1 + index
        post[1, slab, body] = swept(top, post.at[0], slab, RIM, fine_rows)

    run(nx + 2, fifth)

    def sixth(index):
        out[index] = swept(top, post.at[1], EDGE + index, PAD, ny)

    run(nx, sixth)


IN_VMEM = pl.BlockSpec(memory_space=pltpu.VMEM)


def call(kernel, outs, scratch=(), from_hbm=False):
    ins = pl.BlockSpec(memory_space=pl.ANY) if from_hbm else IN_VMEM

    def launch(*args):
        if from_hbm:
            args = [pltpu.with_memory_space_constraint(arg, pltpu.HBM) for arg in args]
        return pl.pallas_call(
            kernel,
            out_shape=[pltpu.VMEM(shape, F32) for shape in outs],
            in_specs=[ins] * len(args),
            out_specs=[IN_VMEM] * len(outs),
            scratch_shapes=[pltpu.VMEM(s, F32) if isinstance(s, tuple) else s for s in scratch],
            compiler_params=pltpu.CompilerParams(vmem_limit_bytes=24 * 2**20),
        )(*args)

    return launch


def pair_route(axis):
    return [(i, i ^ 1) for i in range(lax.axis_size(axis))]


def swap_route(axis):
    count = lax.axis_size(axis)
    return [(i, (i + 1 ^ 1) - 1) for i in range(1, count - 1)]


def by_partner(low, high, axis):
    odd = lax.axis_index(axis) % 2 == 1
    return jnp.where(odd, low, high), jnp.where(odd, high, low)


def from_sides(low, high, axis):
    pair, swap = by_partner(low, high, axis)
    pair = lax.ppermute(pair, axis, pair_route(axis))
    swap = lax.ppermute(swap, axis, swap_route(axis))
    return by_partner(pair, swap, axis)


def passed_round(block, axis, stride):
    count = lax.axis_size(axis)
    return [block] + [
        lax.ppermute(block, axis, [(i, i ^ distance) for i in range(count)])
        for distance in range(stride, count, stride)
    ]


def passed_across(block):
    count, size = lax.axis_size("gx"), lax.axis_size("gy")
    blocks = []
    for side in range(2):
        for distance in range(0, size, 2):
            route = [
                (x * size + y, (x ^ side) * size + (y ^ distance)) for x in range(count) for y in range(size)
            ]
            moved = side + distance > 0
            blocks.append(lax.ppermute(block, ("gx", "gy"), route) if moved else block)
    return blocks


def fused_cycle(*fields):
    axes = ("gx", "gy")
    devices_x, devices_y = lax.axis_size("gx"), lax.axis_size("gy")
    nx, ny, nz = fields[0].shape
    coarse_x, coarse_y = nx // 2, ny // 2
    x_shape, y_shape = (x_rows(nx, ny), LANES), (y_rows(nx, ny), LANES)
    own, x_low, x_high = call(
        start_pack, [(5, nx, ny, nz), x_shape, x_shape], [pltpu.SemaphoreType.DMA((5,))], True
    )(*fields)
    x_low, x_high = from_sides(x_low, x_high, "gx")
    faces, coefficients = call(
        coarse_faces,
        [(3, coarse_x, coarse_y, LANES), (16, LANES)],
        [(coarse_x, ny, LANES), (coarse_x // 2, coarse_y, LANES)],
    )(own)
    y_low, y_high = call(pack_y, [y_shape] * 2)(own, x_low, x_high)
    y_low, y_high = from_sides(y_low, y_high, "gy")
    stack = (nx + 2 * EDGE, ny + 4 * RIM, LANES)
    stack_1 = (coarse_x + 2 * RIM, coarse_y + 4 * RIM, LANES)
    half = stack_1[0] // 2
    v_shape = (sum(rim_rows_x(nx, ny)), LANES)
    w_shape = (sum(rim_rows_y(nx, ny)), LANES)
    top, kept, chunk, v_low, v_high = call(
        functools.partial(level_down, axes),
        [(D + 1,) + stack, (2, coarse_x, coarse_y, LANES), (BLOCK_ROWS, LANES), v_shape, v_shape],
        [
            stack,
            (nx // 2, ny, LANES),
            stack_1,
            (half, coarse_y + 2 * RIM, LANES),
            (D + 1,) + stack_1,
            (coarse_x + 3,) + stack[1:],
        ],
    )(own, faces, coefficients, x_low, x_high, y_low, y_high)

    blocks = passed_round(chunk, "gx", 2)
    v_low, v_high = from_sides(v_low, v_high, "gx")
    slow = (len(blocks),) + chunk.shape
    (pieces,) = call(stack_blocks, [slow])(*blocks, v_low, v_high)
    blocks = passed_across(pieces.reshape(-1, LANES))
    w_low, w_high = call(pack_v, [w_shape] * 2)(top, kept, faces, v_low, v_high)
    pair, swap = by_partner(w_low, w_high, "gy")
    message = jnp.concatenate(blocks + [pair])
    swap = lax.ppermute(swap, "gy", swap_route("gy"))
    other = lax.ppermute(message, "gy", pair_route("gy"))
    rows = message.shape[0] - w_shape[0]
    pieces = jnp.stack((message[:rows], other[:rows])).reshape((2, len(blocks)) + slow)
    w_low, w_high = by_partner(other[rows:], swap, "gy")
    count = devices_x * nx // 16
    rows = devices_y * ny // 4
    grid = (devices_x, devices_y)
    coarsest = (devices_x * nx >> LEVELS - 1, devices_y * ny >> LEVELS - 1)
    wide = (count + RIM, rows + 2 * PAD, LANES)
    (coarse,) = call(
        functools.partial(level_two, axes, grid, 4 * max(coarsest), (nx // 4, ny // 4)),
        [wide],
        [(3, devices_x, rows, LANES), wide],
    )(pieces)
    return pl.pallas_call(
        functools.partial(level_up, axes, grid),
        out_shape=jax.ShapeDtypeStruct((nx, ny, nz), F32),
        in_specs=[IN_VMEM] * 8,
        out_specs=IN_VMEM,
        scratch_shapes=[
            pltpu.VMEM(shape, F32)
            for shape in ((D + 1,) + stack_1, stack_1, stack_1, stack_1, (2,) + stack, (coarse_x + 2, ny + 2 * RIM, LANES))
        ],
        compiler_params=pltpu.CompilerParams(vmem_limit_bytes=24 * 2**20),
    )(coarse, top, kept, faces, v_low, v_high, w_low, w_high)


def with_halo(block, sides, width):
    for axis, dim in sides:
        count = lax.axis_size(axis)
        forward = [(i, i + 1) for i in range(count - 1)]
        backward = [(target, source) for source, target in forward]
        low = lax.ppermute(
            lax.slice_in_dim(block, block.shape[dim] - width, None, axis=dim), axis, forward
        )
        high = lax.ppermute(lax.slice_in_dim(block, 0, width, axis=dim), axis, backward)
        block = jnp.concatenate([low, block, high], axis=dim)
    return block


def passed_along(block, axis, distance):
    devices = range(lax.axis_size(axis))
    route = [(i - distance, i) for i in devices if i - distance in devices]
    return lax.ppermute(block, axis, route)


def stencil(padded, padded_x, padded_y, face_z):
    center = padded[1:-1, 1:-1]
    zero_plane = jnp.zeros(center.shape[:2] + (1,), center.dtype)
    above_face = jnp.concatenate((face_z[:, :, 1:], zero_plane), axis=2)
    below_z = jnp.concatenate((zero_plane, center[:, :, :-1]), axis=2)
    above_z = jnp.concatenate((center[:, :, 1:], zero_plane), axis=2)
    lower_x = padded_x[1:-1, 1:-1]
    upper_x = padded_x[2:, 1:-1]
    lower_y = padded_y[1:-1, 1:-1]
    upper_y = padded_y[1:-1, 2:]
    applied = lower_x * (center - padded[:-2, 1:-1]) + upper_x * (center - padded[2:, 1:-1])
    applied = (
        applied + lower_y * (center - padded[1:-1, :-2]) + upper_y * (center - padded[1:-1, 2:])
    )
    applied = applied + face_z * (center - below_z) + above_face * (center - above_z)
    diagonal = lower_x + upper_x + lower_y + upper_y + face_z + above_face
    return (applied, diagonal)


def jacobi_sweep(padded, source, padded_x, padded_y, face_z):
    applied, diagonal = stencil(padded, padded_x, padded_y, face_z)
    return padded[1:-1, 1:-1] + OMEGA * (source - applied) / diagonal


def pad_plane(values, width):
    return jnp.pad(values, ((width, width), (width, width), (0, 0)))


def restrict(residual):
    shape = residual.shape
    blocks = residual.reshape(shape[0] // 2, 2, shape[1] // 2, 2, shape[2] // 2, 2)
    return 4.0 * jnp.mean(blocks, axis=(1, 3, 5))


def coarsen_faces(face_x, face_y, face_z):
    shape = face_x.shape
    blocks = (shape[0] // 2, 2, shape[1] // 2, 2, shape[2] // 2, 2)
    coarse_x = jnp.mean(face_x.reshape(blocks)[:, 0], axis=(2, 4))
    coarse_y = jnp.mean(face_y.reshape(blocks)[:, :, :, 0], axis=(1, 4))
    coarse_z = jnp.mean(face_z.reshape(blocks)[..., 0], axis=(1, 3))
    return (coarse_x, coarse_y, coarse_z)


def prolong(coarse):
    return jnp.repeat(jnp.repeat(jnp.repeat(coarse, 2, axis=0), 2, axis=1), 2, axis=2)


def local_cycle(grid_level, iterate, source, face_x, face_y, face_z):
    padded_x = pad_plane(face_x, 1)
    padded_y = pad_plane(face_y, 1)
    if grid_level == LEVELS - 1:
        count = 4 * max(iterate.shape[0], iterate.shape[1])

        def one_sweep(index, values):
            return jacobi_sweep(pad_plane(values, 1), source, padded_x, padded_y, face_z)

        return lax.fori_loop(0, count, one_sweep, iterate)
    for sweep_index in range(2):
        iterate = jacobi_sweep(pad_plane(iterate, 1), source, padded_x, padded_y, face_z)
    applied, diagonal = stencil(pad_plane(iterate, 1), padded_x, padded_y, face_z)
    coarse_src = restrict(source - applied)
    coarse_x, coarse_y, coarse_z = coarsen_faces(face_x, face_y, face_z)
    correction = local_cycle(
        grid_level + 1, jnp.zeros_like(coarse_src), coarse_src, coarse_x, coarse_y, coarse_z
    )
    iterate = iterate + prolong(correction)
    for sweep_index in range(2):
        iterate = jacobi_sweep(pad_plane(iterate, 1), source, padded_x, padded_y, face_z)
    return iterate


def field_rim(iterate):
    return with_halo(iterate, (("gx", 0), ("gy", 1)), 1)


def sweep_pair_narrow(iterate, source, padded_x, padded_y, face_z, zero_start):
    for sweep_index in range(2):
        if sweep_index == 0 and zero_start:
            padded = pad_plane(iterate, 1)
        else:
            padded = field_rim(iterate)
        iterate = jacobi_sweep(padded, source, padded_x, padded_y, face_z)
    return iterate


def descend(grid_level, iterate, source, face_x, face_y, face_z, zero_start, gather_level):
    if grid_level == gather_level:
        pieces = (
            lax.all_gather(source, "gy", axis=1, tiled=True),
            lax.all_gather(face_x, "gy", axis=1, tiled=True),
            lax.all_gather(face_y, "gy", axis=1, tiled=True),
            lax.all_gather(face_z, "gy", axis=1, tiled=True),
        )
        gathered = (
            lax.all_gather(pieces[0], "gx", axis=0, tiled=True),
            lax.all_gather(pieces[1], "gx", axis=0, tiled=True),
            lax.all_gather(pieces[2], "gx", axis=0, tiled=True),
            lax.all_gather(pieces[3], "gx", axis=0, tiled=True),
        )
        correction = local_cycle(
            grid_level,
            jnp.zeros_like(gathered[0]),
            gathered[0],
            gathered[1],
            gathered[2],
            gathered[3],
        )
        start_x = lax.axis_index("gx") * source.shape[0]
        start_y = lax.axis_index("gy") * source.shape[1]
        return lax.dynamic_slice(
            correction, (start_x, start_y, jnp.zeros((), jnp.int32)), source.shape
        )
    next_x = passed_along(face_x[:1], "gx", -1)
    next_y = passed_along(face_y[:, :1], "gy", -1)
    lower_row = jnp.zeros_like(next_x)
    lower_col = jnp.zeros_like(next_y)
    padded_x = jnp.pad(
        jnp.concatenate((lower_row, face_x, next_x), axis=0), ((0, 0), (1, 1), (0, 0))
    )
    padded_y = jnp.pad(
        jnp.concatenate((lower_col, face_y, next_y), axis=1), ((1, 1), (0, 0), (0, 0))
    )

    def smoother(values, starting):
        return sweep_pair_narrow(values, source, padded_x, padded_y, face_z, starting)

    iterate = smoother(iterate, zero_start)
    applied, diagonal = stencil(field_rim(iterate), padded_x, padded_y, face_z)
    coarse_src = restrict(source - applied)
    coarse_x, coarse_y, coarse_z = coarsen_faces(face_x, face_y, face_z)
    correction = descend(
        grid_level + 1,
        jnp.zeros_like(coarse_src),
        coarse_src,
        coarse_x,
        coarse_y,
        coarse_z,
        True,
        gather_level,
    )
    iterate = iterate + prolong(correction)
    return smoother(iterate, False)


def fits(nx, ny, nz, devices_x, devices_y):
    cells = devices_x * nx * devices_y * ny * nz // 8
    even = devices_x % 8 == 0 and devices_y % 4 == 0
    even = even and devices_x & (devices_x - 1) == 0 and devices_y & (devices_y - 1) == 0
    return cells <= 2**18 and even and (nx, ny, nz) == (16, 16, LANES)


def local(source_term, initial_guess, face_x, face_y, face_z):
    if fits(*source_term.shape, lax.axis_size("gx"), lax.axis_size("gy")):
        return fused_cycle(source_term, initial_guess, face_x, face_y, face_z)
    gather_level = 4
    return descend(0, initial_guess, source_term, face_x, face_y, face_z, False, gather_level)


def solution(mesh):
    placed = (P("gx", "gy", None),) * 5
    return jax.shard_map(
        local, mesh=mesh, in_specs=placed, out_specs=P("gx", "gy", None), check_vma=False
    )
```

```python
import functools

import jax
import jax.numpy as jnp
from jax import lax
from jax.experimental import pallas as pl
from jax.experimental.pallas import tpu as pltpu
from jax.sharding import PartitionSpec as P

LEVELS = 6
OMEGA = 0.8
LANES = 128
RIM = 4
EDGE = 3
PAD = 8
BLOCK_ROWS = 24
F32 = jnp.float32

V, F, FX, FY, ZL, ZH, W, D = range(8)
SLOTS = (F, V, FX, FY, ZL)
X_LAYERS = (2, 3, 3, 2, 2)
Y_LAYERS = (2, 3, 2, 3, 2)
Y_REACH = (1, 2, 2, 2, 1)


def lanes_of(shape):
    return lax.broadcasted_iota(jnp.int32, shape, len(shape) - 1)


def rows_of(shape):
    return lax.broadcasted_iota(jnp.int32, shape, len(shape) - 2)


def roll_lanes(values, step):
    return pltpu.roll(values, step % LANES, values.ndim - 1)


def roll_rows(values, step):
    return pltpu.roll(values, step % values.shape[-2], values.ndim - 2)


def exact_dot(left, right):
    return jnp.dot(left, right, precision=lax.Precision.HIGHEST, preferred_element_type=F32)


def compact(depth, part, even_only=False):
    source = lax.broadcasted_iota(jnp.int32, (LANES, LANES), 0)
    target = lax.broadcasted_iota(jnp.int32, (LANES, LANES), 1)
    half = depth // 2
    hit = target == (source // depth * 2 + part) * half + source % depth // 2
    if even_only:
        hit = hit & (source % 2 == 0)
    return jnp.where(hit, 1.0, 0.0).astype(F32)


def expand(depth, part):
    target = lax.broadcasted_iota(jnp.int32, (LANES, LANES), 0)
    source = lax.broadcasted_iota(jnp.int32, (LANES, LANES), 1)
    half = depth // 2
    hit = target == (source // depth * 2 + part) * half + source % depth // 2
    return jnp.where(hit, 1.0, 0.0).astype(F32)


def merge_lanes(values, depth, even_only=False):
    count, rows, _ = values.shape
    half = count // 2
    flat = values.reshape(2, half * rows, LANES)
    out = exact_dot(flat[0], compact(depth, 0, even_only))
    out = out + exact_dot(flat[1], compact(depth, 1, even_only))
    return out.reshape(half, rows, LANES)


def even_rows(ref, rows):
    return ref[:, pl.ds(0, rows // 2, stride=2), :]


def odd_rows(ref, rows):
    return ref[:, pl.ds(1, rows // 2, stride=2), :]


HALF = LANES // 2


def low_half(values):
    return jnp.where(lanes_of(values.shape) < HALF, values, 0.0)


def two_in_one(first, second):
    return first + roll_lanes(second, HALF)


def one_of_two(values):
    return low_half(values), low_half(roll_lanes(values, HALF))


def x_rows(nx, ny):
    return sum(X_LAYERS) * ny


def y_rows(nx, ny):
    return sum(layers * (nx + 2 * reach) for layers, reach in zip(Y_LAYERS, Y_REACH))


def rim_rows_x(nx, ny):
    slab = RIM // 2 * (ny // 2)
    return slab, 2 * ny, 3 * slab


def rim_rows_y(nx, ny):
    slabs = (nx // 2 + 2 * RIM) // 2 * RIM
    return slabs, 2 * (nx + 4), 3 * slabs


def x_place(index, layer, ny):
    return pl.ds((sum(X_LAYERS[:index]) + layer) * ny, ny)


def y_place(index, slab, nx):
    before = zip(Y_LAYERS[:index], Y_REACH[:index])
    start = sum(layers * (nx + 2 * reach) for layers, reach in before)
    return pl.ds(start + (Y_REACH[index] + slab) * Y_LAYERS[index], Y_LAYERS[index])


def start_pack(*refs):
    fields, (own, x_low, x_high, done) = refs[:5], refs[5:]
    copies = [pltpu.make_async_copy(ref, own.at[index], done.at[index]) for index, ref in enumerate(fields)]
    for copy in copies:
        copy.start()
    nx, ny = own.shape[1:3]
    for index, copy in enumerate(copies):
        copy.wait()
        for layer in range(X_LAYERS[index]):
            x_low[x_place(index, layer, ny)] = own[index, layer]
            x_high[x_place(index, layer, ny)] = own[index, nx - X_LAYERS[index] + layer]


def pair_slabs(ref):
    count = ref.shape[0]
    values = ref[...].reshape((count // 2, 2) + ref.shape[1:])
    return values[:, 0], values[:, 1]


def wide_slab(slab, from_low, own, from_high):
    count = own.shape[0]
    if slab < RIM:
        return from_low(slab)
    if slab < RIM + count:
        return own[slab - RIM]
    return from_high(slab - RIM - count)


def rim_slab(ref, base, rows, layer):
    place = pl.ds(base + layer % (RIM // 2) * rows, rows)
    return one_of_two(ref[place])[layer // (RIM // 2)]


def pack_y(own, x_low, x_high, low, high):
    nx, ny = own.shape[1:3]
    for index in range(5):
        width, layers, reach = Y_LAYERS[index], X_LAYERS[index], Y_REACH[index]
        for out, start in ((low, 0), (high, ny - width)):
            for slab in range(nx):
                out[y_place(index, slab, nx)] = own[index, slab, start : start + width]
            for layer in range(reach):
                rows = pl.ds(x_place(index, layers - reach + layer, ny).start + start, width)
                out[y_place(index, layer - reach, nx)] = x_low[rows]
                rows = pl.ds(x_place(index, layer, ny).start + start, width)
                out[y_place(index, nx + layer, nx)] = x_high[rows]


def fold_four(slabs, even_only=False):
    out = None
    for part in range(2):
        term = exact_dot(two_in_one(slabs[part], slabs[2 + part]), compact(HALF, part, even_only))
        out = term if out is None else out + term
    return out


def coarse_slab_sums(ref_x, ref_y, ref_z, count, first, tmp):
    extra = tmp.shape[0]
    rows = tmp.shape[1]
    for index in range(extra):
        tmp[index] = ref_x[first + 2 * index]
    x = even_rows(tmp, rows) + odd_rows(tmp, rows)
    for index in range(count):
        tmp[index] = ref_y[first + 2 * index] + ref_y[first + 2 * index + 1]
    y = even_rows(tmp, rows)[:count]
    for index in range(count):
        tmp[index] = ref_z[first + 2 * index] + ref_z[first + 2 * index + 1]
    return x, y, (even_rows(tmp, rows) + odd_rows(tmp, rows))[:count]


def halved(values, even_only=False):
    count, rows, _ = values.shape
    flat = exact_dot(values.reshape(count * rows, LANES), compact(LANES, 0, even_only))
    return 0.25 * flat.reshape(count, rows, LANES)


def coarse_faces(own, faces, out, fine, tmp):
    x, y, z = coarse_slab_sums(own.at[2], own.at[3], own.at[4], own.shape[1] // 2, 0, fine)
    faces[0] = halved(x)
    faces[1] = halved(y)
    faces[2] = halved(z, True)
    rows = faces.shape[2]
    coarse = rows // 2
    fx, fy, fz = faces.at[0], faces.at[1], faces.at[2]
    tmp[...] = pair_slabs(fx)[0]
    x = even_rows(tmp, rows) + odd_rows(tmp, rows)
    first, second = pair_slabs(fy)
    tmp[...] = first + second
    y = even_rows(tmp, rows)
    first, second = pair_slabs(fz)
    tmp[...] = first + second
    z = even_rows(tmp, rows) + odd_rows(tmp, rows)
    out[...] = jnp.zeros(out.shape, F32)
    out[:coarse] = 0.25 * fold_four([x[i] for i in range(4)])
    out[coarse : 2 * coarse] = 0.25 * fold_four([y[i] for i in range(4)])
    out[2 * coarse : 3 * coarse] = 0.25 * fold_four([z[i] for i in range(4)], True)


def weighted(lev, src, slab, start, rows, f=None):
    here = pl.ds(start, rows)
    below = pl.ds(start - 1, rows)
    above = pl.ds(start + 1, rows)
    v = src[slab, here]
    f = lev.at[F] if f is None else f
    x = lev[FX, slab, here] * src[slab - 1, here] + lev[FX, slab + 1, here] * src[slab + 1, here]
    y = lev[FY, slab, here] * src[slab, below] + lev[FY, slab, above] * src[slab, above]
    z = lev[ZL, slab, here] * roll_lanes(v, 1) + lev[ZH, slab, here] * roll_lanes(v, -1)
    total = ((x + y) + f[slab, here]) + z
    return v, total


def swept(lev, src, slab, start, rows, f=None):
    v, total = weighted(lev, src, slab, start, rows, f)
    return (1.0 - OMEGA) * v + lev[W, slab, pl.ds(start, rows)] * total


def set_weights(lev, slab, start, rows, depth, inside=None):
    here = pl.ds(start, rows)
    fz = lev[ZL, slab, here]
    z = lanes_of(fz.shape) % depth
    upper = jnp.where(z == depth - 1, 0.0, roll_lanes(fz, -1))
    diagonal = lev[FX, slab, here] + lev[FX, slab + 1, here]
    diagonal = diagonal + lev[FY, slab, here] + lev[FY, slab, pl.ds(start + 1, rows)] + fz + upper
    valid = diagonal > 0.0
    if inside is not None:
        valid = valid & inside
    lev[ZL, slab, here] = jnp.where(z == 0, 0.0, fz)
    lev[ZH, slab, here] = upper
    lev[D, slab, here] = diagonal
    lev[W, slab, here] = jnp.where(valid, OMEGA / jnp.where(valid, diagonal, 1.0), 0.0)


def run(count, body):
    for index in range(count):
        body(index)


def clear_pads(ref, rows):
    for start in (0, RIM + rows):
        ref[:, start : start + RIM] = jnp.zeros((ref.shape[0], RIM, LANES), F32)


def level_down(axes, own, faces, coefficients, x_low, x_high, y_low, y_high, *refs):
    top, kept, chunk, v_low, v_high, other, tmp, one, two, mid, wide = refs
    nx, ny = own.shape[1:3]
    slabs, rows = nx + 2 * EDGE, ny + 2 * RIM
    me_x, me_y = lax.axis_index(axes[0]), lax.axis_index(axes[1])
    inner = pl.ds(PAD, ny)
    for index, slot in enumerate(SLOTS):
        layers, width = X_LAYERS[index], Y_LAYERS[index]
        top[slot, :, :PAD] = jnp.zeros((slabs, PAD, LANES), F32)
        top[slot, :, PAD + ny :] = jnp.zeros((slabs, PAD, LANES), F32)
        top[slot, EDGE : EDGE + nx, inner] = own[index]
        for layer in range(EDGE):
            if layer < layers:
                top[slot, EDGE - layers + layer, inner] = x_low[x_place(index, layer, ny)]
                top[slot, EDGE + nx + layer, inner] = x_high[x_place(index, layer, ny)]
            else:
                top[slot, EDGE - 1 - layer, inner] = jnp.zeros((ny, LANES), F32)
                top[slot, EDGE + nx + layer, inner] = jnp.zeros((ny, LANES), F32)
        for slab in range(-Y_REACH[index], nx + Y_REACH[index]):
            top[slot, EDGE + slab, PAD - width : PAD] = y_low[y_place(index, slab, nx)]
            top[slot, EDGE + slab, PAD + ny : PAD + ny + width] = y_high[y_place(index, slab, nx)]
    clear_pads(other, rows)

    coarse_x, coarse_y = nx // 2, ny // 2
    near = RIM - 1
    for slot in (FX, FY, ZL, ZH, W, D):
        mid[slot] = jnp.zeros(mid.shape[1:], F32)
    x, y, z = coarse_slab_sums(top.at[FX], top.at[FY], top.at[ZL], coarse_x + 2, EDGE - 2, wide)
    mid[FX, near : near + coarse_x + 3, RIM : 3 * RIM + coarse_y] = halved(x)
    mid[FY, near : near + coarse_x + 2, RIM : 3 * RIM + coarse_y] = halved(y)
    mid[ZL, near : near + coarse_x + 2, RIM : 3 * RIM + coarse_y] = halved(z, True)

    row_inside = (rows_of((rows, LANES)) >= RIM) | (me_y > 0)
    main = pl.ds(RIM, rows)
    start_v = top.at[V]

    def first(index):
        slab = index + 1
        inside = row_inside & ((slab >= EDGE) | (me_x > 0))
        set_weights(top, slab, RIM, rows, LANES, inside)
        other[slab, main] = swept(top, start_v, slab, RIM, rows)

    run(slabs - 2, first)

    def second(index):
        slab = index + 2
        top[V, slab, main] = swept(top, other, slab, RIM, rows)

    run(slabs - 4, second)

    def rest(slab):
        v, total = weighted(top, top.at[V], slab, PAD, ny)
        return total - top[D, slab, inner] * v

    def residual(index):
        slab = EDGE + 2 * index
        tmp[index] = rest(slab) + rest(slab + 1)

    run(nx // 2, residual)

    slabs, rows = coarse_x + 2 * RIM, coarse_y + 2 * RIM
    half = slabs // 2
    inner = pl.ds(2 * RIM, coarse_y)
    main = pl.ds(RIM, rows)
    row_inside = (rows_of((rows, LANES)) >= RIM) | (me_y > 0)
    for slab in range(near, near + coarse_x + 2):
        inside = row_inside & (me_x > 0) if slab < RIM else row_inside
        set_weights(mid, slab, RIM, rows, HALF, inside)

    source = even_rows(tmp, ny) + odd_rows(tmp, ny)
    source = 0.5 * exact_dot(source.reshape(coarse_x * coarse_y, LANES), compact(LANES, 0))
    for ref in (mid.at[F], mid.at[V], one):
        ref[...] = jnp.zeros(ref.shape, F32)
    mid[F, RIM : RIM + coarse_x, inner] = source.reshape(coarse_x, coarse_y, LANES)
    for slab in range(RIM, RIM + coarse_x):
        mid[V, slab, inner] = mid[W, slab, inner] * mid[F, slab, inner]
    for layer in range(RIM // 2):
        near, far = RIM + layer, coarse_x + layer
        v_low[layer * coarse_y : (layer + 1) * coarse_y] = two_in_one(
            mid[V, near, inner], mid[V, near + RIM // 2, inner]
        )
        v_high[layer * coarse_y : (layer + 1) * coarse_y] = two_in_one(
            mid[V, far, inner], mid[V, far + RIM // 2, inner]
        )
    kept[0] = mid[F, RIM : RIM + coarse_x, inner]
    kept[1] = mid[V, RIM : RIM + coarse_x, inner]
    base, after, _ = rim_rows_x(nx, ny)
    pairs = RIM // 2
    for face in range(3):
        for layer in range(pairs):
            place = pl.ds(base + after + (face * pairs + layer) * coarse_y, coarse_y)
            far = coarse_x - RIM + layer
            v_low[place] = two_in_one(faces[face, layer], faces[face, layer + pairs])
            v_high[place] = two_in_one(faces[face, far], faces[face, far + pairs])
    for layer in range(2):
        place = pl.ds(base + layer * ny, ny)
        v_low[place] = top[V, EDGE + layer, pl.ds(PAD, ny)]
        v_high[place] = top[V, EDGE + nx - 2 + layer, pl.ds(PAD, ny)]
    for slab in range(RIM - 1, RIM + coarse_x + 1):
        one[slab, main] = swept(mid, mid.at[V], slab, RIM, rows)

    def rest_1(slab):
        v, total = weighted(mid, one, slab, RIM, rows)
        return total - mid[D, slab, main] * v

    two[...] = jnp.zeros(two.shape, F32)
    for pair in range(1, half - 1):
        two[pair] = rest_1(2 * pair) + rest_1(2 * pair + 1)
    pieces = even_rows(two, rows) + odd_rows(two, rows)
    coarse_rows, quarter_rows = rows // 2, rows // 4
    chunk[:coarse_rows] = 0.5 * fold_four([pieces[1 + i] for i in range(4)])
    rest_of = [pieces[5 + i // 2][i % 2 * quarter_rows :][:quarter_rows] for i in range(4)]
    chunk[coarse_rows : coarse_rows + quarter_rows] = 0.5 * fold_four(rest_of)
    chunk[coarse_rows + quarter_rows :] = coefficients[:BLOCK_ROWS - coarse_rows - quarter_rows]
    block = me_x // (lax.axis_size(axes[0]) // 4)
    values = chunk[...]
    for turn in range(1, 4):
        chunk[...] = jnp.where(block == turn, roll_lanes(values, turn * (LANES // 4)), chunk[...])


def pack_v(top, kept, faces, x_low, x_high, low, high):
    coarse_x, coarse_y = faces.shape[1:3]
    nx, ny = 2 * coarse_x, 2 * coarse_y
    slabs = coarse_x + 2 * RIM
    half = slabs // 2
    sizes_x, sizes_y = rim_rows_x(nx, ny), rim_rows_y(nx, ny)

    def folded(own, place_x, place_y):
        values = [
            wide_slab(
                slab,
                lambda layer: rim_slab(x_low, place_x, coarse_y, layer),
                own,
                lambda layer: rim_slab(x_high, place_x, coarse_y, layer),
            )
            for slab in range(slabs)
        ]
        for slab in range(half):
            both = two_in_one(values[slab], values[slab + half])
            rows = pl.ds(place_y + slab * RIM, RIM)
            low[rows] = both[:RIM]
            high[rows] = both[coarse_y - RIM :]

    folded(kept.at[1], 0, 0)
    for face in range(3):
        folded(
            faces.at[face],
            sizes_x[0] + sizes_x[1] + face * sizes_x[0],
            sizes_y[0] + sizes_y[1] + face * sizes_y[0],
        )
    base_x, base_y = sizes_x[0], sizes_y[0]
    for out, start in ((low, 0), (high, ny - 2)):
        for layer in range(2):
            rows = pl.ds(base_x + layer * ny + start, 2)
            out[pl.ds(base_y + 2 * layer, 2)] = x_low[rows]
            out[pl.ds(base_y + 2 * (2 + nx + layer), 2)] = x_high[rows]
        for slab in range(nx):
            out[pl.ds(base_y + 2 * (2 + slab), 2)] = top[V, EDGE + slab, pl.ds(PAD + start, 2)]


def stack_blocks(*refs):
    for index, ref in enumerate(refs[:-1]):
        refs[-1][index] = ref[...]


def hand_on(first, second, _, first_out, second_out):
    first_out[...] = first[...]
    second_out[...] = second[...]


def pair_rows(values, stride):
    return values + roll_rows(values, -stride)


def pair_lanes(values, stride):
    return values + roll_lanes(values, -stride)


class Listed:
    def __init__(self, fx, fy, fz, stride, depth):
        self.fx, self.fy, self.fz, self.stride, self.depth = fx, fy, fz, stride, depth
        shape = fx[0].shape
        rows = shape[0]
        row, lane = rows_of(shape), lanes_of(shape)
        z = lane % depth
        count = self.count = len(fx)
        self.x_high = [
            fx[s + 1] if s + 1 < count else jnp.where(lane < LANES - depth, roll_lanes(fx[0], -depth), 0.0)
            for s in range(count)
        ]
        self.x_low = [fx[s] if s > 0 else jnp.where(lane >= depth, fx[0], 0.0) for s in range(count)]
        self.y_high = [jnp.where(row < rows - stride, roll_rows(f, -stride), 0.0) for f in fy]
        self.y_low = [jnp.where(row >= stride, f, 0.0) for f in fy]
        self.z_high = [jnp.where(z < depth - stride, roll_lanes(f, -stride), 0.0) for f in fz]
        self.z_low = [jnp.where(z >= stride, f, 0.0) for f in fz]
        self.d = [
            fx[s] + self.x_high[s] + fy[s] + self.y_high[s] + fz[s] + self.z_high[s] for s in range(count)
        ]
        self.w = [jnp.where(d > 0.0, OMEGA / jnp.where(d > 0.0, d, 1.0), 0.0) for d in self.d]

    def weighted(self, v, f):
        count = self.count
        out = []
        for s in range(count):
            low = v[s - 1] if s > 0 else roll_lanes(v[count - 1], self.depth)
            high = v[s + 1] if s + 1 < count else roll_lanes(v[0], -self.depth)
            x = self.x_low[s] * low + self.x_high[s] * high
            y = self.y_low[s] * roll_rows(v[s], self.stride) + self.y_high[s] * roll_rows(v[s], -self.stride)
            z = self.z_low[s] * roll_lanes(v[s], self.stride) + self.z_high[s] * roll_lanes(v[s], -self.stride)
            total = (f[s] + y) + (x + z)
            out.append(total)
        return out

    def sweep(self, v, f):
        totals = self.weighted(v, f)
        return [(1.0 - OMEGA) * v[s] + self.w[s] * totals[s] for s in range(self.count)]

    def sweeps(self, count, f):
        folded = [
            [w * c for w, c in zip(self.w, coefficients)]
            for coefficients in (self.x_low, self.x_high, self.y_low, self.y_high, self.z_low, self.z_high)
        ]
        scaled = self.start(f)
        slabs = self.count

        def step(index, v):
            out = []
            for s in range(slabs):
                low = v[s - 1] if s > 0 else roll_lanes(v[slabs - 1], self.depth)
                high = v[s + 1] if s + 1 < slabs else roll_lanes(v[0], -self.depth)
                x = folded[0][s] * low + folded[1][s] * high
                y = folded[2][s] * roll_rows(v[s], self.stride) + folded[3][s] * roll_rows(v[s], -self.stride)
                z = folded[4][s] * roll_lanes(v[s], self.stride) + folded[5][s] * roll_lanes(v[s], -self.stride)
                out.append((((1.0 - OMEGA) * v[s] + scaled[s]) + y) + (x + z))
            return out

        return lax.fori_loop(1, count, step, scaled)

    def start(self, f):
        return [self.w[s] * f[s] for s in range(self.count)]

    def residual(self, v, f):
        totals = self.weighted(v, f)
        return [totals[s] - self.d[s] * v[s] for s in range(self.count)]

    def kept(self):
        shape = self.fx[0].shape
        step = 2 * self.stride
        return (rows_of(shape) % step == 0) & (lanes_of(shape) % step == 0)

    def coarser(self):
        keep, stride = self.kept(), self.stride
        half = range(self.count // 2)

        def kept(values):
            return jnp.where(keep, 0.25 * values, 0.0)

        fx = [kept(pair_lanes(pair_rows(self.fx[2 * s], stride), stride)) for s in half]
        fy = [kept(pair_lanes(self.fy[2 * s] + self.fy[2 * s + 1], stride)) for s in half]
        fz = [kept(pair_rows(self.fz[2 * s] + self.fz[2 * s + 1], stride)) for s in half]
        return Listed(fx, fy, fz, 2 * stride, self.depth)

    def restrict(self, r):
        keep, stride = self.kept(), self.stride
        return [
            jnp.where(keep, 0.5 * pair_lanes(pair_rows(r[2 * s] + r[2 * s + 1], stride), stride), 0.0)
            for s in range(self.count // 2)
        ]

    def prolong(self, e):
        out = []
        for values in e:
            values = values + roll_rows(values, self.stride)
            values = values + roll_lanes(values, self.stride)
            out += [values, values]
        return out


def listed_cycle(levels, sweeps, f):
    level = levels[0]
    if len(levels) == 1:
        return level.sweeps(sweeps, f)
    v = level.sweep(level.start(f), f)
    e = listed_cycle(levels[1:], sweeps, level.restrict(level.residual(v, f)))
    v = [a + b for a, b in zip(v, level.prolong(e))]
    return level.sweep(level.sweep(v, f), f)


def level_two(axes, grid, sweeps, shape, pieces, out, wide, tall):
    devices_x, devices_y = grid
    me_x, me_y = lax.axis_index(axes[0]), lax.axis_index(axes[1])
    own_x, own_y = shape
    quarter = LANES // 4
    reach = RIM // 2
    blocks = 4
    count = devices_x * own_x // blocks
    rows = devices_y * own_y
    main = pl.ds(PAD, rows)
    window = own_y + RIM

    def piece(gx, gy):
        slow, far = (me_x // 2) ^ (gx // 2), (me_y // 2) ^ (gy // 2)
        return ((me_y + gy) % 2, (me_x + gx) % 2 * (devices_y // 2) + far, slow)

    for ref in (wide, tall):
        ref[...] = jnp.zeros(ref.shape, F32)
    per_block = count // own_x

    def merged(values, shift, turn):
        at = lanes_of(values[0].shape) // quarter
        out = values[0]
        for block in range(1, blocks):
            out = jnp.where(at == (shift + block) % blocks, values[block], out)
        return roll_lanes(out, (turn - shift) * quarter)

    lane = lanes_of((window, LANES))
    for gy in range(devices_y):
        sums = [None] * count
        for turn in range(per_block):
            where = [piece(block * per_block + turn, gy) for block in range(blocks)]
            first = [pieces[at + (pl.ds(0, window),)] for at in where]
            second = [pieces[at + (pl.ds(window, window // 2),)] for at in where]
            for local in range(1, 2 * blocks - 1):
                offset = own_x * turn - reach + local
                over, slab = offset // count, offset % count
                if local <= blocks:
                    moved = merged(first, local - 1, over)
                else:
                    at = 2 * (local - blocks - 1)
                    moved = jnp.concatenate([merged(second, at + odd, over) for odd in range(2)])
                if over < 0:
                    moved = jnp.where(lane // quarter == blocks - 1, 0.0, moved)
                elif over > 0:
                    moved = jnp.where(lane // quarter == 0, 0.0, moved)
                sums[slab] = moved if sums[slab] is None else sums[slab] + moved
        place = pl.ds(PAD + own_y * gy - reach, window)
        for slab in range(count):
            tall[slab, place] = tall[slab, place] + sums[slab]
    f = [tall[slab, main] for slab in range(count)]

    lane = lanes_of((rows, LANES))
    for gx in range(devices_x):
        for gy in range(devices_y):
            where = piece(gx, gy)
            for face in range(3):
                values = pieces[where + (pl.ds(window + window // 2 + face * own_y, own_y),)]
                wide[face, gx, gy * own_y : (gy + 1) * own_y] = values
    faces = []
    for face in range(3):
        slabs = []
        for turn in range(per_block):
            values = [wide[face, block * per_block + turn] for block in range(blocks)]
            slabs += [merged(values, local, 0) for local in range(own_x)]
        faces.append(slabs)
    levels = [Listed(*faces, 1, quarter)]
    while len(levels) < LEVELS - 2:
        levels.append(levels[-1].coarser())
    e = listed_cycle(levels, sweeps, f)

    for slab in range(count):
        out[reach + slab, main] = e[slab]
    for slab in range(reach):
        out[slab, main] = jnp.where(lane < quarter, 0.0, roll_lanes(e[count - reach + slab], quarter))
        out[reach + count + slab, main] = jnp.where(
            lane >= LANES - quarter, 0.0, roll_lanes(e[slab], -quarter)
        )
    out[:, :PAD] = jnp.zeros((count + 2 * reach, PAD, LANES), F32)
    out[:, PAD + rows :] = jnp.zeros((count + 2 * reach, PAD, LANES), F32)


def level_up(axes, grid, coarse, top, kept, faces, x_low, x_high, y_low, y_high, *refs):
    out, mid, one, two, right, post, up = refs
    devices_x, devices_y = grid
    me_x, me_y = lax.axis_index(axes[0]), lax.axis_index(axes[1])
    coarse_x, coarse_y = faces.shape[1:3]
    nx, ny = out.shape[:2]
    own_x, own_y = coarse_x // 2, coarse_y // 2
    quarter = LANES // 4
    reach = RIM // 2
    window = own_y + RIM

    slabs, high = coarse_x + 2 * RIM, coarse_y + 2 * RIM
    half = slabs // 2
    inner = pl.ds(2 * RIM, coarse_y)
    body = pl.ds(RIM, high)
    sizes_x, sizes_y = rim_rows_x(nx, ny), rim_rows_y(nx, ny)
    for face, slot in enumerate((FX, FY, ZL)):
        clear_pads(mid.at[slot], high)
        mid[slot, RIM : RIM + coarse_x, inner] = faces[face]
        place_x = sizes_x[0] + sizes_x[1] + face * sizes_x[0]
        place_y = sizes_y[0] + sizes_y[1] + face * sizes_y[0]
        for layer in range(RIM):
            mid[slot, layer, inner] = rim_slab(x_low, place_x, coarse_y, layer)
            mid[slot, RIM + coarse_x + layer, inner] = rim_slab(x_high, place_x, coarse_y, layer)
        for slab in range(half):
            place = pl.ds(place_y + slab * RIM, RIM)
            for message, row in ((y_low, RIM), (y_high, 2 * RIM + coarse_y)):
                pair = one_of_two(message[place])
                mid[slot, slab, row : row + RIM] = pair[0]
                mid[slot, slab + half, row : row + RIM] = pair[1]
    row_inside = (rows_of((high, LANES)) >= RIM) | (me_y > 0)
    for slab in range(slabs - 1):
        inside = row_inside & (me_x > 0) if slab < RIM else row_inside
        set_weights(mid, slab, RIM, high, HALF, inside)
    clear_pads(one, high)
    clear_pads(right, high)
    clear_pads(two, high)
    one[RIM : RIM + coarse_x, inner] = kept[1]
    right[RIM : RIM + coarse_x, inner] = kept[0]
    for layer in range(RIM):
        one[layer, inner] = rim_slab(x_low, 0, coarse_y, layer)
        one[RIM + coarse_x + layer, inner] = rim_slab(x_high, 0, coarse_y, layer)
    for slab in range(half):
        place = pl.ds(slab * RIM, RIM)
        for message, row in ((y_low, RIM), (y_high, 2 * RIM + coarse_y)):
            pair = one_of_two(message[place])
            one[slab, row : row + RIM] = pair[0]
            one[slab + half, row : row + RIM] = pair[1]
    row = rows_of((high, LANES))
    own_row = (row >= RIM) & (row < RIM + coarse_y)
    for slab in range(1, slabs - 1):
        f_rim = one[slab, body] * mid[D, slab, body] * (1.0 / OMEGA)
        if RIM <= slab < RIM + coarse_x:
            f_rim = jnp.where(own_row, right[slab, body], f_rim)
        right[slab, body] = f_rim
        two[slab, body] = swept(mid, one, slab, RIM, high, right)

    per_block = (coarse.shape[0] - 2 * reach) // own_x
    base = me_x % per_block * own_x
    mine = None
    for gy in range(devices_y):
        place = pl.ds(PAD + gy * own_y - reach, window)
        values = jnp.where(me_y == gy, coarse[pl.ds(base, half), place, :], 0.0)
        mine = values if mine is None else mine + values
    source = lax.broadcasted_iota(jnp.int32, (LANES, LANES), 0)
    target = lax.broadcasted_iota(jnp.int32, (LANES, LANES), 1)
    hit = (source == me_x // per_block * quarter + target // 2) & (target < HALF)
    fine = exact_dot(mine.reshape(half * window, LANES), jnp.where(hit, 1.0, 0.0).astype(F32))
    fine = fine.reshape(half, window, LANES)
    for odd in range(2):
        up[:half, pl.ds(odd, window, stride=2), :] = fine
    for pair in range(half):
        for slab in (2 * pair, 2 * pair + 1):
            if 1 <= slab < slabs - 1:
                two[slab, body] = two[slab, body] + up[pair, :high]
    for slab in range(2, slabs - 2):
        one[slab, body] = swept(mid, two, slab, RIM, high, right)
    for slab in range(3, slabs - 3):
        two[slab, body] = swept(mid, one, slab, RIM, high, right)

    steps = coarse_x + 2
    fine_rows = ny + 2 * RIM
    e = two[RIM - 1 : RIM - 1 + steps, body]
    fine = exact_dot(e.reshape(steps * high, LANES), expand(LANES, 0)).reshape(steps, high, LANES)
    fine = fine[:, reach : reach + fine_rows // 2]
    for odd in range(2):
        up[:, pl.ds(odd, fine_rows // 2, stride=2), :] = fine
    body = pl.ds(RIM, fine_rows)
    for slot in (0, 1):
        clear_pads(post.at[slot], fine_rows)
    inner = pl.ds(PAD, ny)
    post[0, EDGE : EDGE + nx, inner] = top[V, EDGE : EDGE + nx, inner]
    base_x, base_y = RIM // 2 * coarse_y, half * RIM
    for layer in range(2):
        place = pl.ds(base_x + layer * ny, ny)
        post[0, EDGE - 2 + layer, inner] = x_low[place]
        post[0, EDGE + nx + layer, inner] = x_high[place]
    for slab in range(nx + 4):
        place = pl.ds(base_y + 2 * slab, 2)
        post[0, slab + EDGE - 2, RIM:PAD] = jnp.zeros((RIM, LANES), F32)
        post[0, slab + EDGE - 2, PAD + ny : PAD + ny + RIM] = jnp.zeros((RIM, LANES), F32)
        post[0, slab + EDGE - 2, PAD - 2 : PAD] = y_low[place]
        post[0, slab + EDGE - 2, PAD + ny : PAD + ny + 2] = y_high[place]

    def raise_level(index):
        for slab in (EDGE - 2 + 2 * index, EDGE - 1 + 2 * index):
            post[0, slab, body] = post[0, slab, body] + up[index]

    run(steps, raise_level)

    def fifth(index):
        slab = EDGE - 1 + index
        post[1, slab, body] = swept(top, post.at[0], slab, RIM, fine_rows)

    run(nx + 2, fifth)

    def sixth(index):
        out[index] = swept(top, post.at[1], EDGE + index, PAD, ny)

    run(nx, sixth)


IN_VMEM = pl.BlockSpec(memory_space=pltpu.VMEM)


def call(kernel, outs, scratch=(), from_hbm=False):
    ins = pl.BlockSpec(memory_space=pl.ANY) if from_hbm else IN_VMEM

    def launch(*args):
        if from_hbm:
            args = [pltpu.with_memory_space_constraint(arg, pltpu.HBM) for arg in args]
        return pl.pallas_call(
            kernel,
            out_shape=[pltpu.VMEM(shape, F32) for shape in outs],
            in_specs=[ins] * len(args),
            out_specs=[IN_VMEM] * len(outs),
            scratch_shapes=[pltpu.VMEM(s, F32) if isinstance(s, tuple) else s for s in scratch],
            compiler_params=pltpu.CompilerParams(vmem_limit_bytes=24 * 2**20),
        )(*args)

    return launch


def pair_route(axis):
    return [(i, i ^ 1) for i in range(lax.axis_size(axis))]


def swap_route(axis):
    count = lax.axis_size(axis)
    return [(i, (i + 1 ^ 1) - 1) for i in range(1, count - 1)]


def by_partner(low, high, axis):
    odd = lax.axis_index(axis) % 2 == 1
    return jnp.where(odd, low, high), jnp.where(odd, high, low)


def from_sides(low, high, axis):
    pair, swap = by_partner(low, high, axis)
    pair = lax.ppermute(pair, axis, pair_route(axis))
    swap = lax.ppermute(swap, axis, swap_route(axis))
    return by_partner(pair, swap, axis)


def passed_round(block, axis, stride):
    count = lax.axis_size(axis)
    return [block] + [
        lax.ppermute(block, axis, [(i, i ^ distance) for i in range(count)])
        for distance in range(stride, count, stride)
    ]


def passed_across(block, rider):
    count, size = lax.axis_size("gx"), lax.axis_size("gy")
    rows = block.shape[0]
    blocks = [block]
    for side in range(2):
        for distance in range(0, size, 2):
            route = [
                (x * size + y, (x ^ side) * size + (y ^ distance)) for x in range(count) for y in range(size)
            ]
            if side == 1 and distance == 0:
                both = lax.ppermute(jnp.concatenate((block, rider)), ("gx", "gy"), route)
                blocks.append(both[:rows])
                rider = both[rows:]
            elif distance > 0:
                blocks.append(lax.ppermute(block, ("gx", "gy"), route))
    return blocks, rider


def fused_cycle(*fields):
    axes = ("gx", "gy")
    devices_x, devices_y = lax.axis_size("gx"), lax.axis_size("gy")
    nx, ny, nz = fields[0].shape
    coarse_x, coarse_y = nx // 2, ny // 2
    x_shape, y_shape = (x_rows(nx, ny), LANES), (y_rows(nx, ny), LANES)
    own, x_low, x_high = call(
        start_pack, [(5, nx, ny, nz), x_shape, x_shape], [pltpu.SemaphoreType.DMA((5,))], True
    )(*fields)
    x_low, x_high = from_sides(x_low, x_high, "gx")
    faces, coefficients = call(
        coarse_faces,
        [(3, coarse_x, coarse_y, LANES), (16, LANES)],
        [(coarse_x, ny, LANES), (coarse_x // 2, coarse_y, LANES)],
    )(own)
    y_low, y_high = call(pack_y, [y_shape] * 2)(own, x_low, x_high)
    y_low, y_high = from_sides(y_low, y_high, "gy")
    stack = (nx + 2 * EDGE, ny + 4 * RIM, LANES)
    stack_1 = (coarse_x + 2 * RIM, coarse_y + 4 * RIM, LANES)
    half = stack_1[0] // 2
    v_shape = (sum(rim_rows_x(nx, ny)), LANES)
    w_shape = (sum(rim_rows_y(nx, ny)), LANES)
    top, kept, chunk, v_low, v_high = call(
        functools.partial(level_down, axes),
        [(D + 1,) + stack, (2, coarse_x, coarse_y, LANES), (BLOCK_ROWS, LANES), v_shape, v_shape],
        [
            stack,
            (nx // 2, ny, LANES),
            stack_1,
            (half, coarse_y + 2 * RIM, LANES),
            (D + 1,) + stack_1,
            (coarse_x + 3,) + stack[1:],
        ],
    )(own, faces, coefficients, x_low, x_high, y_low, y_high)

    blocks = passed_round(chunk, "gx", 2)
    slow = (len(blocks),) + chunk.shape
    (pieces,) = call(stack_blocks, [slow])(*blocks)
    v_low, v_high = call(hand_on, [v_shape, v_shape])(v_low, v_high, pieces)
    pair, swap = by_partner(v_low, v_high, "gx")
    swap = lax.ppermute(swap, "gx", swap_route("gx"))
    blocks, pair = passed_across(pieces.reshape(-1, LANES), pair)
    v_low, v_high = by_partner(pair, swap, "gx")
    w_low, w_high = call(pack_v, [w_shape] * 2)(top, kept, faces, v_low, v_high)
    pair, swap = by_partner(w_low, w_high, "gy")
    message = jnp.concatenate(blocks + [pair])
    swap = lax.ppermute(swap, "gy", swap_route("gy"))
    other = lax.ppermute(message, "gy", pair_route("gy"))
    rows = message.shape[0] - w_shape[0]
    pieces = jnp.stack((message[:rows], other[:rows])).reshape((2, len(blocks)) + slow)
    w_low, w_high = by_partner(other[rows:], swap, "gy")
    count = devices_x * nx // 16
    rows = devices_y * ny // 4
    grid = (devices_x, devices_y)
    coarsest = (devices_x * nx >> LEVELS - 1, devices_y * ny >> LEVELS - 1)
    wide = (count + RIM, rows + 2 * PAD, LANES)
    (coarse,) = call(
        functools.partial(level_two, axes, grid, 4 * max(coarsest), (nx // 4, ny // 4)),
        [wide],
        [(3, devices_x, rows, LANES), wide],
    )(pieces)
    return pl.pallas_call(
        functools.partial(level_up, axes, grid),
        out_shape=jax.ShapeDtypeStruct((nx, ny, nz), F32),
        in_specs=[IN_VMEM] * 8,
        out_specs=IN_VMEM,
        scratch_shapes=[
            pltpu.VMEM(shape, F32)
            for shape in ((D + 1,) + stack_1, stack_1, stack_1, stack_1, (2,) + stack, (coarse_x + 2, ny + 2 * RIM, LANES))
        ],
        compiler_params=pltpu.CompilerParams(vmem_limit_bytes=24 * 2**20),
    )(coarse, top, kept, faces, v_low, v_high, w_low, w_high)


def with_halo(block, sides, width):
    for axis, dim in sides:
        count = lax.axis_size(axis)
        forward = [(i, i + 1) for i in range(count - 1)]
        backward = [(target, source) for source, target in forward]
        low = lax.ppermute(
            lax.slice_in_dim(block, block.shape[dim] - width, None, axis=dim), axis, forward
        )
        high = lax.ppermute(lax.slice_in_dim(block, 0, width, axis=dim), axis, backward)
        block = jnp.concatenate([low, block, high], axis=dim)
    return block


def passed_along(block, axis, distance):
    devices = range(lax.axis_size(axis))
    route = [(i - distance, i) for i in devices if i - distance in devices]
    return lax.ppermute(block, axis, route)


def stencil(padded, padded_x, padded_y, face_z):
    center = padded[1:-1, 1:-1]
    zero_plane = jnp.zeros(center.shape[:2] + (1,), center.dtype)
    above_face = jnp.concatenate((face_z[:, :, 1:], zero_plane), axis=2)
    below_z = jnp.concatenate((zero_plane, center[:, :, :-1]), axis=2)
    above_z = jnp.concatenate((center[:, :, 1:], zero_plane), axis=2)
    lower_x = padded_x[1:-1, 1:-1]
    upper_x = padded_x[2:, 1:-1]
    lower_y = padded_y[1:-1, 1:-1]
    upper_y = padded_y[1:-1, 2:]
    applied = lower_x * (center - padded[:-2, 1:-1]) + upper_x * (center - padded[2:, 1:-1])
    applied = (
        applied + lower_y * (center - padded[1:-1, :-2]) + upper_y * (center - padded[1:-1, 2:])
    )
    applied = applied + face_z * (center - below_z) + above_face * (center - above_z)
    diagonal = lower_x + upper_x + lower_y + upper_y + face_z + above_face
    return (applied, diagonal)


def jacobi_sweep(padded, source, padded_x, padded_y, face_z):
    applied, diagonal = stencil(padded, padded_x, padded_y, face_z)
    return padded[1:-1, 1:-1] + OMEGA * (source - applied) / diagonal


def pad_plane(values, width):
    return jnp.pad(values, ((width, width), (width, width), (0, 0)))


def restrict(residual):
    shape = residual.shape
    blocks = residual.reshape(shape[0] // 2, 2, shape[1] // 2, 2, shape[2] // 2, 2)
    return 4.0 * jnp.mean(blocks, axis=(1, 3, 5))


def coarsen_faces(face_x, face_y, face_z):
    shape = face_x.shape
    blocks = (shape[0] // 2, 2, shape[1] // 2, 2, shape[2] // 2, 2)
    coarse_x = jnp.mean(face_x.reshape(blocks)[:, 0], axis=(2, 4))
    coarse_y = jnp.mean(face_y.reshape(blocks)[:, :, :, 0], axis=(1, 4))
    coarse_z = jnp.mean(face_z.reshape(blocks)[..., 0], axis=(1, 3))
    return (coarse_x, coarse_y, coarse_z)


def prolong(coarse):
    return jnp.repeat(jnp.repeat(jnp.repeat(coarse, 2, axis=0), 2, axis=1), 2, axis=2)


def local_cycle(grid_level, iterate, source, face_x, face_y, face_z):
    padded_x = pad_plane(face_x, 1)
    padded_y = pad_plane(face_y, 1)
    if grid_level == LEVELS - 1:
        count = 4 * max(iterate.shape[0], iterate.shape[1])

        def one_sweep(index, values):
            return jacobi_sweep(pad_plane(values, 1), source, padded_x, padded_y, face_z)

        return lax.fori_loop(0, count, one_sweep, iterate)
    for sweep_index in range(2):
        iterate = jacobi_sweep(pad_plane(iterate, 1), source, padded_x, padded_y, face_z)
    applied, diagonal = stencil(pad_plane(iterate, 1), padded_x, padded_y, face_z)
    coarse_src = restrict(source - applied)
    coarse_x, coarse_y, coarse_z = coarsen_faces(face_x, face_y, face_z)
    correction = local_cycle(
        grid_level + 1, jnp.zeros_like(coarse_src), coarse_src, coarse_x, coarse_y, coarse_z
    )
    iterate = iterate + prolong(correction)
    for sweep_index in range(2):
        iterate = jacobi_sweep(pad_plane(iterate, 1), source, padded_x, padded_y, face_z)
    return iterate


def field_rim(iterate):
    return with_halo(iterate, (("gx", 0), ("gy", 1)), 1)


def sweep_pair_narrow(iterate, source, padded_x, padded_y, face_z, zero_start):
    for sweep_index in range(2):
        if sweep_index == 0 and zero_start:
            padded = pad_plane(iterate, 1)
        else:
            padded = field_rim(iterate)
        iterate = jacobi_sweep(padded, source, padded_x, padded_y, face_z)
    return iterate


def descend(grid_level, iterate, source, face_x, face_y, face_z, zero_start, gather_level):
    if grid_level == gather_level:
        pieces = (
            lax.all_gather(source, "gy", axis=1, tiled=True),
            lax.all_gather(face_x, "gy", axis=1, tiled=True),
            lax.all_gather(face_y, "gy", axis=1, tiled=True),
            lax.all_gather(face_z, "gy", axis=1, tiled=True),
        )
        gathered = (
            lax.all_gather(pieces[0], "gx", axis=0, tiled=True),
            lax.all_gather(pieces[1], "gx", axis=0, tiled=True),
            lax.all_gather(pieces[2], "gx", axis=0, tiled=True),
            lax.all_gather(pieces[3], "gx", axis=0, tiled=True),
        )
        correction = local_cycle(
            grid_level,
            jnp.zeros_like(gathered[0]),
            gathered[0],
            gathered[1],
            gathered[2],
            gathered[3],
        )
        start_x = lax.axis_index("gx") * source.shape[0]
        start_y = lax.axis_index("gy") * source.shape[1]
        return lax.dynamic_slice(
            correction, (start_x, start_y, jnp.zeros((), jnp.int32)), source.shape
        )
    next_x = passed_along(face_x[:1], "gx", -1)
    next_y = passed_along(face_y[:, :1], "gy", -1)
    lower_row = jnp.zeros_like(next_x)
    lower_col = jnp.zeros_like(next_y)
    padded_x = jnp.pad(
        jnp.concatenate((lower_row, face_x, next_x), axis=0), ((0, 0), (1, 1), (0, 0))
    )
    padded_y = jnp.pad(
        jnp.concatenate((lower_col, face_y, next_y), axis=1), ((1, 1), (0, 0), (0, 0))
    )

    def smoother(values, starting):
        return sweep_pair_narrow(values, source, padded_x, padded_y, face_z, starting)

    iterate = smoother(iterate, zero_start)
    applied, diagonal = stencil(field_rim(iterate), padded_x, padded_y, face_z)
    coarse_src = restrict(source - applied)
    coarse_x, coarse_y, coarse_z = coarsen_faces(face_x, face_y, face_z)
    correction = descend(
        grid_level + 1,
        jnp.zeros_like(coarse_src),
        coarse_src,
        coarse_x,
        coarse_y,
        coarse_z,
        True,
        gather_level,
    )
    iterate = iterate + prolong(correction)
    return smoother(iterate, False)


def fits(nx, ny, nz, devices_x, devices_y):
    cells = devices_x * nx * devices_y * ny * nz // 8
    even = devices_x % 8 == 0 and devices_y % 4 == 0
    even = even and devices_x & (devices_x - 1) == 0 and devices_y & (devices_y - 1) == 0
    return cells <= 2**18 and even and (nx, ny, nz) == (16, 16, LANES)


def local(source_term, initial_guess, face_x, face_y, face_z):
    if fits(*source_term.shape, lax.axis_size("gx"), lax.axis_size("gy")):
        return fused_cycle(source_term, initial_guess, face_x, face_y, face_z)
    gather_level = 4
    return descend(0, initial_guess, source_term, face_x, face_y, face_z, False, gather_level)


def solution(mesh):
    placed = (P("gx", "gy", None),) * 5
    return jax.shard_map(
        local, mesh=mesh, in_specs=placed, out_specs=P("gx", "gy", None), check_vma=False
    )
```

```python
import functools

import jax
import jax.numpy as jnp
from jax import lax
from jax.experimental import pallas as pl
from jax.experimental.pallas import tpu as pltpu
from jax.sharding import PartitionSpec as P

LEVELS = 6
OMEGA = 0.8
LANES = 128
RIM = 4
EDGE = 3
PAD = 8
BLOCK_ROWS = 24
F32 = jnp.float32

V, F, FX, FY, ZL, ZH, W, D = range(8)
SLOTS = (F, V, FX, FY, ZL)
X_LAYERS = (2, 3, 3, 2, 2)
Y_LAYERS = (2, 3, 2, 3, 2)
Y_REACH = (1, 2, 2, 2, 1)


def lanes_of(shape):
    return lax.broadcasted_iota(jnp.int32, shape, len(shape) - 1)


def rows_of(shape):
    return lax.broadcasted_iota(jnp.int32, shape, len(shape) - 2)


def roll_lanes(values, step):
    return pltpu.roll(values, step % LANES, values.ndim - 1)


def roll_rows(values, step):
    return pltpu.roll(values, step % values.shape[-2], values.ndim - 2)


def exact_dot(left, right):
    return jnp.dot(left, right, precision=lax.Precision.HIGHEST, preferred_element_type=F32)


def compact(depth, part, even_only=False):
    source = lax.broadcasted_iota(jnp.int32, (LANES, LANES), 0)
    target = lax.broadcasted_iota(jnp.int32, (LANES, LANES), 1)
    half = depth // 2
    hit = target == (source // depth * 2 + part) * half + source % depth // 2
    if even_only:
        hit = hit & (source % 2 == 0)
    return jnp.where(hit, 1.0, 0.0).astype(F32)


def expand(depth, part):
    target = lax.broadcasted_iota(jnp.int32, (LANES, LANES), 0)
    source = lax.broadcasted_iota(jnp.int32, (LANES, LANES), 1)
    half = depth // 2
    hit = target == (source // depth * 2 + part) * half + source % depth // 2
    return jnp.where(hit, 1.0, 0.0).astype(F32)


def merge_lanes(values, depth, even_only=False):
    count, rows, _ = values.shape
    half = count // 2
    flat = values.reshape(2, half * rows, LANES)
    out = exact_dot(flat[0], compact(depth, 0, even_only))
    out = out + exact_dot(flat[1], compact(depth, 1, even_only))
    return out.reshape(half, rows, LANES)


def even_rows(ref, rows):
    return ref[:, pl.ds(0, rows // 2, stride=2), :]


def odd_rows(ref, rows):
    return ref[:, pl.ds(1, rows // 2, stride=2), :]


HALF = LANES // 2


def low_half(values):
    return jnp.where(lanes_of(values.shape) < HALF, values, 0.0)


def two_in_one(first, second):
    return first + roll_lanes(second, HALF)


def one_of_two(values):
    return low_half(values), low_half(roll_lanes(values, HALF))


def x_rows(nx, ny):
    return sum(X_LAYERS) * ny


def y_rows(nx, ny):
    return sum(layers * (nx + 2 * reach) for layers, reach in zip(Y_LAYERS, Y_REACH))


def rim_rows_x(nx, ny):
    slab = RIM // 2 * (ny // 2)
    return slab, 2 * ny, 3 * slab


def rim_rows_y(nx, ny):
    slabs = (nx // 2 + 2 * RIM) // 2 * RIM
    return slabs, 2 * (nx + 4), 3 * slabs


def x_place(index, layer, ny):
    return pl.ds((sum(X_LAYERS[:index]) + layer) * ny, ny)


def y_place(index, slab, nx):
    before = zip(Y_LAYERS[:index], Y_REACH[:index])
    start = sum(layers * (nx + 2 * reach) for layers, reach in before)
    return pl.ds(start + (Y_REACH[index] + slab) * Y_LAYERS[index], Y_LAYERS[index])


def start_pack(*refs):
    fields, (own, x_low, x_high, done) = refs[:5], refs[5:]
    copies = [pltpu.make_async_copy(ref, own.at[index], done.at[index]) for index, ref in enumerate(fields)]
    for copy in copies:
        copy.start()
    nx, ny = own.shape[1:3]
    for index, copy in enumerate(copies):
        copy.wait()
        for layer in range(X_LAYERS[index]):
            x_low[x_place(index, layer, ny)] = own[index, layer]
            x_high[x_place(index, layer, ny)] = own[index, nx - X_LAYERS[index] + layer]


def pair_slabs(ref):
    count = ref.shape[0]
    values = ref[...].reshape((count // 2, 2) + ref.shape[1:])
    return values[:, 0], values[:, 1]


def wide_slab(slab, from_low, own, from_high):
    count = own.shape[0]
    if slab < RIM:
        return from_low(slab)
    if slab < RIM + count:
        return own[slab - RIM]
    return from_high(slab - RIM - count)


def rim_slab(ref, base, rows, layer):
    place = pl.ds(base + layer % (RIM // 2) * rows, rows)
    return one_of_two(ref[place])[layer // (RIM // 2)]


def pack_y(own, x_low, x_high, low, high):
    nx, ny = own.shape[1:3]
    for index in range(5):
        width, layers, reach = Y_LAYERS[index], X_LAYERS[index], Y_REACH[index]
        for out, start in ((low, 0), (high, ny - width)):
            for slab in range(nx):
                out[y_place(index, slab, nx)] = own[index, slab, start : start + width]
            for layer in range(reach):
                rows = pl.ds(x_place(index, layers - reach + layer, ny).start + start, width)
                out[y_place(index, layer - reach, nx)] = x_low[rows]
                rows = pl.ds(x_place(index, layer, ny).start + start, width)
                out[y_place(index, nx + layer, nx)] = x_high[rows]


def fold_four(slabs, even_only=False):
    out = None
    for part in range(2):
        term = exact_dot(two_in_one(slabs[part], slabs[2 + part]), compact(HALF, part, even_only))
        out = term if out is None else out + term
    return out


def coarse_slab_sums(ref_x, ref_y, ref_z, count, first, tmp):
    extra = tmp.shape[0]
    rows = tmp.shape[1]
    for index in range(extra):
        tmp[index] = ref_x[first + 2 * index]
    x = even_rows(tmp, rows) + odd_rows(tmp, rows)
    for index in range(count):
        tmp[index] = ref_y[first + 2 * index] + ref_y[first + 2 * index + 1]
    y = even_rows(tmp, rows)[:count]
    for index in range(count):
        tmp[index] = ref_z[first + 2 * index] + ref_z[first + 2 * index + 1]
    return x, y, (even_rows(tmp, rows) + odd_rows(tmp, rows))[:count]


def halved(values, even_only=False):
    count, rows, _ = values.shape
    flat = exact_dot(values.reshape(count * rows, LANES), compact(LANES, 0, even_only))
    return 0.25 * flat.reshape(count, rows, LANES)


def coarse_faces(own, faces, out, fine, tmp):
    x, y, z = coarse_slab_sums(own.at[2], own.at[3], own.at[4], own.shape[1] // 2, 0, fine)
    faces[0] = halved(x)
    faces[1] = halved(y)
    faces[2] = halved(z, True)
    rows = faces.shape[2]
    coarse = rows // 2
    fx, fy, fz = faces.at[0], faces.at[1], faces.at[2]
    tmp[...] = pair_slabs(fx)[0]
    x = even_rows(tmp, rows) + odd_rows(tmp, rows)
    first, second = pair_slabs(fy)
    tmp[...] = first + second
    y = even_rows(tmp, rows)
    first, second = pair_slabs(fz)
    tmp[...] = first + second
    z = even_rows(tmp, rows) + odd_rows(tmp, rows)
    out[...] = jnp.zeros(out.shape, F32)
    out[:coarse] = 0.25 * fold_four([x[i] for i in range(4)])
    out[coarse : 2 * coarse] = 0.25 * fold_four([y[i] for i in range(4)])
    out[2 * coarse : 3 * coarse] = 0.25 * fold_four([z[i] for i in range(4)], True)


def weighted(lev, src, slab, start, rows, f=None):
    here = pl.ds(start, rows)
    below = pl.ds(start - 1, rows)
    above = pl.ds(start + 1, rows)
    v = src[slab, here]
    f = lev.at[F] if f is None else f
    x = lev[FX, slab, here] * src[slab - 1, here] + lev[FX, slab + 1, here] * src[slab + 1, here]
    y = lev[FY, slab, here] * src[slab, below] + lev[FY, slab, above] * src[slab, above]
    z = lev[ZL, slab, here] * roll_lanes(v, 1) + lev[ZH, slab, here] * roll_lanes(v, -1)
    total = ((x + y) + f[slab, here]) + z
    return v, total


def swept(lev, src, slab, start, rows, f=None):
    v, total = weighted(lev, src, slab, start, rows, f)
    return (1.0 - OMEGA) * v + lev[W, slab, pl.ds(start, rows)] * total


def set_weights(lev, slab, start, rows, depth, inside=None):
    here = pl.ds(start, rows)
    fz = lev[ZL, slab, here]
    z = lanes_of(fz.shape) % depth
    upper = jnp.where(z == depth - 1, 0.0, roll_lanes(fz, -1))
    diagonal = lev[FX, slab, here] + lev[FX, slab + 1, here]
    diagonal = diagonal + lev[FY, slab, here] + lev[FY, slab, pl.ds(start + 1, rows)] + fz + upper
    valid = diagonal > 0.0
    if inside is not None:
        valid = valid & inside
    lev[ZL, slab, here] = jnp.where(z == 0, 0.0, fz)
    lev[ZH, slab, here] = upper
    lev[D, slab, here] = diagonal
    lev[W, slab, here] = jnp.where(valid, OMEGA / jnp.where(valid, diagonal, 1.0), 0.0)


def run(count, body):
    for index in range(count):
        body(index)


def clear_pads(ref, rows):
    for start in (0, RIM + rows):
        ref[:, start : start + RIM] = jnp.zeros((ref.shape[0], RIM, LANES), F32)


def level_down(axes, own, faces, coefficients, x_low, x_high, y_low, y_high, *refs):
    top, kept, chunk, v_low, v_high, other, tmp, one, two, mid, wide = refs
    nx, ny = own.shape[1:3]
    slabs, rows = nx + 2 * EDGE, ny + 2 * RIM
    me_x, me_y = lax.axis_index(axes[0]), lax.axis_index(axes[1])
    inner = pl.ds(PAD, ny)
    for index, slot in enumerate(SLOTS):
        layers, width = X_LAYERS[index], Y_LAYERS[index]
        top[slot, :, :PAD] = jnp.zeros((slabs, PAD, LANES), F32)
        top[slot, :, PAD + ny :] = jnp.zeros((slabs, PAD, LANES), F32)
        top[slot, EDGE : EDGE + nx, inner] = own[index]
        for layer in range(EDGE):
            if layer < layers:
                top[slot, EDGE - layers + layer, inner] = x_low[x_place(index, layer, ny)]
                top[slot, EDGE + nx + layer, inner] = x_high[x_place(index, layer, ny)]
            else:
                top[slot, EDGE - 1 - layer, inner] = jnp.zeros((ny, LANES), F32)
                top[slot, EDGE + nx + layer, inner] = jnp.zeros((ny, LANES), F32)
        for slab in range(-Y_REACH[index], nx + Y_REACH[index]):
            top[slot, EDGE + slab, PAD - width : PAD] = y_low[y_place(index, slab, nx)]
            top[slot, EDGE + slab, PAD + ny : PAD + ny + width] = y_high[y_place(index, slab, nx)]
    clear_pads(other, rows)

    coarse_x, coarse_y = nx // 2, ny // 2
    near = RIM - 1
    for slot in (FX, FY, ZL, ZH, W, D):
        mid[slot] = jnp.zeros(mid.shape[1:], F32)
    x, y, z = coarse_slab_sums(top.at[FX], top.at[FY], top.at[ZL], coarse_x + 2, EDGE - 2, wide)
    both = halved(jnp.concatenate((x, y)))
    mid[FX, near : near + coarse_x + 3, RIM : 3 * RIM + coarse_y] = both[: coarse_x + 3]
    mid[FY, near : near + coarse_x + 2, RIM : 3 * RIM + coarse_y] = both[coarse_x + 3 :]
    mid[ZL, near : near + coarse_x + 2, RIM : 3 * RIM + coarse_y] = halved(z, True)

    row_inside = (rows_of((rows, LANES)) >= RIM) | (me_y > 0)
    main = pl.ds(RIM, rows)
    start_v = top.at[V]

    def first(index):
        slab = index + 1
        inside = row_inside & ((slab >= EDGE) | (me_x > 0))
        set_weights(top, slab, RIM, rows, LANES, inside)
        other[slab, main] = swept(top, start_v, slab, RIM, rows)

    run(slabs - 2, first)

    def second(index):
        slab = index + 2
        top[V, slab, main] = swept(top, other, slab, RIM, rows)

    run(slabs - 4, second)

    def rest(slab):
        v, total = weighted(top, top.at[V], slab, PAD, ny)
        return total - top[D, slab, inner] * v

    def residual(index):
        slab = EDGE + 2 * index
        tmp[index] = rest(slab) + rest(slab + 1)

    run(nx // 2, residual)

    slabs, rows = coarse_x + 2 * RIM, coarse_y + 2 * RIM
    half = slabs // 2
    inner = pl.ds(2 * RIM, coarse_y)
    main = pl.ds(RIM, rows)
    row_inside = (rows_of((rows, LANES)) >= RIM) | (me_y > 0)
    for slab in range(near, near + coarse_x + 2):
        inside = row_inside & (me_x > 0) if slab < RIM else row_inside
        set_weights(mid, slab, RIM, rows, HALF, inside)

    source = even_rows(tmp, ny) + odd_rows(tmp, ny)
    source = 0.5 * exact_dot(source.reshape(coarse_x * coarse_y, LANES), compact(LANES, 0))
    for ref in (mid.at[F], mid.at[V], one):
        ref[...] = jnp.zeros(ref.shape, F32)
    mid[F, RIM : RIM + coarse_x, inner] = source.reshape(coarse_x, coarse_y, LANES)
    for slab in range(RIM, RIM + coarse_x):
        mid[V, slab, inner] = mid[W, slab, inner] * mid[F, slab, inner]
    for layer in range(RIM // 2):
        near, far = RIM + layer, coarse_x + layer
        v_low[layer * coarse_y : (layer + 1) * coarse_y] = two_in_one(
            mid[V, near, inner], mid[V, near + RIM // 2, inner]
        )
        v_high[layer * coarse_y : (layer + 1) * coarse_y] = two_in_one(
            mid[V, far, inner], mid[V, far + RIM // 2, inner]
        )
    kept[0] = mid[F, RIM : RIM + coarse_x, inner]
    kept[1] = mid[V, RIM : RIM + coarse_x, inner]
    base, after, _ = rim_rows_x(nx, ny)
    pairs = RIM // 2
    for face in range(3):
        for layer in range(pairs):
            place = pl.ds(base + after + (face * pairs + layer) * coarse_y, coarse_y)
            far = coarse_x - RIM + layer
            v_low[place] = two_in_one(faces[face, layer], faces[face, layer + pairs])
            v_high[place] = two_in_one(faces[face, far], faces[face, far + pairs])
    for layer in range(2):
        place = pl.ds(base + layer * ny, ny)
        v_low[place] = top[V, EDGE + layer, pl.ds(PAD, ny)]
        v_high[place] = top[V, EDGE + nx - 2 + layer, pl.ds(PAD, ny)]
    for slab in range(RIM - 1, RIM + coarse_x + 1):
        one[slab, main] = swept(mid, mid.at[V], slab, RIM, rows)

    def rest_1(slab):
        v, total = weighted(mid, one, slab, RIM, rows)
        return total - mid[D, slab, main] * v

    two[...] = jnp.zeros(two.shape, F32)
    for pair in range(1, half - 1):
        two[pair] = rest_1(2 * pair) + rest_1(2 * pair + 1)
    pieces = even_rows(two, rows) + odd_rows(two, rows)
    coarse_rows, quarter_rows = rows // 2, rows // 4
    chunk[:coarse_rows] = 0.5 * fold_four([pieces[1 + i] for i in range(4)])
    rest_of = [pieces[5 + i // 2][i % 2 * quarter_rows :][:quarter_rows] for i in range(4)]
    chunk[coarse_rows : coarse_rows + quarter_rows] = 0.5 * fold_four(rest_of)
    chunk[coarse_rows + quarter_rows :] = coefficients[:BLOCK_ROWS - coarse_rows - quarter_rows]
    block = me_x // (lax.axis_size(axes[0]) // 4)
    values = turned = chunk[...]
    for turn in range(1, 4):
        turned = jnp.where(block == turn, roll_lanes(values, turn * (LANES // 4)), turned)
    chunk[...] = turned


def pack_v(top, kept, faces, x_low, x_high, low, high):
    coarse_x, coarse_y = faces.shape[1:3]
    nx, ny = 2 * coarse_x, 2 * coarse_y
    slabs = coarse_x + 2 * RIM
    half = slabs // 2
    sizes_x, sizes_y = rim_rows_x(nx, ny), rim_rows_y(nx, ny)

    def folded(own, place_x, place_y):
        values = [
            wide_slab(
                slab,
                lambda layer: rim_slab(x_low, place_x, coarse_y, layer),
                own,
                lambda layer: rim_slab(x_high, place_x, coarse_y, layer),
            )
            for slab in range(slabs)
        ]
        for slab in range(half):
            both = two_in_one(values[slab], values[slab + half])
            rows = pl.ds(place_y + slab * RIM, RIM)
            low[rows] = both[:RIM]
            high[rows] = both[coarse_y - RIM :]

    folded(kept.at[1], 0, 0)
    for face in range(3):
        folded(
            faces.at[face],
            sizes_x[0] + sizes_x[1] + face * sizes_x[0],
            sizes_y[0] + sizes_y[1] + face * sizes_y[0],
        )
    base_x, base_y = sizes_x[0], sizes_y[0]
    for out, start in ((low, 0), (high, ny - 2)):
        for layer in range(2):
            rows = pl.ds(base_x + layer * ny + start, 2)
            out[pl.ds(base_y + 2 * layer, 2)] = x_low[rows]
            out[pl.ds(base_y + 2 * (2 + nx + layer), 2)] = x_high[rows]
        for slab in range(nx):
            out[pl.ds(base_y + 2 * (2 + slab), 2)] = top[V, EDGE + slab, pl.ds(PAD + start, 2)]


def stack_blocks(*refs):
    for index, ref in enumerate(refs[:-1]):
        refs[-1][index] = ref[...]


def hand_on(first, second, _, first_out, second_out):
    first_out[...] = first[...]
    second_out[...] = second[...]


def pair_rows(values, stride):
    return values + roll_rows(values, -stride)


def pair_lanes(values, stride):
    return values + roll_lanes(values, -stride)


class Listed:
    def __init__(self, fx, fy, fz, stride, depth):
        self.fx, self.fy, self.fz, self.stride, self.depth = fx, fy, fz, stride, depth
        shape = fx[0].shape
        rows = shape[0]
        row, lane = rows_of(shape), lanes_of(shape)
        z = lane % depth
        count = self.count = len(fx)
        self.x_high = [
            fx[s + 1] if s + 1 < count else jnp.where(lane < LANES - depth, roll_lanes(fx[0], -depth), 0.0)
            for s in range(count)
        ]
        self.x_low = [fx[s] if s > 0 else jnp.where(lane >= depth, fx[0], 0.0) for s in range(count)]
        self.y_high = [jnp.where(row < rows - stride, roll_rows(f, -stride), 0.0) for f in fy]
        self.y_low = [jnp.where(row >= stride, f, 0.0) for f in fy]
        self.z_high = [jnp.where(z < depth - stride, roll_lanes(f, -stride), 0.0) for f in fz]
        self.z_low = [jnp.where(z >= stride, f, 0.0) for f in fz]
        self.d = [
            fx[s] + self.x_high[s] + fy[s] + self.y_high[s] + fz[s] + self.z_high[s] for s in range(count)
        ]
        self.w = [jnp.where(d > 0.0, OMEGA / jnp.where(d > 0.0, d, 1.0), 0.0) for d in self.d]

    def weighted(self, v, f):
        count = self.count
        out = []
        for s in range(count):
            low = v[s - 1] if s > 0 else roll_lanes(v[count - 1], self.depth)
            high = v[s + 1] if s + 1 < count else roll_lanes(v[0], -self.depth)
            x = self.x_low[s] * low + self.x_high[s] * high
            y = self.y_low[s] * roll_rows(v[s], self.stride) + self.y_high[s] * roll_rows(v[s], -self.stride)
            z = self.z_low[s] * roll_lanes(v[s], self.stride) + self.z_high[s] * roll_lanes(v[s], -self.stride)
            total = (f[s] + y) + (x + z)
            out.append(total)
        return out

    def sweep(self, v, f):
        totals = self.weighted(v, f)
        return [(1.0 - OMEGA) * v[s] + self.w[s] * totals[s] for s in range(self.count)]

    def sweeps(self, count, f):
        folded = [
            [w * c for w, c in zip(self.w, coefficients)]
            for coefficients in (self.x_low, self.x_high, self.y_low, self.y_high, self.z_low, self.z_high)
        ]
        scaled = self.start(f)
        slabs = self.count

        def step(index, v):
            out = []
            for s in range(slabs):
                low = v[s - 1] if s > 0 else roll_lanes(v[slabs - 1], self.depth)
                high = v[s + 1] if s + 1 < slabs else roll_lanes(v[0], -self.depth)
                x = folded[0][s] * low + folded[1][s] * high
                y = folded[2][s] * roll_rows(v[s], self.stride) + folded[3][s] * roll_rows(v[s], -self.stride)
                z = folded[4][s] * roll_lanes(v[s], self.stride) + folded[5][s] * roll_lanes(v[s], -self.stride)
                out.append((((1.0 - OMEGA) * v[s] + scaled[s]) + y) + (x + z))
            return out

        return lax.fori_loop(1, count, step, scaled)

    def start(self, f):
        return [self.w[s] * f[s] for s in range(self.count)]

    def residual(self, v, f):
        totals = self.weighted(v, f)
        return [totals[s] - self.d[s] * v[s] for s in range(self.count)]

    def kept(self):
        shape = self.fx[0].shape
        step = 2 * self.stride
        return (rows_of(shape) % step == 0) & (lanes_of(shape) % step == 0)

    def coarser(self):
        keep, stride = self.kept(), self.stride
        half = range(self.count // 2)

        def kept(values):
            return jnp.where(keep, 0.25 * values, 0.0)

        fx = [kept(pair_lanes(pair_rows(self.fx[2 * s], stride), stride)) for s in half]
        fy = [kept(pair_lanes(self.fy[2 * s] + self.fy[2 * s + 1], stride)) for s in half]
        fz = [kept(pair_rows(self.fz[2 * s] + self.fz[2 * s + 1], stride)) for s in half]
        return Listed(fx, fy, fz, 2 * stride, self.depth)

    def restrict(self, r):
        keep, stride = self.kept(), self.stride
        return [
            jnp.where(keep, 0.5 * pair_lanes(pair_rows(r[2 * s] + r[2 * s + 1], stride), stride), 0.0)
            for s in range(self.count // 2)
        ]

    def prolong(self, e):
        out = []
        for values in e:
            values = values + roll_rows(values, self.stride)
            values = values + roll_lanes(values, self.stride)
            out += [values, values]
        return out


def listed_cycle(levels, sweeps, f):
    level = levels[0]
    if len(levels) == 1:
        return level.sweeps(sweeps, f)
    v = level.sweep(level.start(f), f)
    e = listed_cycle(levels[1:], sweeps, level.restrict(level.residual(v, f)))
    v = [a + b for a, b in zip(v, level.prolong(e))]
    return level.sweep(level.sweep(v, f), f)


def level_two(axes, grid, sweeps, shape, pieces, out, wide, tall):
    devices_x, devices_y = grid
    me_x, me_y = lax.axis_index(axes[0]), lax.axis_index(axes[1])
    own_x, own_y = shape
    quarter = LANES // 4
    reach = RIM // 2
    blocks = 4
    count = devices_x * own_x // blocks
    rows = devices_y * own_y
    main = pl.ds(PAD, rows)
    window = own_y + RIM

    def piece(gx, gy):
        slow, far = (me_x // 2) ^ (gx // 2), (me_y // 2) ^ (gy // 2)
        return ((me_y + gy) % 2, (me_x + gx) % 2 * (devices_y // 2) + far, slow)

    for ref in (wide, tall):
        ref[...] = jnp.zeros(ref.shape, F32)
    per_block = count // own_x

    def merged(values, shift, turn):
        at = lanes_of(values[0].shape) // quarter
        out = values[0]
        for block in range(1, blocks):
            out = jnp.where(at == (shift + block) % blocks, values[block], out)
        return roll_lanes(out, (turn - shift) * quarter)

    lane = lanes_of((window, LANES))
    for gy in range(devices_y):
        sums = [None] * count
        for turn in range(per_block):
            where = [piece(block * per_block + turn, gy) for block in range(blocks)]
            first = [pieces[at + (pl.ds(0, window),)] for at in where]
            second = [pieces[at + (pl.ds(window, window // 2),)] for at in where]
            for local in range(1, 2 * blocks - 1):
                offset = own_x * turn - reach + local
                over, slab = offset // count, offset % count
                if local <= blocks:
                    moved = merged(first, local - 1, over)
                else:
                    at = 2 * (local - blocks - 1)
                    moved = jnp.concatenate([merged(second, at + odd, over) for odd in range(2)])
                if over < 0:
                    moved = jnp.where(lane // quarter == blocks - 1, 0.0, moved)
                elif over > 0:
                    moved = jnp.where(lane // quarter == 0, 0.0, moved)
                sums[slab] = moved if sums[slab] is None else sums[slab] + moved
        place = pl.ds(PAD + own_y * gy - reach, window)
        for slab in range(count):
            tall[slab, place] = tall[slab, place] + sums[slab]
    f = [tall[slab, main] for slab in range(count)]

    lane = lanes_of((rows, LANES))
    for gx in range(devices_x):
        for gy in range(devices_y):
            where = piece(gx, gy)
            for face in range(3):
                values = pieces[where + (pl.ds(window + window // 2 + face * own_y, own_y),)]
                wide[face, gx, gy * own_y : (gy + 1) * own_y] = values
    faces = []
    for face in range(3):
        slabs = []
        for turn in range(per_block):
            values = [wide[face, block * per_block + turn] for block in range(blocks)]
            slabs += [merged(values, local, 0) for local in range(own_x)]
        faces.append(slabs)
    levels = [Listed(*faces, 1, quarter)]
    while len(levels) < LEVELS - 2:
        levels.append(levels[-1].coarser())
    e = listed_cycle(levels, sweeps, f)

    for slab in range(count):
        out[reach + slab, main] = e[slab]
    for slab in range(reach):
        out[slab, main] = jnp.where(lane < quarter, 0.0, roll_lanes(e[count - reach + slab], quarter))
        out[reach + count + slab, main] = jnp.where(
            lane >= LANES - quarter, 0.0, roll_lanes(e[slab], -quarter)
        )
    out[:, :PAD] = jnp.zeros((count + 2 * reach, PAD, LANES), F32)
    out[:, PAD + rows :] = jnp.zeros((count + 2 * reach, PAD, LANES), F32)


def level_up(axes, grid, coarse, top, kept, faces, x_low, x_high, y_low, y_high, *refs):
    out, mid, one, two, right, post, up = refs
    devices_x, devices_y = grid
    me_x, me_y = lax.axis_index(axes[0]), lax.axis_index(axes[1])
    coarse_x, coarse_y = faces.shape[1:3]
    nx, ny = out.shape[:2]
    own_x, own_y = coarse_x // 2, coarse_y // 2
    quarter = LANES // 4
    reach = RIM // 2
    window = own_y + RIM

    slabs, high = coarse_x + 2 * RIM, coarse_y + 2 * RIM
    half = slabs // 2
    inner = pl.ds(2 * RIM, coarse_y)
    body = pl.ds(RIM, high)
    sizes_x, sizes_y = rim_rows_x(nx, ny), rim_rows_y(nx, ny)
    for face, slot in enumerate((FX, FY, ZL)):
        clear_pads(mid.at[slot], high)
        mid[slot, RIM : RIM + coarse_x, inner] = faces[face]
        place_x = sizes_x[0] + sizes_x[1] + face * sizes_x[0]
        place_y = sizes_y[0] + sizes_y[1] + face * sizes_y[0]
        for layer in range(RIM):
            mid[slot, layer, inner] = rim_slab(x_low, place_x, coarse_y, layer)
            mid[slot, RIM + coarse_x + layer, inner] = rim_slab(x_high, place_x, coarse_y, layer)
        for slab in range(half):
            place = pl.ds(place_y + slab * RIM, RIM)
            for message, row in ((y_low, RIM), (y_high, 2 * RIM + coarse_y)):
                pair = one_of_two(message[place])
                mid[slot, slab, row : row + RIM] = pair[0]
                mid[slot, slab + half, row : row + RIM] = pair[1]
    row_inside = (rows_of((high, LANES)) >= RIM) | (me_y > 0)
    for slab in range(slabs - 1):
        inside = row_inside & (me_x > 0) if slab < RIM else row_inside
        set_weights(mid, slab, RIM, high, HALF, inside)
    clear_pads(one, high)
    clear_pads(right, high)
    clear_pads(two, high)
    one[RIM : RIM + coarse_x, inner] = kept[1]
    right[RIM : RIM + coarse_x, inner] = kept[0]
    for layer in range(RIM):
        one[layer, inner] = rim_slab(x_low, 0, coarse_y, layer)
        one[RIM + coarse_x + layer, inner] = rim_slab(x_high, 0, coarse_y, layer)
    for slab in range(half):
        place = pl.ds(slab * RIM, RIM)
        for message, row in ((y_low, RIM), (y_high, 2 * RIM + coarse_y)):
            pair = one_of_two(message[place])
            one[slab, row : row + RIM] = pair[0]
            one[slab + half, row : row + RIM] = pair[1]
    row = rows_of((high, LANES))
    own_row = (row >= RIM) & (row < RIM + coarse_y)
    for slab in range(1, slabs - 1):
        f_rim = one[slab, body] * mid[D, slab, body] * (1.0 / OMEGA)
        if RIM <= slab < RIM + coarse_x:
            f_rim = jnp.where(own_row, right[slab, body], f_rim)
        right[slab, body] = f_rim
        two[slab, body] = swept(mid, one, slab, RIM, high, right)

    per_block = (coarse.shape[0] - 2 * reach) // own_x
    base = me_x % per_block * own_x
    mine = None
    for gy in range(devices_y):
        place = pl.ds(PAD + gy * own_y - reach, window)
        values = jnp.where(me_y == gy, coarse[pl.ds(base, half), place, :], 0.0)
        mine = values if mine is None else mine + values
    source = lax.broadcasted_iota(jnp.int32, (LANES, LANES), 0)
    target = lax.broadcasted_iota(jnp.int32, (LANES, LANES), 1)
    hit = (source == me_x // per_block * quarter + target // 2) & (target < HALF)
    fine = exact_dot(mine.reshape(half * window, LANES), jnp.where(hit, 1.0, 0.0).astype(F32))
    fine = fine.reshape(half, window, LANES)
    for odd in range(2):
        up[:half, pl.ds(odd, window, stride=2), :] = fine
    for pair in range(half):
        for slab in (2 * pair, 2 * pair + 1):
            if 1 <= slab < slabs - 1:
                two[slab, body] = two[slab, body] + up[pair, :high]
    for slab in range(2, slabs - 2):
        one[slab, body] = swept(mid, two, slab, RIM, high, right)
    for slab in range(3, slabs - 3):
        two[slab, body] = swept(mid, one, slab, RIM, high, right)

    steps = coarse_x + 2
    fine_rows = ny + 2 * RIM
    e = two[RIM - 1 : RIM - 1 + steps, body]
    fine = exact_dot(e.reshape(steps * high, LANES), expand(LANES, 0)).reshape(steps, high, LANES)
    fine = fine[:, reach : reach + fine_rows // 2]
    for odd in range(2):
        up[:, pl.ds(odd, fine_rows // 2, stride=2), :] = fine
    body = pl.ds(RIM, fine_rows)
    for slot in (0, 1):
        clear_pads(post.at[slot], fine_rows)
    inner = pl.ds(PAD, ny)
    post[0, EDGE : EDGE + nx, inner] = top[V, EDGE : EDGE + nx, inner]
    base_x, base_y = RIM // 2 * coarse_y, half * RIM
    for layer in range(2):
        place = pl.ds(base_x + layer * ny, ny)
        post[0, EDGE - 2 + layer, inner] = x_low[place]
        post[0, EDGE + nx + layer, inner] = x_high[place]
    for slab in range(nx + 4):
        place = pl.ds(base_y + 2 * slab, 2)
        post[0, slab + EDGE - 2, RIM:PAD] = jnp.zeros((RIM, LANES), F32)
        post[0, slab + EDGE - 2, PAD + ny : PAD + ny + RIM] = jnp.zeros((RIM, LANES), F32)
        post[0, slab + EDGE - 2, PAD - 2 : PAD] = y_low[place]
        post[0, slab + EDGE - 2, PAD + ny : PAD + ny + 2] = y_high[place]

    def raise_level(index):
        for slab in (EDGE - 2 + 2 * index, EDGE - 1 + 2 * index):
            post[0, slab, body] = post[0, slab, body] + up[index]

    run(steps, raise_level)

    def fifth(index):
        slab = EDGE - 1 + index
        post[1, slab, body] = swept(top, post.at[0], slab, RIM, fine_rows)

    run(nx + 2, fifth)

    def sixth(index):
        out[index] = swept(top, post.at[1], EDGE + index, PAD, ny)

    run(nx, sixth)


IN_VMEM = pl.BlockSpec(memory_space=pltpu.VMEM)


def call(kernel, outs, scratch=(), from_hbm=False):
    ins = pl.BlockSpec(memory_space=pl.ANY) if from_hbm else IN_VMEM

    def launch(*args):
        if from_hbm:
            args = [pltpu.with_memory_space_constraint(arg, pltpu.HBM) for arg in args]
        return pl.pallas_call(
            kernel,
            out_shape=[pltpu.VMEM(shape, F32) for shape in outs],
            in_specs=[ins] * len(args),
            out_specs=[IN_VMEM] * len(outs),
            scratch_shapes=[pltpu.VMEM(s, F32) if isinstance(s, tuple) else s for s in scratch],
            compiler_params=pltpu.CompilerParams(vmem_limit_bytes=24 * 2**20),
        )(*args)

    return launch


def pair_route(axis):
    return [(i, i ^ 1) for i in range(lax.axis_size(axis))]


def swap_route(axis):
    count = lax.axis_size(axis)
    return [(i, (i + 1 ^ 1) - 1) for i in range(1, count - 1)]


def by_partner(low, high, axis):
    odd = lax.axis_index(axis) % 2 == 1
    return jnp.where(odd, low, high), jnp.where(odd, high, low)


def from_sides(low, high, axis):
    pair, swap = by_partner(low, high, axis)
    pair = lax.ppermute(pair, axis, pair_route(axis))
    swap = lax.ppermute(swap, axis, swap_route(axis))
    return by_partner(pair, swap, axis)


def passed_round(block, axis, stride):
    count = lax.axis_size(axis)
    return [block] + [
        lax.ppermute(block, axis, [(i, i ^ distance) for i in range(count)])
        for distance in range(stride, count, stride)
    ]


def passed_across(block, rider):
    count, size = lax.axis_size("gx"), lax.axis_size("gy")
    rows = block.shape[0]
    blocks = [block]
    for side in range(2):
        for distance in range(0, size, 2):
            route = [
                (x * size + y, (x ^ side) * size + (y ^ distance)) for x in range(count) for y in range(size)
            ]
            if side == 1 and distance == 0:
                both = lax.ppermute(jnp.concatenate((block, rider)), ("gx", "gy"), route)
                blocks.append(both[:rows])
                rider = both[rows:]
            elif distance > 0:
                blocks.append(lax.ppermute(block, ("gx", "gy"), route))
    return blocks, rider


def fused_cycle(*fields):
    axes = ("gx", "gy")
    devices_x, devices_y = lax.axis_size("gx"), lax.axis_size("gy")
    nx, ny, nz = fields[0].shape
    coarse_x, coarse_y = nx // 2, ny // 2
    x_shape, y_shape = (x_rows(nx, ny), LANES), (y_rows(nx, ny), LANES)
    own, x_low, x_high = call(
        start_pack, [(5, nx, ny, nz), x_shape, x_shape], [pltpu.SemaphoreType.DMA((5,))], True
    )(*fields)
    x_low, x_high = from_sides(x_low, x_high, "gx")
    faces, coefficients = call(
        coarse_faces,
        [(3, coarse_x, coarse_y, LANES), (16, LANES)],
        [(coarse_x, ny, LANES), (coarse_x // 2, coarse_y, LANES)],
    )(own)
    y_low, y_high = call(pack_y, [y_shape] * 2)(own, x_low, x_high)
    y_low, y_high = from_sides(y_low, y_high, "gy")
    stack = (nx + 2 * EDGE, ny + 4 * RIM, LANES)
    stack_1 = (coarse_x + 2 * RIM, coarse_y + 4 * RIM, LANES)
    half = stack_1[0] // 2
    v_shape = (sum(rim_rows_x(nx, ny)), LANES)
    w_shape = (sum(rim_rows_y(nx, ny)), LANES)
    top, kept, chunk, v_low, v_high = call(
        functools.partial(level_down, axes),
        [(D + 1,) + stack, (2, coarse_x, coarse_y, LANES), (BLOCK_ROWS, LANES), v_shape, v_shape],
        [
            stack,
            (nx // 2, ny, LANES),
            stack_1,
            (half, coarse_y + 2 * RIM, LANES),
            (D + 1,) + stack_1,
            (coarse_x + 3,) + stack[1:],
        ],
    )(own, faces, coefficients, x_low, x_high, y_low, y_high)

    blocks = passed_round(chunk, "gx", 2)
    slow = (len(blocks),) + chunk.shape
    (pieces,) = call(stack_blocks, [slow])(*blocks)
    v_low, v_high = call(hand_on, [v_shape, v_shape])(v_low, v_high, pieces)
    pair, swap = by_partner(v_low, v_high, "gx")
    swap = lax.ppermute(swap, "gx", swap_route("gx"))
    blocks, pair = passed_across(pieces.reshape(-1, LANES), pair)
    v_low, v_high = by_partner(pair, swap, "gx")
    w_low, w_high = call(pack_v, [w_shape] * 2)(top, kept, faces, v_low, v_high)
    pair, swap = by_partner(w_low, w_high, "gy")
    message = jnp.concatenate(blocks + [pair])
    swap = lax.ppermute(swap, "gy", swap_route("gy"))
    other = lax.ppermute(message, "gy", pair_route("gy"))
    rows = message.shape[0] - w_shape[0]
    pieces = jnp.stack((message[:rows], other[:rows])).reshape((2, len(blocks)) + slow)
    w_low, w_high = by_partner(other[rows:], swap, "gy")
    count = devices_x * nx // 16
    rows = devices_y * ny // 4
    grid = (devices_x, devices_y)
    coarsest = (devices_x * nx >> LEVELS - 1, devices_y * ny >> LEVELS - 1)
    wide = (count + RIM, rows + 2 * PAD, LANES)
    (coarse,) = call(
        functools.partial(level_two, axes, grid, 4 * max(coarsest), (nx // 4, ny // 4)),
        [wide],
        [(3, devices_x, rows, LANES), wide],
    )(pieces)
    return pl.pallas_call(
        functools.partial(level_up, axes, grid),
        out_shape=jax.ShapeDtypeStruct((nx, ny, nz), F32),
        in_specs=[IN_VMEM] * 8,
        out_specs=IN_VMEM,
        scratch_shapes=[
            pltpu.VMEM(shape, F32)
            for shape in ((D + 1,) + stack_1, stack_1, stack_1, stack_1, (2,) + stack, (coarse_x + 2, ny + 2 * RIM, LANES))
        ],
        compiler_params=pltpu.CompilerParams(vmem_limit_bytes=24 * 2**20),
    )(coarse, top, kept, faces, v_low, v_high, w_low, w_high)


def with_halo(block, sides, width):
    for axis, dim in sides:
        count = lax.axis_size(axis)
        forward = [(i, i + 1) for i in range(count - 1)]
        backward = [(target, source) for source, target in forward]
        low = lax.ppermute(
            lax.slice_in_dim(block, block.shape[dim] - width, None, axis=dim), axis, forward
        )
        high = lax.ppermute(lax.slice_in_dim(block, 0, width, axis=dim), axis, backward)
        block = jnp.concatenate([low, block, high], axis=dim)
    return block


def passed_along(block, axis, distance):
    devices = range(lax.axis_size(axis))
    route = [(i - distance, i) for i in devices if i - distance in devices]
    return lax.ppermute(block, axis, route)


def stencil(padded, padded_x, padded_y, face_z):
    center = padded[1:-1, 1:-1]
    zero_plane = jnp.zeros(center.shape[:2] + (1,), center.dtype)
    above_face = jnp.concatenate((face_z[:, :, 1:], zero_plane), axis=2)
    below_z = jnp.concatenate((zero_plane, center[:, :, :-1]), axis=2)
    above_z = jnp.concatenate((center[:, :, 1:], zero_plane), axis=2)
    lower_x = padded_x[1:-1, 1:-1]
    upper_x = padded_x[2:, 1:-1]
    lower_y = padded_y[1:-1, 1:-1]
    upper_y = padded_y[1:-1, 2:]
    applied = lower_x * (center - padded[:-2, 1:-1]) + upper_x * (center - padded[2:, 1:-1])
    applied = (
        applied + lower_y * (center - padded[1:-1, :-2]) + upper_y * (center - padded[1:-1, 2:])
    )
    applied = applied + face_z * (center - below_z) + above_face * (center - above_z)
    diagonal = lower_x + upper_x + lower_y + upper_y + face_z + above_face
    return (applied, diagonal)


def jacobi_sweep(padded, source, padded_x, padded_y, face_z):
    applied, diagonal = stencil(padded, padded_x, padded_y, face_z)
    return padded[1:-1, 1:-1] + OMEGA * (source - applied) / diagonal


def pad_plane(values, width):
    return jnp.pad(values, ((width, width), (width, width), (0, 0)))


def restrict(residual):
    shape = residual.shape
    blocks = residual.reshape(shape[0] // 2, 2, shape[1] // 2, 2, shape[2] // 2, 2)
    return 4.0 * jnp.mean(blocks, axis=(1, 3, 5))


def coarsen_faces(face_x, face_y, face_z):
    shape = face_x.shape
    blocks = (shape[0] // 2, 2, shape[1] // 2, 2, shape[2] // 2, 2)
    coarse_x = jnp.mean(face_x.reshape(blocks)[:, 0], axis=(2, 4))
    coarse_y = jnp.mean(face_y.reshape(blocks)[:, :, :, 0], axis=(1, 4))
    coarse_z = jnp.mean(face_z.reshape(blocks)[..., 0], axis=(1, 3))
    return (coarse_x, coarse_y, coarse_z)


def prolong(coarse):
    return jnp.repeat(jnp.repeat(jnp.repeat(coarse, 2, axis=0), 2, axis=1), 2, axis=2)


def local_cycle(grid_level, iterate, source, face_x, face_y, face_z):
    padded_x = pad_plane(face_x, 1)
    padded_y = pad_plane(face_y, 1)
    if grid_level == LEVELS - 1:
        count = 4 * max(iterate.shape[0], iterate.shape[1])

        def one_sweep(index, values):
            return jacobi_sweep(pad_plane(values, 1), source, padded_x, padded_y, face_z)

        return lax.fori_loop(0, count, one_sweep, iterate)
    for sweep_index in range(2):
        iterate = jacobi_sweep(pad_plane(iterate, 1), source, padded_x, padded_y, face_z)
    applied, diagonal = stencil(pad_plane(iterate, 1), padded_x, padded_y, face_z)
    coarse_src = restrict(source - applied)
    coarse_x, coarse_y, coarse_z = coarsen_faces(face_x, face_y, face_z)
    correction = local_cycle(
        grid_level + 1, jnp.zeros_like(coarse_src), coarse_src, coarse_x, coarse_y, coarse_z
    )
    iterate = iterate + prolong(correction)
    for sweep_index in range(2):
        iterate = jacobi_sweep(pad_plane(iterate, 1), source, padded_x, padded_y, face_z)
    return iterate


def field_rim(iterate):
    return with_halo(iterate, (("gx", 0), ("gy", 1)), 1)


def sweep_pair_narrow(iterate, source, padded_x, padded_y, face_z, zero_start):
    for sweep_index in range(2):
        if sweep_index == 0 and zero_start:
            padded = pad_plane(iterate, 1)
        else:
            padded = field_rim(iterate)
        iterate = jacobi_sweep(padded, source, padded_x, padded_y, face_z)
    return iterate


def descend(grid_level, iterate, source, face_x, face_y, face_z, zero_start, gather_level):
    if grid_level == gather_level:
        pieces = (
            lax.all_gather(source, "gy", axis=1, tiled=True),
            lax.all_gather(face_x, "gy", axis=1, tiled=True),
            lax.all_gather(face_y, "gy", axis=1, tiled=True),
            lax.all_gather(face_z, "gy", axis=1, tiled=True),
        )
        gathered = (
            lax.all_gather(pieces[0], "gx", axis=0, tiled=True),
            lax.all_gather(pieces[1], "gx", axis=0, tiled=True),
            lax.all_gather(pieces[2], "gx", axis=0, tiled=True),
            lax.all_gather(pieces[3], "gx", axis=0, tiled=True),
        )
        correction = local_cycle(
            grid_level,
            jnp.zeros_like(gathered[0]),
            gathered[0],
            gathered[1],
            gathered[2],
            gathered[3],
        )
        start_x = lax.axis_index("gx") * source.shape[0]
        start_y = lax.axis_index("gy") * source.shape[1]
        return lax.dynamic_slice(
            correction, (start_x, start_y, jnp.zeros((), jnp.int32)), source.shape
        )
    next_x = passed_along(face_x[:1], "gx", -1)
    next_y = passed_along(face_y[:, :1], "gy", -1)
    lower_row = jnp.zeros_like(next_x)
    lower_col = jnp.zeros_like(next_y)
    padded_x = jnp.pad(
        jnp.concatenate((lower_row, face_x, next_x), axis=0), ((0, 0), (1, 1), (0, 0))
    )
    padded_y = jnp.pad(
        jnp.concatenate((lower_col, face_y, next_y), axis=1), ((1, 1), (0, 0), (0, 0))
    )

    def smoother(values, starting):
        return sweep_pair_narrow(values, source, padded_x, padded_y, face_z, starting)

    iterate = smoother(iterate, zero_start)
    applied, diagonal = stencil(field_rim(iterate), padded_x, padded_y, face_z)
    coarse_src = restrict(source - applied)
    coarse_x, coarse_y, coarse_z = coarsen_faces(face_x, face_y, face_z)
    correction = descend(
        grid_level + 1,
        jnp.zeros_like(coarse_src),
        coarse_src,
        coarse_x,
        coarse_y,
        coarse_z,
        True,
        gather_level,
    )
    iterate = iterate + prolong(correction)
    return smoother(iterate, False)


def fits(nx, ny, nz, devices_x, devices_y):
    cells = devices_x * nx * devices_y * ny * nz // 8
    even = devices_x % 8 == 0 and devices_y % 4 == 0
    even = even and devices_x & (devices_x - 1) == 0 and devices_y & (devices_y - 1) == 0
    return cells <= 2**18 and even and (nx, ny, nz) == (16, 16, LANES)


def local(source_term, initial_guess, face_x, face_y, face_z):
    if fits(*source_term.shape, lax.axis_size("gx"), lax.axis_size("gy")):
        return fused_cycle(source_term, initial_guess, face_x, face_y, face_z)
    gather_level = 4
    return descend(0, initial_guess, source_term, face_x, face_y, face_z, False, gather_level)


def solution(mesh):
    placed = (P("gx", "gy", None),) * 5
    return jax.shard_map(
        local, mesh=mesh, in_specs=placed, out_specs=P("gx", "gy", None), check_vma=False
    )
```

```python
import functools

import jax
import jax.numpy as jnp
from jax import lax
from jax.experimental import pallas as pl
from jax.experimental.pallas import tpu as pltpu
from jax.sharding import PartitionSpec as P

LEVELS = 6
OMEGA = 0.8
LANES = 128
RIM = 4
EDGE = 3
PAD = 8
BLOCK_ROWS = 24
F32 = jnp.float32

V, F, FX, FY, ZL, ZH, W, D = range(8)
SLOTS = (F, V, FX, FY, ZL)
X_LAYERS = (2, 3, 3, 2, 2)
Y_LAYERS = (2, 3, 2, 3, 2)
Y_REACH = (1, 2, 2, 2, 1)


def lanes_of(shape):
    return lax.broadcasted_iota(jnp.int32, shape, len(shape) - 1)


def rows_of(shape):
    return lax.broadcasted_iota(jnp.int32, shape, len(shape) - 2)


def roll_lanes(values, step):
    return pltpu.roll(values, step % LANES, values.ndim - 1)


def roll_rows(values, step):
    return pltpu.roll(values, step % values.shape[-2], values.ndim - 2)


def exact_dot(left, right):
    return jnp.dot(left, right, precision=lax.Precision.HIGHEST, preferred_element_type=F32)


def compact(depth, part, even_only=False):
    source = lax.broadcasted_iota(jnp.int32, (LANES, LANES), 0)
    target = lax.broadcasted_iota(jnp.int32, (LANES, LANES), 1)
    half = depth // 2
    hit = target == (source // depth * 2 + part) * half + source % depth // 2
    if even_only:
        hit = hit & (source % 2 == 0)
    return jnp.where(hit, 1.0, 0.0).astype(F32)


def expand(depth, part):
    target = lax.broadcasted_iota(jnp.int32, (LANES, LANES), 0)
    source = lax.broadcasted_iota(jnp.int32, (LANES, LANES), 1)
    half = depth // 2
    hit = target == (source // depth * 2 + part) * half + source % depth // 2
    return jnp.where(hit, 1.0, 0.0).astype(F32)


def merge_lanes(values, depth, even_only=False):
    count, rows, _ = values.shape
    half = count // 2
    flat = values.reshape(2, half * rows, LANES)
    out = exact_dot(flat[0], compact(depth, 0, even_only))
    out = out + exact_dot(flat[1], compact(depth, 1, even_only))
    return out.reshape(half, rows, LANES)


def even_rows(ref, rows):
    return ref[:, pl.ds(0, rows // 2, stride=2), :]


def odd_rows(ref, rows):
    return ref[:, pl.ds(1, rows // 2, stride=2), :]


HALF = LANES // 2


def low_half(values):
    return jnp.where(lanes_of(values.shape) < HALF, values, 0.0)


def two_in_one(first, second):
    return first + roll_lanes(second, HALF)


def one_of_two(values):
    return low_half(values), low_half(roll_lanes(values, HALF))


def x_rows(nx, ny):
    return sum(X_LAYERS) * ny


def y_rows(nx, ny):
    return sum(layers * (nx + 2 * reach) for layers, reach in zip(Y_LAYERS, Y_REACH))


def rim_rows_x(nx, ny):
    slab = RIM // 2 * (ny // 2)
    return slab, 2 * ny, 3 * slab


def rim_rows_y(nx, ny):
    slabs = (nx // 2 + 2 * RIM) // 2 * RIM
    return slabs, 2 * (nx + 4), 3 * slabs


def x_place(index, layer, ny):
    return pl.ds((sum(X_LAYERS[:index]) + layer) * ny, ny)


def y_place(index, slab, nx):
    before = zip(Y_LAYERS[:index], Y_REACH[:index])
    start = sum(layers * (nx + 2 * reach) for layers, reach in before)
    return pl.ds(start + (Y_REACH[index] + slab) * Y_LAYERS[index], Y_LAYERS[index])


def start_pack(*refs):
    fields, (own, x_low, x_high, done) = refs[:5], refs[5:]
    copies = [pltpu.make_async_copy(ref, own.at[index], done.at[index]) for index, ref in enumerate(fields)]
    for copy in copies:
        copy.start()
    nx, ny = own.shape[1:3]
    for index, copy in enumerate(copies):
        copy.wait()
        for layer in range(X_LAYERS[index]):
            x_low[x_place(index, layer, ny)] = own[index, layer]
            x_high[x_place(index, layer, ny)] = own[index, nx - X_LAYERS[index] + layer]


def pair_slabs(ref):
    count = ref.shape[0]
    values = ref[...].reshape((count // 2, 2) + ref.shape[1:])
    return values[:, 0], values[:, 1]


def wide_slab(slab, from_low, own, from_high):
    count = own.shape[0]
    if slab < RIM:
        return from_low(slab)
    if slab < RIM + count:
        return own[slab - RIM]
    return from_high(slab - RIM - count)


def rim_slab(ref, base, rows, layer):
    place = pl.ds(base + layer % (RIM // 2) * rows, rows)
    return one_of_two(ref[place])[layer // (RIM // 2)]


def pack_y(own, x_low, x_high, low, high):
    nx, ny = own.shape[1:3]
    for index in range(5):
        width, layers, reach = Y_LAYERS[index], X_LAYERS[index], Y_REACH[index]
        for out, start in ((low, 0), (high, ny - width)):
            for slab in range(nx):
                out[y_place(index, slab, nx)] = own[index, slab, start : start + width]
            for layer in range(reach):
                rows = pl.ds(x_place(index, layers - reach + layer, ny).start + start, width)
                out[y_place(index, layer - reach, nx)] = x_low[rows]
                rows = pl.ds(x_place(index, layer, ny).start + start, width)
                out[y_place(index, nx + layer, nx)] = x_high[rows]


def fold_four(slabs, even_only=False):
    out = None
    for part in range(2):
        term = exact_dot(two_in_one(slabs[part], slabs[2 + part]), compact(HALF, part, even_only))
        out = term if out is None else out + term
    return out


def coarse_slab_sums(ref_x, ref_y, ref_z, count, first, tmp):
    extra = tmp.shape[0]
    rows = tmp.shape[1]
    for index in range(extra):
        tmp[index] = ref_x[first + 2 * index]
    x = even_rows(tmp, rows) + odd_rows(tmp, rows)
    for index in range(count):
        tmp[index] = ref_y[first + 2 * index] + ref_y[first + 2 * index + 1]
    y = even_rows(tmp, rows)[:count]
    for index in range(count):
        tmp[index] = ref_z[first + 2 * index] + ref_z[first + 2 * index + 1]
    return x, y, (even_rows(tmp, rows) + odd_rows(tmp, rows))[:count]


def halved(values, even_only=False):
    count, rows, _ = values.shape
    flat = exact_dot(values.reshape(count * rows, LANES), compact(LANES, 0, even_only))
    return 0.25 * flat.reshape(count, rows, LANES)


def coarse_faces(own, faces, out, fine, tmp):
    x, y, z = coarse_slab_sums(own.at[2], own.at[3], own.at[4], own.shape[1] // 2, 0, fine)
    faces[0] = halved(x)
    faces[1] = halved(y)
    faces[2] = halved(z, True)
    rows = faces.shape[2]
    coarse = rows // 2
    fx, fy, fz = faces.at[0], faces.at[1], faces.at[2]
    tmp[...] = pair_slabs(fx)[0]
    x = even_rows(tmp, rows) + odd_rows(tmp, rows)
    first, second = pair_slabs(fy)
    tmp[...] = first + second
    y = even_rows(tmp, rows)
    first, second = pair_slabs(fz)
    tmp[...] = first + second
    z = even_rows(tmp, rows) + odd_rows(tmp, rows)
    out[...] = jnp.zeros(out.shape, F32)
    out[:coarse] = 0.25 * fold_four([x[i] for i in range(4)])
    out[coarse : 2 * coarse] = 0.25 * fold_four([y[i] for i in range(4)])
    out[2 * coarse : 3 * coarse] = 0.25 * fold_four([z[i] for i in range(4)], True)


def weighted(lev, src, slab, start, rows, f=None):
    here = pl.ds(start, rows)
    below = pl.ds(start - 1, rows)
    above = pl.ds(start + 1, rows)
    v = src[slab, here]
    f = lev.at[F] if f is None else f
    x = lev[FX, slab, here] * src[slab - 1, here] + lev[FX, slab + 1, here] * src[slab + 1, here]
    y = lev[FY, slab, here] * src[slab, below] + lev[FY, slab, above] * src[slab, above]
    z = lev[ZL, slab, here] * roll_lanes(v, 1) + lev[ZH, slab, here] * roll_lanes(v, -1)
    total = ((x + y) + f[slab, here]) + z
    return v, total


def swept(lev, src, slab, start, rows, f=None):
    v, total = weighted(lev, src, slab, start, rows, f)
    return (1.0 - OMEGA) * v + lev[W, slab, pl.ds(start, rows)] * total


def set_weights(lev, slab, start, rows, depth, inside=None):
    here = pl.ds(start, rows)
    fz = lev[ZL, slab, here]
    z = lanes_of(fz.shape) % depth
    upper = jnp.where(z == depth - 1, 0.0, roll_lanes(fz, -1))
    diagonal = lev[FX, slab, here] + lev[FX, slab + 1, here]
    diagonal = diagonal + lev[FY, slab, here] + lev[FY, slab, pl.ds(start + 1, rows)] + fz + upper
    valid = diagonal > 0.0
    if inside is not None:
        valid = valid & inside
    lev[ZL, slab, here] = jnp.where(z == 0, 0.0, fz)
    lev[ZH, slab, here] = upper
    lev[D, slab, here] = diagonal
    lev[W, slab, here] = jnp.where(valid, OMEGA / jnp.where(valid, diagonal, 1.0), 0.0)


def run(count, body):
    for index in range(count):
        body(index)


def clear_pads(ref, rows):
    for start in (0, RIM + rows):
        ref[:, start : start + RIM] = jnp.zeros((ref.shape[0], RIM, LANES), F32)


def level_down(axes, own, faces, coefficients, x_low, x_high, y_low, y_high, *refs):
    top, kept, chunk, v_low, v_high, other, tmp, one, two, mid, wide = refs
    nx, ny = own.shape[1:3]
    slabs, rows = nx + 2 * EDGE, ny + 2 * RIM
    me_x, me_y = lax.axis_index(axes[0]), lax.axis_index(axes[1])
    inner = pl.ds(PAD, ny)
    for index, slot in enumerate(SLOTS):
        layers, width = X_LAYERS[index], Y_LAYERS[index]
        top[slot, :, :PAD] = jnp.zeros((slabs, PAD, LANES), F32)
        top[slot, :, PAD + ny :] = jnp.zeros((slabs, PAD, LANES), F32)
        top[slot, EDGE : EDGE + nx, inner] = own[index]
        for layer in range(EDGE):
            if layer < layers:
                top[slot, EDGE - layers + layer, inner] = x_low[x_place(index, layer, ny)]
                top[slot, EDGE + nx + layer, inner] = x_high[x_place(index, layer, ny)]
            else:
                top[slot, EDGE - 1 - layer, inner] = jnp.zeros((ny, LANES), F32)
                top[slot, EDGE + nx + layer, inner] = jnp.zeros((ny, LANES), F32)
        for slab in range(-Y_REACH[index], nx + Y_REACH[index]):
            top[slot, EDGE + slab, PAD - width : PAD] = y_low[y_place(index, slab, nx)]
            top[slot, EDGE + slab, PAD + ny : PAD + ny + width] = y_high[y_place(index, slab, nx)]
    clear_pads(other, rows)

    coarse_x, coarse_y = nx // 2, ny // 2
    near = RIM - 1
    for slot in (FX, FY, ZL, ZH, W, D):
        mid[slot] = jnp.zeros(mid.shape[1:], F32)
    x, y, z = coarse_slab_sums(top.at[FX], top.at[FY], top.at[ZL], coarse_x + 2, EDGE - 2, wide)
    mid[FX, near : near + coarse_x + 3, RIM : 3 * RIM + coarse_y] = halved(x)
    mid[FY, near : near + coarse_x + 2, RIM : 3 * RIM + coarse_y] = halved(y)
    mid[ZL, near : near + coarse_x + 2, RIM : 3 * RIM + coarse_y] = halved(z, True)

    row_inside = (rows_of((rows, LANES)) >= RIM) | (me_y > 0)
    main = pl.ds(RIM, rows)
    start_v = top.at[V]

    def first(index):
        slab = index + 1
        inside = row_inside & ((slab >= EDGE) | (me_x > 0))
        set_weights(top, slab, RIM, rows, LANES, inside)
        other[slab, main] = swept(top, start_v, slab, RIM, rows)

    run(slabs - 2, first)

    def second(index):
        slab = index + 2
        top[V, slab, main] = swept(top, other, slab, RIM, rows)

    run(slabs - 4, second)

    def rest(slab):
        v, total = weighted(top, top.at[V], slab, PAD, ny)
        return total - top[D, slab, inner] * v

    def residual(index):
        slab = EDGE + 2 * index
        tmp[index] = rest(slab) + rest(slab + 1)

    run(nx // 2, residual)

    slabs, rows = coarse_x + 2 * RIM, coarse_y + 2 * RIM
    half = slabs // 2
    inner = pl.ds(2 * RIM, coarse_y)
    main = pl.ds(RIM, rows)
    row_inside = (rows_of((rows, LANES)) >= RIM) | (me_y > 0)
    for slab in range(near, near + coarse_x + 2):
        inside = row_inside & (me_x > 0) if slab < RIM else row_inside
        set_weights(mid, slab, RIM, rows, HALF, inside)

    source = even_rows(tmp, ny) + odd_rows(tmp, ny)
    source = 0.5 * exact_dot(source.reshape(coarse_x * coarse_y, LANES), compact(LANES, 0))
    for ref in (mid.at[F], mid.at[V], one):
        ref[...] = jnp.zeros(ref.shape, F32)
    mid[F, RIM : RIM + coarse_x, inner] = source.reshape(coarse_x, coarse_y, LANES)
    for slab in range(RIM, RIM + coarse_x):
        mid[V, slab, inner] = mid[W, slab, inner] * mid[F, slab, inner]
    for layer in range(RIM // 2):
        near, far = RIM + layer, coarse_x + layer
        v_low[layer * coarse_y : (layer + 1) * coarse_y] = two_in_one(
            mid[V, near, inner], mid[V, near + RIM // 2, inner]
        )
        v_high[layer * coarse_y : (layer + 1) * coarse_y] = two_in_one(
            mid[V, far, inner], mid[V, far + RIM // 2, inner]
        )
    kept[0] = mid[F, RIM : RIM + coarse_x, inner]
    kept[1] = mid[V, RIM : RIM + coarse_x, inner]
    base, after, _ = rim_rows_x(nx, ny)
    pairs = RIM // 2
    for face in range(3):
        for layer in range(pairs):
            place = pl.ds(base + after + (face * pairs + layer) * coarse_y, coarse_y)
            far = coarse_x - RIM + layer
            v_low[place] = two_in_one(faces[face, layer], faces[face, layer + pairs])
            v_high[place] = two_in_one(faces[face, far], faces[face, far + pairs])
    for layer in range(2):
        place = pl.ds(base + layer * ny, ny)
        v_low[place] = top[V, EDGE + layer, pl.ds(PAD, ny)]
        v_high[place] = top[V, EDGE + nx - 2 + layer, pl.ds(PAD, ny)]
    for slab in range(RIM - 1, RIM + coarse_x + 1):
        one[slab, main] = swept(mid, mid.at[V], slab, RIM, rows)

    def rest_1(slab):
        v, total = weighted(mid, one, slab, RIM, rows)
        return total - mid[D, slab, main] * v

    two[...] = jnp.zeros(two.shape, F32)
    for pair in range(1, half - 1):
        two[pair] = rest_1(2 * pair) + rest_1(2 * pair + 1)
    pieces = even_rows(two, rows) + odd_rows(two, rows)
    coarse_rows, quarter_rows = rows // 2, rows // 4
    chunk[:coarse_rows] = 0.5 * fold_four([pieces[1 + i] for i in range(4)])
    rest_of = [pieces[5 + i // 2][i % 2 * quarter_rows :][:quarter_rows] for i in range(4)]
    chunk[coarse_rows : coarse_rows + quarter_rows] = 0.5 * fold_four(rest_of)
    chunk[coarse_rows + quarter_rows :] = coefficients[:BLOCK_ROWS - coarse_rows - quarter_rows]
    block = me_x // (lax.axis_size(axes[0]) // 4)
    values = chunk[...]
    for turn in range(1, 4):
        chunk[...] = jnp.where(block == turn, roll_lanes(values, turn * (LANES // 4)), chunk[...])


def pack_v(top, kept, faces, x_low, x_high, low, high):
    coarse_x, coarse_y = faces.shape[1:3]
    nx, ny = 2 * coarse_x, 2 * coarse_y
    slabs = coarse_x + 2 * RIM
    half = slabs // 2
    sizes_x, sizes_y = rim_rows_x(nx, ny), rim_rows_y(nx, ny)

    def folded(own, place_x, place_y):
        values = [
            wide_slab(
                slab,
                lambda layer: rim_slab(x_low, place_x, coarse_y, layer),
                own,
                lambda layer: rim_slab(x_high, place_x, coarse_y, layer),
            )
            for slab in range(slabs)
        ]
        for slab in range(half):
            both = two_in_one(values[slab], values[slab + half])
            rows = pl.ds(place_y + slab * RIM, RIM)
            low[rows] = both[:RIM]
            high[rows] = both[coarse_y - RIM :]

    folded(kept.at[1], 0, 0)
    for face in range(3):
        folded(
            faces.at[face],
            sizes_x[0] + sizes_x[1] + face * sizes_x[0],
            sizes_y[0] + sizes_y[1] + face * sizes_y[0],
        )
    base_x, base_y = sizes_x[0], sizes_y[0]
    for out, start in ((low, 0), (high, ny - 2)):
        for layer in range(2):
            rows = pl.ds(base_x + layer * ny + start, 2)
            out[pl.ds(base_y + 2 * layer, 2)] = x_low[rows]
            out[pl.ds(base_y + 2 * (2 + nx + layer), 2)] = x_high[rows]
        for slab in range(nx):
            out[pl.ds(base_y + 2 * (2 + slab), 2)] = top[V, EDGE + slab, pl.ds(PAD + start, 2)]


def stack_blocks(*refs):
    for index, ref in enumerate(refs[:-1]):
        refs[-1][index] = ref[...]


def hand_on(first, second, _, first_out, second_out):
    first_out[...] = first[...]
    second_out[...] = second[...]


def pair_rows(values, stride):
    return values + roll_rows(values, -stride)


def pair_lanes(values, stride):
    return values + roll_lanes(values, -stride)


class Listed:
    def __init__(self, fx, fy, fz, stride, depth):
        self.fx, self.fy, self.fz, self.stride, self.depth = fx, fy, fz, stride, depth
        shape = fx[0].shape
        rows = shape[0]
        row, lane = rows_of(shape), lanes_of(shape)
        z = lane % depth
        count = self.count = len(fx)
        self.x_high = [
            fx[s + 1] if s + 1 < count else jnp.where(lane < LANES - depth, roll_lanes(fx[0], -depth), 0.0)
            for s in range(count)
        ]
        self.x_low = [fx[s] if s > 0 else jnp.where(lane >= depth, fx[0], 0.0) for s in range(count)]
        self.y_high = [jnp.where(row < rows - stride, roll_rows(f, -stride), 0.0) for f in fy]
        self.y_low = [jnp.where(row >= stride, f, 0.0) for f in fy]
        self.z_high = [jnp.where(z < depth - stride, roll_lanes(f, -stride), 0.0) for f in fz]
        self.z_low = [jnp.where(z >= stride, f, 0.0) for f in fz]
        self.d = [
            fx[s] + self.x_high[s] + fy[s] + self.y_high[s] + fz[s] + self.z_high[s] for s in range(count)
        ]
        self.w = [jnp.where(d > 0.0, OMEGA / jnp.where(d > 0.0, d, 1.0), 0.0) for d in self.d]

    def weighted(self, v, f):
        count = self.count
        out = []
        for s in range(count):
            low = v[s - 1] if s > 0 else roll_lanes(v[count - 1], self.depth)
            high = v[s + 1] if s + 1 < count else roll_lanes(v[0], -self.depth)
            x = self.x_low[s] * low + self.x_high[s] * high
            y = self.y_low[s] * roll_rows(v[s], self.stride) + self.y_high[s] * roll_rows(v[s], -self.stride)
            z = self.z_low[s] * roll_lanes(v[s], self.stride) + self.z_high[s] * roll_lanes(v[s], -self.stride)
            total = (f[s] + y) + (x + z)
            out.append(total)
        return out

    def sweep(self, v, f):
        totals = self.weighted(v, f)
        return [(1.0 - OMEGA) * v[s] + self.w[s] * totals[s] for s in range(self.count)]

    def sweeps(self, count, f):
        folded = [
            [w * c for w, c in zip(self.w, coefficients)]
            for coefficients in (self.x_low, self.x_high, self.y_low, self.y_high, self.z_low, self.z_high)
        ]
        scaled = self.start(f)
        slabs = self.count

        def step(index, v):
            out = []
            for s in range(slabs):
                low = v[s - 1] if s > 0 else roll_lanes(v[slabs - 1], self.depth)
                high = v[s + 1] if s + 1 < slabs else roll_lanes(v[0], -self.depth)
                x = folded[0][s] * low + folded[1][s] * high
                y = folded[2][s] * roll_rows(v[s], self.stride) + folded[3][s] * roll_rows(v[s], -self.stride)
                z = folded[4][s] * roll_lanes(v[s], self.stride) + folded[5][s] * roll_lanes(v[s], -self.stride)
                out.append((((1.0 - OMEGA) * v[s] + scaled[s]) + y) + (x + z))
            return out

        return lax.fori_loop(1, count, step, scaled)

    def start(self, f):
        return [self.w[s] * f[s] for s in range(self.count)]

    def residual(self, v, f):
        totals = self.weighted(v, f)
        return [totals[s] - self.d[s] * v[s] for s in range(self.count)]

    def kept(self):
        shape = self.fx[0].shape
        step = 2 * self.stride
        return (rows_of(shape) % step == 0) & (lanes_of(shape) % step == 0)

    def coarser(self):
        keep, stride = self.kept(), self.stride
        half = range(self.count // 2)

        def kept(values):
            return jnp.where(keep, 0.25 * values, 0.0)

        fx = [kept(pair_lanes(pair_rows(self.fx[2 * s], stride), stride)) for s in half]
        fy = [kept(pair_lanes(self.fy[2 * s] + self.fy[2 * s + 1], stride)) for s in half]
        fz = [kept(pair_rows(self.fz[2 * s] + self.fz[2 * s + 1], stride)) for s in half]
        return Listed(fx, fy, fz, 2 * stride, self.depth)

    def restrict(self, r):
        keep, stride = self.kept(), self.stride
        return [
            jnp.where(keep, 0.5 * pair_lanes(pair_rows(r[2 * s] + r[2 * s + 1], stride), stride), 0.0)
            for s in range(self.count // 2)
        ]

    def prolong(self, e):
        out = []
        for values in e:
            values = values + roll_rows(values, self.stride)
            values = values + roll_lanes(values, self.stride)
            out += [values, values]
        return out


def listed_cycle(levels, sweeps, f):
    level = levels[0]
    if len(levels) == 1:
        return level.sweeps(sweeps, f)
    v = level.sweep(level.start(f), f)
    e = listed_cycle(levels[1:], sweeps, level.restrict(level.residual(v, f)))
    v = [a + b for a, b in zip(v, level.prolong(e))]
    return level.sweep(level.sweep(v, f), f)


def level_two(axes, grid, sweeps, shape, pieces, out, wide, tall):
    devices_x, devices_y = grid
    me_x, me_y = lax.axis_index(axes[0]), lax.axis_index(axes[1])
    own_x, own_y = shape
    quarter = LANES // 4
    reach = RIM // 2
    blocks = 4
    count = devices_x * own_x // blocks
    rows = devices_y * own_y
    main = pl.ds(PAD, rows)
    window = own_y + RIM

    def piece(gx, gy):
        slow, far = (me_x // 2) ^ (gx // 2), (me_y // 2) ^ (gy // 2)
        return ((me_y + gy) % 2, (me_x + gx) % 2 * (devices_y // 2) + far, slow)

    tall[...] = jnp.zeros(tall.shape, F32)
    per_block = count // own_x

    def merged(values, shift, turn):
        at = lanes_of(values[0].shape) // quarter
        out = values[0]
        for block in range(1, blocks):
            out = jnp.where(at == (shift + block) % blocks, values[block], out)
        return roll_lanes(out, (turn - shift) * quarter)

    lane = lanes_of((window, LANES))
    for gy in range(devices_y):
        sums = [None] * count
        for turn in range(per_block):
            where = [piece(block * per_block + turn, gy) for block in range(blocks)]
            first = [pieces[at + (pl.ds(0, window),)] for at in where]
            second = [pieces[at + (pl.ds(window, window // 2),)] for at in where]
            for local in range(1, 2 * blocks - 1):
                offset = own_x * turn - reach + local
                over, slab = offset // count, offset % count
                if local <= blocks:
                    moved = merged(first, local - 1, over)
                else:
                    at = 2 * (local - blocks - 1)
                    moved = jnp.concatenate([merged(second, at + odd, over) for odd in range(2)])
                if over < 0:
                    moved = jnp.where(lane // quarter == blocks - 1, 0.0, moved)
                elif over > 0:
                    moved = jnp.where(lane // quarter == 0, 0.0, moved)
                sums[slab] = moved if sums[slab] is None else sums[slab] + moved
        place = pl.ds(PAD + own_y * gy - reach, window)
        for slab in range(count):
            tall[slab, place] = tall[slab, place] + sums[slab]
    f = [tall[slab, main] for slab in range(count)]

    lane = lanes_of((rows, LANES))
    for gx in range(devices_x):
        for gy in range(devices_y):
            where = piece(gx, gy)
            for face in range(3):
                values = pieces[where + (pl.ds(window + window // 2 + face * own_y, own_y),)]
                wide[face, gx, gy * own_y : (gy + 1) * own_y] = values
    faces = []
    for face in range(3):
        slabs = []
        for turn in range(per_block):
            values = [wide[face, block * per_block + turn] for block in range(blocks)]
            slabs += [merged(values, local, 0) for local in range(own_x)]
        faces.append(slabs)
    levels = [Listed(*faces, 1, quarter)]
    while len(levels) < LEVELS - 2:
        levels.append(levels[-1].coarser())
    e = listed_cycle(levels, sweeps, f)

    for slab in range(count):
        out[reach + slab, main] = e[slab]
    for slab in range(reach):
        out[slab, main] = jnp.where(lane < quarter, 0.0, roll_lanes(e[count - reach + slab], quarter))
        out[reach + count + slab, main] = jnp.where(
            lane >= LANES - quarter, 0.0, roll_lanes(e[slab], -quarter)
        )
    out[:, :PAD] = jnp.zeros((count + 2 * reach, PAD, LANES), F32)
    out[:, PAD + rows :] = jnp.zeros((count + 2 * reach, PAD, LANES), F32)


def level_up(axes, grid, coarse, top, kept, faces, x_low, x_high, y_low, y_high, *refs):
    out, mid, one, two, right, post, up = refs
    devices_x, devices_y = grid
    me_x, me_y = lax.axis_index(axes[0]), lax.axis_index(axes[1])
    coarse_x, coarse_y = faces.shape[1:3]
    nx, ny = out.shape[:2]
    own_x, own_y = coarse_x // 2, coarse_y // 2
    quarter = LANES // 4
    reach = RIM // 2
    window = own_y + RIM

    slabs, high = coarse_x + 2 * RIM, coarse_y + 2 * RIM
    half = slabs // 2
    inner = pl.ds(2 * RIM, coarse_y)
    body = pl.ds(RIM, high)
    sizes_x, sizes_y = rim_rows_x(nx, ny), rim_rows_y(nx, ny)
    for face, slot in enumerate((FX, FY, ZL)):
        clear_pads(mid.at[slot], high)
        mid[slot, RIM : RIM + coarse_x, inner] = faces[face]
        place_x = sizes_x[0] + sizes_x[1] + face * sizes_x[0]
        place_y = sizes_y[0] + sizes_y[1] + face * sizes_y[0]
        for layer in range(RIM):
            mid[slot, layer, inner] = rim_slab(x_low, place_x, coarse_y, layer)
            mid[slot, RIM + coarse_x + layer, inner] = rim_slab(x_high, place_x, coarse_y, layer)
        for slab in range(half):
            place = pl.ds(place_y + slab * RIM, RIM)
            for message, row in ((y_low, RIM), (y_high, 2 * RIM + coarse_y)):
                pair = one_of_two(message[place])
                mid[slot, slab, row : row + RIM] = pair[0]
                mid[slot, slab + half, row : row + RIM] = pair[1]
    row_inside = (rows_of((high, LANES)) >= RIM) | (me_y > 0)
    for slab in range(slabs - 1):
        inside = row_inside & (me_x > 0) if slab < RIM else row_inside
        set_weights(mid, slab, RIM, high, HALF, inside)
    clear_pads(one, high)
    clear_pads(right, high)
    clear_pads(two, high)
    one[RIM : RIM + coarse_x, inner] = kept[1]
    right[RIM : RIM + coarse_x, inner] = kept[0]
    for layer in range(RIM):
        one[layer, inner] = rim_slab(x_low, 0, coarse_y, layer)
        one[RIM + coarse_x + layer, inner] = rim_slab(x_high, 0, coarse_y, layer)
    for slab in range(half):
        place = pl.ds(slab * RIM, RIM)
        for message, row in ((y_low, RIM), (y_high, 2 * RIM + coarse_y)):
            pair = one_of_two(message[place])
            one[slab, row : row + RIM] = pair[0]
            one[slab + half, row : row + RIM] = pair[1]
    row = rows_of((high, LANES))
    own_row = (row >= RIM) & (row < RIM + coarse_y)
    for slab in range(1, slabs - 1):
        f_rim = one[slab, body] * mid[D, slab, body] * (1.0 / OMEGA)
        if RIM <= slab < RIM + coarse_x:
            f_rim = jnp.where(own_row, right[slab, body], f_rim)
        right[slab, body] = f_rim
        two[slab, body] = swept(mid, one, slab, RIM, high, right)

    per_block = (coarse.shape[0] - 2 * reach) // own_x
    base = me_x % per_block * own_x
    mine = None
    for gy in range(devices_y):
        place = pl.ds(PAD + gy * own_y - reach, window)
        values = jnp.where(me_y == gy, coarse[pl.ds(base, half), place, :], 0.0)
        mine = values if mine is None else mine + values
    source = lax.broadcasted_iota(jnp.int32, (LANES, LANES), 0)
    target = lax.broadcasted_iota(jnp.int32, (LANES, LANES), 1)
    hit = (source == me_x // per_block * quarter + target // 2) & (target < HALF)
    fine = exact_dot(mine.reshape(half * window, LANES), jnp.where(hit, 1.0, 0.0).astype(F32))
    fine = fine.reshape(half, window, LANES)
    for odd in range(2):
        up[:half, pl.ds(odd, window, stride=2), :] = fine
    for pair in range(half):
        for slab in (2 * pair, 2 * pair + 1):
            if 1 <= slab < slabs - 1:
                two[slab, body] = two[slab, body] + up[pair, :high]
    for slab in range(2, slabs - 2):
        one[slab, body] = swept(mid, two, slab, RIM, high, right)
    for slab in range(3, slabs - 3):
        two[slab, body] = swept(mid, one, slab, RIM, high, right)

    steps = coarse_x + 2
    fine_rows = ny + 2 * RIM
    e = two[RIM - 1 : RIM - 1 + steps, body]
    fine = exact_dot(e.reshape(steps * high, LANES), expand(LANES, 0)).reshape(steps, high, LANES)
    fine = fine[:, reach : reach + fine_rows // 2]
    for odd in range(2):
        up[:, pl.ds(odd, fine_rows // 2, stride=2), :] = fine
    body = pl.ds(RIM, fine_rows)
    for slot in (0, 1):
        clear_pads(post.at[slot], fine_rows)
    inner = pl.ds(PAD, ny)
    post[0, EDGE : EDGE + nx, inner] = top[V, EDGE : EDGE + nx, inner]
    base_x, base_y = RIM // 2 * coarse_y, half * RIM
    for layer in range(2):
        place = pl.ds(base_x + layer * ny, ny)
        post[0, EDGE - 2 + layer, inner] = x_low[place]
        post[0, EDGE + nx + layer, inner] = x_high[place]
    for slab in range(nx + 4):
        place = pl.ds(base_y + 2 * slab, 2)
        post[0, slab + EDGE - 2, RIM:PAD] = jnp.zeros((RIM, LANES), F32)
        post[0, slab + EDGE - 2, PAD + ny : PAD + ny + RIM] = jnp.zeros((RIM, LANES), F32)
        post[0, slab + EDGE - 2, PAD - 2 : PAD] = y_low[place]
        post[0, slab + EDGE - 2, PAD + ny : PAD + ny + 2] = y_high[place]

    def raise_level(index):
        for slab in (EDGE - 2 + 2 * index, EDGE - 1 + 2 * index):
            post[0, slab, body] = post[0, slab, body] + up[index]

    run(steps, raise_level)

    def fifth(index):
        slab = EDGE - 1 + index
        post[1, slab, body] = swept(top, post.at[0], slab, RIM, fine_rows)

    run(nx + 2, fifth)

    def sixth(index):
        out[index] = swept(top, post.at[1], EDGE + index, PAD, ny)

    run(nx, sixth)


IN_VMEM = pl.BlockSpec(memory_space=pltpu.VMEM)


def call(kernel, outs, scratch=(), from_hbm=False):
    ins = pl.BlockSpec(memory_space=pl.ANY) if from_hbm else IN_VMEM

    def launch(*args):
        if from_hbm:
            args = [pltpu.with_memory_space_constraint(arg, pltpu.HBM) for arg in args]
        return pl.pallas_call(
            kernel,
            out_shape=[pltpu.VMEM(shape, F32) for shape in outs],
            in_specs=[ins] * len(args),
            out_specs=[IN_VMEM] * len(outs),
            scratch_shapes=[pltpu.VMEM(s, F32) if isinstance(s, tuple) else s for s in scratch],
            compiler_params=pltpu.CompilerParams(vmem_limit_bytes=24 * 2**20),
        )(*args)

    return launch


def pair_route(axis):
    return [(i, i ^ 1) for i in range(lax.axis_size(axis))]


def swap_route(axis):
    count = lax.axis_size(axis)
    return [(i, (i + 1 ^ 1) - 1) for i in range(1, count - 1)]


def by_partner(low, high, axis):
    odd = lax.axis_index(axis) % 2 == 1
    return jnp.where(odd, low, high), jnp.where(odd, high, low)


def from_sides(low, high, axis):
    pair, swap = by_partner(low, high, axis)
    pair = lax.ppermute(pair, axis, pair_route(axis))
    swap = lax.ppermute(swap, axis, swap_route(axis))
    return by_partner(pair, swap, axis)


def passed_round(block, axis, stride):
    count = lax.axis_size(axis)
    return [block] + [
        lax.ppermute(block, axis, [(i, i ^ distance) for i in range(count)])
        for distance in range(stride, count, stride)
    ]


def passed_across(block, rider):
    count, size = lax.axis_size("gx"), lax.axis_size("gy")
    rows = block.shape[0]
    blocks = [block]
    for side in range(2):
        for distance in range(0, size, 2):
            route = [
                (x * size + y, (x ^ side) * size + (y ^ distance)) for x in range(count) for y in range(size)
            ]
            if side == 1 and distance == 0:
                both = lax.ppermute(jnp.concatenate((block, rider)), ("gx", "gy"), route)
                blocks.append(both[:rows])
                rider = both[rows:]
            elif distance > 0:
                blocks.append(lax.ppermute(block, ("gx", "gy"), route))
    return blocks, rider


def fused_cycle(*fields):
    axes = ("gx", "gy")
    devices_x, devices_y = lax.axis_size("gx"), lax.axis_size("gy")
    nx, ny, nz = fields[0].shape
    coarse_x, coarse_y = nx // 2, ny // 2
    x_shape, y_shape = (x_rows(nx, ny), LANES), (y_rows(nx, ny), LANES)
    own, x_low, x_high = call(
        start_pack, [(5, nx, ny, nz), x_shape, x_shape], [pltpu.SemaphoreType.DMA((5,))], True
    )(*fields)
    x_low, x_high = from_sides(x_low, x_high, "gx")
    faces, coefficients = call(
        coarse_faces,
        [(3, coarse_x, coarse_y, LANES), (16, LANES)],
        [(coarse_x, ny, LANES), (coarse_x // 2, coarse_y, LANES)],
    )(own)
    y_low, y_high = call(pack_y, [y_shape] * 2)(own, x_low, x_high)
    y_low, y_high = from_sides(y_low, y_high, "gy")
    stack = (nx + 2 * EDGE, ny + 4 * RIM, LANES)
    stack_1 = (coarse_x + 2 * RIM, coarse_y + 4 * RIM, LANES)
    half = stack_1[0] // 2
    v_shape = (sum(rim_rows_x(nx, ny)), LANES)
    w_shape = (sum(rim_rows_y(nx, ny)), LANES)
    top, kept, chunk, v_low, v_high = call(
        functools.partial(level_down, axes),
        [(D + 1,) + stack, (2, coarse_x, coarse_y, LANES), (BLOCK_ROWS, LANES), v_shape, v_shape],
        [
            stack,
            (nx // 2, ny, LANES),
            stack_1,
            (half, coarse_y + 2 * RIM, LANES),
            (D + 1,) + stack_1,
            (coarse_x + 3,) + stack[1:],
        ],
    )(own, faces, coefficients, x_low, x_high, y_low, y_high)

    blocks = passed_round(chunk, "gx", 2)
    slow = (len(blocks),) + chunk.shape
    (pieces,) = call(stack_blocks, [slow])(*blocks)
    v_low, v_high = call(hand_on, [v_shape, v_shape])(v_low, v_high, pieces)
    pair, swap = by_partner(v_low, v_high, "gx")
    swap = lax.ppermute(swap, "gx", swap_route("gx"))
    blocks, pair = passed_across(pieces.reshape(-1, LANES), pair)
    v_low, v_high = by_partner(pair, swap, "gx")
    w_low, w_high = call(pack_v, [w_shape] * 2)(top, kept, faces, v_low, v_high)
    pair, swap = by_partner(w_low, w_high, "gy")
    message = jnp.concatenate(blocks + [pair])
    swap = lax.ppermute(swap, "gy", swap_route("gy"))
    other = lax.ppermute(message, "gy", pair_route("gy"))
    rows = message.shape[0] - w_shape[0]
    pieces = jnp.stack((message[:rows], other[:rows])).reshape((2, len(blocks)) + slow)
    w_low, w_high = by_partner(other[rows:], swap, "gy")
    count = devices_x * nx // 16
    rows = devices_y * ny // 4
    grid = (devices_x, devices_y)
    coarsest = (devices_x * nx >> LEVELS - 1, devices_y * ny >> LEVELS - 1)
    wide = (count + RIM, rows + 2 * PAD, LANES)
    (coarse,) = call(
        functools.partial(level_two, axes, grid, 4 * max(coarsest), (nx // 4, ny // 4)),
        [wide],
        [(3, devices_x, rows, LANES), wide],
    )(pieces)
    return pl.pallas_call(
        functools.partial(level_up, axes, grid),
        out_shape=jax.ShapeDtypeStruct((nx, ny, nz), F32),
        in_specs=[IN_VMEM] * 8,
        out_specs=IN_VMEM,
        scratch_shapes=[
            pltpu.VMEM(shape, F32)
            for shape in ((D + 1,) + stack_1, stack_1, stack_1, stack_1, (2,) + stack, (coarse_x + 2, ny + 2 * RIM, LANES))
        ],
        compiler_params=pltpu.CompilerParams(vmem_limit_bytes=24 * 2**20),
    )(coarse, top, kept, faces, v_low, v_high, w_low, w_high)


def with_halo(block, sides, width):
    for axis, dim in sides:
        count = lax.axis_size(axis)
        forward = [(i, i + 1) for i in range(count - 1)]
        backward = [(target, source) for source, target in forward]
        low = lax.ppermute(
            lax.slice_in_dim(block, block.shape[dim] - width, None, axis=dim), axis, forward
        )
        high = lax.ppermute(lax.slice_in_dim(block, 0, width, axis=dim), axis, backward)
        block = jnp.concatenate([low, block, high], axis=dim)
    return block


def passed_along(block, axis, distance):
    devices = range(lax.axis_size(axis))
    route = [(i - distance, i) for i in devices if i - distance in devices]
    return lax.ppermute(block, axis, route)


def stencil(padded, padded_x, padded_y, face_z):
    center = padded[1:-1, 1:-1]
    zero_plane = jnp.zeros(center.shape[:2] + (1,), center.dtype)
    above_face = jnp.concatenate((face_z[:, :, 1:], zero_plane), axis=2)
    below_z = jnp.concatenate((zero_plane, center[:, :, :-1]), axis=2)
    above_z = jnp.concatenate((center[:, :, 1:], zero_plane), axis=2)
    lower_x = padded_x[1:-1, 1:-1]
    upper_x = padded_x[2:, 1:-1]
    lower_y = padded_y[1:-1, 1:-1]
    upper_y = padded_y[1:-1, 2:]
    applied = lower_x * (center - padded[:-2, 1:-1]) + upper_x * (center - padded[2:, 1:-1])
    applied = (
        applied + lower_y * (center - padded[1:-1, :-2]) + upper_y * (center - padded[1:-1, 2:])
    )
    applied = applied + face_z * (center - below_z) + above_face * (center - above_z)
    diagonal = lower_x + upper_x + lower_y + upper_y + face_z + above_face
    return (applied, diagonal)


def jacobi_sweep(padded, source, padded_x, padded_y, face_z):
    applied, diagonal = stencil(padded, padded_x, padded_y, face_z)
    return padded[1:-1, 1:-1] + OMEGA * (source - applied) / diagonal


def pad_plane(values, width):
    return jnp.pad(values, ((width, width), (width, width), (0, 0)))


def restrict(residual):
    shape = residual.shape
    blocks = residual.reshape(shape[0] // 2, 2, shape[1] // 2, 2, shape[2] // 2, 2)
    return 4.0 * jnp.mean(blocks, axis=(1, 3, 5))


def coarsen_faces(face_x, face_y, face_z):
    shape = face_x.shape
    blocks = (shape[0] // 2, 2, shape[1] // 2, 2, shape[2] // 2, 2)
    coarse_x = jnp.mean(face_x.reshape(blocks)[:, 0], axis=(2, 4))
    coarse_y = jnp.mean(face_y.reshape(blocks)[:, :, :, 0], axis=(1, 4))
    coarse_z = jnp.mean(face_z.reshape(blocks)[..., 0], axis=(1, 3))
    return (coarse_x, coarse_y, coarse_z)


def prolong(coarse):
    return jnp.repeat(jnp.repeat(jnp.repeat(coarse, 2, axis=0), 2, axis=1), 2, axis=2)


def local_cycle(grid_level, iterate, source, face_x, face_y, face_z):
    padded_x = pad_plane(face_x, 1)
    padded_y = pad_plane(face_y, 1)
    if grid_level == LEVELS - 1:
        count = 4 * max(iterate.shape[0], iterate.shape[1])

        def one_sweep(index, values):
            return jacobi_sweep(pad_plane(values, 1), source, padded_x, padded_y, face_z)

        return lax.fori_loop(0, count, one_sweep, iterate)
    for sweep_index in range(2):
        iterate = jacobi_sweep(pad_plane(iterate, 1), source, padded_x, padded_y, face_z)
    applied, diagonal = stencil(pad_plane(iterate, 1), padded_x, padded_y, face_z)
    coarse_src = restrict(source - applied)
    coarse_x, coarse_y, coarse_z = coarsen_faces(face_x, face_y, face_z)
    correction = local_cycle(
        grid_level + 1, jnp.zeros_like(coarse_src), coarse_src, coarse_x, coarse_y, coarse_z
    )
    iterate = iterate + prolong(correction)
    for sweep_index in range(2):
        iterate = jacobi_sweep(pad_plane(iterate, 1), source, padded_x, padded_y, face_z)
    return iterate


def field_rim(iterate):
    return with_halo(iterate, (("gx", 0), ("gy", 1)), 1)


def sweep_pair_narrow(iterate, source, padded_x, padded_y, face_z, zero_start):
    for sweep_index in range(2):
        if sweep_index == 0 and zero_start:
            padded = pad_plane(iterate, 1)
        else:
            padded = field_rim(iterate)
        iterate = jacobi_sweep(padded, source, padded_x, padded_y, face_z)
    return iterate


def descend(grid_level, iterate, source, face_x, face_y, face_z, zero_start, gather_level):
    if grid_level == gather_level:
        pieces = (
            lax.all_gather(source, "gy", axis=1, tiled=True),
            lax.all_gather(face_x, "gy", axis=1, tiled=True),
            lax.all_gather(face_y, "gy", axis=1, tiled=True),
            lax.all_gather(face_z, "gy", axis=1, tiled=True),
        )
        gathered = (
            lax.all_gather(pieces[0], "gx", axis=0, tiled=True),
            lax.all_gather(pieces[1], "gx", axis=0, tiled=True),
            lax.all_gather(pieces[2], "gx", axis=0, tiled=True),
            lax.all_gather(pieces[3], "gx", axis=0, tiled=True),
        )
        correction = local_cycle(
            grid_level,
            jnp.zeros_like(gathered[0]),
            gathered[0],
            gathered[1],
            gathered[2],
            gathered[3],
        )
        start_x = lax.axis_index("gx") * source.shape[0]
        start_y = lax.axis_index("gy") * source.shape[1]
        return lax.dynamic_slice(
            correction, (start_x, start_y, jnp.zeros((), jnp.int32)), source.shape
        )
    next_x = passed_along(face_x[:1], "gx", -1)
    next_y = passed_along(face_y[:, :1], "gy", -1)
    lower_row = jnp.zeros_like(next_x)
    lower_col = jnp.zeros_like(next_y)
    padded_x = jnp.pad(
        jnp.concatenate((lower_row, face_x, next_x), axis=0), ((0, 0), (1, 1), (0, 0))
    )
    padded_y = jnp.pad(
        jnp.concatenate((lower_col, face_y, next_y), axis=1), ((1, 1), (0, 0), (0, 0))
    )

    def smoother(values, starting):
        return sweep_pair_narrow(values, source, padded_x, padded_y, face_z, starting)

    iterate = smoother(iterate, zero_start)
    applied, diagonal = stencil(field_rim(iterate), padded_x, padded_y, face_z)
    coarse_src = restrict(source - applied)
    coarse_x, coarse_y, coarse_z = coarsen_faces(face_x, face_y, face_z)
    correction = descend(
        grid_level + 1,
        jnp.zeros_like(coarse_src),
        coarse_src,
        coarse_x,
        coarse_y,
        coarse_z,
        True,
        gather_level,
    )
    iterate = iterate + prolong(correction)
    return smoother(iterate, False)


def fits(nx, ny, nz, devices_x, devices_y):
    cells = devices_x * nx * devices_y * ny * nz // 8
    even = devices_x % 8 == 0 and devices_y % 4 == 0
    even = even and devices_x & (devices_x - 1) == 0 and devices_y & (devices_y - 1) == 0
    return cells <= 2**18 and even and (nx, ny, nz) == (16, 16, LANES)


def local(source_term, initial_guess, face_x, face_y, face_z):
    if fits(*source_term.shape, lax.axis_size("gx"), lax.axis_size("gy")):
        return fused_cycle(source_term, initial_guess, face_x, face_y, face_z)
    gather_level = 4
    return descend(0, initial_guess, source_term, face_x, face_y, face_z, False, gather_level)


def solution(mesh):
    placed = (P("gx", "gy", None),) * 5
    return jax.shard_map(
        local, mesh=mesh, in_specs=placed, out_specs=P("gx", "gy", None), check_vma=False
    )
```
